32 devices in a mesh: wide: 16 (over z, y, x), narrow: 2 (over core).
Axes of the slice: x: 2, y: 2, z: 4, core: 2. Of those that a mesh axis runs over, the one named last changes fastest.
Arguments:
- inputs: bfloat16 [1536, 6528], P(('wide', 'narrow')), may hold values from -6 to 6
- cotangent: bfloat16 [1536, 6528], P(('wide', 'narrow')), may hold values from -6 to 6
- master: float32 [296960], P('wide'), may hold values from -1.5 to 1.5, as said below
- first: float32 [296960], P('wide'), may hold values from -0.02734375 to 0.02734375
- second: float32 [296960], P('wide'), may hold values from 1.6837284e-06 to 2.6939655e-05
Outputs:
- block_out: bfloat16 [1536, 6528], P(('wide', 'narrow'))
- input_grad: float32 [1536, 6528], P(('wide', 'narrow'))
- clipped_grad: float32 [296960], P('wide')
- grad_norm: float32 [], replicated
- new_master: float32 [296960], P('wide')
- new_copy: bfloat16 [296960], P('wide')
- new_first: float32 [296960], P('wide')
- new_second: float32 [296960], P('wide')
The draws below stay inside these ranges and needn't reach their ends.
Inputs may be any that keep to these rules, and one draw needn't show every extreme that they name: master holds weights, gains near one and biases of a few tenths.
All inputs are finite; a program needn't handle non-finite values.
Results may differ from the reference program's by a relative error of at most 0.012.
The reference program's roundings to bfloat16 on the way count: a program that leaves them out, or rounds other values in their place, can miss the bound.
Values sent between devices are 32-bit elements; how exact they have to be, the bound alone decides.
A program may use at most 128 MiB of HBM per device.

```python
import math
import jax
import jax.numpy as jnp
from jax import lax

D = 192
HEADS = 8
HEAD_DIM = 24
FF = 256
SEQ = 34
STEP = 5
SAMP_DEV = 48
SAMPLES = 1536
USED = 296960
PARAMS = 296960


def draw_master(key, part):
    key = jax.random.fold_in(key, 11)

    def piece(index, count, scale):
        return jax.random.uniform(jax.random.fold_in(key, index), (count,), jnp.float32, -1.0, 1.0) * (scale * math.sqrt(3.0))

    def gains(index):
        return 1.0 + jax.random.uniform(jax.random.fold_in(key, index), (D,), jnp.float32, -0.5, 0.5)
    parts_list = [piece(1, D * D, D ** (-0.5)), piece(2, D * D, D ** (-0.5)), piece(3, D * D, D ** (-0.5)), piece(4, D * D, 4.0 * D ** (-0.5)), piece(5, 2 * D * FF, D ** (-0.5)), piece(6, FF * D, 2.0 * FF ** (-0.5)), gains(7), piece(8, D, 0.4), piece(9, D, 0.4), piece(10, D, 0.4), piece(12, D, 0.4), gains(13), piece(14, D, 0.4), piece(15, D, 0.4), piece(16, 2 * FF, 0.4), piece(17, PARAMS - USED, 0.05)]
    return jnp.concatenate(parts_list)


def block_levels(rng, shape, pieces, smallest, high):
    factor_of = 1.0
    for position, shards_of in pieces:
        steps = jax.random.uniform(jax.random.fold_in(jax.random.fold_in(rng, 6), position), (shards_of,), jnp.float32, smallest / len(pieces), high / len(pieces))
        factor_of = factor_of * jnp.repeat(jnp.exp(steps), shape[position] // shards_of).reshape((-1,) + (1,) * (len(shape) - 1 - position))
    return factor_of


def scatter_about(own_key, dims, scale, most, pieces=(), dtype=jnp.bfloat16):
    array = scale * jax.random.normal(own_key, dims, jnp.float32)
    if pieces:
        array = array * block_levels(own_key, dims, pieces, -0.22, 0.18)
    return jnp.clip(array, -most, most).astype(dtype)


def setup_inputs(seed: int = 0) -> dict:
    keys = jax.random.split(jax.random.key(seed), 6)
    return {
        "inputs": scatter_about(keys[0], (SAMPLES, SEQ * D), 1.0, 6.0, ((0, 32),)),
        "cotangent": scatter_about(keys[1], (SAMPLES, SEQ * D), 1.0, 6.0, ((0, 32),)),
        "master": draw_master(jax.random.fold_in(keys[5], 71), 0),
        "first": scatter_about(keys[3], (PARAMS,), (USED ** -0.5), 0.02734375, ((0, 16),), jnp.float32),
        "second": jnp.clip(jnp.exp(math.log(2.6939655072055757e-05) - 2.7725887 * jax.random.uniform(keys[4], (PARAMS,), jnp.float32) ** block_levels(keys[4], (PARAMS,), ((0, 16),), -0.2, 0.2)), 1.6837284420034848e-06, 2.6939655072055757e-05),
    }


@jax.custom_vjp
def low(v):
    return lax.optimization_barrier(v.astype(jnp.bfloat16)).astype(jnp.float32)

@jax.custom_vjp
def low_back(v):
    return v

def low_keep(v):
    return (low(v), None)

def low_pass(kept, grad):
    return (grad,)

def back_keep(v):
    return (v, None)

def back_low(kept, grad):
    return (low(grad),)
low.defvjp(low_keep, low_pass)
low_back.defvjp(back_keep, back_low)
highest = lax.Precision.HIGHEST

def layer_norm(value, gain, shift):
    center = value - lax.optimization_barrier(jnp.mean(value, -1, keepdims=True))
    spread = lax.optimization_barrier(jnp.mean(center * center, -1, keepdims=True))
    return center * lax.rsqrt(spread + 1e-05) * gain + shift

def forward(flat, rows):
    size = D * D
    mat_end = 4 * size + 3 * D * FF
    wq = low(flat[0:size]).reshape(D, D)
    wk = low(flat[size:2 * size]).reshape(D, D)
    wv = low(flat[2 * size:3 * size]).reshape(D, D)
    wo = low(flat[3 * size:4 * size]).reshape(D, D)
    w_one = low(flat[4 * size:4 * size + 2 * D * FF]).reshape(D, 2 * FF)
    w_two = low(flat[4 * size + 2 * D * FF:mat_end]).reshape(FF, D)
    vecs = flat[mat_end:mat_end + 8 * D]
    g1, n1, bq, bv, bo, g2, n2, b2 = [vecs[i * D:(i + 1) * D] for i in range(8)]
    b1 = flat[mat_end + 8 * D:mat_end + 8 * D + 2 * FF]
    count = rows.shape[0]
    x = rows.reshape(count, SEQ, D)
    h = low(layer_norm(x, g1, n1))
    q = low(low_back(jnp.einsum('bsd,de->bse', h, wq, precision=highest) + bq)).reshape(count, SEQ, HEADS, HEAD_DIM)
    k = low(low_back(jnp.einsum('bsd,de->bse', h, wk, precision=highest))).reshape(count, SEQ, HEADS, HEAD_DIM)
    v = low(low_back(jnp.einsum('bsd,de->bse', h, wv, precision=highest) + bv)).reshape(count, SEQ, HEADS, HEAD_DIM)
    s = low_back(jnp.einsum('bqhe,bkhe->bhqk', q, k, precision=highest) * (1.0 / math.sqrt(HEAD_DIM)))
    p = low(jax.nn.softmax(s, -1))
    o = low(low_back(jnp.einsum('bhqk,bkhe->bqhe', p, v, precision=highest))).reshape(count, SEQ, D)
    a = low_back(jnp.einsum('bsd,de->bse', o, wo, precision=highest) + bo)
    x2 = x + a
    h2 = low(layer_norm(x2, g2, n2))
    u = low_back(jnp.einsum('bsd,de->bse', h2, w_one, precision=highest) + b1)
    z = low(jax.nn.gelu(u[..., :FF]) * u[..., FF:])
    y = x2 + jnp.einsum('bsf,fd->bsd', z, w_two, precision=highest) + b2
    return y.reshape(count, SEQ * D)

def reference(inputs, cotangent, master, first, second):
    blocks = SAMPLES // SAMP_DEV
    rows_in = inputs.astype(jnp.float32).reshape(blocks, SAMP_DEV, SEQ * D)
    rows_back = cotangent.astype(jnp.float32).reshape(blocks, SAMP_DEV, SEQ * D)

    def one_block(total, pair):
        block_in, block_back = pair
        out, pull = jax.vjp(forward, master, block_in)
        flat_grad, in_grad = pull(block_back)
        return (total + flat_grad, (out.astype(jnp.bfloat16), in_grad))
    total, (outs, in_grads) = lax.scan(one_block, jnp.zeros((PARAMS,), jnp.float32), (rows_in, rows_back))
    grad_norm = jnp.sqrt(jnp.sum(total * total))
    factor = jnp.minimum(1.0, 1.0 / (grad_norm + 1e-06))
    clipped = total * factor
    new_first = 0.5 * first + 0.5 * clipped
    new_second = 0.5 * second + 0.5 * clipped * clipped
    fixed_one = 1.0 - 0.5 ** STEP
    fixed_two = 1.0 - 0.5 ** STEP
    new_master = master - 0.05 * (new_first / fixed_one / (jnp.sqrt(new_second / fixed_two) + 1e-08) + 0.1 * master)
    return (outs.reshape(SAMPLES, SEQ * D), in_grads.reshape(SAMPLES, SEQ * D), clipped, grad_norm, new_master, new_master.astype(jnp.bfloat16), new_first, new_second)
```

```python
import functools
import math

import jax
import jax.numpy as jnp
from jax import lax
from jax.experimental import pallas as pl
from jax.experimental.pallas import tpu as pltpu
from jax.sharding import PartitionSpec as P

D = 192
HEADS = 8
HEAD_DIM = 24
FF = 256
SEQ = 34
STEP = 5
ROWS = 40
GROUP = 3
GROWS = GROUP * ROWS
HJ = HEADS * ROWS
LANES = 128
F32 = jnp.float32
BF16 = jnp.bfloat16
MATS = ((0, D), (288, D), (576, D), (864, D), (1920, FF))
W1_AT = 1152
VEC_AT = 2304
GELU_C = math.sqrt(2.0 / math.pi)


def nn(a, b):
    return lax.dot_general(a, b, (((1,), (0,)), ((), ())), preferred_element_type=F32)


def nt(a, b):
    return lax.dot_general(a, b, (((1,), (1,)), ((), ())), preferred_element_type=F32)


def tn(a, b):
    return lax.dot_general(a, b, (((0,), (0,)), ((), ())), preferred_element_type=F32)


def low_half(v):
    lane = lax.broadcasted_iota(jnp.int32, v.shape, 1)
    return lane < 64


def load_square(flat, base, rows, tmp, out):
    half = rows // 2
    f0 = flat[pl.ds(base, half, stride=3), :]
    f1 = flat[pl.ds(base + 1, half, stride=3), :]
    f2 = flat[pl.ds(base + 2, half, stride=3), :]
    r1 = pltpu.roll(f1, 64, 1)
    r2 = pltpu.roll(f2, 64, 1)
    left = low_half(f0)
    lo, hi = tmp.at[0], tmp.at[1]
    lo[pl.ds(0, half, stride=2), :] = f0
    hi[pl.ds(0, half, stride=2), :] = jnp.where(left, f1, 0.0)
    lo[pl.ds(1, half, stride=2), :] = jnp.where(left, r1, r2)
    hi[pl.ds(1, half, stride=2), :] = jnp.where(left, r2, 0.0)
    out[0:rows, 0:128] = lo[0:rows, :].astype(BF16)
    out[0:rows, 128:256] = hi[0:rows, :].astype(BF16)
    if rows < 256:
        out[rows:256, :] = jnp.zeros((256 - rows, 256), BF16)


def store_square(val, flat, base, rows, tmp):
    half = rows // 2
    lo, hi = tmp.at[0], tmp.at[1]
    lo[0:rows, :] = val[0:rows, 0:128]
    hi[0:rows, :] = val[0:rows, 128:256]
    e0 = lo[pl.ds(0, half, stride=2), :]
    e1 = hi[pl.ds(0, half, stride=2), :]
    o0 = pltpu.roll(lo[pl.ds(1, half, stride=2), :], 64, 1)
    o1 = pltpu.roll(hi[pl.ds(1, half, stride=2), :], 64, 1)
    left = low_half(e0)
    flat[pl.ds(base, half, stride=3), :] = e0
    flat[pl.ds(base + 1, half, stride=3), :] = jnp.where(left, e1, o0)
    flat[pl.ds(base + 2, half, stride=3), :] = jnp.where(left, o0, o1)


def norm_fwd(x):
    mean = jnp.sum(x, -1, keepdims=True) * (1.0 / D)
    right = x[:, 128:256] - mean
    c = jnp.concatenate([x[:, 0:128] - mean, jnp.where(low_half(right), right, 0.0)], 1)
    var = jnp.sum(c * c, -1, keepdims=True) * (1.0 / D)
    r = lax.rsqrt(var + 1e-05)
    return c * r, r


def norm_back(d, xh, r, g):
    e = d * g
    m1 = jnp.sum(e, -1, keepdims=True) * (1.0 / D)
    m2 = jnp.sum(e * xh, -1, keepdims=True) * (1.0 / D)
    return r * (e - m1 - xh * m2)


def rows8(v):
    return jnp.sum(v.reshape(v.shape[0] // 8, 8, v.shape[1]), 0)


def split_pair(v):
    zero = jnp.zeros((v.shape[0], 64), v.dtype)
    even = jnp.concatenate([v[:, 0:D], zero], 1)
    odd = jnp.concatenate([v[:, D : 2 * D], zero], 1)
    return jnp.concatenate([even, odd], 0)


def join_pair(v, n):
    return jnp.concatenate([v[0:n, 0:D], v[n : 2 * n, 0:D]], 1)


def block_kernel(
    x_ref, dy_ref, flat, out_ref, ig_ref, gflat,
    qs, ks, vs, os_, kbd, vbd, psc, xh1, r1, dx2s, h, h2, z, dul, o_t, dal, dyt, dqt, dkt, dvt,
    wq, wk, wv, wo, w1, w2, tmp, hm2, hm, acc, acc2,
):
    n = x_ref.shape[0]
    toks = n * SEQ
    pairs = SEQ // 2
    chunk = 2 * n
    groups = n // GROUP

    for (base, rows), ref in zip(MATS, (wq, wk, wv, wo, w2)):
        load_square(flat, base, rows, tmp, ref)
    for c in range(4):
        w1[0:D, 128 * c : 128 * (c + 1)] = flat[pl.ds(W1_AT + c, D, stride=4), :].astype(BF16)

    w1[D:256, :] = jnp.zeros((256 - D, 2 * FF), BF16)

    def vec(k):
        a = VEC_AT + 3 * (k // 2)
        zero = jnp.zeros((1, 64), F32)
        if k % 2 == 0:
            return jnp.concatenate([flat[a : a + 1, :], flat[a + 1 : a + 2, 0:64], zero], 1)
        return jnp.concatenate([flat[a + 1 : a + 2, 64:128], flat[a + 2 : a + 3, :], zero], 1)

    g1, n1, bq, bv, bo, g2, n2, b2 = [vec(k) for k in range(8)]
    b1 = jnp.concatenate([flat[VEC_AT + 12 + c : VEC_AT + 13 + c, :] for c in range(4)], 1)

    lane = lax.broadcasted_iota(jnp.int32, (80, 256), 1)
    row = lax.broadcasted_iota(jnp.int32, (80, 256), 0)
    for p in range(4):
        lo = jnp.where(row < ROWS, HEAD_DIM * 2 * p, HEAD_DIM * (2 * p + 1))
        hm2[80 * p : 80 * (p + 1), :] = jnp.where(
            (lane >= lo) & (lane < lo + HEAD_DIM), 1.0, 0.0
        ).astype(BF16)
    lane16 = lax.broadcasted_iota(jnp.int32, (16, 256), 1)
    for k in range(HEADS):
        hm[16 * k : 16 * (k + 1), :] = jnp.where(
            (lane16 >= HEAD_DIM * k) & (lane16 < HEAD_DIM * (k + 1)), 1.0, 0.0
        ).astype(BF16)
    ones_lane = (lax.broadcasted_iota(jnp.int32, (toks, 64), 1) == 0).astype(F32).astype(BF16)
    for ref in (h, h2, o_t):
        ref[:, D:256] = ones_lane
    for ref in (qs, ks, vs, os_):
        ref[...] = jnp.zeros(ref.shape, F32)

    def pair_of(ref, i):
        return split_pair(
            ref[:, pl.ds(pl.multiple_of(i * (2 * D), 128), 2 * D)].astype(F32)
        )

    def put_tokens(ref, i, val):
        for half in range(2):
            for par in range(2):
                ref.at[half][pl.ds(2 * i + par, n, stride=ROWS), :] = val[
                    n * par : n * (par + 1), 128 * half : 128 * (half + 1)
                ]

    def get_tokens(ref, i):
        return jnp.concatenate(
            [
                jnp.concatenate(
                    [ref.at[half][pl.ds(2 * i + par, n, stride=ROWS), :] for half in range(2)], 1
                )
                for par in range(2)
            ],
            0,
        )

    def get_rows(ref, start, count):
        return jnp.concatenate([ref[0, pl.ds(start, count), :], ref[1, pl.ds(start, count), :]], 1)

    def put_rows(ref, start, val):
        for half in range(2):
            ref[half, pl.ds(start, val.shape[0]), :] = val[:, 128 * half : 128 * (half + 1)]

    def at(i):
        return pl.ds(pl.multiple_of(i * chunk, 32), chunk)

    def dense1(i, _):
        x = pair_of(x_ref, i)
        xh, r = norm_fwd(x)
        hb = (xh * g1 + n1).astype(BF16)
        xh1[at(i), :] = xh
        r1[at(i), :] = r
        h[at(i), 0:D] = hb[:, 0:D]
        put_tokens(qs, i, (nn(hb, wq[...]) + bq).astype(BF16).astype(F32))
        put_tokens(ks, i, nn(hb, wk[...]).astype(BF16).astype(F32))
        put_tokens(vs, i, (nn(hb, wv[...]) + bv).astype(BF16).astype(F32))
        return 0

    lax.fori_loop(0, pairs, dense1, 0)

    lane3 = lax.broadcasted_iota(jnp.int32, (1, LANES), 1)

    def squeeze(v):
        return jnp.where(
            lane3 < ROWS, v[0:HJ], jnp.where(lane3 < 2 * ROWS, v[HJ : 2 * HJ], v[2 * HJ : 3 * HJ])
        ).reshape(HEADS, ROWS, LANES)

    jrow = lax.broadcasted_iota(jnp.int32, (1, ROWS, LANES), 1)
    cexp = math.log2(math.e) / math.sqrt(HEAD_DIM)
    scale = 1.0 / math.sqrt(HEAD_DIM)

    def attn(g, _):
        r = pl.multiple_of(g * GROWS, 8)
        qg = get_rows(qs, r, LANES).astype(BF16)
        base = pl.multiple_of(g * (3 * HJ), 64)
        for src, dst in ((ks, kbd), (vs, vbd)):
            for b in range(GROUP):
                one = get_rows(src, r + ROWS * b, ROWS)
                two = jnp.concatenate([one, one], 0).astype(BF16)
                for p in range(4):
                    dst[pl.ds(base + HJ * b + 80 * p, 80), :] = two * hm2[80 * p : 80 * (p + 1), :]
        st = squeeze(nt(kbd[pl.ds(base, 3 * HJ), :], qg))
        st = jnp.where(jrow < SEQ, st, -1e30)
        m = jnp.max(st, 1, keepdims=True)
        e = jnp.exp2((st - m) * cexp)
        p = e * (1.0 / jnp.sum(e, 1, keepdims=True))
        p = p.reshape(HJ, LANES)
        psc[pl.ds(pl.multiple_of(g * HJ, 64), HJ), :] = p
        pt = p.T
        for b in range(GROUP):
            ob = nn(
                pt[ROWS * b : ROWS * (b + 1), :].astype(BF16), vbd[pl.ds(base + HJ * b, HJ), :]
            )
            put_rows(os_, r + ROWS * b, ob.astype(BF16).astype(F32)[0:SEQ])
        return 0

    lax.fori_loop(0, groups, attn, 0)

    def dense2(i, carry):
        dg2, dn2, db2 = carry
        o = get_tokens(os_, i).astype(BF16)
        o_t[at(i), 0:D] = o[:, 0:D]
        x2 = pair_of(x_ref, i) + (nn(o, wo[...]) + bo)
        xh, r = norm_fwd(x2)
        hb = (xh * g2 + n2).astype(BF16)
        h2[at(i), 0:D] = hb[:, 0:D]
        u = nn(hb, w1[...]) + b1
        gate, up = u[:, :FF], u[:, FF:]
        sq = gate * gate
        t = jnp.tanh(gate * (GELU_C + (GELU_C * 0.044715) * sq))
        half = 0.5 + 0.5 * t
        act = gate * half
        zb = (act * up).astype(BF16)
        z[at(i), :] = zb
        y = x2 + nn(zb, w2[...]) + b2
        out_ref[:, pl.ds(pl.multiple_of(i * (2 * D), 128), 2 * D)] = join_pair(y, n).astype(BF16)
        dyf = pair_of(dy_ref, i)
        dyb = dyf.astype(BF16)
        dyt[at(i), :] = dyb
        dz = nt(dyb, w2[...])
        slope = half + gate * (0.5 - 0.5 * t * t) * (GELU_C + (3 * GELU_C * 0.044715) * sq)
        du = jnp.concatenate([(dz * up * slope).astype(BF16), (dz * act).astype(BF16)], 1)
        dul[at(i), :] = du
        dh = nt(du, w1[...])
        dx2 = dyf + norm_back(dh, xh, r, g2)
        dx2s[at(i), :] = dx2
        da = dx2.astype(BF16)
        dal[at(i), :] = da
        put_tokens(os_, i, nt(da, wo[...]).astype(BF16).astype(F32))
        return dg2 + rows8(dh * xh), dn2 + rows8(dh), db2 + rows8(dyf)

    zero = jnp.zeros((8, 256), F32)
    dg2, dn2, db2 = lax.fori_loop(0, pairs, dense2, (zero, zero, zero))

    def total(v):
        return jnp.sum(v, 0, keepdims=True)

    def over_tokens(acc, a, b):
        acc[...] = jnp.zeros(acc.shape, F32)

        @pl.loop(0, SEQ // 2)
        def _(i):
            acc[...] += tn(a[at(i), :], b[at(i), :])

        return acc[...]

    store_square(over_tokens(acc, z, dyt), gflat, 1920, FF, tmp)
    dw1 = over_tokens(acc2, h2, dul)
    for c in range(4):
        gflat[pl.ds(W1_AT + c, D, stride=4), :] = dw1[0:D, 128 * c : 128 * (c + 1)]
        gflat[VEC_AT + 12 + c : VEC_AT + 13 + c, :] = dw1[D : D + 1, 128 * c : 128 * (c + 1)]
    dwo = over_tokens(acc, o_t, dal)
    store_square(dwo, gflat, 864, D, tmp)
    dbo = dwo[D : D + 1]

    def attn_back(g, _):
        r = pl.multiple_of(g * GROWS, 8)
        base = pl.multiple_of(g * (3 * HJ), 64)
        qg = get_rows(qs, r, LANES).astype(BF16)
        dg = get_rows(os_, r, LANES).astype(BF16)
        dp = squeeze(nt(vbd[pl.ds(base, 3 * HJ), :], dg))
        p = psc[pl.ds(pl.multiple_of(g * HJ, 64), HJ), :].reshape(HEADS, ROWS, LANES)
        pd = p * dp
        ds = p * dp - p * jnp.sum(pd, 1, keepdims=True)
        dst = ds.reshape(HJ, LANES).T

        def wide(v):
            blocks = []
            for k in range(HEADS):
                one = v[k]
                parts = [
                    jnp.where((lane3 >= ROWS * b) & (lane3 < ROWS * (b + 1)), one, 0.0)
                    for b in range(GROUP)
                ]
                parts.append(jnp.zeros((8, LANES), F32))
                blocks.append(jnp.concatenate(parts, 0).astype(BF16))
            return jnp.concatenate(blocks, 1)

        def masked(v):
            v3 = v.reshape(8, 16, 256)
            return jnp.concatenate(
                [(v3 * hm[16 * k : 16 * (k + 1), :][None]).reshape(128, 256) for k in range(HEADS)], 0
            )

        dv = nn(wide(p), masked(dg))
        dk = nn(wide(ds), masked(qg)) * scale
        for b in range(GROUP):
            dq = nn(
                dst[ROWS * b : ROWS * (b + 1), :].astype(BF16), kbd[pl.ds(base + HJ * b, HJ), :]
            )
            put_rows(qs, r + ROWS * b, (dq * scale).astype(BF16).astype(F32))
        put_rows(vs, r, dv.astype(BF16).astype(F32)[0:GROWS])
        put_rows(ks, r, dk.astype(BF16).astype(F32)[0:GROWS])
        return 0

    lax.fori_loop(0, groups, attn_back, 0)

    def dense3(i, carry):
        dg1, dn1 = carry
        dq = get_tokens(qs, i).astype(BF16)
        dk = get_tokens(ks, i).astype(BF16)
        dv = get_tokens(vs, i).astype(BF16)
        dqt[at(i), :] = dq
        dkt[at(i), :] = dk
        dvt[at(i), :] = dv
        dh = nt(dq, wq[...]) + nt(dk, wk[...]) + nt(dv, wv[...])
        xh = xh1[at(i), :]
        ig = dx2s[at(i), :] + norm_back(dh, xh, r1[at(i), :], g1)
        ig_ref[:, pl.ds(pl.multiple_of(i * (2 * D), 128), 2 * D)] = join_pair(ig, n)
        return dg1 + rows8(dh * xh), dn1 + rows8(dh)

    dg1, dn1 = lax.fori_loop(0, pairs, dense3, (zero, zero))
    dwq = over_tokens(acc, h, dqt)
    store_square(dwq, gflat, 0, D, tmp)
    store_square(over_tokens(acc, h, dkt), gflat, 288, D, tmp)
    dwv = over_tokens(acc, h, dvt)
    store_square(dwv, gflat, 576, D, tmp)

    vecs = [total(dg1), total(dn1), dwq[D : D + 1], dwv[D : D + 1], dbo, total(dg2), total(dn2), total(db2)]
    for k in range(4):
        a, b = vecs[2 * k], vecs[2 * k + 1]
        gflat[VEC_AT + 3 * k : VEC_AT + 3 * k + 1, :] = a[:, 0:128]
        gflat[VEC_AT + 3 * k + 1 : VEC_AT + 3 * k + 2, :] = jnp.concatenate(
            [a[:, 128:192], b[:, 0:64]], 1
        )
        gflat[VEC_AT + 3 * k + 2 : VEC_AT + 3 * k + 3, :] = b[:, 64:192]
    used = VEC_AT + 16
    if gflat.shape[0] > used:
        gflat[used:, :] = jnp.zeros((gflat.shape[0] - used, LANES), F32)


def block(x, dy, flat):
    n = x.shape[0]
    toks = n * SEQ
    sm = (2, n * ROWS + 8, LANES)
    groups = n // GROUP
    vm = pltpu.VMEM
    tok = vm((toks, 256), BF16)
    scratch = (
        [vm(sm, F32)] * 4
        + [vm((groups * 3 * HJ, 256), BF16)] * 2
        + [vm((groups * HJ, LANES), F32)]
        + [vm((toks, 256), F32), vm((toks, 1), F32), vm((toks, 256), F32)]
        + [tok, tok, tok, vm((toks, 2 * FF), BF16), tok]
        + [tok] * 5
        + [vm((256, 256), BF16)] * 4
        + [vm((256, 2 * FF), BF16), vm((FF, 256), BF16), vm((2, FF, 128), F32)]
        + [vm((320, 256), BF16), vm((128, 256), BF16), vm((256, 256), F32), vm((256, 512), F32)]
    )
    return pl.pallas_call(
        block_kernel,
        out_shape=(
            jax.ShapeDtypeStruct(x.shape, BF16),
            jax.ShapeDtypeStruct(x.shape, F32),
            jax.ShapeDtypeStruct(flat.shape, F32),
        ),
        in_specs=[pl.BlockSpec(memory_space=pltpu.VMEM)] * 3,
        out_specs=(pl.BlockSpec(memory_space=pltpu.VMEM),) * 3,
        scratch_shapes=scratch,
        compiler_params=pltpu.CompilerParams(vmem_limit_bytes=60 * 2**20),
        name="block",
    )(x, dy, flat)


def on_device(inputs, cotangent, master, first, second):
    shard = master.shape[0]
    wide = lax.axis_size("wide")
    full = lax.all_gather(master, "wide", axis=0, tiled=True)
    block_out, input_grad, gflat = block(inputs, cotangent, full.reshape(-1, LANES))
    grad = gflat.reshape(-1)
    owned = lax.psum_scatter(grad, "wide", scatter_dimension=0, tiled=True)
    owned = lax.psum(owned, "narrow")
    squares = lax.psum(jnp.sum(owned * owned), "wide")
    grad_norm = jnp.sqrt(squares)
    factor = jnp.minimum(1.0, 1.0 / (grad_norm + 1e-06))
    clipped = owned * factor
    new_first = 0.5 * first + 0.5 * clipped
    new_second = 0.5 * second + 0.5 * clipped * clipped
    fixed = 1.0 - 0.5**STEP
    new_master = master - 0.05 * (
        new_first / fixed / (jnp.sqrt(new_second / fixed) + 1e-08) + 0.1 * master
    )
    return (
        block_out,
        input_grad,
        clipped,
        grad_norm,
        new_master,
        new_master.astype(jnp.bfloat16),
        new_first,
        new_second,
    )


def solution(mesh):
    both, part = P(("wide", "narrow"), None), P("wide")
    return jax.shard_map(
        on_device,
        mesh=mesh,
        in_specs=(both, both, part, part, part),
        out_specs=(both, both, part, P(), part, part, part, part),
        check_vma=False,
    )
```

```python
import functools
import math

import jax
import jax.numpy as jnp
from jax import lax
from jax.experimental import pallas as pl
from jax.experimental.pallas import tpu as pltpu
from jax.sharding import PartitionSpec as P

D = 192
HEADS = 8
HEAD_DIM = 24
FF = 256
SEQ = 34
STEP = 5
ROWS = 40
GROUP = 3
GROWS = GROUP * ROWS
HJ = HEADS * ROWS
LANES = 128
F32 = jnp.float32
BF16 = jnp.bfloat16
MATS = ((0, D), (288, D), (576, D), (864, D), (1920, FF))
W1_AT = 1152
VEC_AT = 2304
GELU_C = math.sqrt(2.0 / math.pi)


def nn(a, b):
    return lax.dot_general(a, b, (((1,), (0,)), ((), ())), preferred_element_type=F32)


def nt(a, b):
    return lax.dot_general(a, b, (((1,), (1,)), ((), ())), preferred_element_type=F32)


def tn(a, b):
    return lax.dot_general(a, b, (((0,), (0,)), ((), ())), preferred_element_type=F32)


def low_half(v):
    lane = lax.broadcasted_iota(jnp.int32, v.shape, 1)
    return lane < 64


def load_square(flat, base, rows, tmp, out):
    half = rows // 2
    f0 = flat[pl.ds(base, half, stride=3), :]
    f1 = flat[pl.ds(base + 1, half, stride=3), :]
    f2 = flat[pl.ds(base + 2, half, stride=3), :]
    r1 = pltpu.roll(f1, 64, 1)
    r2 = pltpu.roll(f2, 64, 1)
    left = low_half(f0)
    lo, hi = tmp.at[0], tmp.at[1]
    lo[pl.ds(0, half, stride=2), :] = f0
    hi[pl.ds(0, half, stride=2), :] = jnp.where(left, f1, 0.0)
    lo[pl.ds(1, half, stride=2), :] = jnp.where(left, r1, r2)
    hi[pl.ds(1, half, stride=2), :] = jnp.where(left, r2, 0.0)
    out[0:rows, 0:128] = lo[0:rows, :].astype(BF16)
    out[0:rows, 128:256] = hi[0:rows, :].astype(BF16)
    if rows < 256:
        out[rows:256, :] = jnp.zeros((256 - rows, 256), BF16)


def store_square(val, flat, base, rows, tmp):
    half = rows // 2
    lo, hi = tmp.at[0], tmp.at[1]
    lo[0:rows, :] = val[0:rows, 0:128]
    hi[0:rows, :] = val[0:rows, 128:256]
    e0 = lo[pl.ds(0, half, stride=2), :]
    e1 = hi[pl.ds(0, half, stride=2), :]
    o0 = pltpu.roll(lo[pl.ds(1, half, stride=2), :], 64, 1)
    o1 = pltpu.roll(hi[pl.ds(1, half, stride=2), :], 64, 1)
    left = low_half(e0)
    flat[pl.ds(base, half, stride=3), :] = e0
    flat[pl.ds(base + 1, half, stride=3), :] = jnp.where(left, e1, o0)
    flat[pl.ds(base + 2, half, stride=3), :] = jnp.where(left, o0, o1)


def norm_fwd(x):
    mean = jnp.sum(x, -1, keepdims=True) * (1.0 / D)
    right = x[:, 128:256] - mean
    c = jnp.concatenate([x[:, 0:128] - mean, jnp.where(low_half(right), right, 0.0)], 1)
    var = jnp.sum(c * c, -1, keepdims=True) * (1.0 / D)
    r = lax.rsqrt(var + 1e-05)
    return c * r, r


def norm_back(d, xh, r, g):
    e = d * g
    m1 = jnp.sum(e, -1, keepdims=True) * (1.0 / D)
    m2 = jnp.sum(e * xh, -1, keepdims=True) * (1.0 / D)
    return r * (e - m1 - xh * m2)


def rows8(v):
    return jnp.sum(v.reshape(v.shape[0] // 8, 8, v.shape[1]), 0)


def split_pair(v):
    zero = jnp.zeros((v.shape[0], 64), v.dtype)
    even = jnp.concatenate([v[:, 0:D], zero], 1)
    odd = jnp.concatenate([v[:, D : 2 * D], zero], 1)
    return jnp.concatenate([even, odd], 0)


def join_pair(v, n):
    return jnp.concatenate([v[0:n, 0:D], v[n : 2 * n, 0:D]], 1)


def block_kernel(
    x_ref, dy_ref, gathered, out_ref, ig_ref, gshards, flat, gflat,
    qs, ks, vs, os_, kbd, vbd, psc, xh1, r1, dx2s, h, h2, z, dul, o_t, dal, dyt, dqt, dkt, dvt,
    wq, wk, wv, wo, w1, w2, tmp, hm2, hm, acc, acc2,
):
    n = x_ref.shape[0]
    toks = n * SEQ
    pairs = SEQ // 2
    chunk = 2 * n
    groups = n // GROUP

    wide, rows_sh = gathered.shape[0], flat.shape[0] // gathered.shape[0]
    for w in range(wide):
        flat[rows_sh * w : rows_sh * (w + 1), :] = gathered[w, 0:rows_sh, :]
    for (base, rows), ref in zip(MATS, (wq, wk, wv, wo, w2)):
        load_square(flat, base, rows, tmp, ref)
    for c in range(4):
        w1[0:D, 128 * c : 128 * (c + 1)] = flat[pl.ds(W1_AT + c, D, stride=4), :].astype(BF16)

    w1[D:256, :] = jnp.zeros((256 - D, 2 * FF), BF16)

    def vec(k):
        a = VEC_AT + 3 * (k // 2)
        zero = jnp.zeros((1, 64), F32)
        if k % 2 == 0:
            return jnp.concatenate([flat[a : a + 1, :], flat[a + 1 : a + 2, 0:64], zero], 1)
        return jnp.concatenate([flat[a + 1 : a + 2, 64:128], flat[a + 2 : a + 3, :], zero], 1)

    g1, n1, bq, bv, bo, g2, n2, b2 = [vec(k) for k in range(8)]
    b1 = jnp.concatenate([flat[VEC_AT + 12 + c : VEC_AT + 13 + c, :] for c in range(4)], 1)

    lane = lax.broadcasted_iota(jnp.int32, (80, 256), 1)
    row = lax.broadcasted_iota(jnp.int32, (80, 256), 0)
    for p in range(4):
        lo = jnp.where(row < ROWS, HEAD_DIM * 2 * p, HEAD_DIM * (2 * p + 1))
        hm2[80 * p : 80 * (p + 1), :] = jnp.where(
            (lane >= lo) & (lane < lo + HEAD_DIM), 1.0, 0.0
        ).astype(BF16)
    lane16 = lax.broadcasted_iota(jnp.int32, (16, 256), 1)
    for k in range(HEADS):
        hm[16 * k : 16 * (k + 1), :] = jnp.where(
            (lane16 >= HEAD_DIM * k) & (lane16 < HEAD_DIM * (k + 1)), 1.0, 0.0
        ).astype(BF16)
    ones_lane = (lax.broadcasted_iota(jnp.int32, (toks, 64), 1) == 0).astype(F32).astype(BF16)
    for ref in (h, h2, o_t):
        ref[:, D:256] = ones_lane
    for ref in (qs, ks, vs, os_):
        ref[...] = jnp.zeros(ref.shape, F32)

    def pair_of(ref, i):
        return split_pair(
            ref[:, pl.ds(pl.multiple_of(i * (2 * D), 128), 2 * D)].astype(F32)
        )

    def put_tokens(ref, i, val):
        for half in range(2):
            for par in range(2):
                ref.at[half][pl.ds(2 * i + par, n, stride=ROWS), :] = val[
                    n * par : n * (par + 1), 128 * half : 128 * (half + 1)
                ]

    def get_tokens(ref, i):
        return jnp.concatenate(
            [
                jnp.concatenate(
                    [ref.at[half][pl.ds(2 * i + par, n, stride=ROWS), :] for half in range(2)], 1
                )
                for par in range(2)
            ],
            0,
        )

    def get_rows(ref, start, count):
        return jnp.concatenate([ref[0, pl.ds(start, count), :], ref[1, pl.ds(start, count), :]], 1)

    def put_rows(ref, start, val):
        for half in range(2):
            ref[half, pl.ds(start, val.shape[0]), :] = val[:, 128 * half : 128 * (half + 1)]

    def at(i):
        return pl.ds(pl.multiple_of(i * chunk, 32), chunk)

    def dense1(i, _):
        x = pair_of(x_ref, i)
        xh, r = norm_fwd(x)
        hb = (xh * g1 + n1).astype(BF16)
        xh1[at(i), :] = xh
        r1[at(i), :] = r
        h[at(i), 0:D] = hb[:, 0:D]
        put_tokens(qs, i, (nn(hb, wq[...]) + bq).astype(BF16).astype(F32))
        put_tokens(ks, i, nn(hb, wk[...]).astype(BF16).astype(F32))
        put_tokens(vs, i, (nn(hb, wv[...]) + bv).astype(BF16).astype(F32))
        return 0

    lax.fori_loop(0, pairs, dense1, 0)

    lane3 = lax.broadcasted_iota(jnp.int32, (1, LANES), 1)

    def squeeze(v):
        return jnp.where(
            lane3 < ROWS, v[0:HJ], jnp.where(lane3 < 2 * ROWS, v[HJ : 2 * HJ], v[2 * HJ : 3 * HJ])
        ).reshape(HEADS, ROWS, LANES)

    jrow = lax.broadcasted_iota(jnp.int32, (1, ROWS, LANES), 1)
    cexp = math.log2(math.e) / math.sqrt(HEAD_DIM)
    scale = 1.0 / math.sqrt(HEAD_DIM)

    def attn(g, _):
        r = pl.multiple_of(g * GROWS, 8)
        qg = get_rows(qs, r, LANES).astype(BF16)
        base = pl.multiple_of(g * (3 * HJ), 64)
        for src, dst in ((ks, kbd), (vs, vbd)):
            for b in range(GROUP):
                one = get_rows(src, r + ROWS * b, ROWS)
                two = jnp.concatenate([one, one], 0).astype(BF16)
                for p in range(4):
                    dst[pl.ds(base + HJ * b + 80 * p, 80), :] = two * hm2[80 * p : 80 * (p + 1), :]
        st = squeeze(nt(kbd[pl.ds(base, 3 * HJ), :], qg))
        st = jnp.where(jrow < SEQ, st, -1e30)
        m = jnp.max(st, 1, keepdims=True)
        e = jnp.exp2((st - m) * cexp)
        p = e * (1.0 / jnp.sum(e, 1, keepdims=True))
        p = p.reshape(HJ, LANES)
        psc[pl.ds(pl.multiple_of(g * HJ, 64), HJ), :] = p
        pt = p.T
        for b in range(GROUP):
            ob = nn(
                pt[ROWS * b : ROWS * (b + 1), :].astype(BF16), vbd[pl.ds(base + HJ * b, HJ), :]
            )
            put_rows(os_, r + ROWS * b, ob.astype(BF16).astype(F32)[0:SEQ])
        return 0

    lax.fori_loop(0, groups, attn, 0)

    def dense2(i, carry):
        dg2, dn2, db2 = carry
        o = get_tokens(os_, i).astype(BF16)
        o_t[at(i), 0:D] = o[:, 0:D]
        x2 = pair_of(x_ref, i) + (nn(o, wo[...]) + bo)
        xh, r = norm_fwd(x2)
        hb = (xh * g2 + n2).astype(BF16)
        h2[at(i), 0:D] = hb[:, 0:D]
        u = nn(hb, w1[...]) + b1
        gate, up = u[:, :FF], u[:, FF:]
        sq = gate * gate
        t = jnp.tanh(gate * (GELU_C + (GELU_C * 0.044715) * sq))
        half = 0.5 + 0.5 * t
        act = gate * half
        zb = (act * up).astype(BF16)
        z[at(i), :] = zb
        y = x2 + nn(zb, w2[...]) + b2
        out_ref[:, pl.ds(pl.multiple_of(i * (2 * D), 128), 2 * D)] = join_pair(y, n).astype(BF16)
        dyf = pair_of(dy_ref, i)
        dyb = dyf.astype(BF16)
        dyt[at(i), :] = dyb
        dz = nt(dyb, w2[...])
        slope = half + gate * (0.5 - 0.5 * t * t) * (GELU_C + (3 * GELU_C * 0.044715) * sq)
        du = jnp.concatenate([(dz * up * slope).astype(BF16), (dz * act).astype(BF16)], 1)
        dul[at(i), :] = du
        dh = nt(du, w1[...])
        dx2 = dyf + norm_back(dh, xh, r, g2)
        dx2s[at(i), :] = dx2
        da = dx2.astype(BF16)
        dal[at(i), :] = da
        put_tokens(os_, i, nt(da, wo[...]).astype(BF16).astype(F32))
        return dg2 + rows8(dh * xh), dn2 + rows8(dh), db2 + rows8(dyf)

    zero = jnp.zeros((8, 256), F32)
    dg2, dn2, db2 = lax.fori_loop(0, pairs, dense2, (zero, zero, zero))

    def total(v):
        return jnp.sum(v, 0, keepdims=True)

    def over_tokens(acc, a, b):
        acc[...] = jnp.zeros(acc.shape, F32)

        @pl.loop(0, SEQ // 2)
        def _(i):
            acc[...] += tn(a[at(i), :], b[at(i), :])

        return acc[...]

    store_square(over_tokens(acc, z, dyt), gflat, 1920, FF, tmp)
    dw1 = over_tokens(acc2, h2, dul)
    for c in range(4):
        gflat[pl.ds(W1_AT + c, D, stride=4), :] = dw1[0:D, 128 * c : 128 * (c + 1)]
        gflat[VEC_AT + 12 + c : VEC_AT + 13 + c, :] = dw1[D : D + 1, 128 * c : 128 * (c + 1)]
    dwo = over_tokens(acc, o_t, dal)
    store_square(dwo, gflat, 864, D, tmp)
    dbo = dwo[D : D + 1]

    def attn_back(g, _):
        r = pl.multiple_of(g * GROWS, 8)
        base = pl.multiple_of(g * (3 * HJ), 64)
        qg = get_rows(qs, r, LANES).astype(BF16)
        dg = get_rows(os_, r, LANES).astype(BF16)
        dp = squeeze(nt(vbd[pl.ds(base, 3 * HJ), :], dg))
        p = psc[pl.ds(pl.multiple_of(g * HJ, 64), HJ), :].reshape(HEADS, ROWS, LANES)
        pd = p * dp
        ds = p * dp - p * jnp.sum(pd, 1, keepdims=True)
        dst = ds.reshape(HJ, LANES).T

        def wide(v):
            blocks = []
            for k in range(HEADS):
                one = v[k]
                parts = [
                    jnp.where((lane3 >= ROWS * b) & (lane3 < ROWS * (b + 1)), one, 0.0)
                    for b in range(GROUP)
                ]
                parts.append(jnp.zeros((8, LANES), F32))
                blocks.append(jnp.concatenate(parts, 0).astype(BF16))
            return jnp.concatenate(blocks, 1)

        def masked(v):
            v3 = v.reshape(8, 16, 256)
            return jnp.concatenate(
                [(v3 * hm[16 * k : 16 * (k + 1), :][None]).reshape(128, 256) for k in range(HEADS)], 0
            )

        dv = nn(wide(p), masked(dg))
        dk = nn(wide(ds), masked(qg)) * scale
        for b in range(GROUP):
            dq = nn(
                dst[ROWS * b : ROWS * (b + 1), :].astype(BF16), kbd[pl.ds(base + HJ * b, HJ), :]
            )
            put_rows(qs, r + ROWS * b, (dq * scale).astype(BF16).astype(F32))
        put_rows(vs, r, dv.astype(BF16).astype(F32)[0:GROWS])
        put_rows(ks, r, dk.astype(BF16).astype(F32)[0:GROWS])
        return 0

    lax.fori_loop(0, groups, attn_back, 0)

    def dense3(i, carry):
        dg1, dn1 = carry
        dq = get_tokens(qs, i).astype(BF16)
        dk = get_tokens(ks, i).astype(BF16)
        dv = get_tokens(vs, i).astype(BF16)
        dqt[at(i), :] = dq
        dkt[at(i), :] = dk
        dvt[at(i), :] = dv
        dh = nt(dq, wq[...]) + nt(dk, wk[...]) + nt(dv, wv[...])
        xh = xh1[at(i), :]
        ig = dx2s[at(i), :] + norm_back(dh, xh, r1[at(i), :], g1)
        ig_ref[:, pl.ds(pl.multiple_of(i * (2 * D), 128), 2 * D)] = join_pair(ig, n)
        return dg1 + rows8(dh * xh), dn1 + rows8(dh)

    dg1, dn1 = lax.fori_loop(0, pairs, dense3, (zero, zero))
    dwq = over_tokens(acc, h, dqt)
    store_square(dwq, gflat, 0, D, tmp)
    store_square(over_tokens(acc, h, dkt), gflat, 288, D, tmp)
    dwv = over_tokens(acc, h, dvt)
    store_square(dwv, gflat, 576, D, tmp)

    vecs = [total(dg1), total(dn1), dwq[D : D + 1], dwv[D : D + 1], dbo, total(dg2), total(dn2), total(db2)]
    for k in range(4):
        a, b = vecs[2 * k], vecs[2 * k + 1]
        gflat[VEC_AT + 3 * k : VEC_AT + 3 * k + 1, :] = a[:, 0:128]
        gflat[VEC_AT + 3 * k + 1 : VEC_AT + 3 * k + 2, :] = jnp.concatenate(
            [a[:, 128:192], b[:, 0:64]], 1
        )
        gflat[VEC_AT + 3 * k + 2 : VEC_AT + 3 * k + 3, :] = b[:, 64:192]
    used = VEC_AT + 16
    if gflat.shape[0] > used:
        gflat[used:, :] = jnp.zeros((gflat.shape[0] - used, LANES), F32)
    for w in range(wide):
        gshards[w, 0:rows_sh, :] = gflat[rows_sh * w : rows_sh * (w + 1), :]
        gshards[w, rows_sh:, :] = jnp.zeros((gshards.shape[1] - rows_sh, LANES), F32)


def block(x, dy, gathered, rows_sh):
    n = x.shape[0]
    toks = n * SEQ
    sm = (2, n * ROWS + 8, LANES)
    groups = n // GROUP
    vm = pltpu.VMEM
    tok = vm((toks, 256), BF16)
    flat = vm((gathered.shape[0] * rows_sh, LANES), F32)
    scratch = (
        [flat, flat]
        + [vm(sm, F32)] * 4
        + [vm((groups * 3 * HJ, 256), BF16)] * 2
        + [vm((groups * HJ, LANES), F32)]
        + [vm((toks, 256), F32), vm((toks, 1), F32), vm((toks, 256), F32)]
        + [tok, tok, tok, vm((toks, 2 * FF), BF16), tok]
        + [tok] * 5
        + [vm((256, 256), BF16)] * 4
        + [vm((256, 2 * FF), BF16), vm((FF, 256), BF16), vm((2, FF, 128), F32)]
        + [vm((320, 256), BF16), vm((128, 256), BF16), vm((256, 256), F32), vm((256, 512), F32)]
    )
    return pl.pallas_call(
        block_kernel,
        out_shape=(
            jax.ShapeDtypeStruct(x.shape, BF16),
            jax.ShapeDtypeStruct(x.shape, F32),
            jax.ShapeDtypeStruct(gathered.shape, F32),
        ),
        in_specs=[pl.BlockSpec(memory_space=pltpu.VMEM)] * 3,
        out_specs=(pl.BlockSpec(memory_space=pltpu.VMEM),) * 3,
        scratch_shapes=scratch,
        compiler_params=pltpu.CompilerParams(vmem_limit_bytes=60 * 2**20),
        name="block",
    )(x, dy, gathered)


def factors(wide):
    inner = max(k for k in range(1, int(math.isqrt(wide)) + 1) if wide % k == 0)
    return wide // inner, inner


def remote(src, dst, send, recv, where):
    return pltpu.make_async_remote_copy(
        src_ref=src,
        dst_ref=dst,
        send_sem=send,
        recv_sem=recv,
        device_id=where,
        device_id_type=pl.DeviceIdType.MESH,
    )


def greet(devices):
    barrier = pltpu.get_barrier_semaphore()
    for dev in devices:
        pl.semaphore_signal(barrier, inc=1, device_id=dev, device_id_type=pl.DeviceIdType.MESH)
    pl.semaphore_wait(barrier, len(devices))


def gather_kernel(wide, shard, buf, send, send_sib, recv, recv_sib):
    outer, inner = factors(wide)
    me, core = lax.axis_index("wide"), lax.axis_index("narrow")
    zo, pi = me // inner, lax.rem(me, inner)
    rows, half = shard.shape[0], buf.shape[1] // 2
    mine = pl.ds(pl.multiple_of(core * half, 8), half)
    plane = [(zo * inner + lax.rem(pi + k, inner), core) for k in range(1, inner)]
    column = [(lax.rem(zo + k, outer) * inner + pi, core) for k in range(1, outer)]
    sibling = (me, 1 - core)
    greet(plane + column + [sibling])

    buf[me, 0:rows, :] = shard[...]
    buf[me, rows:, :] = jnp.zeros((buf.shape[1] - rows, LANES), F32)
    started = []

    def push(s, where, sems, k, recvs):
        copy = remote(buf.at[s, mine], buf.at[s, mine], sems.at[k], recvs.at[s], where)
        copy.start()
        started.append(copy)

    def arrived(s, recvs, part):
        remote(buf.at[s, part], buf.at[s, part], send.at[0], recvs.at[s], sibling).wait_recv()

    count = 0
    for where in column + plane:
        push(me, where, send, count, recv)
        count += 1
    sib = 0
    for k in range(outer - 1, 0, -1):
        s = lax.rem(zo + k, outer) * inner + pi
        arrived(s, recv, mine)
        for where in plane:
            push(s, where, send, count, recv)
            count += 1
        push(s, sibling, send_sib, sib, recv_sib)
        sib += 1
    for j in range(outer):
        for k in range(1, inner):
            s = lax.rem(zo + j, outer) * inner + lax.rem(pi + k, inner)
            arrived(s, recv, mine)
            push(s, sibling, send_sib, sib, recv_sib)
            sib += 1
    theirs = pl.ds(pl.multiple_of((1 - core) * half, 8), half)
    for k in range(1, wide):
        arrived(lax.rem(me + k, wide), recv_sib, theirs)
    for copy in started:
        copy.wait_send()


def gather(master, wide, padded):
    outer, inner = factors(wide)
    sends = outer - 1 + inner - 1 + (outer - 1) * (inner - 1)
    return pl.pallas_call(
        functools.partial(gather_kernel, wide),
        out_shape=jax.ShapeDtypeStruct((wide, padded, LANES), F32),
        in_specs=[pl.BlockSpec(memory_space=pltpu.VMEM)],
        out_specs=pl.BlockSpec(memory_space=pltpu.VMEM),
        scratch_shapes=[
            pltpu.SemaphoreType.DMA((sends,)),
            pltpu.SemaphoreType.DMA((wide - 1,)),
            pltpu.SemaphoreType.DMA((wide,)),
            pltpu.SemaphoreType.DMA((wide,)),
        ],
        compiler_params=pltpu.CompilerParams(
            collective_id=0, has_side_effects=True, vmem_limit_bytes=16 * 2**20
        ),
        name="gather",
    )(master)


def scatter_kernel(
    wide, parts, own, squares, sib_in, plane_in, col_in, res, sq, out_p, out_c,
    sib_send, sib_recv, plane_send, plane_recv, col_send, col_recv, fin, sq_send, sq_recv,
):
    outer, inner = factors(wide)
    me, core = lax.axis_index("wide"), lax.axis_index("narrow")
    zo, pi = me // inner, lax.rem(me, inner)
    rows, half = own.shape[0], res.shape[0] // 2
    mine = pl.ds(pl.multiple_of(core * half, 8), half)
    theirs = pl.ds(pl.multiple_of((1 - core) * half, 8), half)
    sibling = (me, 1 - core)
    others = [(lax.rem(me + k, wide), core) for k in range(1, wide)]
    greet(others + [sibling])
    started = []

    def go(copy):
        copy.start()
        started.append(copy)

    order = [lax.rem(pi + k, inner) for k in range(1, inner)] + [pi]
    for k, q in enumerate(order):
        go(remote(parts.at[:, q, theirs], sib_in.at[q], sib_send.at[k], sib_recv.at[q], sibling))
    for k, q in enumerate(order):
        remote(sib_in.at[q], sib_in.at[q], sib_send.at[k], sib_recv.at[q], sibling).wait_recv()
        both = parts[:, q, mine, :] + sib_in[q]
        if k < inner - 1:
            out_p[k] = both
            go(
                remote(
                    out_p.at[k], plane_in.at[pi], plane_send.at[k], plane_recv.at[pi],
                    (zo * inner + q, core),
                )
            )
        else:
            plane_in[pi] = both
    for q in order[:-1]:
        remote(
            plane_in.at[q], plane_in.at[q], plane_send.at[0], plane_recv.at[q], sibling
        ).wait_recv()
    levels = [lax.rem(zo + k, outer) for k in range(1, outer)] + [zo]
    for k, t in enumerate(levels):
        line = plane_in[0, t]
        for q in range(1, inner):
            line = line + plane_in[q, t]
        if k < outer - 1:
            out_c[k] = line
            go(
                remote(
                    out_c.at[k], col_in.at[zo], col_send.at[k], col_recv.at[zo],
                    (t * inner + pi, core),
                )
            )
        else:
            col_in[zo] = line
    for t in levels[:-1]:
        remote(col_in.at[t], col_in.at[t], col_send.at[0], col_recv.at[t], sibling).wait_recv()
    line = col_in[0]
    for t in range(1, outer):
        line = line + col_in[t]
    res[mine, :] = line
    last = remote(res.at[mine], res.at[mine], fin.at[0], fin.at[1], sibling)
    last.start()
    started.append(last)
    remote(res.at[theirs], res.at[theirs], fin.at[0], fin.at[1], sibling).wait_recv()
    full = res[...]
    own[...] = full[0:rows]
    sq[me] = rows8(full * full)
    for k, where in enumerate(others):
        go(remote(sq.at[me], sq.at[me], sq_send.at[k], sq_recv.at[me], where))
    for k in range(1, wide):
        s = lax.rem(me + k, wide)
        remote(sq.at[s], sq.at[s], sq_send.at[0], sq_recv.at[s], sibling).wait_recv()
    squares[...] = jnp.broadcast_to(jnp.sum(jnp.sum(sq[...], 0), keepdims=True), squares.shape)
    for copy in started:
        copy.wait_send()


def scatter(parts, rows, wide):
    outer, inner = factors(wide)
    padded = parts.shape[1]
    half = padded // 2
    vm, dma = pltpu.VMEM, pltpu.SemaphoreType.DMA
    return pl.pallas_call(
        functools.partial(scatter_kernel, wide),
        out_shape=(
            jax.ShapeDtypeStruct((rows, LANES), F32),
            jax.ShapeDtypeStruct((8, LANES), F32),
        ),
        in_specs=[pl.BlockSpec(memory_space=pltpu.VMEM)],
        out_specs=(pl.BlockSpec(memory_space=pltpu.VMEM),) * 2,
        scratch_shapes=[
            vm((inner, outer, half, LANES), F32),
            vm((inner, outer, half, LANES), F32),
            vm((outer, half, LANES), F32),
            vm((padded, LANES), F32),
            vm((wide, 8, LANES), F32),
            vm((inner - 1, outer, half, LANES), F32),
            vm((outer - 1, half, LANES), F32),
            dma((inner,)),
            dma((inner,)),
            dma((inner - 1,)),
            dma((inner,)),
            dma((outer - 1,)),
            dma((outer,)),
            dma((2,)),
            dma((wide - 1,)),
            dma((wide,)),
        ],
        compiler_params=pltpu.CompilerParams(
            collective_id=1, has_side_effects=True, vmem_limit_bytes=32 * 2**20
        ),
        name="scatter",
    )(parts.reshape(outer, inner, padded, LANES))


def on_device(inputs, cotangent, master, first, second):
    wide = lax.axis_size("wide")
    rows = master.shape[0] // LANES
    padded = (rows + 15) // 16 * 16
    gathered = gather(master.reshape(rows, LANES), wide, padded)
    block_out, input_grad, parts = block(inputs, cotangent, gathered, rows)
    owned, squares = scatter(parts, rows, wide)
    owned = owned.reshape(-1)
    squares = squares[0, 0]
    grad_norm = jnp.sqrt(squares)
    factor = jnp.minimum(1.0, 1.0 / (grad_norm + 1e-06))
    clipped = owned * factor
    new_first = 0.5 * first + 0.5 * clipped
    new_second = 0.5 * second + 0.5 * clipped * clipped
    fixed = 1.0 - 0.5**STEP
    new_master = master - 0.05 * (
        new_first / fixed / (jnp.sqrt(new_second / fixed) + 1e-08) + 0.1 * master
    )
    return (
        block_out,
        input_grad,
        clipped,
        grad_norm,
        new_master,
        new_master.astype(jnp.bfloat16),
        new_first,
        new_second,
    )


def solution(mesh):
    both, part = P(("wide", "narrow"), None), P("wide")
    return jax.shard_map(
        on_device,
        mesh=mesh,
        in_specs=(both, both, part, part, part),
        out_specs=(both, both, part, P(), part, part, part, part),
        check_vma=False,
    )
```

```python
import functools
import math

import jax
import jax.numpy as jnp
from jax import lax
from jax.experimental import pallas as pl
from jax.experimental.pallas import tpu as pltpu
from jax.sharding import PartitionSpec as P

D = 192
HEADS = 8
HEAD_DIM = 24
FF = 256
SEQ = 34
STEP = 5
ROWS = 40
GROUP = 3
GROWS = GROUP * ROWS
HJ = HEADS * ROWS
LANES = 128
F32 = jnp.float32
BF16 = jnp.bfloat16
MATS = ((0, D), (288, D), (576, D), (864, D), (1920, FF))
W1_AT = 1152
WIDTH1, WIDTH2, WIDTH3, DW_STEPS = 4, 4, 4, 2
LOCK1, LOCK2 = 4, 4
VEC_AT = 2304
GELU_C = math.sqrt(2.0 / math.pi)


def nn(a, b):
    return lax.dot_general(a, b, (((1,), (0,)), ((), ())), preferred_element_type=F32)


def nt(a, b):
    return lax.dot_general(a, b, (((1,), (1,)), ((), ())), preferred_element_type=F32)


def tn(a, b):
    return lax.dot_general(a, b, (((0,), (0,)), ((), ())), preferred_element_type=F32)


def low_half(v):
    lane = lax.broadcasted_iota(jnp.int32, v.shape, 1)
    return lane < 64


def load_square(flat, base, rows, tmp, out):
    half = rows // 2
    f0 = flat[pl.ds(base, half, stride=3), :]
    f1 = flat[pl.ds(base + 1, half, stride=3), :]
    f2 = flat[pl.ds(base + 2, half, stride=3), :]
    r1 = pltpu.roll(f1, 64, 1)
    r2 = pltpu.roll(f2, 64, 1)
    left = low_half(f0)
    lo, hi = tmp.at[0], tmp.at[1]
    lo[pl.ds(0, half, stride=2), :] = f0
    hi[pl.ds(0, half, stride=2), :] = jnp.where(left, f1, 0.0)
    lo[pl.ds(1, half, stride=2), :] = jnp.where(left, r1, r2)
    hi[pl.ds(1, half, stride=2), :] = jnp.where(left, r2, 0.0)
    out[0:rows, 0:128] = lo[0:rows, :].astype(BF16)
    out[0:rows, 128:256] = hi[0:rows, :].astype(BF16)
    if rows < 256:
        out[rows:256, :] = jnp.zeros((256 - rows, 256), BF16)


def store_square(val, flat, base, rows, tmp):
    half = rows // 2
    lo, hi = tmp.at[0], tmp.at[1]
    lo[0:rows, :] = val[0:rows, 0:128]
    hi[0:rows, :] = val[0:rows, 128:256]
    e0 = lo[pl.ds(0, half, stride=2), :]
    e1 = hi[pl.ds(0, half, stride=2), :]
    o0 = pltpu.roll(lo[pl.ds(1, half, stride=2), :], 64, 1)
    o1 = pltpu.roll(hi[pl.ds(1, half, stride=2), :], 64, 1)
    left = low_half(e0)
    flat[pl.ds(base, half, stride=3), :] = e0
    flat[pl.ds(base + 1, half, stride=3), :] = jnp.where(left, e1, o0)
    flat[pl.ds(base + 2, half, stride=3), :] = jnp.where(left, o0, o1)


def norm_fwd(x):
    mean = jnp.sum(x, -1, keepdims=True) * (1.0 / D)
    right = x[:, 128:256] - mean
    c = jnp.concatenate([x[:, 0:128] - mean, jnp.where(low_half(right), right, 0.0)], 1)
    var = jnp.sum(c * c, -1, keepdims=True) * (1.0 / D)
    r = lax.rsqrt(var + 1e-05)
    return c * r, r


def norm_back(d, xh, r, g):
    e = d * g
    m1 = jnp.sum(e, -1, keepdims=True) * (1.0 / D)
    m2 = jnp.sum(e * xh, -1, keepdims=True) * (1.0 / D)
    return r * (e - m1 - xh * m2)


def rows8(v):
    return jnp.sum(v.reshape(v.shape[0] // 8, 8, v.shape[1]), 0)


def split_tokens(v, count):
    zero = jnp.zeros((v.shape[0], 256 - D), v.dtype)
    return jnp.concatenate(
        [jnp.concatenate([v[:, D * t : D * (t + 1)], zero], 1) for t in range(count)], 0
    )


def join_tokens(v, n):
    return jnp.concatenate([v[n * t : n * (t + 1), 0:D] for t in range(v.shape[0] // n)], 1)


def block_kernel(
    x_ref, dy_ref, gathered, out_ref, ig_ref, gshards, flat, gflat,
    qs, ks, vs, os_, kbd, vbd, psc, xh1, r1, dx2s, h, h2, z, dul, o_t, dal, dyt, dqkv,
    wq, wk, wv, wo, w1, w2, tmp, hm2, hm, acc, acc2, acc3,
):
    n = x_ref.shape[0]
    toks = n * SEQ
    pairs = SEQ // 2
    groups = n // GROUP

    wide, rows_sh = gathered.shape[0], flat.shape[0] // gathered.shape[0]
    for w in range(wide):
        flat[rows_sh * w : rows_sh * (w + 1), :] = gathered[w, 0:rows_sh, :]
    for (base, rows), ref in zip(MATS, (wq, wk, wv, wo, w2)):
        load_square(flat, base, rows, tmp, ref)
    for c in range(4):
        w1[0:D, 128 * c : 128 * (c + 1)] = flat[pl.ds(W1_AT + c, D, stride=4), :].astype(BF16)

    w1[D:256, :] = jnp.zeros((256 - D, 2 * FF), BF16)

    def vec(k):
        a = VEC_AT + 3 * (k // 2)
        zero = jnp.zeros((1, 64), F32)
        if k % 2 == 0:
            return jnp.concatenate([flat[a : a + 1, :], flat[a + 1 : a + 2, 0:64], zero], 1)
        return jnp.concatenate([flat[a + 1 : a + 2, 64:128], flat[a + 2 : a + 3, :], zero], 1)

    g1, n1, bq, bv, bo, g2, n2, b2 = [vec(k) for k in range(8)]
    b1 = jnp.concatenate([flat[VEC_AT + 12 + c : VEC_AT + 13 + c, :] for c in range(4)], 1)

    lane = lax.broadcasted_iota(jnp.int32, (80, 256), 1)
    row = lax.broadcasted_iota(jnp.int32, (80, 256), 0)
    for p in range(4):
        lo = jnp.where(row < ROWS, HEAD_DIM * 2 * p, HEAD_DIM * (2 * p + 1))
        hm2[80 * p : 80 * (p + 1), :] = jnp.where(
            (lane >= lo) & (lane < lo + HEAD_DIM), 1.0, 0.0
        ).astype(BF16)
    lane16 = lax.broadcasted_iota(jnp.int32, (16, 256), 1)
    for k in range(HEADS):
        hm[16 * k : 16 * (k + 1), :] = jnp.where(
            (lane16 >= HEAD_DIM * k) & (lane16 < HEAD_DIM * (k + 1)), 1.0, 0.0
        ).astype(BF16)
    ones_lane = (lax.broadcasted_iota(jnp.int32, (toks, 64), 1) == 0).astype(F32).astype(BF16)
    for ref in (h, h2, o_t):
        ref[:, D:256] = ones_lane
    for ref in (qs, ks, vs, os_):
        ref[...] = jnp.zeros(ref.shape, F32)

    def tokens_of(ref, t, count):
        return split_tokens(
            ref[:, pl.ds(pl.multiple_of(t * D, 128), count * D)].astype(F32), count
        )

    def put_tokens(ref, t, val):
        for half in range(2):
            for k in range(val.shape[0] // n):
                ref.at[half][pl.ds(t + k, n, stride=ROWS), :] = val[
                    n * k : n * (k + 1), 128 * half : 128 * (half + 1)
                ]

    def get_tokens(ref, t, count):
        return jnp.concatenate(
            [
                jnp.concatenate(
                    [ref.at[half][pl.ds(t + k, n, stride=ROWS), :] for half in range(2)], 1
                )
                for k in range(count)
            ],
            0,
        )

    def over_token_chunks(body, width, carry):
        whole = pairs // width
        carry = lax.fori_loop(0, whole, lambda i, c: body(i * (2 * width), 2 * width, c), carry)
        if pairs % width:
            carry = body(whole * 2 * width, 2 * (pairs % width), carry)
        return carry

    def get_rows(ref, start, count):
        return jnp.concatenate([ref[0, pl.ds(start, count), :], ref[1, pl.ds(start, count), :]], 1)

    def put_rows(ref, start, val):
        for half in range(2):
            ref[half, pl.ds(start, val.shape[0]), :] = val[:, 128 * half : 128 * (half + 1)]

    def rows_at(t, count):
        return pl.ds(pl.multiple_of(t * n, 32), count * n)

    def dense1(t, count, carry):
        at = rows_at(t, count)
        xh, r = norm_fwd(tokens_of(x_ref, t, count))
        hb = (xh * g1 + n1).astype(BF16)
        xh1[at, :] = xh
        r1[at, :] = r
        h[at, 0:D] = hb[:, 0:D]
        put_tokens(qs, t, (nn(hb, wq[...]) + bq).astype(BF16).astype(F32))
        put_tokens(ks, t, nn(hb, wk[...]).astype(BF16).astype(F32))
        put_tokens(vs, t, (nn(hb, wv[...]) + bv).astype(BF16).astype(F32))
        return carry

    over_token_chunks(dense1, WIDTH1, 0)

    lane3 = lax.broadcasted_iota(jnp.int32, (1, LANES), 1)

    def squeeze(v):
        return jnp.where(
            lane3 < ROWS, v[0:HJ], jnp.where(lane3 < 2 * ROWS, v[HJ : 2 * HJ], v[2 * HJ : 3 * HJ])
        ).reshape(HEADS, ROWS, LANES)

    jrow = lax.broadcasted_iota(jnp.int32, (1, ROWS, LANES), 1)
    cexp = math.log2(math.e) / math.sqrt(HEAD_DIM)
    scale = 1.0 / math.sqrt(HEAD_DIM)

    def attn(i, carry):
        r0 = pl.multiple_of(i * (LOCK1 * GROWS), 8)
        base0 = pl.multiple_of(i * (LOCK1 * 3 * HJ), 64)
        p0 = pl.multiple_of(i * (LOCK1 * HJ), 64)
        sets = range(LOCK1)
        qg = [get_rows(qs, r0 + GROWS * k, LANES).astype(BF16) for k in sets]
        for k in sets:
            for src, dst in ((ks, kbd), (vs, vbd)):
                for b in range(GROUP):
                    one = get_rows(src, r0 + GROWS * k + ROWS * b, ROWS)
                    two = jnp.concatenate([one, one], 0).astype(BF16)
                    for p in range(4):
                        dst[pl.ds(base0 + HJ * (3 * k + b) + 80 * p, 80), :] = (
                            two * hm2[80 * p : 80 * (p + 1), :]
                        )
        st = [squeeze(nt(kbd[pl.ds(base0 + 3 * HJ * k, 3 * HJ), :], qg[k])) for k in sets]
        st = [jnp.where(jrow < SEQ, v, -1e30) for v in st]
        m = [jnp.max(v, 1, keepdims=True) for v in st]
        e = [jnp.exp2((st[k] - m[k]) * cexp) for k in sets]
        l = [1.0 / jnp.sum(v, 1, keepdims=True) for v in e]
        p = [(e[k] * l[k]).reshape(HJ, LANES) for k in sets]
        for k in sets:
            psc[pl.ds(p0 + HJ * k, HJ), :] = p[k]
        pt = [v.T for v in p]
        for b in range(GROUP):
            for k in sets:
                ob = nn(
                    pt[k][ROWS * b : ROWS * (b + 1), :].astype(BF16),
                    vbd[pl.ds(base0 + HJ * (3 * k + b), HJ), :],
                )
                put_rows(os_, r0 + GROWS * k + ROWS * b, ob.astype(BF16).astype(F32)[0:SEQ])
        return carry

    lax.fori_loop(0, groups // LOCK1, attn, 0)

    def dense2(t0, count, carry):
        dg2, dn2, db2 = carry
        at = rows_at(t0, count)
        o = get_tokens(os_, t0, count).astype(BF16)
        o_t[at, 0:D] = o[:, 0:D]
        x2 = tokens_of(x_ref, t0, count) + (nn(o, wo[...]) + bo)
        xh, r = norm_fwd(x2)
        hb = (xh * g2 + n2).astype(BF16)
        h2[at, 0:D] = hb[:, 0:D]
        u = nn(hb, w1[...]) + b1
        gate, up = u[:, :FF], u[:, FF:]
        sq = gate * gate
        t = jnp.tanh(gate * (GELU_C + (GELU_C * 0.044715) * sq))
        half = 0.5 + 0.5 * t
        act = gate * half
        zb = (act * up).astype(BF16)
        z[at, :] = zb
        y = x2 + nn(zb, w2[...]) + b2
        out_ref[:, pl.ds(pl.multiple_of(t0 * D, 128), count * D)] = join_tokens(y, n).astype(BF16)
        dyf = tokens_of(dy_ref, t0, count)
        dyb = dyf.astype(BF16)
        dyt[at, :] = dyb
        dz = nt(dyb, w2[...])
        slope = half + gate * (0.5 - 0.5 * t * t) * (GELU_C + (3 * GELU_C * 0.044715) * sq)
        du = jnp.concatenate([(dz * up * slope).astype(BF16), (dz * act).astype(BF16)], 1)
        dul[at, :] = du
        dh = nt(du, w1[...])
        dx2 = dyf + norm_back(dh, xh, r, g2)
        dx2s[at, :] = dx2
        da = dx2.astype(BF16)
        dal[at, :] = da
        put_tokens(os_, t0, nt(da, wo[...]).astype(BF16).astype(F32))
        return dg2 + rows8(dh * xh), dn2 + rows8(dh), db2 + rows8(dyf)

    zero = jnp.zeros((8, 256), F32)
    dg2, dn2, db2 = over_token_chunks(dense2, WIDTH2, (zero, zero, zero))

    def total(v):
        return jnp.sum(v, 0, keepdims=True)

    def over_tokens(acc, a, b):
        acc[...] = jnp.zeros(acc.shape, F32)
        steps = DW_STEPS
        size = toks // steps

        @pl.loop(0, steps)
        def _(i):
            at = pl.ds(pl.multiple_of(i * size, 16), size)
            acc[...] += tn(a[at, :], b[at, :])

        return acc[...]

    store_square(over_tokens(acc, z, dyt), gflat, 1920, FF, tmp)
    dw1 = over_tokens(acc2, h2, dul)
    for c in range(4):
        gflat[pl.ds(W1_AT + c, D, stride=4), :] = dw1[0:D, 128 * c : 128 * (c + 1)]
        gflat[VEC_AT + 12 + c : VEC_AT + 13 + c, :] = dw1[D : D + 1, 128 * c : 128 * (c + 1)]
    dwo = over_tokens(acc, o_t, dal)
    store_square(dwo, gflat, 864, D, tmp)
    dbo = dwo[D : D + 1]

    def wide_rows(v):
        blocks = []
        for k in range(HEADS):
            one = v[k]
            parts = [
                jnp.where((lane3 >= ROWS * b) & (lane3 < ROWS * (b + 1)), one, 0.0)
                for b in range(GROUP)
            ]
            parts.append(jnp.zeros((8, LANES), F32))
            blocks.append(jnp.concatenate(parts, 0).astype(BF16))
        return jnp.concatenate(blocks, 1)

    def masked(v):
        v3 = v.reshape(8, 16, 256)
        return jnp.concatenate(
            [(v3 * hm[16 * k : 16 * (k + 1), :][None]).reshape(128, 256) for k in range(HEADS)], 0
        )

    def attn_back(i, carry):
        r0 = pl.multiple_of(i * (LOCK2 * GROWS), 8)
        base0 = pl.multiple_of(i * (LOCK2 * 3 * HJ), 64)
        p0 = pl.multiple_of(i * (LOCK2 * HJ), 64)
        sets = range(LOCK2)
        qg = [get_rows(qs, r0 + GROWS * k, LANES).astype(BF16) for k in sets]
        dg = [get_rows(os_, r0 + GROWS * k, LANES).astype(BF16) for k in sets]
        dp = [squeeze(nt(vbd[pl.ds(base0 + 3 * HJ * k, 3 * HJ), :], dg[k])) for k in sets]
        p = [psc[pl.ds(p0 + HJ * k, HJ), :].reshape(HEADS, ROWS, LANES) for k in sets]
        t = [jnp.sum(p[k] * dp[k], 1, keepdims=True) for k in sets]
        ds = [p[k] * (dp[k] - t[k]) for k in sets]
        dst = [v.reshape(HJ, LANES).T for v in ds]
        dv = [nn(wide_rows(p[k]), masked(dg[k])) for k in sets]
        dk = [nn(wide_rows(ds[k]), masked(qg[k])) * scale for k in sets]
        for b in range(GROUP):
            for k in sets:
                dq = nn(
                    dst[k][ROWS * b : ROWS * (b + 1), :].astype(BF16),
                    kbd[pl.ds(base0 + HJ * (3 * k + b), HJ), :],
                )
                put_rows(qs, r0 + GROWS * k + ROWS * b, (dq * scale).astype(BF16).astype(F32))
        for k in sets:
            put_rows(vs, r0 + GROWS * k, dv[k].astype(BF16).astype(F32)[0:GROWS])
            put_rows(ks, r0 + GROWS * k, dk[k].astype(BF16).astype(F32)[0:GROWS])
        return carry

    lax.fori_loop(0, groups // LOCK2, attn_back, 0)

    def dense3(t0, count, carry):
        dg1, dn1 = carry
        at = rows_at(t0, count)
        dq = get_tokens(qs, t0, count).astype(BF16)
        dk = get_tokens(ks, t0, count).astype(BF16)
        dv = get_tokens(vs, t0, count).astype(BF16)
        dqkv[at, :] = jnp.concatenate([dq, dk, dv], 1)
        dh = nt(dq, wq[...]) + nt(dk, wk[...]) + nt(dv, wv[...])
        xh = xh1[at, :]
        ig = dx2s[at, :] + norm_back(dh, xh, r1[at, :], g1)
        ig_ref[:, pl.ds(pl.multiple_of(t0 * D, 128), count * D)] = join_tokens(ig, n)
        return dg1 + rows8(dh * xh), dn1 + rows8(dh)

    dg1, dn1 = over_token_chunks(dense3, WIDTH3, (zero, zero))
    dw = over_tokens(acc3, h, dqkv)
    for k in range(3):
        store_square(dw[:, 256 * k : 256 * (k + 1)], gflat, 288 * k, D, tmp)

    vecs = [total(dg1), total(dn1), dw[D : D + 1, 0:256], dw[D : D + 1, 512:768], dbo, total(dg2), total(dn2), total(db2)]
    for k in range(4):
        a, b = vecs[2 * k], vecs[2 * k + 1]
        gflat[VEC_AT + 3 * k : VEC_AT + 3 * k + 1, :] = a[:, 0:128]
        gflat[VEC_AT + 3 * k + 1 : VEC_AT + 3 * k + 2, :] = jnp.concatenate(
            [a[:, 128:192], b[:, 0:64]], 1
        )
        gflat[VEC_AT + 3 * k + 2 : VEC_AT + 3 * k + 3, :] = b[:, 64:192]
    used = VEC_AT + 16
    if gflat.shape[0] > used:
        gflat[used:, :] = jnp.zeros((gflat.shape[0] - used, LANES), F32)
    for w in range(wide):
        gshards[w, 0:rows_sh, :] = gflat[rows_sh * w : rows_sh * (w + 1), :]
        gshards[w, rows_sh:, :] = jnp.zeros((gshards.shape[1] - rows_sh, LANES), F32)


def block(x, dy, gathered, rows_sh):
    n = x.shape[0]
    toks = n * SEQ
    sm = (2, n * ROWS + 8, LANES)
    groups = n // GROUP
    vm = pltpu.VMEM
    tok = vm((toks, 256), BF16)
    flat = vm((gathered.shape[0] * rows_sh, LANES), F32)
    scratch = (
        [flat, flat]
        + [vm(sm, F32)] * 4
        + [vm((groups * 3 * HJ, 256), BF16)] * 2
        + [vm((groups * HJ, LANES), F32)]
        + [vm((toks, 256), F32), vm((toks, 1), F32), vm((toks, 256), F32)]
        + [tok, tok, tok, vm((toks, 2 * FF), BF16), tok]
        + [tok, tok, vm((toks, 3 * 256), BF16)]
        + [vm((256, 256), BF16)] * 4
        + [vm((256, 2 * FF), BF16), vm((FF, 256), BF16), vm((2, FF, 128), F32)]
        + [vm((320, 256), BF16), vm((128, 256), BF16), vm((256, 256), F32), vm((256, 512), F32), vm((256, 768), F32)]
    )
    return pl.pallas_call(
        block_kernel,
        out_shape=(
            jax.ShapeDtypeStruct(x.shape, BF16),
            jax.ShapeDtypeStruct(x.shape, F32),
            jax.ShapeDtypeStruct(gathered.shape, F32),
        ),
        in_specs=[pl.BlockSpec(memory_space=pltpu.VMEM)] * 3,
        out_specs=(pl.BlockSpec(memory_space=pltpu.VMEM),) * 3,
        scratch_shapes=scratch,
        compiler_params=pltpu.CompilerParams(vmem_limit_bytes=60 * 2**20),
        name="block",
    )(x, dy, gathered)


def factors(wide):
    inner = max(k for k in range(1, int(math.isqrt(wide)) + 1) if wide % k == 0)
    return wide // inner, inner


def remote(src, dst, send, recv, where):
    return pltpu.make_async_remote_copy(
        src_ref=src,
        dst_ref=dst,
        send_sem=send,
        recv_sem=recv,
        device_id=where,
        device_id_type=pl.DeviceIdType.MESH,
    )


def greet(devices):
    barrier = pltpu.get_barrier_semaphore()
    for dev in devices:
        pl.semaphore_signal(barrier, inc=1, device_id=dev, device_id_type=pl.DeviceIdType.MESH)
    pl.semaphore_wait(barrier, len(devices))


def gather_kernel(wide, shard, buf, send, send_sib, recv, recv_sib):
    outer, inner = factors(wide)
    me, core = lax.axis_index("wide"), lax.axis_index("narrow")
    zo, pi = me // inner, lax.rem(me, inner)
    rows, half = shard.shape[0], buf.shape[1] // 2
    mine = pl.ds(pl.multiple_of(core * half, 8), half)
    plane = [(zo * inner + lax.rem(pi + k, inner), core) for k in range(1, inner)]
    column = [(lax.rem(zo + k, outer) * inner + pi, core) for k in range(1, outer)]
    sibling = (me, 1 - core)
    greet(plane + column + [sibling])

    buf[me, 0:rows, :] = shard[...]
    buf[me, rows:, :] = jnp.zeros((buf.shape[1] - rows, LANES), F32)
    started = []

    def push(s, where, sems, k, recvs):
        copy = remote(buf.at[s, mine], buf.at[s, mine], sems.at[k], recvs.at[s], where)
        copy.start()
        started.append(copy)

    def arrived(s, recvs, part):
        remote(buf.at[s, part], buf.at[s, part], send.at[0], recvs.at[s], sibling).wait_recv()

    count = 0
    for where in column + plane:
        push(me, where, send, count, recv)
        count += 1
    sib = 0
    for k in range(outer - 1, 0, -1):
        s = lax.rem(zo + k, outer) * inner + pi
        arrived(s, recv, mine)
        for where in plane:
            push(s, where, send, count, recv)
            count += 1
        push(s, sibling, send_sib, sib, recv_sib)
        sib += 1
    for j in range(outer):
        for k in range(1, inner):
            s = lax.rem(zo + j, outer) * inner + lax.rem(pi + k, inner)
            arrived(s, recv, mine)
            push(s, sibling, send_sib, sib, recv_sib)
            sib += 1
    theirs = pl.ds(pl.multiple_of((1 - core) * half, 8), half)
    for k in range(1, wide):
        arrived(lax.rem(me + k, wide), recv_sib, theirs)
    for copy in started:
        copy.wait_send()


def gather(master, wide, padded):
    outer, inner = factors(wide)
    sends = outer - 1 + inner - 1 + (outer - 1) * (inner - 1)
    return pl.pallas_call(
        functools.partial(gather_kernel, wide),
        out_shape=jax.ShapeDtypeStruct((wide, padded, LANES), F32),
        in_specs=[pl.BlockSpec(memory_space=pltpu.VMEM)],
        out_specs=pl.BlockSpec(memory_space=pltpu.VMEM),
        scratch_shapes=[
            pltpu.SemaphoreType.DMA((sends,)),
            pltpu.SemaphoreType.DMA((wide - 1,)),
            pltpu.SemaphoreType.DMA((wide,)),
            pltpu.SemaphoreType.DMA((wide,)),
        ],
        compiler_params=pltpu.CompilerParams(
            collective_id=0, has_side_effects=True, vmem_limit_bytes=16 * 2**20
        ),
        name="gather",
    )(master)


def scatter_kernel(
    wide, parts, own, squares, sib_in, plane_in, col_in, res, sq, out_p, out_c,
    sib_send, sib_recv, plane_send, plane_recv, col_send, col_recv, fin, sq_send, sq_recv,
):
    outer, inner = factors(wide)
    me, core = lax.axis_index("wide"), lax.axis_index("narrow")
    zo, pi = me // inner, lax.rem(me, inner)
    rows, half = own.shape[0], res.shape[0] // 2
    mine = pl.ds(pl.multiple_of(core * half, 8), half)
    theirs = pl.ds(pl.multiple_of((1 - core) * half, 8), half)
    sibling = (me, 1 - core)
    others = [(lax.rem(me + k, wide), core) for k in range(1, wide)]
    greet(others + [sibling])
    started = []

    def go(copy):
        copy.start()
        started.append(copy)

    order = [lax.rem(pi + k, inner) for k in range(1, inner)] + [pi]
    for k, q in enumerate(order):
        go(remote(parts.at[:, q, theirs], sib_in.at[q], sib_send.at[k], sib_recv.at[q], sibling))
    for k, q in enumerate(order):
        remote(sib_in.at[q], sib_in.at[q], sib_send.at[k], sib_recv.at[q], sibling).wait_recv()
        both = parts[:, q, mine, :] + sib_in[q]
        if k < inner - 1:
            out_p[k] = both
            go(
                remote(
                    out_p.at[k], plane_in.at[pi], plane_send.at[k], plane_recv.at[pi],
                    (zo * inner + q, core),
                )
            )
        else:
            plane_in[pi] = both
    for q in order[:-1]:
        remote(
            plane_in.at[q], plane_in.at[q], plane_send.at[0], plane_recv.at[q], sibling
        ).wait_recv()
    levels = [lax.rem(zo + k, outer) for k in range(1, outer)] + [zo]
    for k, t in enumerate(levels):
        line = plane_in[0, t]
        for q in range(1, inner):
            line = line + plane_in[q, t]
        if k < outer - 1:
            out_c[k] = line
            go(
                remote(
                    out_c.at[k], col_in.at[zo], col_send.at[k], col_recv.at[zo],
                    (t * inner + pi, core),
                )
            )
        else:
            col_in[zo] = line
    for t in levels[:-1]:
        remote(col_in.at[t], col_in.at[t], col_send.at[0], col_recv.at[t], sibling).wait_recv()
    line = col_in[0]
    for t in range(1, outer):
        line = line + col_in[t]
    res[mine, :] = line
    last = remote(res.at[mine], res.at[mine], fin.at[0], fin.at[1], sibling)
    last.start()
    started.append(last)
    remote(res.at[theirs], res.at[theirs], fin.at[0], fin.at[1], sibling).wait_recv()
    full = res[...]
    own[...] = full[0:rows]
    sq[me] = rows8(full * full)
    for k, where in enumerate(others):
        go(remote(sq.at[me], sq.at[me], sq_send.at[k], sq_recv.at[me], where))
    for k in range(1, wide):
        s = lax.rem(me + k, wide)
        remote(sq.at[s], sq.at[s], sq_send.at[0], sq_recv.at[s], sibling).wait_recv()
    squares[...] = jnp.broadcast_to(jnp.sum(jnp.sum(sq[...], 0), keepdims=True), squares.shape)
    for copy in started:
        copy.wait_send()


def scatter(parts, rows, wide):
    outer, inner = factors(wide)
    padded = parts.shape[1]
    half = padded // 2
    vm, dma = pltpu.VMEM, pltpu.SemaphoreType.DMA
    return pl.pallas_call(
        functools.partial(scatter_kernel, wide),
        out_shape=(
            jax.ShapeDtypeStruct((rows, LANES), F32),
            jax.ShapeDtypeStruct((8, LANES), F32),
        ),
        in_specs=[pl.BlockSpec(memory_space=pltpu.VMEM)],
        out_specs=(pl.BlockSpec(memory_space=pltpu.VMEM),) * 2,
        scratch_shapes=[
            vm((inner, outer, half, LANES), F32),
            vm((inner, outer, half, LANES), F32),
            vm((outer, half, LANES), F32),
            vm((padded, LANES), F32),
            vm((wide, 8, LANES), F32),
            vm((inner - 1, outer, half, LANES), F32),
            vm((outer - 1, half, LANES), F32),
            dma((inner,)),
            dma((inner,)),
            dma((inner - 1,)),
            dma((inner,)),
            dma((outer - 1,)),
            dma((outer,)),
            dma((2,)),
            dma((wide - 1,)),
            dma((wide,)),
        ],
        compiler_params=pltpu.CompilerParams(
            collective_id=1, has_side_effects=True, vmem_limit_bytes=32 * 2**20
        ),
        name="scatter",
    )(parts.reshape(outer, inner, padded, LANES))


def on_device(inputs, cotangent, master, first, second):
    wide = lax.axis_size("wide")
    rows = master.shape[0] // LANES
    padded = (rows + 15) // 16 * 16
    gathered = gather(master.reshape(rows, LANES), wide, padded)
    block_out, input_grad, parts = block(inputs, cotangent, gathered, rows)
    owned, squares = scatter(parts, rows, wide)
    owned = owned.reshape(-1)
    squares = squares[0, 0]
    grad_norm = jnp.sqrt(squares)
    factor = jnp.minimum(1.0, 1.0 / (grad_norm + 1e-06))
    clipped = owned * factor
    new_first = 0.5 * first + 0.5 * clipped
    new_second = 0.5 * second + 0.5 * clipped * clipped
    fixed = 1.0 - 0.5**STEP
    new_master = master - 0.05 * (
        new_first / fixed / (jnp.sqrt(new_second / fixed) + 1e-08) + 0.1 * master
    )
    return (
        block_out,
        input_grad,
        clipped,
        grad_norm,
        new_master,
        new_master.astype(jnp.bfloat16),
        new_first,
        new_second,
    )


def solution(mesh):
    both, part = P(("wide", "narrow"), None), P("wide")
    return jax.shard_map(
        on_device,
        mesh=mesh,
        in_specs=(both, both, part, part, part),
        out_specs=(both, both, part, P(), part, part, part, part),
        check_vma=False,
    )
```

```python
import functools
import math

import jax
import jax.numpy as jnp
from jax import lax
from jax.experimental import pallas as pl
from jax.experimental.pallas import tpu as pltpu
from jax.sharding import PartitionSpec as P

D = 192
HEADS = 8
HEAD_DIM = 24
FF = 256
SEQ = 34
STEP = 5
ROWS = 40
GROUP = 3
GROWS = GROUP * ROWS
HJ = HEADS * ROWS
LANES = 128
F32 = jnp.float32
BF16 = jnp.bfloat16
MATS = ((0, D), (288, D), (576, D), (864, D), (1920, FF))
W1_AT = 1152
WIDTH1, WIDTH2, WIDTH3, DW_STEPS = 4, 4, 4, 2
LOCK1, LOCK2 = 4, 4
VEC_AT = 2304
USED_ROWS = VEC_AT + 16
QKV_ROWS = 864
GELU_C = math.sqrt(2.0 / math.pi)


def nn(a, b):
    return lax.dot_general(a, b, (((1,), (0,)), ((), ())), preferred_element_type=F32)


def nt(a, b):
    return lax.dot_general(a, b, (((1,), (1,)), ((), ())), preferred_element_type=F32)


def tn(a, b):
    return lax.dot_general(a, b, (((0,), (0,)), ((), ())), preferred_element_type=F32)


def low_half(v):
    lane = lax.broadcasted_iota(jnp.int32, v.shape, 1)
    return lane < 64


def load_square(flat, base, rows, tmp, out):
    half = rows // 2
    f0 = flat[pl.ds(base, half, stride=3), :]
    f1 = flat[pl.ds(base + 1, half, stride=3), :]
    f2 = flat[pl.ds(base + 2, half, stride=3), :]
    r1 = pltpu.roll(f1, 64, 1)
    r2 = pltpu.roll(f2, 64, 1)
    left = low_half(f0)
    lo, hi = tmp.at[0], tmp.at[1]
    lo[pl.ds(0, half, stride=2), :] = f0
    hi[pl.ds(0, half, stride=2), :] = jnp.where(left, f1, 0.0)
    lo[pl.ds(1, half, stride=2), :] = jnp.where(left, r1, r2)
    hi[pl.ds(1, half, stride=2), :] = jnp.where(left, r2, 0.0)
    out[0:rows, 0:128] = lo[0:rows, :].astype(BF16)
    out[0:rows, 128:256] = hi[0:rows, :].astype(BF16)
    if rows < 256:
        out[rows:256, :] = jnp.zeros((256 - rows, 256), BF16)


def store_square(val, flat, base, rows, tmp):
    half = rows // 2
    lo, hi = tmp.at[0], tmp.at[1]
    lo[0:rows, :] = val[0:rows, 0:128]
    hi[0:rows, :] = val[0:rows, 128:256]
    e0 = lo[pl.ds(0, half, stride=2), :]
    e1 = hi[pl.ds(0, half, stride=2), :]
    o0 = pltpu.roll(lo[pl.ds(1, half, stride=2), :], 64, 1)
    o1 = pltpu.roll(hi[pl.ds(1, half, stride=2), :], 64, 1)
    left = low_half(e0)
    flat[pl.ds(base, half, stride=3), :] = e0
    flat[pl.ds(base + 1, half, stride=3), :] = jnp.where(left, e1, o0)
    flat[pl.ds(base + 2, half, stride=3), :] = jnp.where(left, o0, o1)


def norm_fwd(x):
    mean = jnp.sum(x, -1, keepdims=True) * (1.0 / D)
    right = x[:, 128:256] - mean
    c = jnp.concatenate([x[:, 0:128] - mean, jnp.where(low_half(right), right, 0.0)], 1)
    var = jnp.sum(c * c, -1, keepdims=True) * (1.0 / D)
    r = lax.rsqrt(var + 1e-05)
    return c * r, r


def norm_back(d, xh, r, g):
    e = d * g
    m1 = jnp.sum(e, -1, keepdims=True) * (1.0 / D)
    m2 = jnp.sum(e * xh, -1, keepdims=True) * (1.0 / D)
    return r * (e - m1 - xh * m2)


def rows8(v):
    return jnp.sum(v.reshape(v.shape[0] // 8, 8, v.shape[1]), 0)


def split_tokens(v, count):
    zero = jnp.zeros((v.shape[0], 256 - D), v.dtype)
    return jnp.concatenate(
        [jnp.concatenate([v[:, D * t : D * (t + 1)], zero], 1) for t in range(count)], 0
    )


def join_tokens(v, n):
    return jnp.concatenate([v[n * t : n * (t + 1), 0:D] for t in range(v.shape[0] // n)], 1)


def factors(wide):
    inner = max(k for k in range(1, int(math.isqrt(wide)) + 1) if wide % k == 0)
    return wide // inner, inner


def remote(src, dst, send, recv, where):
    return pltpu.make_async_remote_copy(
        src_ref=src,
        dst_ref=dst,
        send_sem=send,
        recv_sem=recv,
        device_id=where,
        device_id_type=pl.DeviceIdType.MESH,
    )


def greet(devices):
    barrier = pltpu.get_barrier_semaphore()
    for dev in devices:
        pl.semaphore_signal(barrier, inc=1, device_id=dev, device_id_type=pl.DeviceIdType.MESH)
    pl.semaphore_wait(barrier, len(devices))


def step_kernel(
    wide,
    x_hbm, dy_hbm, shard, out_hbm, ig_hbm, own, squares,
    x_ref, dy_ref, out_ref, ig_ref, flat, gflat,
    qs, ks, vs, os_, kbd, vbd, psc, xh1, r1, dx2s, h, h2, z, dul, o_t, dal, dyt, dqkv,
    wq, wk, wv, wo, w1, w2, tmp, hm2, hm, acc, acc2, acc3,
    buf, parts, sib_in, plane_in, out_p, col_in, out_c, res, vec_own, vec_sib, vec_plane, vec_col,
    vec_at, sq_plane, sq_col,
    io_sem, g_col, g_fw, g_sib, g_recv, g_recv_sib, s_send, s_recv, p_send, p_recv, c_send, c_recv,
    f_sem, v_send, v_recv, n_send, n_recv,
):
    n = x_ref.shape[0]
    toks = n * SEQ
    pairs = SEQ // 2
    groups = n // GROUP
    rows = shard.shape[0]
    half = buf.shape[1] // 2
    outer, inner = factors(wide)
    me, core = lax.axis_index("wide"), lax.axis_index("narrow")
    zo, pi = me // inner, lax.rem(me, inner)
    mine = pl.ds(pl.multiple_of(core * half, 8), half)
    theirs = pl.ds(pl.multiple_of((1 - core) * half, 8), half)
    sibling = (me, 1 - core)
    around = [lax.rem(pi + k, inner) for k in range(1, inner)]
    along = [lax.rem(zo + k, outer) for k in range(1, outer)]
    plane = [(zo * inner + q, core) for q in around]
    column = [(t * inner + pi, core) for t in along]
    first = -(-QKV_ROWS // (rows * inner))

    copies_in = [
        pltpu.make_async_copy(x_hbm, x_ref, io_sem.at[0]),
        pltpu.make_async_copy(dy_hbm, dy_ref, io_sem.at[1]),
    ]
    for copy in copies_in:
        copy.start()

    greet(plane + column + [sibling])
    buf[me, 0:rows, :] = shard[...]
    buf[me, rows:, :] = jnp.zeros((buf.shape[1] - rows, LANES), F32)

    def push(s, send, recvs, where):
        return remote(buf.at[s, mine], buf.at[s, mine], send, recvs.at[s], where)

    def arrived(s, recvs, part):
        remote(buf.at[s, part], buf.at[s, part], g_sib.at[s], recvs.at[s], sibling).wait_recv()

    def forwards(t, s):
        return [push(s, g_fw.at[t, k], g_recv, where) for k, where in enumerate(plane)]

    own_pushes = [push(me, g_col.at[k], g_recv, where) for k, where in enumerate(column)]
    own_pushes += forwards(zo, me)
    for copy in own_pushes:
        copy.start()

    def to_sibling(s):
        return push(s, g_sib.at[s], g_recv_sib, sibling)

    def forward_level(t):
        s = t * inner + pi

        @pl.when(t != zo)
        def _():
            arrived(s, g_recv, mine)
            for copy in forwards(t, s):
                copy.start()
            to_sibling(s).start()

    def pass_level(t):
        for q in around:
            s = t * inner + q
            arrived(s, g_recv, mine)
            to_sibling(s).start()

    def whole_shard(s):
        @pl.when(s != me)
        def _():
            arrived(s, g_recv_sib, theirs)

    def unpack(s):
        flat[rows * s : rows * (s + 1), :] = buf[s, 0:rows, :]

    vec_shards = range(VEC_AT // rows, (USED_ROWS - 1) // rows + 1)
    early_shards = [s for s in range(wide) if s < first * inner or s in vec_shards]
    late_shards = [s for s in range(wide) if s not in early_shards]

    lane = lax.broadcasted_iota(jnp.int32, (80, 256), 1)
    row = lax.broadcasted_iota(jnp.int32, (80, 256), 0)
    for p in range(4):
        lo = jnp.where(row < ROWS, HEAD_DIM * 2 * p, HEAD_DIM * (2 * p + 1))
        hm2[80 * p : 80 * (p + 1), :] = jnp.where(
            (lane >= lo) & (lane < lo + HEAD_DIM), 1.0, 0.0
        ).astype(BF16)
    lane16 = lax.broadcasted_iota(jnp.int32, (16, 256), 1)
    for k in range(HEADS):
        hm[16 * k : 16 * (k + 1), :] = jnp.where(
            (lane16 >= HEAD_DIM * k) & (lane16 < HEAD_DIM * (k + 1)), 1.0, 0.0
        ).astype(BF16)
    ones_lane = (lax.broadcasted_iota(jnp.int32, (toks, 64), 1) == 0).astype(F32).astype(BF16)
    for ref in (h, h2, o_t):
        ref[:, D:256] = ones_lane
    for ref in (qs, ks, vs, os_):
        ref[...] = jnp.zeros(ref.shape, F32)

    parts[...] = jnp.zeros(parts.shape, F32)
    vec_at[...] = jnp.zeros(vec_at.shape, F32)
    for t in range(outer):
        forward_level(t)

    def tokens_of(ref, t, count):
        return split_tokens(
            ref[:, pl.ds(pl.multiple_of(t * D, 128), count * D)].astype(F32), count
        )

    def put_tokens(ref, t, val):
        for half in range(2):
            for k in range(val.shape[0] // n):
                ref.at[half][pl.ds(t + k, n, stride=ROWS), :] = val[
                    n * k : n * (k + 1), 128 * half : 128 * (half + 1)
                ]

    def get_tokens(ref, t, count):
        return jnp.concatenate(
            [
                jnp.concatenate(
                    [ref.at[half][pl.ds(t + k, n, stride=ROWS), :] for half in range(2)], 1
                )
                for k in range(count)
            ],
            0,
        )

    def over_token_chunks(body, width, carry, hook=lambda i: None):
        whole = pairs // width

        def step(i, c):
            hook(i)
            return body(i * (2 * width), 2 * width, c)

        carry = lax.fori_loop(0, whole, step, carry)
        if pairs % width:
            carry = body(whole * 2 * width, 2 * (pairs % width), carry)
        return carry

    def get_rows(ref, start, count):
        return jnp.concatenate([ref[0, pl.ds(start, count), :], ref[1, pl.ds(start, count), :]], 1)

    def put_rows(ref, start, val):
        for half in range(2):
            ref[half, pl.ds(start, val.shape[0]), :] = val[:, 128 * half : 128 * (half + 1)]

    def rows_at(t, count):
        return pl.ds(pl.multiple_of(t * n, 32), count * n)

    def norm1(t, count, carry):
        at = rows_at(t, count)
        xh, r = norm_fwd(tokens_of(x_ref, t, count))
        xh1[at, :] = xh
        r1[at, :] = r
        return carry

    copies_in[0].wait()
    over_token_chunks(norm1, WIDTH1, 0)

    for t in range(first):
        pass_level(t)
    for t in range(first, outer):
        if any(s // inner == t for s in vec_shards):
            pass_level(t)
    for s in early_shards:
        whole_shard(s)
        unpack(s)
    for (base, count), ref in zip(MATS[0:3], (wq, wk, wv)):
        load_square(flat, base, count, tmp, ref)

    def vec(k):
        a = VEC_AT + 3 * (k // 2)
        zero = jnp.zeros((1, 64), F32)
        if k % 2 == 0:
            return jnp.concatenate([flat[a : a + 1, :], flat[a + 1 : a + 2, 0:64], zero], 1)
        return jnp.concatenate([flat[a + 1 : a + 2, 64:128], flat[a + 2 : a + 3, :], zero], 1)

    g1, n1, bq, bv, bo, g2, n2, b2 = [vec(k) for k in range(8)]
    b1 = jnp.concatenate([flat[VEC_AT + 12 + c : VEC_AT + 13 + c, :] for c in range(4)], 1)

    def dense1(t, count, carry):
        at = rows_at(t, count)
        hb = (xh1[at, :] * g1 + n1).astype(BF16)
        h[at, 0:D] = hb[:, 0:D]
        put_tokens(qs, t, (nn(hb, wq[...]) + bq).astype(BF16).astype(F32))
        put_tokens(ks, t, nn(hb, wk[...]).astype(BF16).astype(F32))
        put_tokens(vs, t, (nn(hb, wv[...]) + bv).astype(BF16).astype(F32))
        return carry

    over_token_chunks(dense1, WIDTH1, 0)

    lane3 = lax.broadcasted_iota(jnp.int32, (1, LANES), 1)

    def squeeze(v):
        return jnp.where(
            lane3 < ROWS, v[0:HJ], jnp.where(lane3 < 2 * ROWS, v[HJ : 2 * HJ], v[2 * HJ : 3 * HJ])
        ).reshape(HEADS, ROWS, LANES)

    jrow = lax.broadcasted_iota(jnp.int32, (1, ROWS, LANES), 1)
    cexp = math.log2(math.e) / math.sqrt(HEAD_DIM)
    scale = 1.0 / math.sqrt(HEAD_DIM)

    def attn(i, carry):
        @pl.when(i == 1)
        def _():
            for t in range(first, outer):
                if not any(s // inner == t for s in vec_shards):
                    pass_level(t)

        r0 = pl.multiple_of(i * (LOCK1 * GROWS), 8)
        base0 = pl.multiple_of(i * (LOCK1 * 3 * HJ), 64)
        p0 = pl.multiple_of(i * (LOCK1 * HJ), 64)
        sets = range(LOCK1)
        qg = [get_rows(qs, r0 + GROWS * k, LANES).astype(BF16) for k in sets]
        for k in sets:
            for src, dst in ((ks, kbd), (vs, vbd)):
                for b in range(GROUP):
                    one = get_rows(src, r0 + GROWS * k + ROWS * b, ROWS)
                    two = jnp.concatenate([one, one], 0).astype(BF16)
                    for p in range(4):
                        dst[pl.ds(base0 + HJ * (3 * k + b) + 80 * p, 80), :] = (
                            two * hm2[80 * p : 80 * (p + 1), :]
                        )
        st = [squeeze(nt(kbd[pl.ds(base0 + 3 * HJ * k, 3 * HJ), :], qg[k])) for k in sets]
        st = [jnp.where(jrow < SEQ, v, -1e30) for v in st]
        m = [jnp.max(v, 1, keepdims=True) for v in st]
        e = [jnp.exp2((st[k] - m[k]) * cexp) for k in sets]
        l = [1.0 / jnp.sum(v, 1, keepdims=True) for v in e]
        p = [(e[k] * l[k]).reshape(HJ, LANES) for k in sets]
        for k in sets:
            psc[pl.ds(p0 + HJ * k, HJ), :] = p[k]
        pt = [v.T for v in p]
        for b in range(GROUP):
            for k in sets:
                ob = nn(
                    pt[k][ROWS * b : ROWS * (b + 1), :].astype(BF16),
                    vbd[pl.ds(base0 + HJ * (3 * k + b), HJ), :],
                )
                put_rows(os_, r0 + GROWS * k + ROWS * b, ob.astype(BF16).astype(F32)[0:SEQ])
        return carry

    lax.fori_loop(0, groups // LOCK1, attn, 0)

    for s in late_shards:
        whole_shard(s)
        unpack(s)
    for (base, count), ref in zip(MATS[3:5], (wo, w2)):
        load_square(flat, base, count, tmp, ref)
    for c in range(4):
        w1[0:D, 128 * c : 128 * (c + 1)] = flat[pl.ds(W1_AT + c, D, stride=4), :].astype(BF16)
    w1[D:256, :] = jnp.zeros((256 - D, 2 * FF), BF16)
    copies_in[1].wait()

    def dense2(t0, count, carry):
        dg2, dn2, db2 = carry
        at = rows_at(t0, count)
        o = get_tokens(os_, t0, count).astype(BF16)
        o_t[at, 0:D] = o[:, 0:D]
        x2 = tokens_of(x_ref, t0, count) + (nn(o, wo[...]) + bo)
        xh, r = norm_fwd(x2)
        hb = (xh * g2 + n2).astype(BF16)
        h2[at, 0:D] = hb[:, 0:D]
        u = nn(hb, w1[...]) + b1
        gate, up = u[:, :FF], u[:, FF:]
        sq = gate * gate
        t = jnp.tanh(gate * (GELU_C + (GELU_C * 0.044715) * sq))
        half = 0.5 + 0.5 * t
        act = gate * half
        zb = (act * up).astype(BF16)
        z[at, :] = zb
        y = x2 + nn(zb, w2[...]) + b2
        out_ref[:, pl.ds(pl.multiple_of(t0 * D, 128), count * D)] = join_tokens(y, n).astype(BF16)
        dyf = tokens_of(dy_ref, t0, count)
        dyb = dyf.astype(BF16)
        dyt[at, :] = dyb
        dz = nt(dyb, w2[...])
        slope = half + gate * (0.5 - 0.5 * t * t) * (GELU_C + (3 * GELU_C * 0.044715) * sq)
        du = jnp.concatenate([(dz * up * slope).astype(BF16), (dz * act).astype(BF16)], 1)
        dul[at, :] = du
        dh = nt(du, w1[...])
        dx2 = dyf + norm_back(dh, xh, r, g2)
        dx2s[at, :] = dx2
        da = dx2.astype(BF16)
        dal[at, :] = da
        put_tokens(os_, t0, nt(da, wo[...]).astype(BF16).astype(F32))
        return dg2 + rows8(dh * xh), dn2 + rows8(dh), db2 + rows8(dyf)

    zero = jnp.zeros((8, 256), F32)
    dg2, dn2, db2 = over_token_chunks(dense2, WIDTH2, (zero, zero, zero))

    copy_out = pltpu.make_async_copy(out_ref, out_hbm, io_sem.at[2])
    copy_out.start()

    def total(v):
        return jnp.sum(v, 0, keepdims=True)

    def over_tokens(acc, a, b):
        acc[...] = jnp.zeros(acc.shape, F32)
        steps = DW_STEPS
        size = toks // steps

        @pl.loop(0, steps)
        def _(i):
            at = pl.ds(pl.multiple_of(i * size, 16), size)
            acc[...] += tn(a[at, :], b[at, :])

        return acc[...]

    store_square(over_tokens(acc, z, dyt), gflat, 1920, FF, tmp)
    dw1 = over_tokens(acc2, h2, dul)
    for c in range(4):
        gflat[pl.ds(W1_AT + c, D, stride=4), :] = dw1[0:D, 128 * c : 128 * (c + 1)]
        vec_own[12 + c : 13 + c, :] = dw1[D : D + 1, 128 * c : 128 * (c + 1)]
    dwo = over_tokens(acc, o_t, dal)
    store_square(dwo, gflat, 864, D, tmp)
    dbo = dwo[D : D + 1]

    def pack(lo, hi):
        for s in range(lo * inner, hi * inner):
            stop = min(rows * (s + 1), VEC_AT)
            if stop > rows * s:
                parts[s // inner, s % inner, 0 : stop - rows * s, :] = gflat[rows * s : stop, :]

    places = around + [pi]

    def sib_copies(part, lo, hi):
        return [
            remote(
                parts.at[lo:hi, q, theirs], sib_in.at[lo:hi, q],
                s_send.at[part, k], s_recv.at[part, q], sibling,
            )
            for k, q in enumerate(places)
        ]

    def plane_copies(part, lo, hi):
        return [
            remote(
                out_p.at[k, lo:hi], plane_in.at[pi, lo:hi],
                p_send.at[part, k], p_recv.at[part, pi], plane[k],
            )
            for k in range(inner - 1)
        ]

    def col_copy(t):
        return remote(
            out_c.at[t], col_in.at[zo], c_send.at[t], c_recv.at[zo], (t * inner + pi, core)
        )

    def sum_cores(part, lo, hi):
        sends = plane_copies(part, lo, hi)
        for k, q in enumerate(places):
            remote(
                sib_in.at[lo:hi, q], sib_in.at[lo:hi, q],
                s_send.at[part, k], s_recv.at[part, q], sibling,
            ).wait_recv()
            both = parts[lo:hi, q, mine, :] + sib_in[lo:hi, q]
            if k < inner - 1:
                out_p[k, lo:hi] = both
                sends[k].start()
            else:
                plane_in[pi, lo:hi] = both

    def sum_plane(part, lo, hi):
        for k, q in enumerate(around):
            remote(
                plane_in.at[q, lo:hi], plane_in.at[q, lo:hi],
                p_send.at[part, k], p_recv.at[part, q], sibling,
            ).wait_recv()
        for t in range(lo, hi):
            line = plane_in[0, t]
            for q in range(1, inner):
                line = line + plane_in[q, t]
            out_c[t] = line

            @pl.when(t != zo)
            def _():
                col_copy(t).start()

    pack(first, outer)
    for copy in sib_copies(0, first, outer):
        copy.start()

    def wide_rows(v):
        blocks = []
        for k in range(HEADS):
            one = v[k]
            parts = [
                jnp.where((lane3 >= ROWS * b) & (lane3 < ROWS * (b + 1)), one, 0.0)
                for b in range(GROUP)
            ]
            parts.append(jnp.zeros((8, LANES), F32))
            blocks.append(jnp.concatenate(parts, 0).astype(BF16))
        return jnp.concatenate(blocks, 1)

    def masked(v):
        v3 = v.reshape(8, 16, 256)
        return jnp.concatenate(
            [(v3 * hm[16 * k : 16 * (k + 1), :][None]).reshape(128, 256) for k in range(HEADS)], 0
        )

    def attn_back(i, carry):
        @pl.when(i == 1)
        def _():
            sum_cores(0, first, outer)

        @pl.when(i == 3)
        def _():
            sum_plane(0, first, outer)

        r0 = pl.multiple_of(i * (LOCK2 * GROWS), 8)
        base0 = pl.multiple_of(i * (LOCK2 * 3 * HJ), 64)
        p0 = pl.multiple_of(i * (LOCK2 * HJ), 64)
        sets = range(LOCK2)
        qg = [get_rows(qs, r0 + GROWS * k, LANES).astype(BF16) for k in sets]
        dg = [get_rows(os_, r0 + GROWS * k, LANES).astype(BF16) for k in sets]
        dp = [squeeze(nt(vbd[pl.ds(base0 + 3 * HJ * k, 3 * HJ), :], dg[k])) for k in sets]
        p = [psc[pl.ds(p0 + HJ * k, HJ), :].reshape(HEADS, ROWS, LANES) for k in sets]
        t = [jnp.sum(p[k] * dp[k], 1, keepdims=True) for k in sets]
        ds = [p[k] * (dp[k] - t[k]) for k in sets]
        dst = [v.reshape(HJ, LANES).T for v in ds]
        dv = [nn(wide_rows(p[k]), masked(dg[k])) for k in sets]
        dk = [nn(wide_rows(ds[k]), masked(qg[k])) * scale for k in sets]
        for b in range(GROUP):
            for k in sets:
                dq = nn(
                    dst[k][ROWS * b : ROWS * (b + 1), :].astype(BF16),
                    kbd[pl.ds(base0 + HJ * (3 * k + b), HJ), :],
                )
                put_rows(qs, r0 + GROWS * k + ROWS * b, (dq * scale).astype(BF16).astype(F32))
        for k in sets:
            put_rows(vs, r0 + GROWS * k, dv[k].astype(BF16).astype(F32)[0:GROWS])
            put_rows(ks, r0 + GROWS * k, dk[k].astype(BF16).astype(F32)[0:GROWS])
        return carry

    lax.fori_loop(0, groups // LOCK2, attn_back, 0)

    def collect(t0, count, carry):
        at = rows_at(t0, count)
        dqkv[at, :] = jnp.concatenate(
            [get_tokens(ref, t0, count).astype(BF16) for ref in (qs, ks, vs)], 1
        )
        return carry

    over_token_chunks(collect, WIDTH3, 0)
    dw = over_tokens(acc3, h, dqkv)
    for k in range(3):
        store_square(dw[:, 256 * k : 256 * (k + 1)], gflat, 288 * k, D, tmp)
    pack(0, first)
    for copy in sib_copies(1, 0, first):
        copy.start()

    def dense3(t0, count, carry):
        dg1, dn1 = carry
        at = rows_at(t0, count)
        dh = (
            nt(dqkv[at, 0:256], wq[...])
            + nt(dqkv[at, 256:512], wk[...])
            + nt(dqkv[at, 512:768], wv[...])
        )
        xh = xh1[at, :]
        ig = dx2s[at, :] + norm_back(dh, xh, r1[at, :], g1)
        ig_ref[:, pl.ds(pl.multiple_of(t0 * D, 128), count * D)] = join_tokens(ig, n)
        return dg1 + rows8(dh * xh), dn1 + rows8(dh)

    def hook3(i):
        @pl.when(i == 1)
        def _():
            sum_cores(1, 0, first)

    dg1, dn1 = over_token_chunks(dense3, WIDTH3, (zero, zero), hook3)

    vecs = [
        total(dg1), total(dn1), dw[D : D + 1, 0:256], dw[D : D + 1, 512:768],
        dbo, total(dg2), total(dn2), total(db2),
    ]
    for k in range(4):
        a, b = vecs[2 * k], vecs[2 * k + 1]
        vec_own[3 * k : 3 * k + 1, :] = a[:, 0:128]
        vec_own[3 * k + 1 : 3 * k + 2, :] = jnp.concatenate([a[:, 128:192], b[:, 0:64]], 1)
        vec_own[3 * k + 2 : 3 * k + 3, :] = b[:, 64:192]
    vec_sends = [remote(vec_own, vec_sib, v_send.at[0], v_recv.at[0], sibling)]
    vec_sends[0].start()
    copy_ig = pltpu.make_async_copy(ig_ref, ig_hbm, io_sem.at[3])
    copy_ig.start()

    def spread(slots, at, sends, recvs, base, where):
        out = [
            remote(slots.at[at], slots.at[at], sends.at[base + k], recvs.at[base + at], dev)
            for k, dev in enumerate(where)
        ]
        for copy in out:
            copy.start()
        return out

    def collected(slots, others, sends, recvs, base):
        for k, q in enumerate(others):
            remote(
                slots.at[q], slots.at[q], sends.at[base + k], recvs.at[base + q], sibling
            ).wait_recv()
        return jnp.sum(slots[...], 0)

    remote(vec_sib, vec_sib, v_send.at[0], v_recv.at[0], sibling).wait_recv()
    vec_plane[pi] = vec_own[...] + vec_sib[...]
    vec_sends += spread(vec_plane, pi, v_send, v_recv, 1, plane)
    sum_plane(1, 0, first)
    vec_col[zo] = collected(vec_plane, around, v_send, v_recv, 1)
    vec_sends += spread(vec_col, zo, v_send, v_recv, 1 + inner, column)

    col_in[zo] = out_c[zo]
    for t in along:
        remote(col_in.at[t], col_in.at[t], c_send.at[t], c_recv.at[t], sibling).wait_recv()
    line = col_in[0]
    for t in range(1, outer):
        line = line + col_in[t]
    res[mine, :] = line
    last = remote(res.at[mine], res.at[mine], f_sem.at[0], f_sem.at[1], sibling)
    last.start()
    vec = collected(vec_col, along, v_send, v_recv, 1 + inner)
    vec_at[VEC_AT:USED_ROWS, :] = vec
    remote(res.at[theirs], res.at[theirs], f_sem.at[0], f_sem.at[1], sibling).wait_recv()
    full = res[...]
    sq_plane[pi] = rows8(full * full)
    sq_sends = spread(sq_plane, pi, n_send, n_recv, 0, plane)
    own[...] = full[0:rows] + vec_at[pl.ds(me * rows, rows), :]
    sq_col[zo] = collected(sq_plane, around, n_send, n_recv, 0)
    sq_sends += spread(sq_col, zo, n_send, n_recv, inner, column)
    both = collected(sq_col, along, n_send, n_recv, inner) + rows8(vec * vec)
    squares[...] = jnp.broadcast_to(jnp.sum(both, keepdims=True), squares.shape)

    for copy in own_pushes + vec_sends + sq_sends + [last]:
        copy.wait_send()
    for t in range(outer):
        @pl.when(t != zo)
        def _(t=t):
            for copy in forwards(t, t * inner + pi):
                copy.wait_send()
            to_sibling(t * inner + pi).wait_send()
            col_copy(t).wait_send()

        for q in around:
            to_sibling(t * inner + q).wait_send()
    for part, lo, hi in ((0, first, outer), (1, 0, first)):
        for copy in sib_copies(part, lo, hi) + plane_copies(part, lo, hi):
            copy.wait_send()
    copy_out.wait()
    copy_ig.wait()


def step(x, dy, shard, wide):
    outer, inner = factors(wide)
    n, rows = x.shape[0], shard.shape[0]
    toks = n * SEQ
    groups = n // GROUP
    padded = (rows + 15) // 16 * 16
    half = padded // 2
    vm, dma = pltpu.VMEM, pltpu.SemaphoreType.DMA
    sm = vm((2, n * ROWS + 8, LANES), F32)
    tok = vm((toks, 256), BF16)
    tile = (8, LANES)
    scratch = (
        [vm(x.shape, BF16), vm(x.shape, BF16), vm(x.shape, BF16), vm(x.shape, F32)]
        + [vm((wide * rows, LANES), F32)] * 2
        + [sm] * 4
        + [vm((groups * 3 * HJ, 256), BF16)] * 2
        + [vm((groups * HJ, LANES), F32)]
        + [vm((toks, 256), F32), vm((toks, 1), F32), vm((toks, 256), F32)]
        + [tok, tok, tok, vm((toks, 2 * FF), BF16), tok]
        + [tok, tok, vm((toks, 3 * 256), BF16)]
        + [vm((256, 256), BF16)] * 4
        + [vm((256, 2 * FF), BF16), vm((FF, 256), BF16), vm((2, FF, 128), F32)]
        + [vm((320, 256), BF16), vm((128, 256), BF16)]
        + [vm((256, 256), F32), vm((256, 512), F32), vm((256, 768), F32)]
        + [vm((wide, padded, LANES), F32), vm((outer, inner, padded, LANES), F32)]
        + [vm((outer, inner, half, LANES), F32), vm((inner, outer, half, LANES), F32)]
        + [vm((inner - 1, outer, half, LANES), F32)]
        + [vm((outer, half, LANES), F32)] * 2
        + [vm((padded, LANES), F32)]
        + [vm((16, LANES), F32)] * 2
        + [vm((inner, 16, LANES), F32), vm((outer, 16, LANES), F32)]
        + [vm((wide * rows, LANES), F32)]
        + [vm((inner, *tile), F32), vm((outer, *tile), F32)]
        + [dma((4,)), dma((outer - 1,)), dma((outer, inner - 1)), dma((wide,)), dma((wide,)), dma((wide,))]
        + [dma((2, inner)), dma((2, inner)), dma((2, inner)), dma((2, inner))]
        + [dma((outer,)), dma((outer,)), dma((2,))]
        + [dma((1 + inner + outer,))] * 2
        + [dma((inner + outer,))] * 2
    )
    anywhere, vmem = pl.BlockSpec(memory_space=pl.ANY), pl.BlockSpec(memory_space=pltpu.VMEM)
    return pl.pallas_call(
        functools.partial(step_kernel, wide),
        out_shape=(
            jax.ShapeDtypeStruct(x.shape, BF16),
            jax.ShapeDtypeStruct(x.shape, F32),
            jax.ShapeDtypeStruct((rows, LANES), F32),
            jax.ShapeDtypeStruct(tile, F32),
        ),
        in_specs=[anywhere, anywhere, vmem],
        out_specs=(anywhere, anywhere, vmem, vmem),
        scratch_shapes=scratch,
        compiler_params=pltpu.CompilerParams(
            collective_id=0, has_side_effects=True, vmem_limit_bytes=60 * 2**20
        ),
        name="step",
    )(x, dy, shard)


def on_device(inputs, cotangent, master, first, second):
    rows = master.shape[0] // LANES
    block_out, input_grad, owned, squares = step(
        inputs, cotangent, master.reshape(rows, LANES), lax.axis_size("wide")
    )
    owned = owned.reshape(-1)
    squares = squares[0, 0]
    grad_norm = jnp.sqrt(squares)
    factor = jnp.minimum(1.0, 1.0 / (grad_norm + 1e-06))
    clipped = owned * factor
    new_first = 0.5 * first + 0.5 * clipped
    new_second = 0.5 * second + 0.5 * clipped * clipped
    fixed = 1.0 - 0.5**STEP
    new_master = master - 0.05 * (
        new_first / fixed / (jnp.sqrt(new_second / fixed) + 1e-08) + 0.1 * master
    )
    return (
        block_out,
        input_grad,
        clipped,
        grad_norm,
        new_master,
        new_master.astype(jnp.bfloat16),
        new_first,
        new_second,
    )


def solution(mesh):
    both, part = P(("wide", "narrow"), None), P("wide")
    return jax.shard_map(
        on_device,
        mesh=mesh,
        in_specs=(both, both, part, part, part),
        out_specs=(both, both, part, P(), part, part, part, part),
        check_vma=False,
    )
```

```python
import functools
import math

import jax
import jax.numpy as jnp
from jax import lax
from jax.experimental import pallas as pl
from jax.experimental.pallas import tpu as pltpu
from jax.sharding import PartitionSpec as P

D = 192
HEADS = 8
HEAD_DIM = 24
FF = 256
SEQ = 34
STEP = 5
ROWS = 40
GROUP = 3
GROWS = GROUP * ROWS
HJ = HEADS * ROWS
LANES = 128
F32 = jnp.float32
BF16 = jnp.bfloat16
MATS = ((0, D), (288, D), (576, D), (864, D), (1920, FF))
W1_AT = 1152
WIDTH1, WIDTH2, WIDTH3, DW_STEPS = 4, 4, 4, 2
LOCK1, LOCK2 = 4, 4
PIECES = 1
VEC_AT = 2304
USED_ROWS = VEC_AT + 16
QKV_ROWS = 864
GELU_C = math.sqrt(2.0 / math.pi)


def nn(a, b):
    return lax.dot_general(a, b, (((1,), (0,)), ((), ())), preferred_element_type=F32)


def nt(a, b):
    return lax.dot_general(a, b, (((1,), (1,)), ((), ())), preferred_element_type=F32)


def tn(a, b):
    return lax.dot_general(a, b, (((0,), (0,)), ((), ())), preferred_element_type=F32)


def low_half(v):
    lane = lax.broadcasted_iota(jnp.int32, v.shape, 1)
    return lane < 64


def load_square(flat, base, rows, tmp, out):
    half = rows // 2
    f0 = flat[pl.ds(base, half, stride=3), :]
    f1 = flat[pl.ds(base + 1, half, stride=3), :]
    f2 = flat[pl.ds(base + 2, half, stride=3), :]
    r1 = pltpu.roll(f1, 64, 1)
    r2 = pltpu.roll(f2, 64, 1)
    left = low_half(f0)
    lo, hi = tmp.at[0], tmp.at[1]
    lo[pl.ds(0, half, stride=2), :] = f0
    hi[pl.ds(0, half, stride=2), :] = jnp.where(left, f1, 0.0)
    lo[pl.ds(1, half, stride=2), :] = jnp.where(left, r1, r2)
    hi[pl.ds(1, half, stride=2), :] = jnp.where(left, r2, 0.0)
    out[0:rows, 0:128] = lo[0:rows, :].astype(BF16)
    out[0:rows, 128:256] = hi[0:rows, :].astype(BF16)
    if rows < 256:
        out[rows:256, :] = jnp.zeros((256 - rows, 256), BF16)


def store_square(val, flat, base, rows, tmp):
    half = rows // 2
    lo, hi = tmp.at[0], tmp.at[1]
    lo[0:rows, :] = val[0:rows, 0:128]
    hi[0:rows, :] = val[0:rows, 128:256]
    e0 = lo[pl.ds(0, half, stride=2), :]
    e1 = hi[pl.ds(0, half, stride=2), :]
    o0 = pltpu.roll(lo[pl.ds(1, half, stride=2), :], 64, 1)
    o1 = pltpu.roll(hi[pl.ds(1, half, stride=2), :], 64, 1)
    left = low_half(e0)
    flat[pl.ds(base, half, stride=3), :] = e0
    flat[pl.ds(base + 1, half, stride=3), :] = jnp.where(left, e1, o0)
    flat[pl.ds(base + 2, half, stride=3), :] = jnp.where(left, o0, o1)


def norm_fwd(x):
    mean = jnp.sum(x, -1, keepdims=True) * (1.0 / D)
    right = x[:, 128:256] - mean
    c = jnp.concatenate([x[:, 0:128] - mean, jnp.where(low_half(right), right, 0.0)], 1)
    var = jnp.sum(c * c, -1, keepdims=True) * (1.0 / D)
    r = lax.rsqrt(var + 1e-05)
    return c * r, r


def norm_back(d, xh, r, g):
    e = d * g
    m1 = jnp.sum(e, -1, keepdims=True) * (1.0 / D)
    m2 = jnp.sum(e * xh, -1, keepdims=True) * (1.0 / D)
    return r * (e - m1 - xh * m2)


def rows8(v):
    return jnp.sum(v.reshape(v.shape[0] // 8, 8, v.shape[1]), 0)


def split_tokens(v, count):
    zero = jnp.zeros((v.shape[0], 256 - D), v.dtype)
    return jnp.concatenate(
        [jnp.concatenate([v[:, D * t : D * (t + 1)], zero], 1) for t in range(count)], 0
    )


def join_tokens(v, n):
    return jnp.concatenate([v[n * t : n * (t + 1), 0:D] for t in range(v.shape[0] // n)], 1)


def factors(wide):
    inner = max(k for k in range(1, int(math.isqrt(wide)) + 1) if wide % k == 0)
    return wide // inner, inner


def remote(src, dst, send, recv, where):
    return pltpu.make_async_remote_copy(
        src_ref=src,
        dst_ref=dst,
        send_sem=send,
        recv_sem=recv,
        device_id=where,
        device_id_type=pl.DeviceIdType.MESH,
    )


def greet(devices):
    for dev in devices:
        pl.semaphore_signal(
            pltpu.get_barrier_semaphore(), inc=1, device_id=dev,
            device_id_type=pl.DeviceIdType.MESH,
        )


def step_kernel(
    wide,
    x_hbm, dy_hbm, shard, out_hbm, ig_hbm, own, squares,
    x_ref, dy_ref, out_ref, ig_ref, flat, gflat,
    qs, ks, vs, os_, kbd, vbd, psc, xh1, r1, dx2s, h, h2, z, dul, o_t, dal, dyt, dqkv,
    wq, wk, wv, wo, w1, w2, tmp, hm2, hm, acc, acc2, acc3,
    buf, parts, sib_in, plane_in, out_p, col_in, out_c, res, vec_own, vec_sib, vec_plane, vec_col,
    vec_at, sq_plane, sq_col,
    io_sem, g_col, g_fw, g_sib, g_recv, g_recv_sib, s_send, s_recv, p_send, p_recv, c_send, c_recv,
    f_sem, v_send, v_recv, n_send, n_recv,
):
    n = x_ref.shape[0]
    toks = n * SEQ
    pairs = SEQ // 2
    groups = n // GROUP
    rows = shard.shape[0]
    half = buf.shape[1] // 2
    outer, inner = factors(wide)
    me, core = lax.axis_index("wide"), lax.axis_index("narrow")
    zo, pi = me // inner, lax.rem(me, inner)
    mine = pl.ds(pl.multiple_of(core * half, 8), half)
    theirs = pl.ds(pl.multiple_of((1 - core) * half, 8), half)
    sibling = (me, 1 - core)
    around = [lax.rem(pi + k, inner) for k in range(1, inner)]
    along = [lax.rem(zo + k, outer) for k in range(1, outer)]
    plane = [(zo * inner + q, core) for q in around]
    column = [(t * inner + pi, core) for t in along]
    first = -(-QKV_ROWS // (rows * inner))

    copies_in = [
        pltpu.make_async_copy(x_hbm, x_ref, io_sem.at[0]),
        pltpu.make_async_copy(dy_hbm, dy_ref, io_sem.at[1]),
    ]
    for copy in copies_in:
        copy.start()

    cross = [(zo * inner + q, 1 - core) for q in around]
    known = plane + cross + column + [sibling]
    greet(known)
    lane = lax.broadcasted_iota(jnp.int32, (80, 256), 1)
    row = lax.broadcasted_iota(jnp.int32, (80, 256), 0)
    for p in range(4):
        lo = jnp.where(row < ROWS, HEAD_DIM * 2 * p, HEAD_DIM * (2 * p + 1))
        hm2[80 * p : 80 * (p + 1), :] = jnp.where(
            (lane >= lo) & (lane < lo + HEAD_DIM), 1.0, 0.0
        ).astype(BF16)
    lane16 = lax.broadcasted_iota(jnp.int32, (16, 256), 1)
    for k in range(HEADS):
        hm[16 * k : 16 * (k + 1), :] = jnp.where(
            (lane16 >= HEAD_DIM * k) & (lane16 < HEAD_DIM * (k + 1)), 1.0, 0.0
        ).astype(BF16)
    ones_lane = (lax.broadcasted_iota(jnp.int32, (toks, 64), 1) == 0).astype(F32).astype(BF16)
    for ref in (h, h2, o_t):
        ref[:, D:256] = ones_lane
    for ref in (qs, ks, vs, os_):
        ref[...] = jnp.zeros(ref.shape, F32)

    parts[...] = jnp.zeros(parts.shape, F32)
    vec_at[...] = jnp.zeros(vec_at.shape, F32)
    pl.semaphore_wait(pltpu.get_barrier_semaphore(), len(known))
    buf[me, 0:rows, :] = shard[...]
    buf[me, rows:, :] = jnp.zeros((buf.shape[1] - rows, LANES), F32)

    def push(s, send, recvs, where):
        return remote(buf.at[s, mine], buf.at[s, mine], send, recvs.at[s], where)

    def arrived(s, recvs, part):
        remote(buf.at[s, part], buf.at[s, part], g_sib.at[s], recvs.at[s], sibling).wait_recv()

    def forwards(t, s):
        return [push(s, g_fw.at[t, k], g_recv, where) for k, where in enumerate(plane)]

    own_pushes = [push(me, g_col.at[k], g_recv, where) for k, where in enumerate(column)]
    own_pushes += forwards(zo, me)
    for copy in own_pushes:
        copy.start()

    def to_sibling(s):
        return push(s, g_sib.at[s], g_recv_sib, sibling)

    def forward_level(t):
        s = t * inner + pi

        @pl.when(t != zo)
        def _():
            arrived(s, g_recv, mine)
            for copy in forwards(t, s):
                copy.start()
            to_sibling(s).start()

    def pass_level(t):
        for q in around:
            s = t * inner + q
            arrived(s, g_recv, mine)
            to_sibling(s).start()

    def whole_shard(s):
        @pl.when(s != me)
        def _():
            arrived(s, g_recv_sib, theirs)

    def unpack(s):
        flat[rows * s : rows * (s + 1), :] = buf[s, 0:rows, :]

    vec_shards = range(VEC_AT // rows, (USED_ROWS - 1) // rows + 1)
    early_shards = [s for s in range(wide) if s < first * inner or s in vec_shards]
    late_shards = [s for s in range(wide) if s not in early_shards]

    for t in range(outer):
        forward_level(t)

    def tokens_of(ref, t, count):
        return split_tokens(
            ref[:, pl.ds(pl.multiple_of(t * D, 128), count * D)].astype(F32), count
        )

    def put_tokens(ref, t, val):
        for half in range(2):
            for k in range(val.shape[0] // n):
                ref.at[half][pl.ds(t + k, n, stride=ROWS), :] = val[
                    n * k : n * (k + 1), 128 * half : 128 * (half + 1)
                ]

    def get_tokens(ref, t, count):
        return jnp.concatenate(
            [
                jnp.concatenate(
                    [ref.at[half][pl.ds(t + k, n, stride=ROWS), :] for half in range(2)], 1
                )
                for k in range(count)
            ],
            0,
        )

    def over_token_chunks(body, width, carry, hook=lambda i: None):
        whole = pairs // width

        def step(i, c):
            hook(i)
            return body(i * (2 * width), 2 * width, c)

        carry = lax.fori_loop(0, whole, step, carry)
        if pairs % width:
            carry = body(whole * 2 * width, 2 * (pairs % width), carry)
        return carry

    def get_rows(ref, start, count):
        return jnp.concatenate([ref[0, pl.ds(start, count), :], ref[1, pl.ds(start, count), :]], 1)

    def put_rows(ref, start, val):
        for half in range(2):
            ref[half, pl.ds(start, val.shape[0]), :] = val[:, 128 * half : 128 * (half + 1)]

    def rows_at(t, count):
        return pl.ds(pl.multiple_of(t * n, 32), count * n)

    def norm1(t, count, carry):
        at = rows_at(t, count)
        xh, r = norm_fwd(tokens_of(x_ref, t, count))
        xh1[at, :] = xh
        r1[at, :] = r
        return carry

    copies_in[0].wait()
    over_token_chunks(norm1, WIDTH1, 0)

    for t in range(first):
        pass_level(t)
    for t in range(first, outer):
        if any(s // inner == t for s in vec_shards):
            pass_level(t)
    for s in early_shards:
        whole_shard(s)
        unpack(s)
    for (base, count), ref in zip(MATS[0:3], (wq, wk, wv)):
        load_square(flat, base, count, tmp, ref)

    def vec(k):
        a = VEC_AT + 3 * (k // 2)
        zero = jnp.zeros((1, 64), F32)
        if k % 2 == 0:
            return jnp.concatenate([flat[a : a + 1, :], flat[a + 1 : a + 2, 0:64], zero], 1)
        return jnp.concatenate([flat[a + 1 : a + 2, 64:128], flat[a + 2 : a + 3, :], zero], 1)

    g1, n1, bq, bv, bo, g2, n2, b2 = [vec(k) for k in range(8)]
    b1 = jnp.concatenate([flat[VEC_AT + 12 + c : VEC_AT + 13 + c, :] for c in range(4)], 1)

    def dense1(t, count, carry):
        at = rows_at(t, count)
        hb = (xh1[at, :] * g1 + n1).astype(BF16)
        h[at, 0:D] = hb[:, 0:D]
        put_tokens(qs, t, (nn(hb, wq[...]) + bq).astype(BF16).astype(F32))
        put_tokens(ks, t, nn(hb, wk[...]).astype(BF16).astype(F32))
        put_tokens(vs, t, (nn(hb, wv[...]) + bv).astype(BF16).astype(F32))
        return carry

    over_token_chunks(dense1, WIDTH1, 0)

    lane3 = lax.broadcasted_iota(jnp.int32, (1, LANES), 1)

    def squeeze(v):
        return jnp.where(
            lane3 < ROWS, v[0:HJ], jnp.where(lane3 < 2 * ROWS, v[HJ : 2 * HJ], v[2 * HJ : 3 * HJ])
        ).reshape(HEADS, ROWS, LANES)

    jrow = lax.broadcasted_iota(jnp.int32, (1, ROWS, LANES), 1)
    cexp = math.log2(math.e) / math.sqrt(HEAD_DIM)
    scale = 1.0 / math.sqrt(HEAD_DIM)

    def attn(i, carry):
        @pl.when(i == 1)
        def _():
            for t in range(first, outer):
                if not any(s // inner == t for s in vec_shards):
                    pass_level(t)

        r0 = pl.multiple_of(i * (LOCK1 * GROWS), 8)
        base0 = pl.multiple_of(i * (LOCK1 * 3 * HJ), 64)
        p0 = pl.multiple_of(i * (LOCK1 * HJ), 64)
        sets = range(LOCK1)
        qg = [get_rows(qs, r0 + GROWS * k, LANES).astype(BF16) for k in sets]
        for k in sets:
            for src, dst in ((ks, kbd), (vs, vbd)):
                for b in range(GROUP):
                    one = get_rows(src, r0 + GROWS * k + ROWS * b, ROWS)
                    two = jnp.concatenate([one, one], 0).astype(BF16)
                    for p in range(4):
                        dst[pl.ds(base0 + HJ * (3 * k + b) + 80 * p, 80), :] = (
                            two * hm2[80 * p : 80 * (p + 1), :]
                        )
        st = [squeeze(nt(kbd[pl.ds(base0 + 3 * HJ * k, 3 * HJ), :], qg[k])) for k in sets]
        st = [jnp.where(jrow < SEQ, v, -1e30) for v in st]
        m = [jnp.max(v, 1, keepdims=True) for v in st]
        e = [jnp.exp2((st[k] - m[k]) * cexp) for k in sets]
        l = [1.0 / jnp.sum(v, 1, keepdims=True) for v in e]
        p = [(e[k] * l[k]).reshape(HJ, LANES) for k in sets]
        for k in sets:
            psc[pl.ds(p0 + HJ * k, HJ), :] = p[k]
        pt = [v.T for v in p]
        for b in range(GROUP):
            for k in sets:
                ob = nn(
                    pt[k][ROWS * b : ROWS * (b + 1), :].astype(BF16),
                    vbd[pl.ds(base0 + HJ * (3 * k + b), HJ), :],
                )
                put_rows(os_, r0 + GROWS * k + ROWS * b, ob.astype(BF16).astype(F32)[0:SEQ])
        return carry

    lax.fori_loop(0, groups // LOCK1, attn, 0)

    for s in late_shards:
        whole_shard(s)
        unpack(s)
    for (base, count), ref in zip(MATS[3:5], (wo, w2)):
        load_square(flat, base, count, tmp, ref)
    for c in range(4):
        w1[0:D, 128 * c : 128 * (c + 1)] = flat[pl.ds(W1_AT + c, D, stride=4), :].astype(BF16)
    w1[D:256, :] = jnp.zeros((256 - D, 2 * FF), BF16)
    copies_in[1].wait()

    def dense2(t0, count, carry):
        dg2, dn2, db2 = carry
        at = rows_at(t0, count)
        o = get_tokens(os_, t0, count).astype(BF16)
        o_t[at, 0:D] = o[:, 0:D]
        x2 = tokens_of(x_ref, t0, count) + (nn(o, wo[...]) + bo)
        xh, r = norm_fwd(x2)
        hb = (xh * g2 + n2).astype(BF16)
        h2[at, 0:D] = hb[:, 0:D]
        u = nn(hb, w1[...]) + b1
        gate, up = u[:, :FF], u[:, FF:]
        sq = gate * gate
        t = jnp.tanh(gate * (GELU_C + (GELU_C * 0.044715) * sq))
        half = 0.5 + 0.5 * t
        act = gate * half
        zb = (act * up).astype(BF16)
        z[at, :] = zb
        y = x2 + nn(zb, w2[...]) + b2
        out_ref[:, pl.ds(pl.multiple_of(t0 * D, 128), count * D)] = join_tokens(y, n).astype(BF16)
        dyf = tokens_of(dy_ref, t0, count)
        dyb = dyf.astype(BF16)
        dyt[at, :] = dyb
        dz = nt(dyb, w2[...])
        slope = half + gate * (0.5 - 0.5 * t * t) * (GELU_C + (3 * GELU_C * 0.044715) * sq)
        du = jnp.concatenate([(dz * up * slope).astype(BF16), (dz * act).astype(BF16)], 1)
        dul[at, :] = du
        dh = nt(du, w1[...])
        dx2 = dyf + norm_back(dh, xh, r, g2)
        dx2s[at, :] = dx2
        da = dx2.astype(BF16)
        dal[at, :] = da
        put_tokens(os_, t0, nt(da, wo[...]).astype(BF16).astype(F32))
        return dg2 + rows8(dh * xh), dn2 + rows8(dh), db2 + rows8(dyf)

    zero = jnp.zeros((8, 256), F32)
    dg2, dn2, db2 = over_token_chunks(dense2, WIDTH2, (zero, zero, zero))

    copy_out = pltpu.make_async_copy(out_ref, out_hbm, io_sem.at[2])
    copy_out.start()

    def total(v):
        return jnp.sum(v, 0, keepdims=True)

    def over_tokens(acc, a, b):
        acc[...] = jnp.zeros(acc.shape, F32)
        steps = DW_STEPS
        size = toks // steps

        @pl.loop(0, steps)
        def _(i):
            at = pl.ds(pl.multiple_of(i * size, 16), size)
            acc[...] += tn(a[at, :], b[at, :])

        return acc[...]

    store_square(over_tokens(acc, z, dyt), gflat, 1920, FF, tmp)
    dw1 = over_tokens(acc2, h2, dul)
    for c in range(4):
        gflat[pl.ds(W1_AT + c, D, stride=4), :] = dw1[0:D, 128 * c : 128 * (c + 1)]
        vec_own[12 + c : 13 + c, :] = dw1[D : D + 1, 128 * c : 128 * (c + 1)]
    dwo = over_tokens(acc, o_t, dal)
    store_square(dwo, gflat, 864, D, tmp)
    dbo = dwo[D : D + 1]

    def pack(lo, hi):
        for s in range(lo * inner, hi * inner):
            stop = min(rows * (s + 1), VEC_AT)
            if stop > rows * s:
                parts[s // inner, s % inner, 0 : stop - rows * s, :] = gflat[rows * s : stop, :]

    places = around + [pi]

    def sib_copies(part, lo, hi):
        return [
            remote(
                parts.at[lo:hi, q, theirs], sib_in.at[lo:hi, q],
                s_send.at[part, k], s_recv.at[part, q], sibling,
            )
            for k, q in enumerate(places)
        ]

    def plane_copies(part, lo, hi):
        return [
            remote(
                out_p.at[k, lo:hi], plane_in.at[pi, lo:hi],
                p_send.at[part, k], p_recv.at[part, pi], plane[k],
            )
            for k in range(inner - 1)
        ]

    def col_copy(t):
        return remote(
            out_c.at[t], col_in.at[zo], c_send.at[t], c_recv.at[zo], (t * inner + pi, core)
        )

    def sum_cores(part, lo, hi):
        sends = plane_copies(part, lo, hi)
        for k, q in enumerate(places):
            remote(
                sib_in.at[lo:hi, q], sib_in.at[lo:hi, q],
                s_send.at[part, k], s_recv.at[part, q], sibling,
            ).wait_recv()
            both = parts[lo:hi, q, mine, :] + sib_in[lo:hi, q]
            if k < inner - 1:
                out_p[k, lo:hi] = both
                sends[k].start()
            else:
                plane_in[pi, lo:hi] = both

    def sum_plane(part, lo, hi):
        for k, q in enumerate(around):
            remote(
                plane_in.at[q, lo:hi], plane_in.at[q, lo:hi],
                p_send.at[part, k], p_recv.at[part, q], sibling,
            ).wait_recv()
        for t in range(lo, hi):
            line = plane_in[0, t]
            for q in range(1, inner):
                line = line + plane_in[q, t]
            out_c[t] = line

            @pl.when(t != zo)
            def _():
                col_copy(t).start()

    pack(first, outer)
    for copy in sib_copies(0, first, outer):
        copy.start()

    def wide_rows(v):
        blocks = []
        for k in range(HEADS):
            one = v[k]
            parts = [
                jnp.where((lane3 >= ROWS * b) & (lane3 < ROWS * (b + 1)), one, 0.0)
                for b in range(GROUP)
            ]
            parts.append(jnp.zeros((8, LANES), F32))
            blocks.append(jnp.concatenate(parts, 0).astype(BF16))
        return jnp.concatenate(blocks, 1)

    def masked(v):
        v3 = v.reshape(8, 16, 256)
        return jnp.concatenate(
            [(v3 * hm[16 * k : 16 * (k + 1), :][None]).reshape(128, 256) for k in range(HEADS)], 0
        )

    def attn_back(i, carry):
        @pl.when(i == 1)
        def _():
            sum_cores(0, first, outer)

        @pl.when(i == 3)
        def _():
            sum_plane(0, first, outer)

        r0 = pl.multiple_of(i * (LOCK2 * GROWS), 8)
        base0 = pl.multiple_of(i * (LOCK2 * 3 * HJ), 64)
        p0 = pl.multiple_of(i * (LOCK2 * HJ), 64)
        sets = range(LOCK2)
        qg = [get_rows(qs, r0 + GROWS * k, LANES).astype(BF16) for k in sets]
        dg = [get_rows(os_, r0 + GROWS * k, LANES).astype(BF16) for k in sets]
        dp = [squeeze(nt(vbd[pl.ds(base0 + 3 * HJ * k, 3 * HJ), :], dg[k])) for k in sets]
        p = [psc[pl.ds(p0 + HJ * k, HJ), :].reshape(HEADS, ROWS, LANES) for k in sets]
        t = [jnp.sum(p[k] * dp[k], 1, keepdims=True) for k in sets]
        ds = [p[k] * (dp[k] - t[k]) for k in sets]
        dst = [v.reshape(HJ, LANES).T for v in ds]
        dv = [nn(wide_rows(p[k]), masked(dg[k])) for k in sets]
        dk = [nn(wide_rows(ds[k]), masked(qg[k])) * scale for k in sets]
        for b in range(GROUP):
            for k in sets:
                dq = nn(
                    dst[k][ROWS * b : ROWS * (b + 1), :].astype(BF16),
                    kbd[pl.ds(base0 + HJ * (3 * k + b), HJ), :],
                )
                put_rows(qs, r0 + GROWS * k + ROWS * b, (dq * scale).astype(BF16).astype(F32))
        for k in sets:
            put_rows(vs, r0 + GROWS * k, dv[k].astype(BF16).astype(F32)[0:GROWS])
            put_rows(ks, r0 + GROWS * k, dk[k].astype(BF16).astype(F32)[0:GROWS])
        return carry

    lax.fori_loop(0, groups // LOCK2, attn_back, 0)

    def collect(t0, count, carry):
        at = rows_at(t0, count)
        dqkv[at, :] = jnp.concatenate(
            [get_tokens(ref, t0, count).astype(BF16) for ref in (qs, ks, vs)], 1
        )
        return carry

    over_token_chunks(collect, WIDTH3, 0)
    dw = over_tokens(acc3, h, dqkv)
    for k in range(3):
        store_square(dw[:, 256 * k : 256 * (k + 1)], gflat, 288 * k, D, tmp)
    pack(0, first)
    for copy in sib_copies(1, 0, first):
        copy.start()

    def dense3(t0, count, carry):
        dg1, dn1 = carry
        at = rows_at(t0, count)
        dh = (
            nt(dqkv[at, 0:256], wq[...])
            + nt(dqkv[at, 256:512], wk[...])
            + nt(dqkv[at, 512:768], wv[...])
        )
        xh = xh1[at, :]
        ig = dx2s[at, :] + norm_back(dh, xh, r1[at, :], g1)
        ig_ref[:, pl.ds(pl.multiple_of(t0 * D, 128), count * D)] = join_tokens(ig, n)
        return dg1 + rows8(dh * xh), dn1 + rows8(dh)

    def hook3(i):
        @pl.when(i == 1)
        def _():
            sum_cores(1, 0, first)

    dg1, dn1 = over_token_chunks(dense3, WIDTH3, (zero, zero), hook3)

    vecs = [
        total(dg1), total(dn1), dw[D : D + 1, 0:256], dw[D : D + 1, 512:768],
        dbo, total(dg2), total(dn2), total(db2),
    ]
    for k in range(4):
        a, b = vecs[2 * k], vecs[2 * k + 1]
        vec_own[3 * k : 3 * k + 1, :] = a[:, 0:128]
        vec_own[3 * k + 1 : 3 * k + 2, :] = jnp.concatenate([a[:, 128:192], b[:, 0:64]], 1)
        vec_own[3 * k + 2 : 3 * k + 3, :] = b[:, 64:192]
    vec_sends = [remote(vec_own, vec_sib, v_send.at[0], v_recv.at[0], sibling)]
    vec_sends[0].start()
    copy_ig = pltpu.make_async_copy(ig_ref, ig_hbm, io_sem.at[3])
    copy_ig.start()

    def spread(slots, at, sends, recvs, base, where):
        out = [
            remote(slots.at[at], slots.at[at], sends.at[base + k], recvs.at[base + at], dev)
            for k, dev in enumerate(where)
        ]
        for copy in out:
            copy.start()
        return out

    def collected(slots, others, sends, recvs, base):
        for k, q in enumerate(others):
            remote(
                slots.at[q], slots.at[q], sends.at[base + k], recvs.at[base + q], sibling
            ).wait_recv()
        return jnp.sum(slots[...], 0)

    remote(vec_sib, vec_sib, v_send.at[0], v_recv.at[0], sibling).wait_recv()
    vec_plane[pi] = vec_own[...] + vec_sib[...]
    vec_sends += spread(vec_plane, pi, v_send, v_recv, 1, plane)
    sum_plane(1, 0, first)
    vec_col[zo] = collected(vec_plane, around, v_send, v_recv, 1)
    vec_sends += spread(vec_col, zo, v_send, v_recv, 1 + inner, column)

    col_in[zo] = out_c[zo]
    for t in along:
        remote(col_in.at[t], col_in.at[t], c_send.at[t], c_recv.at[t], sibling).wait_recv()
    line = col_in[0]
    for t in range(1, outer):
        line = line + col_in[t]
    res[mine, :] = line
    last = remote(res.at[mine], res.at[mine], f_sem.at[0], f_sem.at[1], sibling)
    last.start()
    slot = 2 * pi + core
    near = [2 * q + core for q in around] + [2 * q + 1 - core for q in around] + [2 * pi + 1 - core]
    sq_plane[slot] = rows8(line * line)
    sq_sends = spread(sq_plane, slot, n_send, n_recv, 0, plane + cross + [sibling])
    vec = collected(vec_col, along, v_send, v_recv, 1 + inner)
    vec_at[VEC_AT:USED_ROWS, :] = vec
    remote(res.at[theirs], res.at[theirs], f_sem.at[0], f_sem.at[1], sibling).wait_recv()
    own[...] = res[0:rows, :] + vec_at[pl.ds(me * rows, rows), :]
    sq_col[zo] = collected(sq_plane, near, n_send, n_recv, 0)
    sq_sends += spread(sq_col, zo, n_send, n_recv, 2 * inner, column)
    both = collected(sq_col, along, n_send, n_recv, 2 * inner) + rows8(vec * vec)
    squares[...] = jnp.broadcast_to(jnp.sum(both, keepdims=True), squares.shape)

    for copy in own_pushes + vec_sends + sq_sends + [last]:
        copy.wait_send()
    for t in range(outer):
        @pl.when(t != zo)
        def _(t=t):
            for copy in forwards(t, t * inner + pi):
                copy.wait_send()
            to_sibling(t * inner + pi).wait_send()
            col_copy(t).wait_send()

        for q in around:
            to_sibling(t * inner + q).wait_send()
    for part, lo, hi in ((0, first, outer), (1, 0, first)):
        for copy in sib_copies(part, lo, hi) + plane_copies(part, lo, hi):
            copy.wait_send()
    copy_out.wait()
    copy_ig.wait()


def step(x, dy, shard, wide):
    outer, inner = factors(wide)
    n, rows = x.shape[0], shard.shape[0]
    toks = n * SEQ
    groups = n // GROUP
    padded = (rows + 15) // 16 * 16
    half = padded // 2
    vm, dma = pltpu.VMEM, pltpu.SemaphoreType.DMA
    sm = vm((2, n * ROWS + 8, LANES), F32)
    tok = vm((toks, 256), BF16)
    tile = (8, LANES)
    scratch = (
        [vm(x.shape, BF16), vm(x.shape, BF16), vm(x.shape, BF16), vm(x.shape, F32)]
        + [vm((wide * rows, LANES), F32)] * 2
        + [sm] * 4
        + [vm((groups * 3 * HJ, 256), BF16)] * 2
        + [vm((groups * HJ, LANES), F32)]
        + [vm((toks, 256), F32), vm((toks, 1), F32), vm((toks, 256), F32)]
        + [tok, tok, tok, vm((toks, 2 * FF), BF16), tok]
        + [tok, tok, vm((toks, 3 * 256), BF16)]
        + [vm((256, 256), BF16)] * 4
        + [vm((256, 2 * FF), BF16), vm((FF, 256), BF16), vm((2, FF, 128), F32)]
        + [vm((320, 256), BF16), vm((128, 256), BF16)]
        + [vm((256, 256), F32), vm((256, 512), F32), vm((256, 768), F32)]
        + [vm((wide, padded, LANES), F32), vm((outer, inner, padded, LANES), F32)]
        + [vm((outer, inner, half, LANES), F32), vm((inner, outer, half, LANES), F32)]
        + [vm((inner - 1, outer, half, LANES), F32)]
        + [vm((outer, half, LANES), F32)] * 2
        + [vm((padded, LANES), F32)]
        + [vm((16, LANES), F32)] * 2
        + [vm((inner, 16, LANES), F32), vm((outer, 16, LANES), F32)]
        + [vm((wide * rows, LANES), F32)]
        + [vm((2 * inner, *tile), F32), vm((outer, *tile), F32)]
        + [dma((4,)), dma((outer - 1,)), dma((outer, inner - 1)), dma((wide,)), dma((wide,)), dma((wide,))]
        + [dma((2, inner)), dma((2, inner)), dma((2, inner)), dma((2, inner))]
        + [dma((outer,)), dma((outer,)), dma((2,))]
        + [dma((1 + inner + outer,))] * 2
        + [dma((2 * inner + outer,))] * 2
    )
    anywhere, vmem = pl.BlockSpec(memory_space=pl.ANY), pl.BlockSpec(memory_space=pltpu.VMEM)
    return pl.pallas_call(
        functools.partial(step_kernel, wide),
        out_shape=(
            jax.ShapeDtypeStruct(x.shape, BF16),
            jax.ShapeDtypeStruct(x.shape, F32),
            jax.ShapeDtypeStruct((rows, LANES), F32),
            jax.ShapeDtypeStruct(tile, F32),
        ),
        in_specs=[anywhere, anywhere, vmem],
        out_specs=(anywhere, anywhere, vmem, vmem),
        scratch_shapes=scratch,
        compiler_params=pltpu.CompilerParams(
            collective_id=0, has_side_effects=True, vmem_limit_bytes=60 * 2**20
        ),
        name="step",
    )(x, dy, shard)


def finish_kernel(*refs):
    big_in, small_in = refs[0:2], refs[2:7]
    big_out, norm_out, small_out = refs[7:9], refs[9], refs[10:15]
    stages, ins, norm, outs = refs[15:17], refs[17:22], refs[22], refs[23:28]
    sem_in, sem_out, sem_small = refs[28:31]
    pieces = []
    for k in range(2):
        size = big_in[k].shape[0] // PIECES
        for p in range(PIECES):
            at = pl.ds(size * p, size)
            pieces.append(
                (
                    pltpu.make_async_copy(big_in[k].at[at], stages[k].at[at], sem_in.at[k, p]),
                    pltpu.make_async_copy(stages[k].at[at], big_out[k].at[at], sem_out.at[k, p]),
                )
            )
    loads = [pltpu.make_async_copy(small_in[k], ins[k], sem_small.at[k]) for k in range(5)]
    for copy in loads:
        copy.start()
    for come, _ in pieces:
        come.start()
    for copy in loads:
        copy.wait()
    own, squares, master, first, second = ins
    clipped, new_master, new_copy, new_first, new_second = outs
    grad_norm = jnp.sqrt(squares[...])
    norm[...] = grad_norm[0:1, 0:1]
    factor = jnp.minimum(1.0, 1.0 / (grad_norm[0:1, :] + 1e-06))
    grad = own[...] * factor
    clipped[...] = grad
    one = 0.5 * first[...] + 0.5 * grad
    two = 0.5 * second[...] + 0.5 * grad * grad
    new_first[...] = one
    new_second[...] = two
    fixed = 1.0 - 0.5**STEP
    old = master[...]
    new = old - 0.05 * ((one / fixed) / (jnp.sqrt(two / fixed) + 1e-08) + 0.1 * old)
    new_master[...] = new
    new_copy[...] = new.astype(BF16)
    stores = [
        pltpu.make_async_copy(src, dst, sem_small.at[5 + k])
        for k, (src, dst) in enumerate(zip((norm, *outs), (norm_out, *small_out)))
    ]
    for copy in stores:
        copy.start()
    for come, go in pieces:
        come.wait()
        go.start()
    for copy in stores:
        copy.wait()
    for _, go in pieces:
        go.wait()


def finish(block_out, input_grad, owned, squares, master, first, second):
    anywhere, vm = pl.BlockSpec(memory_space=pl.ANY), pltpu.VMEM
    one, flat = (1, 1), owned.shape
    kinds = [(flat, F32), (flat, F32), (flat, BF16), (flat, F32), (flat, F32)]
    like = jax.ShapeDtypeStruct
    return pl.pallas_call(
        finish_kernel,
        out_shape=(
            like(block_out.shape, BF16),
            like(input_grad.shape, F32),
            like(one, F32),
            *[like(*kind) for kind in kinds],
        ),
        in_specs=[anywhere] * 7,
        out_specs=(anywhere,) * 8,
        scratch_shapes=[
            vm(block_out.shape, BF16),
            vm(input_grad.shape, F32),
            vm(flat, F32),
            vm(squares.shape, F32),
            vm(flat, F32),
            vm(flat, F32),
            vm(flat, F32),
            vm(one, F32),
            *[vm(*kind) for kind in kinds],
            pltpu.SemaphoreType.DMA((2, PIECES)),
            pltpu.SemaphoreType.DMA((2, PIECES)),
            pltpu.SemaphoreType.DMA((11,)),
        ],
        compiler_params=pltpu.CompilerParams(vmem_limit_bytes=60 * 2**20),
        name="finish",
    )(block_out, input_grad, owned, squares, master, first, second)


def on_device(inputs, cotangent, master, first, second):
    flat = lambda a: a.reshape(-1)
    tall = lambda a: a.reshape(-1, LANES)
    block_out, input_grad, owned, squares = step(
        inputs, cotangent, tall(master), lax.axis_size("wide")
    )
    block_out, input_grad, norm, clipped, new_master, new_copy, new_first, new_second = finish(
        block_out, input_grad, owned, squares, tall(master), tall(first), tall(second)
    )
    return (
        block_out,
        input_grad,
        flat(clipped),
        norm.reshape(()),
        flat(new_master),
        flat(new_copy),
        flat(new_first),
        flat(new_second),
    )


def solution(mesh):
    both, part = P(("wide", "narrow"), None), P("wide")
    return jax.shard_map(
        on_device,
        mesh=mesh,
        in_specs=(both, both, part, part, part),
        out_specs=(both, both, part, P(), part, part, part, part),
        check_vma=False,
    )
```

```python
import functools
import math

import jax
import jax.numpy as jnp
from jax import lax
from jax.experimental import pallas as pl
from jax.experimental.pallas import tpu as pltpu
from jax.sharding import PartitionSpec as P

D = 192
HEADS = 8
HEAD_DIM = 24
FF = 256
SEQ = 34
STEP = 5
ROWS = 40
GROUP = 3
GROWS = GROUP * ROWS
HJ = HEADS * ROWS
LANES = 128
F32 = jnp.float32
BF16 = jnp.bfloat16
MATS = ((0, D), (288, D), (576, D), (864, D), (1920, FF))
W1_AT = 1152
WIDTH1, WIDTH2, WIDTH3, DW_STEPS = 4, 4, 4, 2
LOCK1, LOCK2 = 4, 4
PIECES = 1
VEC_AT = 2304
USED_ROWS = VEC_AT + 16
QK_ROWS = 576
QKV_ROWS = 864
GELU_C = math.sqrt(2.0 / math.pi)


def nn(a, b):
    return lax.dot_general(a, b, (((1,), (0,)), ((), ())), preferred_element_type=F32)


def nt(a, b):
    return lax.dot_general(a, b, (((1,), (1,)), ((), ())), preferred_element_type=F32)


def tn(a, b):
    return lax.dot_general(a, b, (((0,), (0,)), ((), ())), preferred_element_type=F32)


def low_half(v):
    lane = lax.broadcasted_iota(jnp.int32, v.shape, 1)
    return lane < 64


def load_square(flat, base, rows, tmp, out):
    half = rows // 2
    f0 = flat[pl.ds(base, half, stride=3), :]
    f1 = flat[pl.ds(base + 1, half, stride=3), :]
    f2 = flat[pl.ds(base + 2, half, stride=3), :]
    r1 = pltpu.roll(f1, 64, 1)
    r2 = pltpu.roll(f2, 64, 1)
    left = low_half(f0)
    lo, hi = tmp.at[0], tmp.at[1]
    lo[pl.ds(0, half, stride=2), :] = f0
    hi[pl.ds(0, half, stride=2), :] = jnp.where(left, f1, 0.0)
    lo[pl.ds(1, half, stride=2), :] = jnp.where(left, r1, r2)
    hi[pl.ds(1, half, stride=2), :] = jnp.where(left, r2, 0.0)
    out[0:rows, 0:128] = lo[0:rows, :].astype(BF16)
    out[0:rows, 128:256] = hi[0:rows, :].astype(BF16)
    if rows < 256:
        out[rows:256, :] = jnp.zeros((256 - rows, 256), BF16)


def store_square(val, flat, base, rows, tmp):
    half = rows // 2
    lo, hi = tmp.at[0], tmp.at[1]
    lo[0:rows, :] = val[0:rows, 0:128]
    hi[0:rows, :] = val[0:rows, 128:256]
    e0 = lo[pl.ds(0, half, stride=2), :]
    e1 = hi[pl.ds(0, half, stride=2), :]
    o0 = pltpu.roll(lo[pl.ds(1, half, stride=2), :], 64, 1)
    o1 = pltpu.roll(hi[pl.ds(1, half, stride=2), :], 64, 1)
    left = low_half(e0)
    flat[pl.ds(base, half, stride=3), :] = e0
    flat[pl.ds(base + 1, half, stride=3), :] = jnp.where(left, e1, o0)
    flat[pl.ds(base + 2, half, stride=3), :] = jnp.where(left, o0, o1)


def norm_fwd(x):
    mean = jnp.sum(x, -1, keepdims=True) * (1.0 / D)
    right = x[:, 128:256] - mean
    c = jnp.concatenate([x[:, 0:128] - mean, jnp.where(low_half(right), right, 0.0)], 1)
    var = jnp.sum(c * c, -1, keepdims=True) * (1.0 / D)
    r = lax.rsqrt(var + 1e-05)
    return c * r, r


def norm_back(d, xh, r, g):
    e = d * g
    m1 = jnp.sum(e, -1, keepdims=True) * (1.0 / D)
    m2 = jnp.sum(e * xh, -1, keepdims=True) * (1.0 / D)
    return r * (e - m1 - xh * m2)


def rows8(v):
    return jnp.sum(v.reshape(v.shape[0] // 8, 8, v.shape[1]), 0)


def split_tokens(v, count):
    zero = jnp.zeros((v.shape[0], 256 - D), v.dtype)
    return jnp.concatenate(
        [jnp.concatenate([v[:, D * t : D * (t + 1)], zero], 1) for t in range(count)], 0
    )


def join_tokens(v, n):
    return jnp.concatenate([v[n * t : n * (t + 1), 0:D] for t in range(v.shape[0] // n)], 1)


def factors(wide):
    inner = max(k for k in range(1, int(math.isqrt(wide)) + 1) if wide % k == 0)
    return wide // inner, inner


def remote(src, dst, send, recv, where):
    return pltpu.make_async_remote_copy(
        src_ref=src,
        dst_ref=dst,
        send_sem=send,
        recv_sem=recv,
        device_id=where,
        device_id_type=pl.DeviceIdType.MESH,
    )


def greet(devices):
    for dev in devices:
        pl.semaphore_signal(
            pltpu.get_barrier_semaphore(), inc=1, device_id=dev,
            device_id_type=pl.DeviceIdType.MESH,
        )


def step_kernel(
    wide,
    x_hbm, dy_hbm, shard, out_hbm, ig_hbm, own, squares,
    x_ref, dy_ref, out_ref, ig_ref, flat, gflat,
    qs, ks, vs, os_, kbd, vbd, psc, xh1, r1, dx2s, h, h2, z, dul, o_t, dal, dyt, dqkv,
    wq, wk, wv, wo, w1, w2, tmp, hm2, acc, acc2, acc3,
    buf, parts, sib_in, plane_in, out_p, col_in, out_c, res, vec_own, vec_sib, vec_plane, vec_col,
    vec_at, sq_plane, sq_col, vec_in,
    io_sem, g_col, g_fw, g_sib, g_recv, g_recv_sib, s_send, s_recv, p_send, p_recv, c_send, c_recv,
    f_sem, v_send, v_recv, n_send, n_recv, vg_send, vg_recv,
):
    n = x_ref.shape[0]
    toks = n * SEQ
    pairs = SEQ // 2
    groups = n // GROUP
    rows = shard.shape[0]
    half = buf.shape[1] // 2
    outer, inner = factors(wide)
    me, core = lax.axis_index("wide"), lax.axis_index("narrow")
    zo, pi = me // inner, lax.rem(me, inner)
    mine = pl.ds(pl.multiple_of(core * half, 8), half)
    theirs = pl.ds(pl.multiple_of((1 - core) * half, 8), half)
    sibling = (me, 1 - core)
    around = [lax.rem(pi + k, inner) for k in range(1, inner)]
    along = [lax.rem(zo + k, outer) for k in range(1, outer)]
    plane = [(zo * inner + q, core) for q in around]
    column = [(t * inner + pi, core) for t in along]
    late = -(-QK_ROWS // (rows * inner))
    first = -(-QKV_ROWS // (rows * inner))
    bounds = ((first, outer), (late, first), (0, late))

    copies_in = [
        pltpu.make_async_copy(x_hbm, x_ref, io_sem.at[0]),
        pltpu.make_async_copy(dy_hbm, dy_ref, io_sem.at[1]),
    ]
    for copy in copies_in:
        copy.start()

    cross = [(zo * inner + q, 1 - core) for q in around]
    known = plane + cross + column + [sibling]
    greet(known)
    lane = lax.broadcasted_iota(jnp.int32, (80, 256), 1)
    row = lax.broadcasted_iota(jnp.int32, (80, 256), 0)
    for p in range(4):
        lo = jnp.where(row < ROWS, HEAD_DIM * 2 * p, HEAD_DIM * (2 * p + 1))
        hm2[80 * p : 80 * (p + 1), :] = jnp.where(
            (lane >= lo) & (lane < lo + HEAD_DIM), 1.0, 0.0
        ).astype(BF16)
    ones_lane = (lax.broadcasted_iota(jnp.int32, (toks, 64), 1) == 0).astype(F32).astype(BF16)
    for ref in (h, h2, o_t):
        ref[:, D:256] = ones_lane
    for ref in (qs, ks, vs, os_):
        ref[...] = jnp.zeros(ref.shape, F32)

    parts[...] = jnp.zeros(parts.shape, F32)
    vec_at[...] = jnp.zeros(vec_at.shape, F32)
    pl.semaphore_wait(pltpu.get_barrier_semaphore(), len(known))
    buf[me, 0:rows, :] = shard[...]
    buf[me, rows:, :] = jnp.zeros((buf.shape[1] - rows, LANES), F32)

    def push(s, send, recvs, where):
        return remote(buf.at[s, mine], buf.at[s, mine], send, recvs.at[s], where)

    def arrived(s, recvs, part):
        remote(buf.at[s, part], buf.at[s, part], g_sib.at[s], recvs.at[s], sibling).wait_recv()

    def forwards(t, s):
        return [push(s, g_fw.at[t, k], g_recv, where) for k, where in enumerate(plane)]

    vec_rows = [
        (s, max(0, VEC_AT - rows * s) // 8 * 8, max(0, VEC_AT - rows * s), min(rows, USED_ROWS - rows * s))
        for s in range(VEC_AT // rows, (USED_ROWS - 1) // rows + 1)
    ]

    def vec_push(j, where, base):
        return [
            remote(vec_in.at[j], vec_in.at[j], vg_send.at[j, base + k], vg_recv.at[j], dev)
            for k, dev in enumerate(where)
        ]

    def vec_arrived(j):
        remote(vec_in.at[j], vec_in.at[j], vg_send.at[j, 0], vg_recv.at[j], sibling).wait_recv()

    for j, (s, a0, _, end) in enumerate(vec_rows):
        @pl.when(me == s)
        def _(j=j, a0=a0, end=end):
            vec_in[j, 0 : end - a0, :] = shard[a0:end, :]
            for copy in vec_push(j, column, 0) + vec_push(j, plane, outer - 1):
                copy.start()

    own_pushes = [push(me, g_col.at[k], g_recv, where) for k, where in enumerate(column)]
    own_pushes += forwards(zo, me)
    for copy in own_pushes:
        copy.start()

    def to_sibling(s):
        return push(s, g_sib.at[s], g_recv_sib, sibling)

    def forward_level(t):
        s = t * inner + pi

        @pl.when(t != zo)
        def _():
            arrived(s, g_recv, mine)
            for copy in forwards(t, s):
                copy.start()
            to_sibling(s).start()

    def pass_level(t):
        for q in around:
            s = t * inner + q
            arrived(s, g_recv, mine)
            to_sibling(s).start()

    def whole_shard(s):
        @pl.when(s != me)
        def _():
            arrived(s, g_recv_sib, theirs)

    def unpack(s):
        flat[rows * s : rows * (s + 1), :] = buf[s, 0:rows, :]

    for j, (s, _, _, _) in enumerate(vec_rows):
        @pl.when((me != s) & (pi == s % inner))
        def _(j=j):
            vec_arrived(j)
            for copy in vec_push(j, plane, outer - 1):
                copy.start()

    for t in range(outer):
        forward_level(t)

    def tokens_of(ref, t, count):
        return split_tokens(
            ref[:, pl.ds(pl.multiple_of(t * D, 128), count * D)].astype(F32), count
        )

    def put_tokens(ref, t, val):
        for half in range(2):
            for k in range(val.shape[0] // n):
                ref.at[half][pl.ds(t + k, n, stride=ROWS), :] = val[
                    n * k : n * (k + 1), 128 * half : 128 * (half + 1)
                ]

    def get_tokens(ref, t, count):
        return jnp.concatenate(
            [
                jnp.concatenate(
                    [ref.at[half][pl.ds(t + k, n, stride=ROWS), :] for half in range(2)], 1
                )
                for k in range(count)
            ],
            0,
        )

    def over_token_chunks(body, width, carry, hook=lambda i: None):
        whole = pairs // width

        def step(i, c):
            hook(i)
            return body(i * (2 * width), 2 * width, c)

        carry = lax.fori_loop(0, whole, step, carry)
        if pairs % width:
            carry = body(whole * 2 * width, 2 * (pairs % width), carry)
        return carry

    def get_rows(ref, start, count):
        return jnp.concatenate([ref[0, pl.ds(start, count), :], ref[1, pl.ds(start, count), :]], 1)

    def put_rows(ref, start, val):
        for half in range(2):
            ref[half, pl.ds(start, val.shape[0]), :] = val[:, 128 * half : 128 * (half + 1)]

    def rows_at(t, count):
        return pl.ds(pl.multiple_of(t * n, 32), count * n)

    def norm1(t, count, carry):
        at = rows_at(t, count)
        xh, r = norm_fwd(tokens_of(x_ref, t, count))
        xh1[at, :] = xh
        r1[at, :] = r
        return carry

    copies_in[0].wait()
    over_token_chunks(norm1, WIDTH1, 0)

    for t in range(first):
        pass_level(t)
    for s in range(first * inner):
        whole_shard(s)
        unpack(s)
    for j, (s, a0, begin, end) in enumerate(vec_rows):
        @pl.when(pi != s % inner)
        def _(j=j):
            vec_arrived(j)

        flat[rows * s + begin : rows * s + end, :] = vec_in[j, begin - a0 : end - a0, :]
    for (base, count), ref in zip(MATS[0:3], (wq, wk, wv)):
        load_square(flat, base, count, tmp, ref)

    def vec(k):
        a = VEC_AT + 3 * (k // 2)
        zero = jnp.zeros((1, 64), F32)
        if k % 2 == 0:
            return jnp.concatenate([flat[a : a + 1, :], flat[a + 1 : a + 2, 0:64], zero], 1)
        return jnp.concatenate([flat[a + 1 : a + 2, 64:128], flat[a + 2 : a + 3, :], zero], 1)

    g1, n1, bq, bv, bo, g2, n2, b2 = [vec(k) for k in range(8)]
    b1 = jnp.concatenate([flat[VEC_AT + 12 + c : VEC_AT + 13 + c, :] for c in range(4)], 1)

    def dense1(t, count, carry):
        at = rows_at(t, count)
        hb = (xh1[at, :] * g1 + n1).astype(BF16)
        h[at, 0:D] = hb[:, 0:D]
        put_tokens(qs, t, (nn(hb, wq[...]) + bq).astype(BF16).astype(F32))
        put_tokens(ks, t, nn(hb, wk[...]).astype(BF16).astype(F32))
        put_tokens(vs, t, (nn(hb, wv[...]) + bv).astype(BF16).astype(F32))
        return carry

    over_token_chunks(dense1, WIDTH1, 0)

    lane3 = lax.broadcasted_iota(jnp.int32, (1, LANES), 1)

    def squeeze(v):
        return jnp.where(
            lane3 < ROWS, v[0:HJ], jnp.where(lane3 < 2 * ROWS, v[HJ : 2 * HJ], v[2 * HJ : 3 * HJ])
        ).reshape(HEADS, ROWS, LANES)

    jrow = lax.broadcasted_iota(jnp.int32, (1, ROWS, LANES), 1)
    cexp = math.log2(math.e) / math.sqrt(HEAD_DIM)
    scale = 1.0 / math.sqrt(HEAD_DIM)

    def attn(i, carry):
        @pl.when(i == 1)
        def _():
            for t in range(first, outer):
                pass_level(t)

        r0 = pl.multiple_of(i * (LOCK1 * GROWS), 8)
        base0 = pl.multiple_of(i * (LOCK1 * 3 * HJ), 64)
        p0 = pl.multiple_of(i * (LOCK1 * HJ), 64)
        sets = range(LOCK1)
        qg = [get_rows(qs, r0 + GROWS * k, LANES).astype(BF16) for k in sets]
        for k in sets:
            for src, dst in ((ks, kbd), (vs, vbd)):
                for b in range(GROUP):
                    one = get_rows(src, r0 + GROWS * k + ROWS * b, ROWS)
                    two = jnp.concatenate([one, one], 0).astype(BF16)
                    for p in range(4):
                        dst[pl.ds(base0 + HJ * (3 * k + b) + 80 * p, 80), :] = (
                            two * hm2[80 * p : 80 * (p + 1), :]
                        )
        st = [squeeze(nt(kbd[pl.ds(base0 + 3 * HJ * k, 3 * HJ), :], qg[k])) for k in sets]
        st = [jnp.where(jrow < SEQ, v, -1e30) for v in st]
        m = [jnp.max(v, 1, keepdims=True) for v in st]
        e = [jnp.exp2((st[k] - m[k]) * cexp) for k in sets]
        l = [1.0 / jnp.sum(v, 1, keepdims=True) for v in e]
        p = [(e[k] * l[k]).reshape(HJ, LANES) for k in sets]
        for k in sets:
            psc[pl.ds(p0 + HJ * k, HJ), :] = p[k]
        pt = [v.T for v in p]
        for b in range(GROUP):
            for k in sets:
                ob = nn(
                    pt[k][ROWS * b : ROWS * (b + 1), :].astype(BF16),
                    vbd[pl.ds(base0 + HJ * (3 * k + b), HJ), :],
                )
                put_rows(os_, r0 + GROWS * k + ROWS * b, ob.astype(BF16).astype(F32)[0:SEQ])
        return carry

    lax.fori_loop(0, groups // LOCK1, attn, 0)

    for s in range(first * inner, wide):
        whole_shard(s)
        unpack(s)
    for (base, count), ref in zip(MATS[3:5], (wo, w2)):
        load_square(flat, base, count, tmp, ref)
    for c in range(4):
        w1[0:D, 128 * c : 128 * (c + 1)] = flat[pl.ds(W1_AT + c, D, stride=4), :].astype(BF16)
    w1[D:256, :] = jnp.zeros((256 - D, 2 * FF), BF16)
    copies_in[1].wait()

    def dense2(t0, count, carry):
        dg2, dn2, db2 = carry
        at = rows_at(t0, count)
        o = get_tokens(os_, t0, count).astype(BF16)
        o_t[at, 0:D] = o[:, 0:D]
        x2 = tokens_of(x_ref, t0, count) + (nn(o, wo[...]) + bo)
        xh, r = norm_fwd(x2)
        hb = (xh * g2 + n2).astype(BF16)
        h2[at, 0:D] = hb[:, 0:D]
        u = nn(hb, w1[...]) + b1
        gate, up = u[:, :FF], u[:, FF:]
        sq = gate * gate
        t = jnp.tanh(gate * (GELU_C + (GELU_C * 0.044715) * sq))
        half = 0.5 + 0.5 * t
        act = gate * half
        zb = (act * up).astype(BF16)
        z[at, :] = zb
        y = x2 + nn(zb, w2[...]) + b2
        out_ref[:, pl.ds(pl.multiple_of(t0 * D, 128), count * D)] = join_tokens(y, n).astype(BF16)
        dyf = tokens_of(dy_ref, t0, count)
        dyb = dyf.astype(BF16)
        dyt[at, :] = dyb
        dz = nt(dyb, w2[...])
        slope = half + gate * (0.5 - 0.5 * t * t) * (GELU_C + (3 * GELU_C * 0.044715) * sq)
        du = jnp.concatenate([(dz * up * slope).astype(BF16), (dz * act).astype(BF16)], 1)
        dul[at, :] = du
        dh = nt(du, w1[...])
        dx2 = dyf + norm_back(dh, xh, r, g2)
        dx2s[at, :] = dx2
        da = dx2.astype(BF16)
        dal[at, :] = da
        put_tokens(os_, t0, nt(da, wo[...]).astype(BF16).astype(F32))
        return dg2 + rows8(dh * xh), dn2 + rows8(dh), db2 + rows8(dyf)

    zero = jnp.zeros((8, 256), F32)
    dg2, dn2, db2 = over_token_chunks(dense2, WIDTH2, (zero, zero, zero))

    copy_out = pltpu.make_async_copy(out_ref, out_hbm, io_sem.at[2])
    copy_out.start()

    def total(v):
        return jnp.sum(v, 0, keepdims=True)

    def over_tokens(*products):
        for acc, _, _ in products:
            acc[...] = jnp.zeros(acc.shape, F32)
        size = toks // DW_STEPS

        @pl.loop(0, DW_STEPS)
        def _(i):
            at = pl.ds(pl.multiple_of(i * size, 16), size)
            for acc, a, b in products:
                acc[...] += tn(a[at, :], b[at, :])

    over_tokens((acc, z, dyt), (acc2, h2, dul), (acc3, o_t, dal))
    store_square(acc[...], gflat, 1920, FF, tmp)
    for c in range(4):
        gflat[pl.ds(W1_AT + c, D, stride=4), :] = acc2[0:D, 128 * c : 128 * (c + 1)]
        vec_own[12 + c : 13 + c, :] = acc2[D : D + 1, 128 * c : 128 * (c + 1)]
    store_square(acc3[...], gflat, 864, D, tmp)
    dbo = acc3[D : D + 1, :]

    def pack(lo, hi):
        for s in range(lo * inner, hi * inner):
            stop = min(rows * (s + 1), VEC_AT)
            if stop > rows * s:
                parts[s // inner, s % inner, 0 : stop - rows * s, :] = gflat[rows * s : stop, :]

    places = around + [pi]

    def sib_copies(part, lo, hi):
        return [
            remote(
                parts.at[lo:hi, q, theirs], sib_in.at[lo:hi, q],
                s_send.at[part, k], s_recv.at[part, q], sibling,
            )
            for k, q in enumerate(places)
        ]

    def plane_copies(part, lo, hi):
        return [
            remote(
                out_p.at[k, lo:hi], plane_in.at[pi, lo:hi],
                p_send.at[part, k], p_recv.at[part, pi], plane[k],
            )
            for k in range(inner - 1)
        ]

    def col_copy(t):
        return remote(
            out_c.at[t], col_in.at[zo], c_send.at[t], c_recv.at[zo], (t * inner + pi, core)
        )

    def sum_cores(part):
        lo, hi = bounds[part]
        sends = plane_copies(part, lo, hi)
        for k, q in enumerate(places):
            remote(
                sib_in.at[lo:hi, q], sib_in.at[lo:hi, q],
                s_send.at[part, k], s_recv.at[part, q], sibling,
            ).wait_recv()
            both = parts[lo:hi, q, mine, :] + sib_in[lo:hi, q]
            if k < inner - 1:
                out_p[k, lo:hi] = both
                sends[k].start()
            else:
                plane_in[pi, lo:hi] = both

    def sum_plane(part):
        lo, hi = bounds[part]
        for k, q in enumerate(around):
            remote(
                plane_in.at[q, lo:hi], plane_in.at[q, lo:hi],
                p_send.at[part, k], p_recv.at[part, q], sibling,
            ).wait_recv()
        for t in range(lo, hi):
            line = plane_in[0, t]
            for q in range(1, inner):
                line = line + plane_in[q, t]
            out_c[t] = line

            @pl.when(t != zo)
            def _():
                col_copy(t).start()

    def send_cores(part):
        pack(*bounds[part])
        for copy in sib_copies(part, *bounds[part]):
            copy.start()

    send_cores(0)

    def by_sample(v):
        return jnp.concatenate(
            [
                jnp.where((lane3 >= ROWS * b) & (lane3 < ROWS * (b + 1)), v, 0.0).reshape(HJ, LANES)
                for b in range(GROUP)
            ],
            0,
        ).astype(BF16)

    def own_lanes(v):
        v = v.reshape(GROUP, HEADS, ROWS, 256)
        out = []
        for b in range(GROUP):
            lo, hi = v[b, 0, :, 0:128], v[b, 5, :, 128:256]
            for k in range(1, 6):
                lo = jnp.where(lane3 >= HEAD_DIM * k, v[b, k, :, 0:128], lo)
            for k in range(6, HEADS):
                hi = jnp.where(lane3 >= HEAD_DIM * k - 128, v[b, k, :, 128:256], hi)
            out.append(jnp.concatenate([lo, hi], 1))
        return jnp.concatenate(out, 0)

    def probs(at):
        return psc[pl.ds(at, HJ), :].reshape(HEADS, ROWS, LANES)

    def attn_back_v(i, carry):
        @pl.when(i == 2)
        def _():
            sum_cores(0)

        r0 = pl.multiple_of(i * (LOCK2 * GROWS), 8)
        p0 = pl.multiple_of(i * (LOCK2 * HJ), 64)
        for k in range(LOCK2):
            dg = get_rows(os_, r0 + GROWS * k, LANES).astype(BF16)
            dv = own_lanes(nn(by_sample(probs(p0 + HJ * k)), dg))
            put_rows(vs, r0 + GROWS * k, dv.astype(BF16).astype(F32))
        return carry

    lax.fori_loop(0, groups // LOCK2, attn_back_v, 0)

    def collect(refs):
        def chunk(t0, count, carry):
            at = rows_at(t0, count)
            for k, ref in refs:
                dqkv[at, 256 * k : 256 * (k + 1)] = get_tokens(ref, t0, count).astype(BF16)
            return carry

        over_token_chunks(chunk, WIDTH3, 0)

    collect([(2, vs)])
    over_tokens((acc, h, dqkv.at[:, 512:768]))
    store_square(acc[...], gflat, 576, D, tmp)
    dbv = acc[D : D + 1, :]
    send_cores(1)

    def attn_back(i, carry):
        @pl.when(i == 1)
        def _():
            sum_cores(1)

        @pl.when(i == 3)
        def _():
            sum_plane(0)

        r0 = pl.multiple_of(i * (LOCK2 * GROWS), 8)
        base0 = pl.multiple_of(i * (LOCK2 * 3 * HJ), 64)
        p0 = pl.multiple_of(i * (LOCK2 * HJ), 64)
        sets = range(LOCK2)
        qg = [get_rows(qs, r0 + GROWS * k, LANES).astype(BF16) for k in sets]
        dg = [get_rows(os_, r0 + GROWS * k, LANES).astype(BF16) for k in sets]
        dp = [squeeze(nt(vbd[pl.ds(base0 + 3 * HJ * k, 3 * HJ), :], dg[k])) for k in sets]
        p = [probs(p0 + HJ * k) for k in sets]
        t = [jnp.sum(p[k] * dp[k], 1, keepdims=True) for k in sets]
        ds = [p[k] * (dp[k] - t[k]) for k in sets]
        dst = [v.reshape(HJ, LANES).T for v in ds]
        dk = [own_lanes(nn(by_sample(ds[k]), qg[k])) * scale for k in sets]
        for b in range(GROUP):
            for k in sets:
                dq = nn(
                    dst[k][ROWS * b : ROWS * (b + 1), :].astype(BF16),
                    kbd[pl.ds(base0 + HJ * (3 * k + b), HJ), :],
                )
                put_rows(qs, r0 + GROWS * k + ROWS * b, (dq * scale).astype(BF16).astype(F32))
        for k in sets:
            put_rows(ks, r0 + GROWS * k, dk[k].astype(BF16).astype(F32))
        return carry

    lax.fori_loop(0, groups // LOCK2, attn_back, 0)

    collect([(0, qs), (1, ks)])
    over_tokens((acc2, h, dqkv.at[:, 0:512]))
    for k in range(2):
        store_square(acc2[:, 256 * k : 256 * (k + 1)], gflat, 288 * k, D, tmp)
    send_cores(2)

    def dense3(t0, count, carry):
        dg1, dn1 = carry
        at = rows_at(t0, count)
        dh = (
            nt(dqkv[at, 0:256], wq[...])
            + nt(dqkv[at, 256:512], wk[...])
            + nt(dqkv[at, 512:768], wv[...])
        )
        xh = xh1[at, :]
        ig = dx2s[at, :] + norm_back(dh, xh, r1[at, :], g1)
        ig_ref[:, pl.ds(pl.multiple_of(t0 * D, 128), count * D)] = join_tokens(ig, n)
        return dg1 + rows8(dh * xh), dn1 + rows8(dh)

    def hook3(i):
        @pl.when(i == 1)
        def _():
            sum_cores(2)
            sum_plane(1)

    dg1, dn1 = over_token_chunks(dense3, WIDTH3, (zero, zero), hook3)

    vecs = [
        total(dg1), total(dn1), acc2[D : D + 1, 0:256], dbv,
        dbo, total(dg2), total(dn2), total(db2),
    ]
    for k in range(4):
        a, b = vecs[2 * k], vecs[2 * k + 1]
        vec_own[3 * k : 3 * k + 1, :] = a[:, 0:128]
        vec_own[3 * k + 1 : 3 * k + 2, :] = jnp.concatenate([a[:, 128:192], b[:, 0:64]], 1)
        vec_own[3 * k + 2 : 3 * k + 3, :] = b[:, 64:192]
    vec_sends = [remote(vec_own, vec_sib, v_send.at[0], v_recv.at[0], sibling)]
    vec_sends[0].start()
    copy_ig = pltpu.make_async_copy(ig_ref, ig_hbm, io_sem.at[3])
    copy_ig.start()

    def spread(slots, at, sends, recvs, base, where):
        out = [
            remote(slots.at[at], slots.at[at], sends.at[base + k], recvs.at[base + at], dev)
            for k, dev in enumerate(where)
        ]
        for copy in out:
            copy.start()
        return out

    def collected(slots, others, sends, recvs, base):
        for k, q in enumerate(others):
            remote(
                slots.at[q], slots.at[q], sends.at[base + k], recvs.at[base + q], sibling
            ).wait_recv()
        return jnp.sum(slots[...], 0)

    remote(vec_sib, vec_sib, v_send.at[0], v_recv.at[0], sibling).wait_recv()
    vec_plane[pi] = vec_own[...] + vec_sib[...]
    vec_sends += spread(vec_plane, pi, v_send, v_recv, 1, plane)
    sum_plane(2)
    vec_col[zo] = collected(vec_plane, around, v_send, v_recv, 1)
    vec_sends += spread(vec_col, zo, v_send, v_recv, 1 + inner, column)

    col_in[zo] = out_c[zo]
    for t in along:
        remote(col_in.at[t], col_in.at[t], c_send.at[t], c_recv.at[t], sibling).wait_recv()
    line = col_in[0]
    for t in range(1, outer):
        line = line + col_in[t]
    res[mine, :] = line
    last = remote(res.at[mine], res.at[mine], f_sem.at[0], f_sem.at[1], sibling)
    last.start()
    slot = 2 * pi + core
    near = [2 * q + core for q in around] + [2 * q + 1 - core for q in around] + [2 * pi + 1 - core]
    sq_plane[slot] = rows8(line * line)
    sq_sends = spread(sq_plane, slot, n_send, n_recv, 0, plane + cross + [sibling])
    vec = collected(vec_col, along, v_send, v_recv, 1 + inner)
    vec_at[VEC_AT:USED_ROWS, :] = vec
    remote(res.at[theirs], res.at[theirs], f_sem.at[0], f_sem.at[1], sibling).wait_recv()
    own[...] = res[0:rows, :] + vec_at[pl.ds(me * rows, rows), :]
    sq_col[zo] = collected(sq_plane, near, n_send, n_recv, 0)
    sq_sends += spread(sq_col, zo, n_send, n_recv, 2 * inner, column)
    both = collected(sq_col, along, n_send, n_recv, 2 * inner) + rows8(vec * vec)
    squares[...] = jnp.broadcast_to(jnp.sum(both, keepdims=True), squares.shape)

    for copy in own_pushes + vec_sends + sq_sends + [last]:
        copy.wait_send()
    for t in range(outer):
        @pl.when(t != zo)
        def _(t=t):
            for copy in forwards(t, t * inner + pi):
                copy.wait_send()
            to_sibling(t * inner + pi).wait_send()
            col_copy(t).wait_send()

        for q in around:
            to_sibling(t * inner + q).wait_send()
    for j, (s, _, _, _) in enumerate(vec_rows):
        @pl.when(me == s)
        def _(j=j):
            for copy in vec_push(j, column, 0):
                copy.wait_send()

        @pl.when(pi == s % inner)
        def _(j=j):
            for copy in vec_push(j, plane, outer - 1):
                copy.wait_send()

    for part, (lo, hi) in enumerate(bounds):
        for copy in sib_copies(part, lo, hi) + plane_copies(part, lo, hi):
            copy.wait_send()
    copy_out.wait()
    copy_ig.wait()


def step(x, dy, shard, wide):
    outer, inner = factors(wide)
    n, rows = x.shape[0], shard.shape[0]
    toks = n * SEQ
    groups = n // GROUP
    padded = (rows + 15) // 16 * 16
    half = padded // 2
    vecs = (USED_ROWS - 1) // rows - VEC_AT // rows + 1
    vm, dma = pltpu.VMEM, pltpu.SemaphoreType.DMA
    sm = vm((2, n * ROWS + 8, LANES), F32)
    tok = vm((toks, 256), BF16)
    tile = (8, LANES)
    scratch = (
        [vm(x.shape, BF16), vm(x.shape, BF16), vm(x.shape, BF16), vm(x.shape, F32)]
        + [vm((wide * rows, LANES), F32)] * 2
        + [sm] * 4
        + [vm((groups * 3 * HJ, 256), BF16)] * 2
        + [vm((groups * HJ, LANES), F32)]
        + [vm((toks, 256), F32), vm((toks, 1), F32), vm((toks, 256), F32)]
        + [tok, tok, tok, vm((toks, 2 * FF), BF16), tok]
        + [tok, tok, vm((toks, 3 * 256), BF16)]
        + [vm((256, 256), BF16)] * 4
        + [vm((256, 2 * FF), BF16), vm((FF, 256), BF16), vm((2, FF, 128), F32)]
        + [vm((320, 256), BF16)]
        + [vm((256, 256), F32), vm((256, 512), F32), vm((256, 256), F32)]
        + [vm((wide, padded, LANES), F32), vm((outer, inner, padded, LANES), F32)]
        + [vm((outer, inner, half, LANES), F32), vm((inner, outer, half, LANES), F32)]
        + [vm((inner - 1, outer, half, LANES), F32)]
        + [vm((outer, half, LANES), F32)] * 2
        + [vm((padded, LANES), F32)]
        + [vm((16, LANES), F32)] * 2
        + [vm((inner, 16, LANES), F32), vm((outer, 16, LANES), F32)]
        + [vm((wide * rows, LANES), F32)]
        + [vm((2 * inner, *tile), F32), vm((outer, *tile), F32)]
        + [vm((vecs, min(24, padded), LANES), F32)]
        + [dma((4,)), dma((outer - 1,)), dma((outer, inner - 1)), dma((wide,)), dma((wide,)), dma((wide,))]
        + [dma((3, inner))] * 4
        + [dma((outer,)), dma((outer,)), dma((2,))]
        + [dma((1 + inner + outer,))] * 2
        + [dma((2 * inner + outer,))] * 2
        + [dma((vecs, outer + inner - 2)), dma((vecs,))]
    )
    anywhere, vmem = pl.BlockSpec(memory_space=pl.ANY), pl.BlockSpec(memory_space=pltpu.VMEM)
    return pl.pallas_call(
        functools.partial(step_kernel, wide),
        out_shape=(
            jax.ShapeDtypeStruct(x.shape, BF16),
            jax.ShapeDtypeStruct(x.shape, F32),
            jax.ShapeDtypeStruct((rows, LANES), F32),
            jax.ShapeDtypeStruct(tile, F32),
        ),
        in_specs=[anywhere, anywhere, vmem],
        out_specs=(anywhere, anywhere, vmem, vmem),
        scratch_shapes=scratch,
        compiler_params=pltpu.CompilerParams(
            collective_id=0, has_side_effects=True, vmem_limit_bytes=60 * 2**20
        ),
        name="step",
    )(x, dy, shard)


def finish_kernel(*refs):
    big_in, small_in = refs[0:2], refs[2:7]
    big_out, norm_out, small_out = refs[7:9], refs[9], refs[10:15]
    stages, ins, norm, outs = refs[15:17], refs[17:22], refs[22], refs[23:28]
    sem_in, sem_out, sem_small = refs[28:31]
    pieces = []
    for k in range(2):
        size = big_in[k].shape[0] // PIECES
        for p in range(PIECES):
            at = pl.ds(size * p, size)
            pieces.append(
                (
                    pltpu.make_async_copy(big_in[k].at[at], stages[k].at[at], sem_in.at[k, p]),
                    pltpu.make_async_copy(stages[k].at[at], big_out[k].at[at], sem_out.at[k, p]),
                )
            )
    loads = [pltpu.make_async_copy(small_in[k], ins[k], sem_small.at[k]) for k in range(5)]
    for copy in loads:
        copy.start()
    for come, _ in pieces:
        come.start()
    for copy in loads:
        copy.wait()
    own, squares, master, first, second = ins
    clipped, new_master, new_copy, new_first, new_second = outs
    grad_norm = jnp.sqrt(squares[...])
    norm[...] = grad_norm[0:1, 0:1]
    factor = jnp.minimum(1.0, 1.0 / (grad_norm[0:1, :] + 1e-06))
    grad = own[...] * factor
    clipped[...] = grad
    one = 0.5 * first[...] + 0.5 * grad
    two = 0.5 * second[...] + 0.5 * grad * grad
    new_first[...] = one
    new_second[...] = two
    fixed = 1.0 - 0.5**STEP
    old = master[...]
    new = old - 0.05 * ((one / fixed) / (jnp.sqrt(two / fixed) + 1e-08) + 0.1 * old)
    new_master[...] = new
    new_copy[...] = new.astype(BF16)
    stores = [
        pltpu.make_async_copy(src, dst, sem_small.at[5 + k])
        for k, (src, dst) in enumerate(zip((norm, *outs), (norm_out, *small_out)))
    ]
    for copy in stores:
        copy.start()
    for come, go in pieces:
        come.wait()
        go.start()
    for copy in stores:
        copy.wait()
    for _, go in pieces:
        go.wait()


def finish(block_out, input_grad, owned, squares, master, first, second):
    anywhere, vm = pl.BlockSpec(memory_space=pl.ANY), pltpu.VMEM
    one, flat = (1, 1), owned.shape
    kinds = [(flat, F32), (flat, F32), (flat, BF16), (flat, F32), (flat, F32)]
    like = jax.ShapeDtypeStruct
    return pl.pallas_call(
        finish_kernel,
        out_shape=(
            like(block_out.shape, BF16),
            like(input_grad.shape, F32),
            like(one, F32),
            *[like(*kind) for kind in kinds],
        ),
        in_specs=[anywhere] * 7,
        out_specs=(anywhere,) * 8,
        scratch_shapes=[
            vm(block_out.shape, BF16),
            vm(input_grad.shape, F32),
            vm(flat, F32),
            vm(squares.shape, F32),
            vm(flat, F32),
            vm(flat, F32),
            vm(flat, F32),
            vm(one, F32),
            *[vm(*kind) for kind in kinds],
            pltpu.SemaphoreType.DMA((2, PIECES)),
            pltpu.SemaphoreType.DMA((2, PIECES)),
            pltpu.SemaphoreType.DMA((11,)),
        ],
        compiler_params=pltpu.CompilerParams(vmem_limit_bytes=60 * 2**20),
        name="finish",
    )(block_out, input_grad, owned, squares, master, first, second)


def on_device(inputs, cotangent, master, first, second):
    flat = lambda a: a.reshape(-1)
    tall = lambda a: a.reshape(-1, LANES)
    block_out, input_grad, owned, squares = step(
        inputs, cotangent, tall(master), lax.axis_size("wide")
    )
    block_out, input_grad, norm, clipped, new_master, new_copy, new_first, new_second = finish(
        block_out, input_grad, owned, squares, tall(master), tall(first), tall(second)
    )
    return (
        block_out,
        input_grad,
        flat(clipped),
        norm.reshape(()),
        flat(new_master),
        flat(new_copy),
        flat(new_first),
        flat(new_second),
    )


def solution(mesh):
    both, part = P(("wide", "narrow"), None), P("wide")
    return jax.shard_map(
        on_device,
        mesh=mesh,
        in_specs=(both, both, part, part, part),
        out_specs=(both, both, part, P(), part, part, part, part),
        check_vma=False,
    )
```

```python
import functools
import math

import jax
import jax.numpy as jnp
from jax import lax
from jax.experimental import pallas as pl
from jax.experimental.pallas import tpu as pltpu
from jax.sharding import PartitionSpec as P

D = 192
HEADS = 8
HEAD_DIM = 24
FF = 256
SEQ = 34
STEP = 5
ROWS = 40
GROUP = 3
GROWS = GROUP * ROWS
PAIRS = HEADS // 2
PAIR_DIM = 2 * HEAD_DIM
HJ = PAIRS * ROWS
LANES = 128
F32 = jnp.float32
BF16 = jnp.bfloat16
MATS = ((0, D), (288, D), (576, D), (864, D), (1920, FF))
W1_AT = 1152
WIDTH1, WIDTH2, WIDTH3, DW_STEPS = 4, 4, 4, 2
LOCK1, LOCK2 = 4, 4
PIECES = 1
VEC_AT = 2304
USED_ROWS = VEC_AT + 16
QK_ROWS = 576
QKV_ROWS = 864
GELU_C = math.sqrt(2.0 / math.pi)


def nn(a, b):
    return lax.dot_general(a, b, (((1,), (0,)), ((), ())), preferred_element_type=F32)


def nt(a, b):
    return lax.dot_general(a, b, (((1,), (1,)), ((), ())), preferred_element_type=F32)


def tn(a, b):
    return lax.dot_general(a, b, (((0,), (0,)), ((), ())), preferred_element_type=F32)


def low_half(v):
    lane = lax.broadcasted_iota(jnp.int32, v.shape, 1)
    return lane < 64


def load_square(flat, base, rows, tmp, out):
    half = rows // 2
    f0 = flat[pl.ds(base, half, stride=3), :]
    f1 = flat[pl.ds(base + 1, half, stride=3), :]
    f2 = flat[pl.ds(base + 2, half, stride=3), :]
    r1 = pltpu.roll(f1, 64, 1)
    r2 = pltpu.roll(f2, 64, 1)
    left = low_half(f0)
    lo, hi = tmp.at[0], tmp.at[1]
    lo[pl.ds(0, half, stride=2), :] = f0
    hi[pl.ds(0, half, stride=2), :] = jnp.where(left, f1, 0.0)
    lo[pl.ds(1, half, stride=2), :] = jnp.where(left, r1, r2)
    hi[pl.ds(1, half, stride=2), :] = jnp.where(left, r2, 0.0)
    out[0:rows, 0:128] = lo[0:rows, :].astype(BF16)
    out[0:rows, 128:256] = hi[0:rows, :].astype(BF16)
    if rows < 256:
        out[rows:256, :] = jnp.zeros((256 - rows, 256), BF16)


def store_square(val, flat, base, rows, tmp):
    half = rows // 2
    lo, hi = tmp.at[0], tmp.at[1]
    lo[0:rows, :] = val[0:rows, 0:128]
    hi[0:rows, :] = val[0:rows, 128:256]
    e0 = lo[pl.ds(0, half, stride=2), :]
    e1 = hi[pl.ds(0, half, stride=2), :]
    o0 = pltpu.roll(lo[pl.ds(1, half, stride=2), :], 64, 1)
    o1 = pltpu.roll(hi[pl.ds(1, half, stride=2), :], 64, 1)
    left = low_half(e0)
    flat[pl.ds(base, half, stride=3), :] = e0
    flat[pl.ds(base + 1, half, stride=3), :] = jnp.where(left, e1, o0)
    flat[pl.ds(base + 2, half, stride=3), :] = jnp.where(left, o0, o1)


def norm_fwd(x):
    mean = jnp.sum(x, -1, keepdims=True) * (1.0 / D)
    right = x[:, 128:256] - mean
    c = jnp.concatenate([x[:, 0:128] - mean, jnp.where(low_half(right), right, 0.0)], 1)
    var = jnp.sum(c * c, -1, keepdims=True) * (1.0 / D)
    r = lax.rsqrt(var + 1e-05)
    return c * r, r


def norm_back(d, xh, r, g):
    e = d * g
    m1 = jnp.sum(e, -1, keepdims=True) * (1.0 / D)
    m2 = jnp.sum(e * xh, -1, keepdims=True) * (1.0 / D)
    return r * (e - m1 - xh * m2)


def rows8(v):
    return jnp.sum(v.reshape(v.shape[0] // 8, 8, v.shape[1]), 0)


def split_tokens(v, count):
    zero = jnp.zeros((v.shape[0], 256 - D), v.dtype)
    return jnp.concatenate(
        [jnp.concatenate([v[:, D * t : D * (t + 1)], zero], 1) for t in range(count)], 0
    )


def join_tokens(v, n):
    return jnp.concatenate([v[n * t : n * (t + 1), 0:D] for t in range(v.shape[0] // n)], 1)


def factors(wide):
    inner = max(k for k in range(1, int(math.isqrt(wide)) + 1) if wide % k == 0)
    return wide // inner, inner


def remote(src, dst, send, recv, where):
    return pltpu.make_async_remote_copy(
        src_ref=src,
        dst_ref=dst,
        send_sem=send,
        recv_sem=recv,
        device_id=where,
        device_id_type=pl.DeviceIdType.MESH,
    )


def greet(devices):
    for dev in devices:
        pl.semaphore_signal(
            pltpu.get_barrier_semaphore(), inc=1, device_id=dev,
            device_id_type=pl.DeviceIdType.MESH,
        )


def step_kernel(
    wide,
    x_hbm, dy_hbm, shard, out_hbm, ig_hbm, own, squares,
    x_ref, dy_ref, out_ref, ig_ref, flat, gflat,
    qs, ks, vs, os_, kbd, vbd, psc, xh1, r1, dx2s, h, h2, z, dul, o_t, dal, dyt, dqkv,
    wq, wk, wv, wo, w1, w2, tmp, hm2, parity, acc, acc2, acc3,
    buf, parts, sib_in, plane_in, out_p, col_in, out_c, res, vec_own, vec_sib, vec_plane, vec_col,
    vec_at, sq_plane, sq_col, vec_in,
    io_sem, g_col, g_fw, g_sib, g_recv, g_recv_sib, s_send, s_recv, p_send, p_recv, c_send, c_recv,
    f_sem, v_send, v_recv, n_send, n_recv, vg_send, vg_recv,
):
    n = x_ref.shape[0]
    toks = n * SEQ
    pairs = SEQ // 2
    groups = n // GROUP
    rows = shard.shape[0]
    half = buf.shape[1] // 2
    outer, inner = factors(wide)
    me, core = lax.axis_index("wide"), lax.axis_index("narrow")
    zo, pi = me // inner, lax.rem(me, inner)
    mine = pl.ds(pl.multiple_of(core * half, 8), half)
    theirs = pl.ds(pl.multiple_of((1 - core) * half, 8), half)
    sibling = (me, 1 - core)
    around = [lax.rem(pi + k, inner) for k in range(1, inner)]
    along = [lax.rem(zo + k, outer) for k in range(1, outer)]
    plane = [(zo * inner + q, core) for q in around]
    column = [(t * inner + pi, core) for t in along]
    late = -(-QK_ROWS // (rows * inner))
    first = -(-QKV_ROWS // (rows * inner))
    bounds = ((first, outer), (late, first), (0, late))

    copies_in = [
        pltpu.make_async_copy(x_hbm, x_ref, io_sem.at[0]),
        pltpu.make_async_copy(dy_hbm, dy_ref, io_sem.at[1]),
    ]
    for copy in copies_in:
        copy.start()

    cross = [(zo * inner + q, 1 - core) for q in around]
    known = plane + cross + column + [sibling]
    greet(known)
    lane = lax.broadcasted_iota(jnp.int32, (80, 256), 1)
    row = lax.broadcasted_iota(jnp.int32, (80, 256), 0)
    for p in range(PAIRS // 2):
        lo = jnp.where(row < ROWS, PAIR_DIM * 2 * p, PAIR_DIM * (2 * p + 1))
        hm2[80 * p : 80 * (p + 1), :] = jnp.where(
            (lane >= lo) & (lane < lo + PAIR_DIM), 1.0, 0.0
        ).astype(BF16)
    head = lax.broadcasted_iota(jnp.int32, (16, 256), 1) // HEAD_DIM
    for k in range(2):
        parity[16 * k : 16 * (k + 1), :] = jnp.where(
            (lax.rem(head, 2) == k) & (head < HEADS), 1.0, 0.0
        ).astype(BF16)
    ones_lane = (lax.broadcasted_iota(jnp.int32, (toks, 64), 1) == 0).astype(F32).astype(BF16)
    for ref in (h, h2, o_t):
        ref[:, D:256] = ones_lane
    for ref in (qs, ks, vs, os_):
        ref[...] = jnp.zeros(ref.shape, F32)

    parts[...] = jnp.zeros(parts.shape, F32)
    vec_at[...] = jnp.zeros(vec_at.shape, F32)
    pl.semaphore_wait(pltpu.get_barrier_semaphore(), len(known))
    buf[me, 0:rows, :] = shard[...]
    buf[me, rows:, :] = jnp.zeros((buf.shape[1] - rows, LANES), F32)

    def push(s, send, recvs, where):
        return remote(buf.at[s, mine], buf.at[s, mine], send, recvs.at[s], where)

    def arrived(s, recvs, part):
        remote(buf.at[s, part], buf.at[s, part], g_sib.at[s], recvs.at[s], sibling).wait_recv()

    def forwards(t, s):
        return [push(s, g_fw.at[t, k], g_recv, where) for k, where in enumerate(plane)]

    vec_rows = [
        (s, max(0, VEC_AT - rows * s) // 8 * 8, max(0, VEC_AT - rows * s), min(rows, USED_ROWS - rows * s))
        for s in range(VEC_AT // rows, (USED_ROWS - 1) // rows + 1)
    ]

    def vec_push(j, where, base):
        return [
            remote(vec_in.at[j], vec_in.at[j], vg_send.at[j, base + k], vg_recv.at[j], dev)
            for k, dev in enumerate(where)
        ]

    def vec_arrived(j):
        remote(vec_in.at[j], vec_in.at[j], vg_send.at[j, 0], vg_recv.at[j], sibling).wait_recv()

    for j, (s, a0, _, end) in enumerate(vec_rows):
        @pl.when(me == s)
        def _(j=j, a0=a0, end=end):
            vec_in[j, 0 : end - a0, :] = shard[a0:end, :]
            for copy in vec_push(j, column, 0) + vec_push(j, plane, outer - 1):
                copy.start()

    own_pushes = [push(me, g_col.at[k], g_recv, where) for k, where in enumerate(column)]
    own_pushes += forwards(zo, me)
    for copy in own_pushes:
        copy.start()

    def to_sibling(s):
        return push(s, g_sib.at[s], g_recv_sib, sibling)

    def forward_level(t):
        s = t * inner + pi

        @pl.when(t != zo)
        def _():
            arrived(s, g_recv, mine)
            for copy in forwards(t, s):
                copy.start()
            to_sibling(s).start()

    def pass_level(t):
        for q in around:
            s = t * inner + q
            arrived(s, g_recv, mine)
            to_sibling(s).start()

    def whole_shard(s):
        @pl.when(s != me)
        def _():
            arrived(s, g_recv_sib, theirs)

    def unpack(s):
        flat[rows * s : rows * (s + 1), :] = buf[s, 0:rows, :]

    for j, (s, _, _, _) in enumerate(vec_rows):
        @pl.when((me != s) & (pi == s % inner))
        def _(j=j):
            vec_arrived(j)
            for copy in vec_push(j, plane, outer - 1):
                copy.start()

    for t in range(outer):
        forward_level(t)

    def tokens_of(ref, t, count):
        return split_tokens(
            ref[:, pl.ds(pl.multiple_of(t * D, 128), count * D)].astype(F32), count
        )

    def put_tokens(ref, t, val):
        for half in range(2):
            for k in range(val.shape[0] // n):
                ref.at[half][pl.ds(t + k, n, stride=ROWS), :] = val[
                    n * k : n * (k + 1), 128 * half : 128 * (half + 1)
                ]

    def get_tokens(ref, t, count):
        return jnp.concatenate(
            [
                jnp.concatenate(
                    [ref.at[half][pl.ds(t + k, n, stride=ROWS), :] for half in range(2)], 1
                )
                for k in range(count)
            ],
            0,
        )

    def over_token_chunks(body, width, carry, hook=lambda i: None):
        whole = pairs // width

        def step(i, c):
            hook(i)
            return body(i * (2 * width), 2 * width, c)

        carry = lax.fori_loop(0, whole, step, carry)
        if pairs % width:
            carry = body(whole * 2 * width, 2 * (pairs % width), carry)
        return carry

    def get_rows(ref, start, count):
        return jnp.concatenate([ref[0, pl.ds(start, count), :], ref[1, pl.ds(start, count), :]], 1)

    def put_rows(ref, start, val):
        for half in range(2):
            ref[half, pl.ds(start, val.shape[0]), :] = val[:, 128 * half : 128 * (half + 1)]

    def rows_at(t, count):
        return pl.ds(pl.multiple_of(t * n, 32), count * n)

    def norm1(t, count, carry):
        at = rows_at(t, count)
        xh, r = norm_fwd(tokens_of(x_ref, t, count))
        xh1[at, :] = xh
        r1[at, :] = r
        return carry

    copies_in[0].wait()
    over_token_chunks(norm1, WIDTH1, 0)

    for t in range(first):
        pass_level(t)
    for s in range(first * inner):
        whole_shard(s)
        unpack(s)
    for j, (s, a0, begin, end) in enumerate(vec_rows):
        @pl.when(pi != s % inner)
        def _(j=j):
            vec_arrived(j)

        flat[rows * s + begin : rows * s + end, :] = vec_in[j, begin - a0 : end - a0, :]
    for (base, count), ref in zip(MATS[0:3], (wq, wk, wv)):
        load_square(flat, base, count, tmp, ref)

    def vec(k):
        a = VEC_AT + 3 * (k // 2)
        zero = jnp.zeros((1, 64), F32)
        if k % 2 == 0:
            return jnp.concatenate([flat[a : a + 1, :], flat[a + 1 : a + 2, 0:64], zero], 1)
        return jnp.concatenate([flat[a + 1 : a + 2, 64:128], flat[a + 2 : a + 3, :], zero], 1)

    g1, n1, bq, bv, bo, g2, n2, b2 = [vec(k) for k in range(8)]
    b1 = jnp.concatenate([flat[VEC_AT + 12 + c : VEC_AT + 13 + c, :] for c in range(4)], 1)

    def dense1(t, count, carry):
        at = rows_at(t, count)
        hb = (xh1[at, :] * g1 + n1).astype(BF16)
        h[at, 0:D] = hb[:, 0:D]
        put_tokens(qs, t, (nn(hb, wq[...]) + bq).astype(BF16).astype(F32))
        put_tokens(ks, t, nn(hb, wk[...]).astype(BF16).astype(F32))
        put_tokens(vs, t, (nn(hb, wv[...]) + bv).astype(BF16).astype(F32))
        return carry

    over_token_chunks(dense1, WIDTH1, 0)

    lane3 = lax.rem(lax.broadcasted_iota(jnp.int32, (1, 256), 1), LANES)
    odd_head = lax.rem(lax.broadcasted_iota(jnp.int32, (1, 256), 1) // HEAD_DIM, 2) == 1

    def squeeze(v):
        return jnp.where(
            lane3 < ROWS, v[0:HJ], jnp.where(lane3 < 2 * ROWS, v[HJ : 2 * HJ], v[2 * HJ : 3 * HJ])
        ).reshape(PAIRS, ROWS, 256)

    def by_parity(v):
        v3 = v.reshape(8, 16, 256)
        return jnp.concatenate(
            [(v3 * parity[16 * k : 16 * (k + 1), :][None]).reshape(LANES, 256) for k in range(2)], 0
        )

    def per_query(left, right, b):
        rows2 = jnp.concatenate([left[128 * k + ROWS * b : 128 * k + ROWS * (b + 1)] for k in range(2)], 0)
        both = nn(rows2.astype(BF16), right)
        return jnp.where(odd_head, both[ROWS : 2 * ROWS], both[0:ROWS])

    jrow = lax.broadcasted_iota(jnp.int32, (1, ROWS, 256), 1)
    cexp = math.log2(math.e) / math.sqrt(HEAD_DIM)
    scale = 1.0 / math.sqrt(HEAD_DIM)

    def attn(i, carry):
        @pl.when(i == 1)
        def _():
            for t in range(first, outer):
                pass_level(t)

        r0 = pl.multiple_of(i * (LOCK1 * GROWS), 8)
        base0 = pl.multiple_of(i * (LOCK1 * 3 * HJ), 32)
        p0 = pl.multiple_of(i * (LOCK1 * HJ), 32)
        sets = range(LOCK1)
        qg = [by_parity(get_rows(qs, r0 + GROWS * k, LANES).astype(BF16)) for k in sets]
        for k in sets:
            for src, dst in ((ks, kbd), (vs, vbd)):
                for b in range(GROUP):
                    one = get_rows(src, r0 + GROWS * k + ROWS * b, ROWS)
                    two = jnp.concatenate([one, one], 0).astype(BF16)
                    for p in range(PAIRS // 2):
                        dst[pl.ds(base0 + HJ * (3 * k + b) + 80 * p, 80), :] = (
                            two * hm2[80 * p : 80 * (p + 1), :]
                        )
        st = [squeeze(nt(kbd[pl.ds(base0 + 3 * HJ * k, 3 * HJ), :], qg[k])) for k in sets]
        st = [jnp.where(jrow < SEQ, v, -1e30) for v in st]
        m = [jnp.max(v, 1, keepdims=True) for v in st]
        e = [jnp.exp2((st[k] - m[k]) * cexp) for k in sets]
        l = [1.0 / jnp.sum(v, 1, keepdims=True) for v in e]
        p = [(e[k] * l[k]).reshape(HJ, 256) for k in sets]
        for k in sets:
            psc[pl.ds(p0 + HJ * k, HJ), :] = p[k]
        pt = [v.T for v in p]
        for b in range(GROUP):
            for k in sets:
                ob = per_query(pt[k], vbd[pl.ds(base0 + HJ * (3 * k + b), HJ), :], b)
                put_rows(os_, r0 + GROWS * k + ROWS * b, ob.astype(BF16).astype(F32)[0:SEQ])
        return carry

    lax.fori_loop(0, groups // LOCK1, attn, 0)

    for s in range(first * inner, wide):
        whole_shard(s)
        unpack(s)
    for (base, count), ref in zip(MATS[3:5], (wo, w2)):
        load_square(flat, base, count, tmp, ref)
    for c in range(4):
        w1[0:D, 128 * c : 128 * (c + 1)] = flat[pl.ds(W1_AT + c, D, stride=4), :].astype(BF16)
    w1[D:256, :] = jnp.zeros((256 - D, 2 * FF), BF16)
    copies_in[1].wait()

    def dense2(t0, count, carry):
        dg2, dn2, db2 = carry
        at = rows_at(t0, count)
        o = get_tokens(os_, t0, count).astype(BF16)
        o_t[at, 0:D] = o[:, 0:D]
        x2 = tokens_of(x_ref, t0, count) + (nn(o, wo[...]) + bo)
        xh, r = norm_fwd(x2)
        hb = (xh * g2 + n2).astype(BF16)
        h2[at, 0:D] = hb[:, 0:D]
        u = nn(hb, w1[...]) + b1
        gate, up = u[:, :FF], u[:, FF:]
        sq = gate * gate
        t = jnp.tanh(gate * (GELU_C + (GELU_C * 0.044715) * sq))
        half = 0.5 + 0.5 * t
        act = gate * half
        zb = (act * up).astype(BF16)
        z[at, :] = zb
        y = x2 + nn(zb, w2[...]) + b2
        out_ref[:, pl.ds(pl.multiple_of(t0 * D, 128), count * D)] = join_tokens(y, n).astype(BF16)
        dyf = tokens_of(dy_ref, t0, count)
        dyb = dyf.astype(BF16)
        dyt[at, :] = dyb
        dz = nt(dyb, w2[...])
        slope = half + gate * (0.5 - 0.5 * t * t) * (GELU_C + (3 * GELU_C * 0.044715) * sq)
        du = jnp.concatenate([(dz * up * slope).astype(BF16), (dz * act).astype(BF16)], 1)
        dul[at, :] = du
        dh = nt(du, w1[...])
        dx2 = dyf + norm_back(dh, xh, r, g2)
        dx2s[at, :] = dx2
        da = dx2.astype(BF16)
        dal[at, :] = da
        put_tokens(os_, t0, nt(da, wo[...]).astype(BF16).astype(F32))
        return dg2 + rows8(dh * xh), dn2 + rows8(dh), db2 + rows8(dyf)

    zero = jnp.zeros((8, 256), F32)
    dg2, dn2, db2 = over_token_chunks(dense2, WIDTH2, (zero, zero, zero))

    copy_out = pltpu.make_async_copy(out_ref, out_hbm, io_sem.at[2])
    copy_out.start()

    def total(v):
        return jnp.sum(v, 0, keepdims=True)

    def over_tokens(*products):
        for acc, _, _ in products:
            acc[...] = jnp.zeros(acc.shape, F32)
        size = toks // DW_STEPS

        @pl.loop(0, DW_STEPS)
        def _(i):
            at = pl.ds(pl.multiple_of(i * size, 16), size)
            for acc, a, b in products:
                acc[...] += tn(a[at, :], b[at, :])

    over_tokens((acc, z, dyt), (acc2, h2, dul), (acc3, o_t, dal))
    store_square(acc[...], gflat, 1920, FF, tmp)
    for c in range(4):
        gflat[pl.ds(W1_AT + c, D, stride=4), :] = acc2[0:D, 128 * c : 128 * (c + 1)]
        vec_own[12 + c : 13 + c, :] = acc2[D : D + 1, 128 * c : 128 * (c + 1)]
    store_square(acc3[...], gflat, 864, D, tmp)
    dbo = acc3[D : D + 1, :]

    def pack(lo, hi):
        for s in range(lo * inner, hi * inner):
            stop = min(rows * (s + 1), VEC_AT)
            if stop > rows * s:
                parts[s // inner, s % inner, 0 : stop - rows * s, :] = gflat[rows * s : stop, :]

    places = around + [pi]

    def sib_copies(part, lo, hi):
        return [
            remote(
                parts.at[lo:hi, q, theirs], sib_in.at[lo:hi, q],
                s_send.at[part, k], s_recv.at[part, q], sibling,
            )
            for k, q in enumerate(places)
        ]

    def plane_copies(part, lo, hi):
        return [
            remote(
                out_p.at[k, lo:hi], plane_in.at[pi, lo:hi],
                p_send.at[part, k], p_recv.at[part, pi], plane[k],
            )
            for k in range(inner - 1)
        ]

    def col_copy(t):
        return remote(
            out_c.at[t], col_in.at[zo], c_send.at[t], c_recv.at[zo], (t * inner + pi, core)
        )

    def sum_cores(part):
        lo, hi = bounds[part]
        sends = plane_copies(part, lo, hi)
        for k, q in enumerate(places):
            remote(
                sib_in.at[lo:hi, q], sib_in.at[lo:hi, q],
                s_send.at[part, k], s_recv.at[part, q], sibling,
            ).wait_recv()
            both = parts[lo:hi, q, mine, :] + sib_in[lo:hi, q]
            if k < inner - 1:
                out_p[k, lo:hi] = both
                sends[k].start()
            else:
                plane_in[pi, lo:hi] = both

    def sum_plane(part):
        lo, hi = bounds[part]
        for k, q in enumerate(around):
            remote(
                plane_in.at[q, lo:hi], plane_in.at[q, lo:hi],
                p_send.at[part, k], p_recv.at[part, q], sibling,
            ).wait_recv()
        for t in range(lo, hi):
            line = plane_in[0, t]
            for q in range(1, inner):
                line = line + plane_in[q, t]
            out_c[t] = line

            @pl.when(t != zo)
            def _():
                col_copy(t).start()

    def send_cores(part):
        pack(*bounds[part])
        for copy in sib_copies(part, *bounds[part]):
            copy.start()

    send_cores(0)

    def by_sample(v):
        return jnp.concatenate(
            [
                jnp.where((lane3 >= ROWS * b) & (lane3 < ROWS * (b + 1)), v, 0.0).reshape(HJ, 256)
                for b in range(GROUP)
            ],
            0,
        ).astype(BF16)

    pair_lane = lax.broadcasted_iota(jnp.int32, (1, LANES), 1)

    def own_lanes(v):
        v = v.reshape(GROUP, PAIRS, ROWS, 256)
        out = []
        for b in range(GROUP):
            lo = jnp.where(pair_lane < PAIR_DIM, v[b, 0, :, 0:128], v[b, 1, :, 0:128])
            lo = jnp.where(pair_lane < 2 * PAIR_DIM, lo, v[b, 2, :, 0:128])
            hi = jnp.where(
                pair_lane < 3 * PAIR_DIM - 128, v[b, 2, :, 128:256], v[b, 3, :, 128:256]
            )
            out.append(jnp.concatenate([lo, hi], 1))
        return jnp.concatenate(out, 0)

    def probs(at):
        return psc[pl.ds(at, HJ), :].reshape(PAIRS, ROWS, 256)

    def attn_back_v(i, carry):
        @pl.when(i == 2)
        def _():
            sum_cores(0)

        r0 = pl.multiple_of(i * (LOCK2 * GROWS), 8)
        p0 = pl.multiple_of(i * (LOCK2 * HJ), 32)
        for k in range(LOCK2):
            dg = by_parity(get_rows(os_, r0 + GROWS * k, LANES).astype(BF16))
            dv = own_lanes(nn(by_sample(probs(p0 + HJ * k)), dg))
            put_rows(vs, r0 + GROWS * k, dv.astype(BF16).astype(F32))
        return carry

    lax.fori_loop(0, groups // LOCK2, attn_back_v, 0)

    def collect(refs):
        def chunk(t0, count, carry):
            at = rows_at(t0, count)
            for k, ref in refs:
                dqkv[at, 256 * k : 256 * (k + 1)] = get_tokens(ref, t0, count).astype(BF16)
            return carry

        over_token_chunks(chunk, WIDTH3, 0)

    collect([(2, vs)])
    over_tokens((acc, h, dqkv.at[:, 512:768]))
    store_square(acc[...], gflat, 576, D, tmp)
    dbv = acc[D : D + 1, :]
    send_cores(1)

    def attn_back(i, carry):
        @pl.when(i == 1)
        def _():
            sum_cores(1)

        @pl.when(i == 3)
        def _():
            sum_plane(0)

        r0 = pl.multiple_of(i * (LOCK2 * GROWS), 8)
        base0 = pl.multiple_of(i * (LOCK2 * 3 * HJ), 32)
        p0 = pl.multiple_of(i * (LOCK2 * HJ), 32)
        sets = range(LOCK2)
        qg = [by_parity(get_rows(qs, r0 + GROWS * k, LANES).astype(BF16)) for k in sets]
        dg = [by_parity(get_rows(os_, r0 + GROWS * k, LANES).astype(BF16)) for k in sets]
        dp = [squeeze(nt(vbd[pl.ds(base0 + 3 * HJ * k, 3 * HJ), :], dg[k])) for k in sets]
        p = [probs(p0 + HJ * k) for k in sets]
        t = [jnp.sum(p[k] * dp[k], 1, keepdims=True) for k in sets]
        ds = [p[k] * (dp[k] - t[k]) for k in sets]
        dst = [v.reshape(HJ, 256).T for v in ds]
        dk = [own_lanes(nn(by_sample(ds[k]), qg[k])) * scale for k in sets]
        for b in range(GROUP):
            for k in sets:
                dq = per_query(dst[k], kbd[pl.ds(base0 + HJ * (3 * k + b), HJ), :], b)
                put_rows(qs, r0 + GROWS * k + ROWS * b, (dq * scale).astype(BF16).astype(F32))
        for k in sets:
            put_rows(ks, r0 + GROWS * k, dk[k].astype(BF16).astype(F32))
        return carry

    lax.fori_loop(0, groups // LOCK2, attn_back, 0)

    collect([(0, qs), (1, ks)])
    over_tokens((acc2, h, dqkv.at[:, 0:512]))
    for k in range(2):
        store_square(acc2[:, 256 * k : 256 * (k + 1)], gflat, 288 * k, D, tmp)
    send_cores(2)

    def dense3(t0, count, carry):
        dg1, dn1 = carry
        at = rows_at(t0, count)
        dh = (
            nt(dqkv[at, 0:256], wq[...])
            + nt(dqkv[at, 256:512], wk[...])
            + nt(dqkv[at, 512:768], wv[...])
        )
        xh = xh1[at, :]
        ig = dx2s[at, :] + norm_back(dh, xh, r1[at, :], g1)
        ig_ref[:, pl.ds(pl.multiple_of(t0 * D, 128), count * D)] = join_tokens(ig, n)
        return dg1 + rows8(dh * xh), dn1 + rows8(dh)

    def hook3(i):
        @pl.when(i == 1)
        def _():
            sum_cores(2)
            sum_plane(1)

    dg1, dn1 = over_token_chunks(dense3, WIDTH3, (zero, zero), hook3)

    vecs = [
        total(dg1), total(dn1), acc2[D : D + 1, 0:256], dbv,
        dbo, total(dg2), total(dn2), total(db2),
    ]
    for k in range(4):
        a, b = vecs[2 * k], vecs[2 * k + 1]
        vec_own[3 * k : 3 * k + 1, :] = a[:, 0:128]
        vec_own[3 * k + 1 : 3 * k + 2, :] = jnp.concatenate([a[:, 128:192], b[:, 0:64]], 1)
        vec_own[3 * k + 2 : 3 * k + 3, :] = b[:, 64:192]
    vec_sends = [remote(vec_own, vec_sib, v_send.at[0], v_recv.at[0], sibling)]
    vec_sends[0].start()
    copy_ig = pltpu.make_async_copy(ig_ref, ig_hbm, io_sem.at[3])
    copy_ig.start()

    def spread(slots, at, sends, recvs, base, where):
        out = [
            remote(slots.at[at], slots.at[at], sends.at[base + k], recvs.at[base + at], dev)
            for k, dev in enumerate(where)
        ]
        for copy in out:
            copy.start()
        return out

    def collected(slots, others, sends, recvs, base):
        for k, q in enumerate(others):
            remote(
                slots.at[q], slots.at[q], sends.at[base + k], recvs.at[base + q], sibling
            ).wait_recv()
        return jnp.sum(slots[...], 0)

    remote(vec_sib, vec_sib, v_send.at[0], v_recv.at[0], sibling).wait_recv()
    vec_plane[pi] = vec_own[...] + vec_sib[...]
    vec_sends += spread(vec_plane, pi, v_send, v_recv, 1, plane)
    sum_plane(2)
    vec_col[zo] = collected(vec_plane, around, v_send, v_recv, 1)
    vec_sends += spread(vec_col, zo, v_send, v_recv, 1 + inner, column)

    col_in[zo] = out_c[zo]
    for t in along:
        remote(col_in.at[t], col_in.at[t], c_send.at[t], c_recv.at[t], sibling).wait_recv()
    line = col_in[0]
    for t in range(1, outer):
        line = line + col_in[t]
    res[mine, :] = line
    last = remote(res.at[mine], res.at[mine], f_sem.at[0], f_sem.at[1], sibling)
    last.start()
    slot = 2 * pi + core
    near = [2 * q + core for q in around] + [2 * q + 1 - core for q in around] + [2 * pi + 1 - core]
    sq_plane[slot] = rows8(line * line)
    sq_sends = spread(sq_plane, slot, n_send, n_recv, 0, plane + cross + [sibling])
    vec = collected(vec_col, along, v_send, v_recv, 1 + inner)
    vec_at[VEC_AT:USED_ROWS, :] = vec
    remote(res.at[theirs], res.at[theirs], f_sem.at[0], f_sem.at[1], sibling).wait_recv()
    own[...] = res[0:rows, :] + vec_at[pl.ds(me * rows, rows), :]
    sq_col[zo] = collected(sq_plane, near, n_send, n_recv, 0)
    sq_sends += spread(sq_col, zo, n_send, n_recv, 2 * inner, column)
    both = collected(sq_col, along, n_send, n_recv, 2 * inner) + rows8(vec * vec)
    squares[...] = jnp.broadcast_to(jnp.sum(both, keepdims=True), squares.shape)

    for copy in own_pushes + vec_sends + sq_sends + [last]:
        copy.wait_send()
    for t in range(outer):
        @pl.when(t != zo)
        def _(t=t):
            for copy in forwards(t, t * inner + pi):
                copy.wait_send()
            to_sibling(t * inner + pi).wait_send()
            col_copy(t).wait_send()

        for q in around:
            to_sibling(t * inner + q).wait_send()
    for j, (s, _, _, _) in enumerate(vec_rows):
        @pl.when(me == s)
        def _(j=j):
            for copy in vec_push(j, column, 0):
                copy.wait_send()

        @pl.when(pi == s % inner)
        def _(j=j):
            for copy in vec_push(j, plane, outer - 1):
                copy.wait_send()

    for part, (lo, hi) in enumerate(bounds):
        for copy in sib_copies(part, lo, hi) + plane_copies(part, lo, hi):
            copy.wait_send()
    copy_out.wait()
    copy_ig.wait()


def step(x, dy, shard, wide):
    outer, inner = factors(wide)
    n, rows = x.shape[0], shard.shape[0]
    toks = n * SEQ
    groups = n // GROUP
    padded = (rows + 15) // 16 * 16
    half = padded // 2
    vecs = (USED_ROWS - 1) // rows - VEC_AT // rows + 1
    vm, dma = pltpu.VMEM, pltpu.SemaphoreType.DMA
    sm = vm((2, n * ROWS + 8, LANES), F32)
    tok = vm((toks, 256), BF16)
    tile = (8, LANES)
    scratch = (
        [vm(x.shape, BF16), vm(x.shape, BF16), vm(x.shape, BF16), vm(x.shape, F32)]
        + [vm((wide * rows, LANES), F32)] * 2
        + [sm] * 4
        + [vm((groups * 3 * HJ, 256), BF16)] * 2
        + [vm((groups * HJ, 256), F32)]
        + [vm((toks, 256), F32), vm((toks, 1), F32), vm((toks, 256), F32)]
        + [tok, tok, tok, vm((toks, 2 * FF), BF16), tok]
        + [tok, tok, vm((toks, 3 * 256), BF16)]
        + [vm((256, 256), BF16)] * 4
        + [vm((256, 2 * FF), BF16), vm((FF, 256), BF16), vm((2, FF, 128), F32)]
        + [vm((HJ, 256), BF16), vm((32, 256), BF16)]
        + [vm((256, 256), F32), vm((256, 512), F32), vm((256, 256), F32)]
        + [vm((wide, padded, LANES), F32), vm((outer, inner, padded, LANES), F32)]
        + [vm((outer, inner, half, LANES), F32), vm((inner, outer, half, LANES), F32)]
        + [vm((inner - 1, outer, half, LANES), F32)]
        + [vm((outer, half, LANES), F32)] * 2
        + [vm((padded, LANES), F32)]
        + [vm((16, LANES), F32)] * 2
        + [vm((inner, 16, LANES), F32), vm((outer, 16, LANES), F32)]
        + [vm((wide * rows, LANES), F32)]
        + [vm((2 * inner, *tile), F32), vm((outer, *tile), F32)]
        + [vm((vecs, min(24, padded), LANES), F32)]
        + [dma((4,)), dma((outer - 1,)), dma((outer, inner - 1)), dma((wide,)), dma((wide,)), dma((wide,))]
        + [dma((3, inner))] * 4
        + [dma((outer,)), dma((outer,)), dma((2,))]
        + [dma((1 + inner + outer,))] * 2
        + [dma((2 * inner + outer,))] * 2
        + [dma((vecs, outer + inner - 2)), dma((vecs,))]
    )
    anywhere, vmem = pl.BlockSpec(memory_space=pl.ANY), pl.BlockSpec(memory_space=pltpu.VMEM)
    return pl.pallas_call(
        functools.partial(step_kernel, wide),
        out_shape=(
            jax.ShapeDtypeStruct(x.shape, BF16),
            jax.ShapeDtypeStruct(x.shape, F32),
            jax.ShapeDtypeStruct((rows, LANES), F32),
            jax.ShapeDtypeStruct(tile, F32),
        ),
        in_specs=[anywhere, anywhere, vmem],
        out_specs=(anywhere, anywhere, vmem, vmem),
        scratch_shapes=scratch,
        compiler_params=pltpu.CompilerParams(
            collective_id=0, has_side_effects=True, vmem_limit_bytes=60 * 2**20
        ),
        name="step",
    )(x, dy, shard)


def finish_kernel(*refs):
    big_in, small_in = refs[0:2], refs[2:7]
    big_out, norm_out, small_out = refs[7:9], refs[9], refs[10:15]
    stages, ins, norm, outs = refs[15:17], refs[17:22], refs[22], refs[23:28]
    sem_in, sem_out, sem_small = refs[28:31]
    pieces = []
    for k in range(2):
        size = big_in[k].shape[0] // PIECES
        for p in range(PIECES):
            at = pl.ds(size * p, size)
            pieces.append(
                (
                    pltpu.make_async_copy(big_in[k].at[at], stages[k].at[at], sem_in.at[k, p]),
                    pltpu.make_async_copy(stages[k].at[at], big_out[k].at[at], sem_out.at[k, p]),
                )
            )
    loads = [pltpu.make_async_copy(small_in[k], ins[k], sem_small.at[k]) for k in range(5)]
    for copy in loads:
        copy.start()
    for come, _ in pieces:
        come.start()
    for copy in loads:
        copy.wait()
    own, squares, master, first, second = ins
    clipped, new_master, new_copy, new_first, new_second = outs
    grad_norm = jnp.sqrt(squares[...])
    norm[...] = grad_norm[0:1, 0:1]
    factor = jnp.minimum(1.0, 1.0 / (grad_norm[0:1, :] + 1e-06))
    grad = own[...] * factor
    clipped[...] = grad
    one = 0.5 * first[...] + 0.5 * grad
    two = 0.5 * second[...] + 0.5 * grad * grad
    new_first[...] = one
    new_second[...] = two
    fixed = 1.0 - 0.5**STEP
    old = master[...]
    new = old - 0.05 * ((one / fixed) / (jnp.sqrt(two / fixed) + 1e-08) + 0.1 * old)
    new_master[...] = new
    new_copy[...] = new.astype(BF16)
    stores = [
        pltpu.make_async_copy(src, dst, sem_small.at[5 + k])
        for k, (src, dst) in enumerate(zip((norm, *outs), (norm_out, *small_out)))
    ]
    for copy in stores:
        copy.start()
    for come, go in pieces:
        come.wait()
        go.start()
    for copy in stores:
        copy.wait()
    for _, go in pieces:
        go.wait()


def finish(block_out, input_grad, owned, squares, master, first, second):
    anywhere, vm = pl.BlockSpec(memory_space=pl.ANY), pltpu.VMEM
    one, flat = (1, 1), owned.shape
    kinds = [(flat, F32), (flat, F32), (flat, BF16), (flat, F32), (flat, F32)]
    like = jax.ShapeDtypeStruct
    return pl.pallas_call(
        finish_kernel,
        out_shape=(
            like(block_out.shape, BF16),
            like(input_grad.shape, F32),
            like(one, F32),
            *[like(*kind) for kind in kinds],
        ),
        in_specs=[anywhere] * 7,
        out_specs=(anywhere,) * 8,
        scratch_shapes=[
            vm(block_out.shape, BF16),
            vm(input_grad.shape, F32),
            vm(flat, F32),
            vm(squares.shape, F32),
            vm(flat, F32),
            vm(flat, F32),
            vm(flat, F32),
            vm(one, F32),
            *[vm(*kind) for kind in kinds],
            pltpu.SemaphoreType.DMA((2, PIECES)),
            pltpu.SemaphoreType.DMA((2, PIECES)),
            pltpu.SemaphoreType.DMA((11,)),
        ],
        compiler_params=pltpu.CompilerParams(vmem_limit_bytes=60 * 2**20),
        name="finish",
    )(block_out, input_grad, owned, squares, master, first, second)


def on_device(inputs, cotangent, master, first, second):
    flat = lambda a: a.reshape(-1)
    tall = lambda a: a.reshape(-1, LANES)
    block_out, input_grad, owned, squares = step(
        inputs, cotangent, tall(master), lax.axis_size("wide")
    )
    block_out, input_grad, norm, clipped, new_master, new_copy, new_first, new_second = finish(
        block_out, input_grad, owned, squares, tall(master), tall(first), tall(second)
    )
    return (
        block_out,
        input_grad,
        flat(clipped),
        norm.reshape(()),
        flat(new_master),
        flat(new_copy),
        flat(new_first),
        flat(new_second),
    )


def solution(mesh):
    both, part = P(("wide", "narrow"), None), P("wide")
    return jax.shard_map(
        on_device,
        mesh=mesh,
        in_specs=(both, both, part, part, part),
        out_specs=(both, both, part, P(), part, part, part, part),
        check_vma=False,
    )
```

```python
import functools
import math

import jax
import jax.numpy as jnp
from jax import lax
from jax.experimental import pallas as pl
from jax.experimental.pallas import tpu as pltpu
from jax.sharding import PartitionSpec as P

D = 192
HEADS = 8
HEAD_DIM = 24
FF = 256
SEQ = 34
STEP = 5
ROWS = 40
GROUP = 3
GROWS = GROUP * ROWS
PAIRS = HEADS // 2
PAIR_DIM = 2 * HEAD_DIM
HJ = PAIRS * ROWS
LANES = 128
F32 = jnp.float32
BF16 = jnp.bfloat16
MATS = ((0, D), (288, D), (576, D), (864, D), (1920, FF))
W1_AT = 1152
WIDTH1, WIDTH2, WIDTH3, DW_STEPS = 4, 6, 4, 2
LOCK1, LOCK2 = 8, 4
PIECES = 1
VEC_AT = 2304
USED_ROWS = VEC_AT + 16
QK_ROWS = 576
QKV_ROWS = 864
GELU_C = math.sqrt(2.0 / math.pi)


def nn(a, b):
    return lax.dot_general(a, b, (((1,), (0,)), ((), ())), preferred_element_type=F32)


def nt(a, b):
    return lax.dot_general(a, b, (((1,), (1,)), ((), ())), preferred_element_type=F32)


def tn(a, b):
    return lax.dot_general(a, b, (((0,), (0,)), ((), ())), preferred_element_type=F32)


def low_half(v):
    lane = lax.broadcasted_iota(jnp.int32, v.shape, 1)
    return lane < 64


def load_square(flat, base, rows, tmp, out):
    half = rows // 2
    f0 = flat[pl.ds(base, half, stride=3), :]
    f1 = flat[pl.ds(base + 1, half, stride=3), :]
    f2 = flat[pl.ds(base + 2, half, stride=3), :]
    r1 = pltpu.roll(f1, 64, 1)
    r2 = pltpu.roll(f2, 64, 1)
    left = low_half(f0)
    lo, hi = tmp.at[0], tmp.at[1]
    lo[pl.ds(0, half, stride=2), :] = f0
    hi[pl.ds(0, half, stride=2), :] = jnp.where(left, f1, 0.0)
    lo[pl.ds(1, half, stride=2), :] = jnp.where(left, r1, r2)
    hi[pl.ds(1, half, stride=2), :] = jnp.where(left, r2, 0.0)
    out[0:rows, 0:128] = lo[0:rows, :].astype(BF16)
    out[0:rows, 128:256] = hi[0:rows, :].astype(BF16)
    if rows < 256:
        out[rows:256, :] = jnp.zeros((256 - rows, 256), BF16)


def store_square(val, flat, base, rows, tmp):
    half = rows // 2
    lo, hi = tmp.at[0], tmp.at[1]
    lo[0:rows, :] = val[0:rows, 0:128]
    hi[0:rows, :] = val[0:rows, 128:256]
    e0 = lo[pl.ds(0, half, stride=2), :]
    e1 = hi[pl.ds(0, half, stride=2), :]
    o0 = pltpu.roll(lo[pl.ds(1, half, stride=2), :], 64, 1)
    o1 = pltpu.roll(hi[pl.ds(1, half, stride=2), :], 64, 1)
    left = low_half(e0)
    flat[pl.ds(base, half, stride=3), :] = e0
    flat[pl.ds(base + 1, half, stride=3), :] = jnp.where(left, e1, o0)
    flat[pl.ds(base + 2, half, stride=3), :] = jnp.where(left, o0, o1)


def norm_fwd(x):
    mean = jnp.sum(x, -1, keepdims=True) * (1.0 / D)
    right = x[:, 128:256] - mean
    c = jnp.concatenate([x[:, 0:128] - mean, jnp.where(low_half(right), right, 0.0)], 1)
    var = jnp.sum(c * c, -1, keepdims=True) * (1.0 / D)
    r = lax.rsqrt(var + 1e-05)
    return c * r, r


def norm_back(d, xh, r, g):
    e = d * g
    m1 = jnp.sum(e, -1, keepdims=True) * (1.0 / D)
    m2 = jnp.sum(e * xh, -1, keepdims=True) * (1.0 / D)
    return r * (e - m1 - xh * m2)


def rows8(v):
    return jnp.sum(v.reshape(v.shape[0] // 8, 8, v.shape[1]), 0)


def split_tokens(v, count):
    zero = jnp.zeros((v.shape[0], 256 - D), v.dtype)
    return jnp.concatenate(
        [jnp.concatenate([v[:, D * t : D * (t + 1)], zero], 1) for t in range(count)], 0
    )


def join_tokens(v, n):
    return jnp.concatenate([v[n * t : n * (t + 1), 0:D] for t in range(v.shape[0] // n)], 1)


def factors(wide):
    inner = max(k for k in range(1, int(math.isqrt(wide)) + 1) if wide % k == 0)
    return wide // inner, inner


def remote(src, dst, send, recv, where):
    return pltpu.make_async_remote_copy(
        src_ref=src,
        dst_ref=dst,
        send_sem=send,
        recv_sem=recv,
        device_id=where,
        device_id_type=pl.DeviceIdType.MESH,
    )


def greet(devices):
    for dev in devices:
        pl.semaphore_signal(
            pltpu.get_barrier_semaphore(), inc=1, device_id=dev,
            device_id_type=pl.DeviceIdType.MESH,
        )


def step_kernel(
    wide,
    x_hbm, dy_hbm, shard, out_hbm, ig_hbm, own, squares,
    x_ref, dy_ref, out_ref, ig_ref, flat, gflat,
    qs, ks, vs, os_, kbd, vbd, psc, xh1, r1, dx2s, h, h2, z, dul, o_t, dal, dyt, dqkv,
    wq, wk, wv, wo, w1, w2, tmp, hm2, parity, acc, acc2, acc3,
    buf, parts, sib_in, plane_in, out_p, col_in, out_c, res, vec_own, vec_plane, vec_col,
    vec_at, sq_plane, sq_col, vec_in,
    io_sem, g_col, g_fw, g_sib, g_recv, g_recv_sib, s_send, s_recv, p_send, p_recv, c_send, c_recv,
    f_sem, v_send, v_recv, n_send, n_recv, vg_send, vg_recv,
):
    n = x_ref.shape[0]
    toks = n * SEQ
    pairs = SEQ // 2
    groups = n // GROUP
    rows = shard.shape[0]
    half = buf.shape[1] // 2
    outer, inner = factors(wide)
    me, core = lax.axis_index("wide"), lax.axis_index("narrow")
    zo, pi = me // inner, lax.rem(me, inner)
    mine = pl.ds(pl.multiple_of(core * half, 8), half)
    theirs = pl.ds(pl.multiple_of((1 - core) * half, 8), half)
    sibling = (me, 1 - core)
    around = [lax.rem(pi + k, inner) for k in range(1, inner)]
    along = [lax.rem(zo + k, outer) for k in range(1, outer)]
    plane = [(zo * inner + q, core) for q in around]
    column = [(t * inner + pi, core) for t in along]
    late = -(-QK_ROWS // (rows * inner))
    first = -(-QKV_ROWS // (rows * inner))
    bounds = ((first, outer), (late, first), (0, late))

    copies_in = [
        pltpu.make_async_copy(x_hbm, x_ref, io_sem.at[0]),
        pltpu.make_async_copy(dy_hbm, dy_ref, io_sem.at[1]),
    ]
    for copy in copies_in:
        copy.start()

    cross = [(zo * inner + q, 1 - core) for q in around]
    known = plane + cross + column + [sibling]
    greet(known)
    lane = lax.broadcasted_iota(jnp.int32, (80, 256), 1)
    row = lax.broadcasted_iota(jnp.int32, (80, 256), 0)
    for p in range(PAIRS // 2):
        lo = jnp.where(row < ROWS, PAIR_DIM * 2 * p, PAIR_DIM * (2 * p + 1))
        hm2[80 * p : 80 * (p + 1), :] = jnp.where(
            (lane >= lo) & (lane < lo + PAIR_DIM), 1.0, 0.0
        ).astype(BF16)
    head = lax.broadcasted_iota(jnp.int32, (16, 256), 1) // HEAD_DIM
    for k in range(2):
        parity[16 * k : 16 * (k + 1), :] = jnp.where(
            (lax.rem(head, 2) == k) & (head < HEADS), 1.0, 0.0
        ).astype(BF16)
    ones_lane = (lax.broadcasted_iota(jnp.int32, (toks, 64), 1) == 0).astype(F32).astype(BF16)
    for ref in (h, h2, o_t):
        ref[:, D:256] = ones_lane
    for ref in (qs, ks, vs, os_):
        ref[...] = jnp.zeros(ref.shape, F32)

    parts[...] = jnp.zeros(parts.shape, F32)
    vec_at[...] = jnp.zeros(vec_at.shape, F32)
    pl.semaphore_wait(pltpu.get_barrier_semaphore(), len(known))
    buf[me, 0:rows, :] = shard[...]
    buf[me, rows:, :] = jnp.zeros((buf.shape[1] - rows, LANES), F32)

    def push(s, send, recvs, where):
        return remote(buf.at[s, mine], buf.at[s, mine], send, recvs.at[s], where)

    def arrived(s, recvs, part):
        remote(buf.at[s, part], buf.at[s, part], g_sib.at[s], recvs.at[s], sibling).wait_recv()

    def forwards(t, s):
        return [push(s, g_fw.at[t, k], g_recv, where) for k, where in enumerate(plane)]

    vec_rows = [
        (s, max(0, VEC_AT - rows * s) // 8 * 8, max(0, VEC_AT - rows * s), min(rows, USED_ROWS - rows * s))
        for s in range(VEC_AT // rows, (USED_ROWS - 1) // rows + 1)
    ]

    def vec_push(j, where, base):
        return [
            remote(vec_in.at[j], vec_in.at[j], vg_send.at[j, base + k], vg_recv.at[j], dev)
            for k, dev in enumerate(where)
        ]

    def vec_arrived(j):
        remote(vec_in.at[j], vec_in.at[j], vg_send.at[j, 0], vg_recv.at[j], sibling).wait_recv()

    for j, (s, a0, _, end) in enumerate(vec_rows):
        @pl.when(me == s)
        def _(j=j, a0=a0, end=end):
            vec_in[j, 0 : end - a0, :] = shard[a0:end, :]
            for copy in vec_push(j, column, 0) + vec_push(j, plane, outer - 1):
                copy.start()

    own_pushes = [push(me, g_col.at[k], g_recv, where) for k, where in enumerate(column)]
    own_pushes += forwards(zo, me)
    for copy in own_pushes:
        copy.start()

    def to_sibling(s):
        return push(s, g_sib.at[s], g_recv_sib, sibling)

    def forward_level(t):
        s = t * inner + pi

        @pl.when(t != zo)
        def _():
            arrived(s, g_recv, mine)
            for copy in forwards(t, s):
                copy.start()
            to_sibling(s).start()

    def pass_level(t):
        for q in around:
            s = t * inner + q
            arrived(s, g_recv, mine)
            to_sibling(s).start()

    def whole_shard(s):
        @pl.when(s != me)
        def _():
            arrived(s, g_recv_sib, theirs)

    def unpack(s):
        flat[rows * s : rows * (s + 1), :] = buf[s, 0:rows, :]

    for j, (s, _, _, _) in enumerate(vec_rows):
        @pl.when((me != s) & (pi == s % inner))
        def _(j=j):
            vec_arrived(j)
            for copy in vec_push(j, plane, outer - 1):
                copy.start()

    for t in range(outer):
        forward_level(t)

    def tokens_of(ref, t, count):
        return split_tokens(
            ref[:, pl.ds(pl.multiple_of(t * D, 128), count * D)].astype(F32), count
        )

    def put_tokens(ref, t, val):
        for half in range(2):
            for k in range(val.shape[0] // n):
                ref.at[half][pl.ds(t + k, n, stride=ROWS), :] = val[
                    n * k : n * (k + 1), 128 * half : 128 * (half + 1)
                ]

    def get_tokens(ref, t, count):
        return jnp.concatenate(
            [
                jnp.concatenate(
                    [ref.at[half][pl.ds(t + k, n, stride=ROWS), :] for half in range(2)], 1
                )
                for k in range(count)
            ],
            0,
        )

    def over_token_chunks(body, width, carry, hook=lambda i: None):
        whole = pairs // width

        def step(i, c):
            hook(i)
            return body(i * (2 * width), 2 * width, c)

        carry = lax.fori_loop(0, whole, step, carry)
        if pairs % width:
            carry = body(whole * 2 * width, 2 * (pairs % width), carry)
        return carry

    def get_rows(ref, start, count):
        return jnp.concatenate([ref[0, pl.ds(start, count), :], ref[1, pl.ds(start, count), :]], 1)

    def put_rows(ref, start, val):
        for half in range(2):
            ref[half, pl.ds(start, val.shape[0]), :] = val[:, 128 * half : 128 * (half + 1)]

    def rows_at(t, count):
        return pl.ds(pl.multiple_of(t * n, 32), count * n)

    copies_in[0].wait()
    for j, (s, a0, begin, end) in enumerate(vec_rows):
        @pl.when(pi != s % inner)
        def _(j=j):
            vec_arrived(j)

        flat[rows * s + begin : rows * s + end, :] = vec_in[j, begin - a0 : end - a0, :]

    def vec(k):
        a = VEC_AT + 3 * (k // 2)
        zero = jnp.zeros((1, 64), F32)
        if k % 2 == 0:
            return jnp.concatenate([flat[a : a + 1, :], flat[a + 1 : a + 2, 0:64], zero], 1)
        return jnp.concatenate([flat[a + 1 : a + 2, 64:128], flat[a + 2 : a + 3, :], zero], 1)

    g1, n1, bq, bv, bo, g2, n2, b2 = [vec(k) for k in range(8)]
    b1 = jnp.concatenate([flat[VEC_AT + 12 + c : VEC_AT + 13 + c, :] for c in range(4)], 1)

    def norm1(t, count, carry):
        at = rows_at(t, count)
        xh, r = norm_fwd(tokens_of(x_ref, t, count))
        xh1[at, :] = xh
        r1[at, :] = r
        h[at, 0:D] = (xh * g1 + n1).astype(BF16)[:, 0:D]
        return carry

    over_token_chunks(norm1, WIDTH1, 0)

    def take_levels(lo, hi):
        for s in range(lo * inner, hi * inner):
            whole_shard(s)
            unpack(s)

    for t in range(late):
        pass_level(t)
    take_levels(0, late)
    for (base, count), ref in zip(MATS[0:2], (wq, wk)):
        load_square(flat, base, count, tmp, ref)

    def pass_v(i):
        @pl.when(i == 1)
        def _():
            for t in range(late, first):
                pass_level(t)

    def dense_qk(t, count, carry):
        hb = h[rows_at(t, count), :]
        put_tokens(qs, t, (nn(hb, wq[...]) + bq).astype(BF16).astype(F32))
        put_tokens(ks, t, nn(hb, wk[...]).astype(BF16).astype(F32))
        return carry

    over_token_chunks(dense_qk, WIDTH1, 0, pass_v)
    take_levels(late, first)
    load_square(flat, MATS[2][0], MATS[2][1], tmp, wv)

    def dense_v(t, count, carry):
        hb = h[rows_at(t, count), :]
        put_tokens(vs, t, (nn(hb, wv[...]) + bv).astype(BF16).astype(F32))
        return carry

    over_token_chunks(dense_v, WIDTH1, 0)

    lane3 = lax.rem(lax.broadcasted_iota(jnp.int32, (1, 256), 1), LANES)
    odd_head = lax.rem(lax.broadcasted_iota(jnp.int32, (1, 256), 1) // HEAD_DIM, 2) == 1

    def squeeze(v):
        return jnp.where(
            lane3 < ROWS, v[0:HJ], jnp.where(lane3 < 2 * ROWS, v[HJ : 2 * HJ], v[2 * HJ : 3 * HJ])
        ).reshape(PAIRS, ROWS, 256)

    def by_parity(v):
        v3 = v.reshape(8, 16, 256)
        return jnp.concatenate(
            [(v3 * parity[16 * k : 16 * (k + 1), :][None]).reshape(LANES, 256) for k in range(2)], 0
        )

    def per_query(left, right, b):
        rows2 = jnp.concatenate([left[128 * k + ROWS * b : 128 * k + ROWS * (b + 1)] for k in range(2)], 0)
        both = nn(rows2.astype(BF16), right)
        return jnp.where(odd_head, both[ROWS : 2 * ROWS], both[0:ROWS])

    jrow = lax.broadcasted_iota(jnp.int32, (1, ROWS, 256), 1)
    cexp = math.log2(math.e) / math.sqrt(HEAD_DIM)
    scale = 1.0 / math.sqrt(HEAD_DIM)

    def attn(i, carry):
        @pl.when(i == 1)
        def _():
            for t in range(first, outer):
                pass_level(t)

        r0 = pl.multiple_of(i * (LOCK1 * GROWS), 8)
        base0 = pl.multiple_of(i * (LOCK1 * 3 * HJ), 32)
        p0 = pl.multiple_of(i * (LOCK1 * HJ), 32)
        sets = range(LOCK1)
        qg = [by_parity(get_rows(qs, r0 + GROWS * k, LANES).astype(BF16)) for k in sets]
        for k in sets:
            for src, dst in ((ks, kbd), (vs, vbd)):
                for b in range(GROUP):
                    one = get_rows(src, r0 + GROWS * k + ROWS * b, ROWS)
                    two = jnp.concatenate([one, one], 0).astype(BF16)
                    for p in range(PAIRS // 2):
                        dst[pl.ds(base0 + HJ * (3 * k + b) + 80 * p, 80), :] = (
                            two * hm2[80 * p : 80 * (p + 1), :]
                        )
        st = [squeeze(nt(kbd[pl.ds(base0 + 3 * HJ * k, 3 * HJ), :], qg[k])) for k in sets]
        st = [jnp.where(jrow < SEQ, v, -1e30) for v in st]
        m = [jnp.max(v, 1, keepdims=True) for v in st]
        e = [jnp.exp2((st[k] - m[k]) * cexp) for k in sets]
        l = [1.0 / jnp.sum(v, 1, keepdims=True) for v in e]
        p = [(e[k] * l[k]).reshape(HJ, 256) for k in sets]
        for k in sets:
            psc[pl.ds(p0 + HJ * k, HJ), :] = p[k]
        pt = [v.T for v in p]
        for b in range(GROUP):
            for k in sets:
                ob = per_query(pt[k], vbd[pl.ds(base0 + HJ * (3 * k + b), HJ), :], b)
                put_rows(os_, r0 + GROWS * k + ROWS * b, ob.astype(BF16).astype(F32)[0:SEQ])
        return carry

    lax.fori_loop(0, groups // LOCK1, attn, 0)

    take_levels(first, outer)
    for (base, count), ref in zip(MATS[3:5], (wo, w2)):
        load_square(flat, base, count, tmp, ref)
    for c in range(4):
        w1[0:D, 128 * c : 128 * (c + 1)] = flat[pl.ds(W1_AT + c, D, stride=4), :].astype(BF16)
    w1[D:256, :] = jnp.zeros((256 - D, 2 * FF), BF16)
    copies_in[1].wait()

    def dense2(t0, count, carry):
        dg2, dn2, db2 = carry
        at = rows_at(t0, count)
        o = get_tokens(os_, t0, count).astype(BF16)
        o_t[at, 0:D] = o[:, 0:D]
        x2 = tokens_of(x_ref, t0, count) + (nn(o, wo[...]) + bo)
        xh, r = norm_fwd(x2)
        hb = (xh * g2 + n2).astype(BF16)
        h2[at, 0:D] = hb[:, 0:D]
        u = nn(hb, w1[...]) + b1
        gate, up = u[:, :FF], u[:, FF:]
        sq = gate * gate
        t = jnp.tanh(gate * (GELU_C + (GELU_C * 0.044715) * sq))
        half = 0.5 + 0.5 * t
        act = gate * half
        zb = (act * up).astype(BF16)
        z[at, :] = zb
        y = x2 + nn(zb, w2[...]) + b2
        out_ref[:, pl.ds(pl.multiple_of(t0 * D, 128), count * D)] = join_tokens(y, n).astype(BF16)
        dyf = tokens_of(dy_ref, t0, count)
        dyb = dyf.astype(BF16)
        dyt[at, :] = dyb
        dz = nt(dyb, w2[...])
        slope = half + gate * (0.5 - 0.5 * t * t) * (GELU_C + (3 * GELU_C * 0.044715) * sq)
        du = jnp.concatenate([(dz * up * slope).astype(BF16), (dz * act).astype(BF16)], 1)
        dul[at, :] = du
        dh = nt(du, w1[...])
        dx2 = dyf + norm_back(dh, xh, r, g2)
        dx2s[at, :] = dx2
        da = dx2.astype(BF16)
        dal[at, :] = da
        put_tokens(os_, t0, nt(da, wo[...]).astype(BF16).astype(F32))
        return dg2 + rows8(dh * xh), dn2 + rows8(dh), db2 + rows8(dyf)

    zero = jnp.zeros((8, 256), F32)
    dg2, dn2, db2 = over_token_chunks(dense2, WIDTH2, (zero, zero, zero))

    copy_out = pltpu.make_async_copy(out_ref, out_hbm, io_sem.at[2])
    copy_out.start()

    def total(v):
        return jnp.sum(v, 0, keepdims=True)

    def over_tokens(*products):
        for acc, _, _ in products:
            acc[...] = jnp.zeros(acc.shape, F32)
        size = toks // DW_STEPS

        @pl.loop(0, DW_STEPS)
        def _(i):
            at = pl.ds(pl.multiple_of(i * size, 16), size)
            for acc, a, b in products:
                acc[...] += tn(a[at, :], b[at, :])

    over_tokens((acc, z, dyt), (acc2, h2, dul), (acc3, o_t, dal))
    store_square(acc[...], gflat, 1920, FF, tmp)
    for c in range(4):
        gflat[pl.ds(W1_AT + c, D, stride=4), :] = acc2[0:D, 128 * c : 128 * (c + 1)]
        vec_own[12 + c : 13 + c, :] = acc2[D : D + 1, 128 * c : 128 * (c + 1)]
    store_square(acc3[...], gflat, 864, D, tmp)
    dbo = acc3[D : D + 1, :]

    def pack(lo, hi):
        for s in range(lo * inner, hi * inner):
            stop = min(rows * (s + 1), VEC_AT)
            if stop > rows * s:
                parts[s // inner, s % inner, 0 : stop - rows * s, :] = gflat[rows * s : stop, :]

    places = around + [pi]

    def sib_copies(part, lo, hi):
        return [
            remote(
                parts.at[lo:hi, q, theirs], sib_in.at[lo:hi, q],
                s_send.at[part, k], s_recv.at[part, q], sibling,
            )
            for k, q in enumerate(places)
        ]

    def plane_copies(part, lo, hi):
        return [
            remote(
                out_p.at[k, lo:hi], plane_in.at[pi, lo:hi],
                p_send.at[part, k], p_recv.at[part, pi], plane[k],
            )
            for k in range(inner - 1)
        ]

    def col_copy(t):
        return remote(
            out_c.at[t], col_in.at[zo], c_send.at[t], c_recv.at[zo], (t * inner + pi, core)
        )

    def sum_cores(part):
        lo, hi = bounds[part]
        sends = plane_copies(part, lo, hi)
        for k, q in enumerate(places):
            remote(
                sib_in.at[lo:hi, q], sib_in.at[lo:hi, q],
                s_send.at[part, k], s_recv.at[part, q], sibling,
            ).wait_recv()
            both = parts[lo:hi, q, mine, :] + sib_in[lo:hi, q]
            if k < inner - 1:
                out_p[k, lo:hi] = both
                sends[k].start()
            else:
                plane_in[pi, lo:hi] = both

    def sum_plane(part):
        lo, hi = bounds[part]
        for k, q in enumerate(around):
            remote(
                plane_in.at[q, lo:hi], plane_in.at[q, lo:hi],
                p_send.at[part, k], p_recv.at[part, q], sibling,
            ).wait_recv()
        for t in range(lo, hi):
            line = plane_in[0, t]
            for q in range(1, inner):
                line = line + plane_in[q, t]
            out_c[t] = line

            @pl.when(t != zo)
            def _():
                col_copy(t).start()

    def send_cores(part):
        pack(*bounds[part])
        for copy in sib_copies(part, *bounds[part]):
            copy.start()

    send_cores(0)

    def by_sample(v):
        return jnp.concatenate(
            [
                jnp.where((lane3 >= ROWS * b) & (lane3 < ROWS * (b + 1)), v, 0.0).reshape(HJ, 256)
                for b in range(GROUP)
            ],
            0,
        ).astype(BF16)

    pair_lane = lax.broadcasted_iota(jnp.int32, (1, LANES), 1)

    def own_lanes(v):
        v = v.reshape(GROUP, PAIRS, ROWS, 256)
        out = []
        for b in range(GROUP):
            lo = jnp.where(pair_lane < PAIR_DIM, v[b, 0, :, 0:128], v[b, 1, :, 0:128])
            lo = jnp.where(pair_lane < 2 * PAIR_DIM, lo, v[b, 2, :, 0:128])
            hi = jnp.where(
                pair_lane < 3 * PAIR_DIM - 128, v[b, 2, :, 128:256], v[b, 3, :, 128:256]
            )
            out.append(jnp.concatenate([lo, hi], 1))
        return jnp.concatenate(out, 0)

    def probs(at):
        return psc[pl.ds(at, HJ), :].reshape(PAIRS, ROWS, 256)

    def attn_back_v(i, carry):
        @pl.when(i == 2)
        def _():
            sum_cores(0)

        r0 = pl.multiple_of(i * (LOCK2 * GROWS), 8)
        p0 = pl.multiple_of(i * (LOCK2 * HJ), 32)
        for k in range(LOCK2):
            dg = by_parity(get_rows(os_, r0 + GROWS * k, LANES).astype(BF16))
            dv = own_lanes(nn(by_sample(probs(p0 + HJ * k)), dg))
            put_rows(vs, r0 + GROWS * k, dv.astype(BF16).astype(F32))
        return carry

    lax.fori_loop(0, groups // LOCK2, attn_back_v, 0)

    def collect(refs):
        def chunk(t0, count, carry):
            at = rows_at(t0, count)
            for k, ref in refs:
                dqkv[at, 256 * k : 256 * (k + 1)] = get_tokens(ref, t0, count).astype(BF16)
            return carry

        over_token_chunks(chunk, WIDTH3, 0)

    collect([(2, vs)])
    over_tokens((acc, h, dqkv.at[:, 512:768]))
    store_square(acc[...], gflat, 576, D, tmp)
    dbv = acc[D : D + 1, :]
    send_cores(1)

    def attn_back(i, carry):
        @pl.when(i == 1)
        def _():
            sum_cores(1)

        @pl.when(i == 3)
        def _():
            sum_plane(0)

        r0 = pl.multiple_of(i * (LOCK2 * GROWS), 8)
        base0 = pl.multiple_of(i * (LOCK2 * 3 * HJ), 32)
        p0 = pl.multiple_of(i * (LOCK2 * HJ), 32)
        sets = range(LOCK2)
        qg = [by_parity(get_rows(qs, r0 + GROWS * k, LANES).astype(BF16)) for k in sets]
        dg = [by_parity(get_rows(os_, r0 + GROWS * k, LANES).astype(BF16)) for k in sets]
        dp = [squeeze(nt(vbd[pl.ds(base0 + 3 * HJ * k, 3 * HJ), :], dg[k])) for k in sets]
        p = [probs(p0 + HJ * k) for k in sets]
        t = [jnp.sum(p[k] * dp[k], 1, keepdims=True) for k in sets]
        ds = [p[k] * (dp[k] - t[k]) for k in sets]
        dst = [v.reshape(HJ, 256).T for v in ds]
        dk = [own_lanes(nn(by_sample(ds[k]), qg[k])) * scale for k in sets]
        for b in range(GROUP):
            for k in sets:
                dq = per_query(dst[k], kbd[pl.ds(base0 + HJ * (3 * k + b), HJ), :], b)
                put_rows(qs, r0 + GROWS * k + ROWS * b, (dq * scale).astype(BF16).astype(F32))
        for k in sets:
            put_rows(ks, r0 + GROWS * k, dk[k].astype(BF16).astype(F32))
        return carry

    lax.fori_loop(0, groups // LOCK2, attn_back, 0)

    collect([(0, qs), (1, ks)])
    over_tokens((acc2, h, dqkv.at[:, 0:512]))
    for k in range(2):
        store_square(acc2[:, 256 * k : 256 * (k + 1)], gflat, 288 * k, D, tmp)
    send_cores(2)

    def dense3(t0, count, carry):
        dg1, dn1 = carry
        at = rows_at(t0, count)
        dh = (
            nt(dqkv[at, 0:256], wq[...])
            + nt(dqkv[at, 256:512], wk[...])
            + nt(dqkv[at, 512:768], wv[...])
        )
        xh = xh1[at, :]
        ig = dx2s[at, :] + norm_back(dh, xh, r1[at, :], g1)
        ig_ref[:, pl.ds(pl.multiple_of(t0 * D, 128), count * D)] = join_tokens(ig, n)
        return dg1 + rows8(dh * xh), dn1 + rows8(dh)

    def hook3(i):
        @pl.when(i == 1)
        def _():
            sum_cores(2)
            sum_plane(1)

    dg1, dn1 = over_token_chunks(dense3, WIDTH3, (zero, zero), hook3)

    vecs = [
        total(dg1), total(dn1), acc2[D : D + 1, 0:256], dbv,
        dbo, total(dg2), total(dn2), total(db2),
    ]
    for k in range(4):
        a, b = vecs[2 * k], vecs[2 * k + 1]
        vec_own[3 * k : 3 * k + 1, :] = a[:, 0:128]
        vec_own[3 * k + 1 : 3 * k + 2, :] = jnp.concatenate([a[:, 128:192], b[:, 0:64]], 1)
        vec_own[3 * k + 2 : 3 * k + 3, :] = b[:, 64:192]
    copy_ig = pltpu.make_async_copy(ig_ref, ig_hbm, io_sem.at[3])
    copy_ig.start()

    def spread(slots, at, sends, recvs, base, where):
        out = [
            remote(slots.at[at], slots.at[at], sends.at[base + k], recvs.at[base + at], dev)
            for k, dev in enumerate(where)
        ]
        for copy in out:
            copy.start()
        return out

    def collected(slots, others, sends, recvs, base):
        for k, q in enumerate(others):
            remote(
                slots.at[q], slots.at[q], sends.at[base + k], recvs.at[base + q], sibling
            ).wait_recv()
        return jnp.sum(slots[...], 0)

    slot = 2 * pi + core
    near = [2 * q + core for q in around] + [2 * q + 1 - core for q in around] + [2 * pi + 1 - core]
    disc = plane + cross + [sibling]
    vec_plane[slot] = vec_own[...]
    vec_sends = spread(vec_plane, slot, v_send, v_recv, 0, disc)
    sum_plane(2)
    vec_col[zo] = collected(vec_plane, near, v_send, v_recv, 0)
    vec_sends += spread(vec_col, zo, v_send, v_recv, 2 * inner, column)

    col_in[zo] = out_c[zo]
    for t in along:
        remote(col_in.at[t], col_in.at[t], c_send.at[t], c_recv.at[t], sibling).wait_recv()
    line = col_in[0]
    for t in range(1, outer):
        line = line + col_in[t]
    res[mine, :] = line
    last = remote(res.at[mine], res.at[mine], f_sem.at[0], f_sem.at[1], sibling)
    last.start()
    sq_plane[slot] = rows8(line * line)
    sq_sends = spread(sq_plane, slot, n_send, n_recv, 0, disc)
    vec = collected(vec_col, along, v_send, v_recv, 2 * inner)
    vec_at[VEC_AT:USED_ROWS, :] = vec
    remote(res.at[theirs], res.at[theirs], f_sem.at[0], f_sem.at[1], sibling).wait_recv()
    own[...] = res[0:rows, :] + vec_at[pl.ds(me * rows, rows), :]
    sq_col[zo] = collected(sq_plane, near, n_send, n_recv, 0)
    sq_sends += spread(sq_col, zo, n_send, n_recv, 2 * inner, column)
    both = collected(sq_col, along, n_send, n_recv, 2 * inner) + rows8(vec * vec)
    squares[...] = jnp.broadcast_to(jnp.sum(both, keepdims=True), squares.shape)

    for copy in own_pushes + vec_sends + sq_sends + [last]:
        copy.wait_send()
    for t in range(outer):
        @pl.when(t != zo)
        def _(t=t):
            for copy in forwards(t, t * inner + pi):
                copy.wait_send()
            to_sibling(t * inner + pi).wait_send()
            col_copy(t).wait_send()

        for q in around:
            to_sibling(t * inner + q).wait_send()
    for j, (s, _, _, _) in enumerate(vec_rows):
        @pl.when(me == s)
        def _(j=j):
            for copy in vec_push(j, column, 0):
                copy.wait_send()

        @pl.when(pi == s % inner)
        def _(j=j):
            for copy in vec_push(j, plane, outer - 1):
                copy.wait_send()

    for part, (lo, hi) in enumerate(bounds):
        for copy in sib_copies(part, lo, hi) + plane_copies(part, lo, hi):
            copy.wait_send()
    copy_out.wait()
    copy_ig.wait()


def step(x, dy, shard, wide):
    outer, inner = factors(wide)
    n, rows = x.shape[0], shard.shape[0]
    toks = n * SEQ
    groups = n // GROUP
    padded = (rows + 15) // 16 * 16
    half = padded // 2
    vecs = (USED_ROWS - 1) // rows - VEC_AT // rows + 1
    vm, dma = pltpu.VMEM, pltpu.SemaphoreType.DMA
    sm = vm((2, n * ROWS + 8, LANES), F32)
    tok = vm((toks, 256), BF16)
    tile = (8, LANES)
    scratch = (
        [vm(x.shape, BF16), vm(x.shape, BF16), vm(x.shape, BF16), vm(x.shape, F32)]
        + [vm((wide * rows, LANES), F32)] * 2
        + [sm] * 4
        + [vm((groups * 3 * HJ, 256), BF16)] * 2
        + [vm((groups * HJ, 256), F32)]
        + [vm((toks, 256), F32), vm((toks, 1), F32), vm((toks, 256), F32)]
        + [tok, tok, tok, vm((toks, 2 * FF), BF16), tok]
        + [tok, tok, vm((toks, 3 * 256), BF16)]
        + [vm((256, 256), BF16)] * 4
        + [vm((256, 2 * FF), BF16), vm((FF, 256), BF16), vm((2, FF, 128), F32)]
        + [vm((HJ, 256), BF16), vm((32, 256), BF16)]
        + [vm((256, 256), F32), vm((256, 512), F32), vm((256, 256), F32)]
        + [vm((wide, padded, LANES), F32), vm((outer, inner, padded, LANES), F32)]
        + [vm((outer, inner, half, LANES), F32), vm((inner, outer, half, LANES), F32)]
        + [vm((inner - 1, outer, half, LANES), F32)]
        + [vm((outer, half, LANES), F32)] * 2
        + [vm((padded, LANES), F32)]
        + [vm((16, LANES), F32), vm((2 * inner, 16, LANES), F32), vm((outer, 16, LANES), F32)]
        + [vm((wide * rows, LANES), F32)]
        + [vm((2 * inner, *tile), F32), vm((outer, *tile), F32)]
        + [vm((vecs, min(24, padded), LANES), F32)]
        + [dma((4,)), dma((outer - 1,)), dma((outer, inner - 1)), dma((wide,)), dma((wide,)), dma((wide,))]
        + [dma((3, inner))] * 4
        + [dma((outer,)), dma((outer,)), dma((2,))]
        + [dma((2 * inner + outer,))] * 4
        + [dma((vecs, outer + inner - 2)), dma((vecs,))]
    )
    anywhere, vmem = pl.BlockSpec(memory_space=pl.ANY), pl.BlockSpec(memory_space=pltpu.VMEM)
    return pl.pallas_call(
        functools.partial(step_kernel, wide),
        out_shape=(
            jax.ShapeDtypeStruct(x.shape, BF16),
            jax.ShapeDtypeStruct(x.shape, F32),
            jax.ShapeDtypeStruct((rows, LANES), F32),
            jax.ShapeDtypeStruct(tile, F32),
        ),
        in_specs=[anywhere, anywhere, vmem],
        out_specs=(anywhere, anywhere, vmem, vmem),
        scratch_shapes=scratch,
        compiler_params=pltpu.CompilerParams(
            collective_id=0, has_side_effects=True, vmem_limit_bytes=60 * 2**20
        ),
        name="step",
    )(x, dy, shard)


def finish_kernel(*refs):
    big_in, small_in = refs[0:2], refs[2:7]
    big_out, norm_out, small_out = refs[7:9], refs[9], refs[10:15]
    stages, ins, norm, outs = refs[15:17], refs[17:22], refs[22], refs[23:28]
    sem_in, sem_out, sem_small = refs[28:31]
    pieces = []
    for k in range(2):
        size = big_in[k].shape[0] // PIECES
        for p in range(PIECES):
            at = pl.ds(size * p, size)
            pieces.append(
                (
                    pltpu.make_async_copy(big_in[k].at[at], stages[k].at[at], sem_in.at[k, p]),
                    pltpu.make_async_copy(stages[k].at[at], big_out[k].at[at], sem_out.at[k, p]),
                )
            )
    loads = [pltpu.make_async_copy(small_in[k], ins[k], sem_small.at[k]) for k in range(5)]
    for copy in loads:
        copy.start()
    for come, _ in pieces:
        come.start()
    for copy in loads:
        copy.wait()
    own, squares, master, first, second = ins
    clipped, new_master, new_copy, new_first, new_second = outs
    grad_norm = jnp.sqrt(squares[...])
    norm[...] = grad_norm[0:1, 0:1]
    factor = jnp.minimum(1.0, 1.0 / (grad_norm[0:1, :] + 1e-06))
    grad = own[...] * factor
    clipped[...] = grad
    one = 0.5 * first[...] + 0.5 * grad
    two = 0.5 * second[...] + 0.5 * grad * grad
    new_first[...] = one
    new_second[...] = two
    fixed = 1.0 - 0.5**STEP
    old = master[...]
    new = old - 0.05 * ((one / fixed) / (jnp.sqrt(two / fixed) + 1e-08) + 0.1 * old)
    new_master[...] = new
    new_copy[...] = new.astype(BF16)
    stores = [
        pltpu.make_async_copy(src, dst, sem_small.at[5 + k])
        for k, (src, dst) in enumerate(zip((norm, *outs), (norm_out, *small_out)))
    ]
    for copy in stores:
        copy.start()
    for come, go in pieces:
        come.wait()
        go.start()
    for copy in stores:
        copy.wait()
    for _, go in pieces:
        go.wait()


def finish(block_out, input_grad, owned, squares, master, first, second):
    anywhere, vm = pl.BlockSpec(memory_space=pl.ANY), pltpu.VMEM
    one, flat = (1, 1), owned.shape
    kinds = [(flat, F32), (flat, F32), (flat, BF16), (flat, F32), (flat, F32)]
    like = jax.ShapeDtypeStruct
    return pl.pallas_call(
        finish_kernel,
        out_shape=(
            like(block_out.shape, BF16),
            like(input_grad.shape, F32),
            like(one, F32),
            *[like(*kind) for kind in kinds],
        ),
        in_specs=[anywhere] * 7,
        out_specs=(anywhere,) * 8,
        scratch_shapes=[
            vm(block_out.shape, BF16),
            vm(input_grad.shape, F32),
            vm(flat, F32),
            vm(squares.shape, F32),
            vm(flat, F32),
            vm(flat, F32),
            vm(flat, F32),
            vm(one, F32),
            *[vm(*kind) for kind in kinds],
            pltpu.SemaphoreType.DMA((2, PIECES)),
            pltpu.SemaphoreType.DMA((2, PIECES)),
            pltpu.SemaphoreType.DMA((11,)),
        ],
        compiler_params=pltpu.CompilerParams(vmem_limit_bytes=60 * 2**20),
        name="finish",
    )(block_out, input_grad, owned, squares, master, first, second)


def on_device(inputs, cotangent, master, first, second):
    flat = lambda a: a.reshape(-1)
    tall = lambda a: a.reshape(-1, LANES)
    block_out, input_grad, owned, squares = step(
        inputs, cotangent, tall(master), lax.axis_size("wide")
    )
    block_out, input_grad, norm, clipped, new_master, new_copy, new_first, new_second = finish(
        block_out, input_grad, owned, squares, tall(master), tall(first), tall(second)
    )
    return (
        block_out,
        input_grad,
        flat(clipped),
        norm.reshape(()),
        flat(new_master),
        flat(new_copy),
        flat(new_first),
        flat(new_second),
    )


def solution(mesh):
    both, part = P(("wide", "narrow"), None), P("wide")
    return jax.shard_map(
        on_device,
        mesh=mesh,
        in_specs=(both, both, part, part, part),
        out_specs=(both, both, part, P(), part, part, part, part),
        check_vma=False,
    )
```

```python
import functools
import math

import jax
import jax.numpy as jnp
from jax import lax
from jax.experimental import pallas as pl
from jax.experimental.pallas import tpu as pltpu
from jax.sharding import PartitionSpec as P

D = 192
HEADS = 8
HEAD_DIM = 24
FF = 256
SEQ = 34
STEP = 5
ROWS = 40
GROUP = 3
GROWS = GROUP * ROWS
PAIRS = HEADS // 2
PAIR_DIM = 2 * HEAD_DIM
HJ = PAIRS * ROWS
LANES = 128
F32 = jnp.float32
BF16 = jnp.bfloat16
MATS = ((0, D), (288, D), (576, D), (864, D), (1920, FF))
W1_AT = 1152
WIDTH1, WIDTH2, WIDTH3, DW_STEPS = 4, 6, 4, 2
LOCK1, LOCK2 = 8, 4
PIECES = 1
VEC_AT = 2304
USED_ROWS = VEC_AT + 16
QK_ROWS = 576
QKV_ROWS = 864
GELU_C = math.sqrt(2.0 / math.pi)


def nn(a, b):
    return lax.dot_general(a, b, (((1,), (0,)), ((), ())), preferred_element_type=F32)


def nt(a, b):
    return lax.dot_general(a, b, (((1,), (1,)), ((), ())), preferred_element_type=F32)


def tn(a, b):
    return lax.dot_general(a, b, (((0,), (0,)), ((), ())), preferred_element_type=F32)


def low_half(v):
    lane = lax.broadcasted_iota(jnp.int32, v.shape, 1)
    return lane < 64


def load_square(flat, base, rows, tmp, out):
    half = rows // 2
    f0 = flat[pl.ds(base, half, stride=3), :]
    f1 = flat[pl.ds(base + 1, half, stride=3), :]
    f2 = flat[pl.ds(base + 2, half, stride=3), :]
    r1 = pltpu.roll(f1, 64, 1)
    r2 = pltpu.roll(f2, 64, 1)
    left = low_half(f0)
    lo, hi = tmp.at[0], tmp.at[1]
    lo[pl.ds(0, half, stride=2), :] = f0
    hi[pl.ds(0, half, stride=2), :] = jnp.where(left, f1, 0.0)
    lo[pl.ds(1, half, stride=2), :] = jnp.where(left, r1, r2)
    hi[pl.ds(1, half, stride=2), :] = jnp.where(left, r2, 0.0)
    out[0:rows, 0:128] = lo[0:rows, :].astype(BF16)
    out[0:rows, 128:256] = hi[0:rows, :].astype(BF16)
    if rows < 256:
        out[rows:256, :] = jnp.zeros((256 - rows, 256), BF16)


def store_square(val, flat, base, rows, tmp):
    half = rows // 2
    lo, hi = tmp.at[0], tmp.at[1]
    lo[0:rows, :] = val[0:rows, 0:128]
    hi[0:rows, :] = val[0:rows, 128:256]
    e0 = lo[pl.ds(0, half, stride=2), :]
    e1 = hi[pl.ds(0, half, stride=2), :]
    o0 = pltpu.roll(lo[pl.ds(1, half, stride=2), :], 64, 1)
    o1 = pltpu.roll(hi[pl.ds(1, half, stride=2), :], 64, 1)
    left = low_half(e0)
    flat[pl.ds(base, half, stride=3), :] = e0
    flat[pl.ds(base + 1, half, stride=3), :] = jnp.where(left, e1, o0)
    flat[pl.ds(base + 2, half, stride=3), :] = jnp.where(left, o0, o1)


def norm_fwd(x):
    mean = jnp.sum(x, -1, keepdims=True) * (1.0 / D)
    right = x[:, 128:256] - mean
    c = jnp.concatenate([x[:, 0:128] - mean, jnp.where(low_half(right), right, 0.0)], 1)
    var = jnp.sum(c * c, -1, keepdims=True) * (1.0 / D)
    r = lax.rsqrt(var + 1e-05)
    return c * r, r


def norm_back(d, xh, r, g):
    e = d * g
    m1 = jnp.sum(e, -1, keepdims=True) * (1.0 / D)
    m2 = jnp.sum(e * xh, -1, keepdims=True) * (1.0 / D)
    return r * (e - m1 - xh * m2)


def rows8(v):
    return jnp.sum(v.reshape(v.shape[0] // 8, 8, v.shape[1]), 0)


def split_tokens(v, count):
    zero = jnp.zeros((v.shape[0], 256 - D), v.dtype)
    return jnp.concatenate(
        [jnp.concatenate([v[:, D * t : D * (t + 1)], zero], 1) for t in range(count)], 0
    )


def join_tokens(v, n):
    return jnp.concatenate([v[n * t : n * (t + 1), 0:D] for t in range(v.shape[0] // n)], 1)


def factors(wide):
    inner = max(k for k in range(1, int(math.isqrt(wide)) + 1) if wide % k == 0)
    return wide // inner, inner


def remote(src, dst, send, recv, where):
    return pltpu.make_async_remote_copy(
        src_ref=src,
        dst_ref=dst,
        send_sem=send,
        recv_sem=recv,
        device_id=where,
        device_id_type=pl.DeviceIdType.MESH,
    )


def greet(devices):
    for dev in devices:
        pl.semaphore_signal(
            pltpu.get_barrier_semaphore(), inc=1, device_id=dev,
            device_id_type=pl.DeviceIdType.MESH,
        )


def step_kernel(
    wide,
    x_hbm, dy_hbm, shard, out_hbm, ig_hbm, own, squares,
    x_ref, dy_ref, out_ref, ig_ref, flat, gflat,
    qs, ks, vs, os_, kbd, vbd, psc, xh1, r1, dx2s, h, h2, z, dul, o_t, dal, dyt, dqkv,
    wq, wk, wv, wo, w1, w2, tmp, hm2, parity, sample, hs, acc, acc2, acc3,
    buf, parts, sib_in, plane_in, out_p, col_in, out_c, res, vec_own, vec_plane, vec_col,
    vec_at, sq_plane, sq_col, vec_in,
    io_sem, g_col, g_fw, g_sib, g_recv, g_recv_sib, s_send, s_recv, p_send, p_recv, c_send, c_recv,
    f_sem, v_send, v_recv, n_send, n_recv, vg_send, vg_recv,
):
    n = x_ref.shape[0]
    toks = n * SEQ
    pairs = SEQ // 2
    groups = n // GROUP
    rows = shard.shape[0]
    half = buf.shape[1] // 2
    outer, inner = factors(wide)
    me, core = lax.axis_index("wide"), lax.axis_index("narrow")
    zo, pi = me // inner, lax.rem(me, inner)
    mine = pl.ds(pl.multiple_of(core * half, 8), half)
    theirs = pl.ds(pl.multiple_of((1 - core) * half, 8), half)
    sibling = (me, 1 - core)
    around = [lax.rem(pi + k, inner) for k in range(1, inner)]
    along = [lax.rem(zo + k, outer) for k in range(1, outer)]
    plane = [(zo * inner + q, core) for q in around]
    column = [(t * inner + pi, core) for t in along]
    late = -(-QK_ROWS // (rows * inner))
    first = -(-QKV_ROWS // (rows * inner))
    bounds = ((first, outer), (late, first), (0, late))

    copies_in = [
        pltpu.make_async_copy(x_hbm, x_ref, io_sem.at[0]),
        pltpu.make_async_copy(dy_hbm, dy_ref, io_sem.at[1]),
    ]
    for copy in copies_in:
        copy.start()

    cross = [(zo * inner + q, 1 - core) for q in around]
    known = plane + cross + column + [sibling]
    greet(known)
    lane = lax.broadcasted_iota(jnp.int32, (80, 256), 1)
    row = lax.broadcasted_iota(jnp.int32, (80, 256), 0)
    for p in range(PAIRS // 2):
        lo = jnp.where(row < ROWS, PAIR_DIM * 2 * p, PAIR_DIM * (2 * p + 1))
        hm2[80 * p : 80 * (p + 1), :] = jnp.where(
            (lane >= lo) & (lane < lo + PAIR_DIM), 1.0, 0.0
        ).astype(BF16)
    lane16 = lax.broadcasted_iota(jnp.int32, (16, 256), 1)
    for b in range(GROUP):
        query = lax.rem(lane16, LANES)
        sample[16 * b : 16 * (b + 1), :] = jnp.where(
            (query >= ROWS * b) & (query < ROWS * (b + 1)), 1.0, 0.0
        ).astype(BF16)
    head = lane16 // HEAD_DIM
    for k in range(2):
        parity[16 * k : 16 * (k + 1), :] = jnp.where(
            (lax.rem(head, 2) == k) & (head < HEADS), 1.0, 0.0
        ).astype(BF16)
    ones_lane = (lax.broadcasted_iota(jnp.int32, (toks, 64), 1) == 0).astype(F32).astype(BF16)
    o_t[:, D:256] = ones_lane
    for ref in (qs, ks, vs, os_):
        ref[...] = jnp.zeros(ref.shape, F32)

    parts[...] = jnp.zeros(parts.shape, F32)
    vec_at[...] = jnp.zeros(vec_at.shape, F32)
    pl.semaphore_wait(pltpu.get_barrier_semaphore(), len(known))
    buf[me, 0:rows, :] = shard[...]
    buf[me, rows:, :] = jnp.zeros((buf.shape[1] - rows, LANES), F32)

    def push(s, send, recvs, where):
        return remote(buf.at[s, mine], buf.at[s, mine], send, recvs.at[s], where)

    def arrived(s, recvs, part):
        remote(buf.at[s, part], buf.at[s, part], g_sib.at[s], recvs.at[s], sibling).wait_recv()

    def forwards(t, s):
        return [push(s, g_fw.at[t, k], g_recv, where) for k, where in enumerate(plane)]

    vec_rows = [
        (s, max(0, VEC_AT - rows * s) // 8 * 8, max(0, VEC_AT - rows * s), min(rows, USED_ROWS - rows * s))
        for s in range(VEC_AT // rows, (USED_ROWS - 1) // rows + 1)
    ]

    def vec_push(j, where, base):
        return [
            remote(vec_in.at[j], vec_in.at[j], vg_send.at[j, base + k], vg_recv.at[j], dev)
            for k, dev in enumerate(where)
        ]

    def vec_arrived(j):
        remote(vec_in.at[j], vec_in.at[j], vg_send.at[j, 0], vg_recv.at[j], sibling).wait_recv()

    for j, (s, a0, _, end) in enumerate(vec_rows):
        @pl.when(me == s)
        def _(j=j, a0=a0, end=end):
            vec_in[j, 0 : end - a0, :] = shard[a0:end, :]
            for copy in vec_push(j, column, 0) + vec_push(j, plane, outer - 1):
                copy.start()

    own_pushes = [push(me, g_col.at[k], g_recv, where) for k, where in enumerate(column)]
    own_pushes += forwards(zo, me)
    for copy in own_pushes:
        copy.start()

    def to_sibling(s):
        return push(s, g_sib.at[s], g_recv_sib, sibling)

    def forward_level(t):
        s = t * inner + pi

        @pl.when(t != zo)
        def _():
            arrived(s, g_recv, mine)
            for copy in forwards(t, s):
                copy.start()
            to_sibling(s).start()

    def pass_level(t):
        for q in around:
            s = t * inner + q
            arrived(s, g_recv, mine)
            to_sibling(s).start()

    def whole_shard(s):
        @pl.when(s != me)
        def _():
            arrived(s, g_recv_sib, theirs)

    def unpack(s):
        flat[rows * s : rows * (s + 1), :] = buf[s, 0:rows, :]

    for j, (s, _, _, _) in enumerate(vec_rows):
        @pl.when((me != s) & (pi == s % inner))
        def _(j=j):
            vec_arrived(j)
            for copy in vec_push(j, plane, outer - 1):
                copy.start()

    for t in range(outer):
        forward_level(t)

    def tokens_of(ref, t, count):
        return split_tokens(
            ref[:, pl.ds(pl.multiple_of(t * D, 128), count * D)].astype(F32), count
        )

    def put_tokens(ref, t, val):
        for half in range(2):
            for k in range(val.shape[0] // n):
                ref.at[half][pl.ds(t + k, n, stride=ROWS), :] = val[
                    n * k : n * (k + 1), 128 * half : 128 * (half + 1)
                ]

    def get_tokens(ref, t, count):
        return jnp.concatenate(
            [
                jnp.concatenate(
                    [ref.at[half][pl.ds(t + k, n, stride=ROWS), :] for half in range(2)], 1
                )
                for k in range(count)
            ],
            0,
        )

    def over_token_chunks(body, width, carry, hook=lambda i: None):
        whole = pairs // width

        def step(i, c):
            hook(i)
            return body(i * (2 * width), 2 * width, c)

        carry = lax.fori_loop(0, whole, step, carry)
        if pairs % width:
            carry = body(whole * 2 * width, 2 * (pairs % width), carry)
        return carry

    def get_rows(ref, start, count):
        return jnp.concatenate([ref[0, pl.ds(start, count), :], ref[1, pl.ds(start, count), :]], 1)

    def put_rows(ref, start, val):
        for half in range(2):
            ref[half, pl.ds(start, val.shape[0]), :] = val[:, 128 * half : 128 * (half + 1)]

    def rows_at(t, count):
        return pl.ds(pl.multiple_of(t * n, 32), count * n)

    copies_in[0].wait()
    for j, (s, a0, begin, end) in enumerate(vec_rows):
        @pl.when(pi != s % inner)
        def _(j=j):
            vec_arrived(j)

        flat[rows * s + begin : rows * s + end, :] = vec_in[j, begin - a0 : end - a0, :]

    ones3 = (lax.broadcasted_iota(jnp.int32, (1, 64), 1) < 3).astype(F32)

    def vec(k):
        a = VEC_AT + 3 * (k // 2)
        zero = ones3 if k in (1, 6) else jnp.zeros((1, 64), F32)
        if k % 2 == 0:
            return jnp.concatenate([flat[a : a + 1, :], flat[a + 1 : a + 2, 0:64], zero], 1)
        return jnp.concatenate([flat[a + 1 : a + 2, 64:128], flat[a + 2 : a + 3, :], zero], 1)

    g1, n1, bq, bv, bo, g2, n2, b2 = [vec(k) for k in range(8)]
    b1 = jnp.concatenate([flat[VEC_AT + 12 + c : VEC_AT + 13 + c, :] for c in range(4)], 1)

    def norm1(t, count, carry):
        at = rows_at(t, count)
        xh, r = norm_fwd(tokens_of(x_ref, t, count))
        xh1[at, :] = xh
        r1[at, :] = r
        hb = (xh * g1 + n1).astype(BF16)
        h[at, :] = hb
        put_tokens(os_, t, hb.astype(F32))
        return carry

    over_token_chunks(norm1, WIDTH1, 0)

    def bias_rows(b):
        row = lax.broadcasted_iota(jnp.int32, (16, b.shape[1]), 0)
        out = jnp.zeros((16, b.shape[1]), F32)
        for k in range(3):
            part = b.astype(BF16).astype(F32)
            out = jnp.where(row == k, part, out)
            b = b - part
        return out.astype(BF16)

    half_groups = LOCK2 * GROWS

    @pl.loop(0, groups // LOCK2)
    def _(i):
        at = pl.ds(pl.multiple_of(i * half_groups, 16), half_groups)
        hs[at, :] = get_rows(os_, pl.multiple_of(i * half_groups, 8), half_groups).astype(BF16)

    def take_levels(lo, hi):
        for s in range(lo * inner, hi * inner):
            whole_shard(s)
            unpack(s)

    for t in range(late):
        pass_level(t)
    take_levels(0, late)
    for (base, count), ref in zip(MATS[0:2], (wq, wk)):
        load_square(flat, base, count, tmp, ref)
    wq[D : D + 16, :] = bias_rows(bq)

    def pass_v(i):
        @pl.when(i == 1)
        def _():
            for t in range(late, first):
                pass_level(t)

    def dense_qk(t, count, carry):
        hb = h[rows_at(t, count), :]
        put_tokens(qs, t, nn(hb, wq[...]).astype(BF16).astype(F32))
        put_tokens(ks, t, nn(hb, wk[...]).astype(BF16).astype(F32))
        return carry

    over_token_chunks(dense_qk, WIDTH1, 0, pass_v)
    take_levels(late, first)
    load_square(flat, MATS[2][0], MATS[2][1], tmp, wv)
    wv[D : D + 16, :] = bias_rows(bv)

    def dense_v(t, count, carry):
        hb = h[rows_at(t, count), :]
        put_tokens(vs, t, nn(hb, wv[...]).astype(BF16).astype(F32))
        return carry

    over_token_chunks(dense_v, WIDTH1, 0)

    lane3 = lax.rem(lax.broadcasted_iota(jnp.int32, (1, 256), 1), LANES)
    odd_head = lax.rem(lax.broadcasted_iota(jnp.int32, (1, 256), 1) // HEAD_DIM, 2) == 1

    def squeeze(v):
        return jnp.where(
            lane3 < ROWS, v[0:HJ], jnp.where(lane3 < 2 * ROWS, v[HJ : 2 * HJ], v[2 * HJ : 3 * HJ])
        ).reshape(PAIRS, ROWS, 256)

    def by_parity(v):
        v3 = v.reshape(8, 16, 256)
        return jnp.concatenate(
            [(v3 * parity[16 * k : 16 * (k + 1), :][None]).reshape(LANES, 256) for k in range(2)], 0
        )

    def per_query(left, right, b):
        rows2 = jnp.concatenate([left[128 * k + ROWS * b : 128 * k + ROWS * (b + 1)] for k in range(2)], 0)
        both = nn(rows2.astype(BF16), right)
        return jnp.where(odd_head, both[ROWS : 2 * ROWS], both[0:ROWS])

    jrow = lax.broadcasted_iota(jnp.int32, (1, ROWS - 32, 256), 1)
    cexp = math.log2(math.e) / math.sqrt(HEAD_DIM)
    scale = 1.0 / math.sqrt(HEAD_DIM)

    def attn(i, carry):
        @pl.when(i == 1)
        def _():
            for t in range(first, outer):
                pass_level(t)

        r0 = pl.multiple_of(i * (LOCK1 * GROWS), 8)
        base0 = pl.multiple_of(i * (LOCK1 * 3 * HJ), 32)
        p0 = pl.multiple_of(i * (LOCK1 * HJ), 32)
        sets = range(LOCK1)
        qg = [by_parity(get_rows(qs, r0 + GROWS * k, LANES).astype(BF16)) for k in sets]
        for k in sets:
            for src, dst in ((ks, kbd), (vs, vbd)):
                for b in range(GROUP):
                    one = get_rows(src, r0 + GROWS * k + ROWS * b, ROWS)
                    two = jnp.concatenate([one, one], 0).astype(BF16)
                    for p in range(PAIRS // 2):
                        dst[pl.ds(base0 + HJ * (3 * k + b) + 80 * p, 80), :] = (
                            two * hm2[80 * p : 80 * (p + 1), :]
                        )
        st = [squeeze(nt(kbd[pl.ds(base0 + 3 * HJ * k, 3 * HJ), :], qg[k])) for k in sets]
        st = [
            jnp.concatenate([v[:, 0:32], jnp.where(jrow < SEQ - 32, v[:, 32:ROWS], -1e30)], 1)
            for v in st
        ]
        m = [jnp.max(v, 1, keepdims=True) for v in st]
        e = [jnp.exp2((st[k] - m[k]) * cexp) for k in sets]
        l = [1.0 / jnp.sum(v, 1, keepdims=True) for v in e]
        p = [(e[k] * l[k]).reshape(HJ, 256) for k in sets]
        for k in sets:
            psc[pl.ds(p0 + HJ * k, HJ), :] = p[k]
        pt = [v.T for v in p]
        for b in range(GROUP):
            for k in sets:
                ob = per_query(pt[k], vbd[pl.ds(base0 + HJ * (3 * k + b), HJ), :], b)
                put_rows(os_, r0 + GROWS * k + ROWS * b, ob.astype(BF16).astype(F32)[0:SEQ])
        return carry

    lax.fori_loop(0, groups // LOCK1, attn, 0)

    take_levels(first, outer)
    for (base, count), ref in zip(MATS[3:5], (wo, w2)):
        load_square(flat, base, count, tmp, ref)
    for c in range(4):
        part = flat[pl.ds(W1_AT + c, D, stride=4), :]
        w1[0:D, 128 * c : 128 * (c + 1)] = (part if c < 2 else 0.5 * part).astype(BF16)
    w1[D : D + 16, :] = bias_rows(jnp.concatenate([b1[:, 0:FF], 0.5 * b1[:, FF:]], 1))
    w1[D + 16 : 256, :] = jnp.zeros((240 - D, 2 * FF), BF16)
    copies_in[1].wait()

    def dense2(t0, count, carry):
        dg2, dn2, db2 = carry
        at = rows_at(t0, count)
        o = get_tokens(os_, t0, count).astype(BF16)
        o_t[at, 0:D] = o[:, 0:D]
        x2 = tokens_of(x_ref, t0, count) + (nn(o, wo[...]) + bo)
        xh, r = norm_fwd(x2)
        hb = (xh * g2 + n2).astype(BF16)
        h2[at, :] = hb
        u = nn(hb, w1[...])
        gate, up = u[:, :FF], u[:, FF:]
        sq = gate * gate
        t = jnp.tanh(gate * (GELU_C + (GELU_C * 0.044715) * sq))
        t1 = 1.0 + t
        act = gate * t1
        zb = (act * up).astype(BF16)
        z[at, :] = zb
        y = x2 + nn(zb, w2[...]) + b2
        out_ref[:, pl.ds(pl.multiple_of(t0 * D, 128), count * D)] = join_tokens(y, n).astype(BF16)
        dyf = tokens_of(dy_ref, t0, count)
        dyb = dyf.astype(BF16)
        dyt[at, :] = dyb
        dz = nt(dyb, w2[...])
        slope = t1 + act * (1.0 - t) * (GELU_C + (3 * GELU_C * 0.044715) * sq)
        du = jnp.concatenate([(dz * up * slope).astype(BF16), (dz * act).astype(BF16)], 1)
        dul[at, :] = du
        dh = nt(du, w1[...])
        dx2 = dyf + norm_back(dh, xh, r, g2)
        dx2s[at, :] = dx2
        da = dx2.astype(BF16)
        dal[at, :] = da
        put_tokens(os_, t0, nt(da, wo[...]).astype(BF16).astype(F32))
        return dg2 + rows8(dh * xh), dn2 + rows8(dh), db2 + rows8(dyf)

    zero = jnp.zeros((8, 256), F32)
    dg2, dn2, db2 = over_token_chunks(dense2, WIDTH2, (zero, zero, zero))

    copy_out = pltpu.make_async_copy(out_ref, out_hbm, io_sem.at[2])
    copy_out.start()

    def total(v):
        return jnp.sum(v, 0, keepdims=True)

    def over_tokens(*products):
        for acc, _, _ in products:
            acc[...] = jnp.zeros(acc.shape, F32)
        size = products[0][1].shape[0] // DW_STEPS

        @pl.loop(0, DW_STEPS)
        def _(i):
            at = pl.ds(pl.multiple_of(i * size, 16), size)
            for acc, a, b in products:
                acc[...] += tn(a[at, :], b[at, :])

    over_tokens((acc, z, dyt), (acc2, h2, dul), (acc3, o_t, dal))
    store_square(acc[...], gflat, 1920, FF, tmp)
    for c in range(4):
        part = acc2[0 : D + 8, 128 * c : 128 * (c + 1)]
        part = part if c < 2 else 0.5 * part
        gflat[pl.ds(W1_AT + c, D, stride=4), :] = part[0:D]
        vec_own[12 + c : 13 + c, :] = part[D : D + 1]
    store_square(acc3[...], gflat, 864, D, tmp)
    dbo = acc3[D : D + 1, :]

    def pack(lo, hi):
        for s in range(lo * inner, hi * inner):
            stop = min(rows * (s + 1), VEC_AT)
            if stop > rows * s:
                parts[s // inner, s % inner, 0 : stop - rows * s, :] = gflat[rows * s : stop, :]

    places = around + [pi]

    def sib_copies(part, lo, hi):
        return [
            remote(
                parts.at[lo:hi, q, theirs], sib_in.at[lo:hi, q],
                s_send.at[part, k], s_recv.at[part, q], sibling,
            )
            for k, q in enumerate(places)
        ]

    def plane_copies(part, lo, hi):
        return [
            remote(
                out_p.at[k, lo:hi], plane_in.at[pi, lo:hi],
                p_send.at[part, k], p_recv.at[part, pi], plane[k],
            )
            for k in range(inner - 1)
        ]

    def col_copy(t):
        return remote(
            out_c.at[t], col_in.at[zo], c_send.at[t], c_recv.at[zo], (t * inner + pi, core)
        )

    def sum_cores(part):
        lo, hi = bounds[part]
        sends = plane_copies(part, lo, hi)
        for k, q in enumerate(places):
            remote(
                sib_in.at[lo:hi, q], sib_in.at[lo:hi, q],
                s_send.at[part, k], s_recv.at[part, q], sibling,
            ).wait_recv()
            both = parts[lo:hi, q, mine, :] + sib_in[lo:hi, q]
            if k < inner - 1:
                out_p[k, lo:hi] = both
                sends[k].start()
            else:
                plane_in[pi, lo:hi] = both

    def sum_plane(part):
        lo, hi = bounds[part]
        for k, q in enumerate(around):
            remote(
                plane_in.at[q, lo:hi], plane_in.at[q, lo:hi],
                p_send.at[part, k], p_recv.at[part, q], sibling,
            ).wait_recv()
        for t in range(lo, hi):
            line = plane_in[0, t]
            for q in range(1, inner):
                line = line + plane_in[q, t]
            out_c[t] = line

            @pl.when(t != zo)
            def _():
                col_copy(t).start()

    def send_cores(part):
        pack(*bounds[part])
        for copy in sib_copies(part, *bounds[part]):
            copy.start()

    send_cores(0)

    def by_sample(v):
        v = v.reshape(HJ, 256).astype(BF16).reshape(HJ // 16, 16, 256)
        return jnp.concatenate(
            [
                (v * sample[16 * b : 16 * (b + 1), :][None]).reshape(HJ, 256)
                for b in range(GROUP)
            ],
            0,
        )

    pair_lane = lax.broadcasted_iota(jnp.int32, (1, LANES), 1)

    def own_lanes(v):
        v = v.reshape(GROUP, PAIRS, ROWS, 256)
        out = []
        for b in range(GROUP):
            lo = jnp.where(pair_lane < PAIR_DIM, v[b, 0, :, 0:128], v[b, 1, :, 0:128])
            lo = jnp.where(pair_lane < 2 * PAIR_DIM, lo, v[b, 2, :, 0:128])
            hi = jnp.where(
                pair_lane < 3 * PAIR_DIM - 128, v[b, 2, :, 128:256], v[b, 3, :, 128:256]
            )
            out.append(jnp.concatenate([lo, hi], 1))
        return jnp.concatenate(out, 0)

    def probs(at):
        return psc[pl.ds(at, HJ), :].reshape(PAIRS, ROWS, 256)

    def attn_back_v(i, carry):
        @pl.when(i == 2)
        def _():
            sum_cores(0)

        r0 = pl.multiple_of(i * (LOCK2 * GROWS), 8)
        p0 = pl.multiple_of(i * (LOCK2 * HJ), 32)
        out = []
        for k in range(LOCK2):
            dg = by_parity(get_rows(os_, r0 + GROWS * k, LANES).astype(BF16))
            out.append(own_lanes(nn(by_sample(probs(p0 + HJ * k)), dg)))
        out = jnp.concatenate(out, 0).astype(BF16)
        dqkv[pl.ds(pl.multiple_of(i * half_groups, 16), half_groups), 512:768] = out
        put_rows(vs, r0, out.astype(F32))
        return carry

    lax.fori_loop(0, groups // LOCK2, attn_back_v, 0)

    over_tokens((acc, hs, dqkv.at[:, 512:768]))
    store_square(acc[...], gflat, 576, D, tmp)
    dbv = acc[D : D + 1, :]
    send_cores(1)

    def attn_back(i, carry):
        @pl.when(i == 1)
        def _():
            sum_cores(1)

        @pl.when(i == 3)
        def _():
            sum_plane(0)

        r0 = pl.multiple_of(i * (LOCK2 * GROWS), 8)
        base0 = pl.multiple_of(i * (LOCK2 * 3 * HJ), 32)
        p0 = pl.multiple_of(i * (LOCK2 * HJ), 32)
        sets = range(LOCK2)
        qg = [by_parity(get_rows(qs, r0 + GROWS * k, LANES).astype(BF16)) for k in sets]
        dg = [by_parity(get_rows(os_, r0 + GROWS * k, LANES).astype(BF16)) for k in sets]
        dp = [squeeze(nt(vbd[pl.ds(base0 + 3 * HJ * k, 3 * HJ), :], dg[k])) for k in sets]
        p = [probs(p0 + HJ * k) for k in sets]
        t = [jnp.sum(p[k] * dp[k], 1, keepdims=True) for k in sets]
        ds = [p[k] * (dp[k] - t[k]) for k in sets]
        dst = [v.reshape(HJ, 256).T for v in ds]
        dk = [own_lanes(nn(by_sample(ds[k]), qg[k])) * scale for k in sets]
        dq = [
            per_query(dst[k], kbd[pl.ds(base0 + HJ * (3 * k + b), HJ), :], b) * scale
            for k in sets
            for b in range(GROUP)
        ]
        at = pl.ds(pl.multiple_of(i * half_groups, 16), half_groups)
        for col, ref, val in ((0, qs, dq), (256, ks, dk)):
            val = jnp.concatenate(val, 0).astype(BF16)
            dqkv[at, col : col + 256] = val
            put_rows(ref, r0, val.astype(F32))
        return carry

    lax.fori_loop(0, groups // LOCK2, attn_back, 0)

    over_tokens((acc2, hs, dqkv.at[:, 0:512]))
    for k in range(2):
        store_square(acc2[:, 256 * k : 256 * (k + 1)], gflat, 288 * k, D, tmp)
    send_cores(2)

    def dense3(t0, count, carry):
        dg1, dn1 = carry
        at = rows_at(t0, count)
        dh = (
            nt(get_tokens(qs, t0, count).astype(BF16), wq[...])
            + nt(get_tokens(ks, t0, count).astype(BF16), wk[...])
            + nt(get_tokens(vs, t0, count).astype(BF16), wv[...])
        )
        xh = xh1[at, :]
        ig = dx2s[at, :] + norm_back(dh, xh, r1[at, :], g1)
        ig_ref[:, pl.ds(pl.multiple_of(t0 * D, 128), count * D)] = join_tokens(ig, n)
        return dg1 + rows8(dh * xh), dn1 + rows8(dh)

    def hook3(i):
        @pl.when(i == 1)
        def _():
            sum_cores(2)
            sum_plane(1)

    dg1, dn1 = over_token_chunks(dense3, WIDTH3, (zero, zero), hook3)

    vecs = [
        total(dg1), total(dn1), acc2[D : D + 1, 0:256], dbv,
        dbo, total(dg2), total(dn2), total(db2),
    ]
    for k in range(4):
        a, b = vecs[2 * k], vecs[2 * k + 1]
        vec_own[3 * k : 3 * k + 1, :] = a[:, 0:128]
        vec_own[3 * k + 1 : 3 * k + 2, :] = jnp.concatenate([a[:, 128:192], b[:, 0:64]], 1)
        vec_own[3 * k + 2 : 3 * k + 3, :] = b[:, 64:192]
    copy_ig = pltpu.make_async_copy(ig_ref, ig_hbm, io_sem.at[3])
    copy_ig.start()

    def spread(slots, at, sends, recvs, base, where):
        out = [
            remote(slots.at[at], slots.at[at], sends.at[base + k], recvs.at[base + at], dev)
            for k, dev in enumerate(where)
        ]
        for copy in out:
            copy.start()
        return out

    def collected(slots, others, sends, recvs, base):
        for k, q in enumerate(others):
            remote(
                slots.at[q], slots.at[q], sends.at[base + k], recvs.at[base + q], sibling
            ).wait_recv()
        return jnp.sum(slots[...], 0)

    slot = 2 * pi + core
    near = [2 * q + core for q in around] + [2 * q + 1 - core for q in around] + [2 * pi + 1 - core]
    disc = plane + cross + [sibling]
    vec_plane[slot] = vec_own[...]
    vec_sends = spread(vec_plane, slot, v_send, v_recv, 0, disc)
    sum_plane(2)
    vec_col[zo] = collected(vec_plane, near, v_send, v_recv, 0)
    vec_sends += spread(vec_col, zo, v_send, v_recv, 2 * inner, column)

    col_in[zo] = out_c[zo]
    for t in along:
        remote(col_in.at[t], col_in.at[t], c_send.at[t], c_recv.at[t], sibling).wait_recv()
    line = col_in[0]
    for t in range(1, outer):
        line = line + col_in[t]
    res[mine, :] = line
    last = remote(res.at[mine], res.at[mine], f_sem.at[0], f_sem.at[1], sibling)
    last.start()
    sq_plane[slot] = rows8(line * line)
    sq_sends = spread(sq_plane, slot, n_send, n_recv, 0, disc)
    vec = collected(vec_col, along, v_send, v_recv, 2 * inner)
    vec_at[VEC_AT:USED_ROWS, :] = vec
    remote(res.at[theirs], res.at[theirs], f_sem.at[0], f_sem.at[1], sibling).wait_recv()
    own[...] = res[0:rows, :] + vec_at[pl.ds(me * rows, rows), :]
    sq_col[zo] = collected(sq_plane, near, n_send, n_recv, 0)
    sq_sends += spread(sq_col, zo, n_send, n_recv, 2 * inner, column)
    both = collected(sq_col, along, n_send, n_recv, 2 * inner) + rows8(vec * vec)
    squares[...] = jnp.broadcast_to(jnp.sum(both, keepdims=True), squares.shape)

    for copy in own_pushes + vec_sends + sq_sends + [last]:
        copy.wait_send()
    for t in range(outer):
        @pl.when(t != zo)
        def _(t=t):
            for copy in forwards(t, t * inner + pi):
                copy.wait_send()
            to_sibling(t * inner + pi).wait_send()
            col_copy(t).wait_send()

        for q in around:
            to_sibling(t * inner + q).wait_send()
    for j, (s, _, _, _) in enumerate(vec_rows):
        @pl.when(me == s)
        def _(j=j):
            for copy in vec_push(j, column, 0):
                copy.wait_send()

        @pl.when(pi == s % inner)
        def _(j=j):
            for copy in vec_push(j, plane, outer - 1):
                copy.wait_send()

    for part, (lo, hi) in enumerate(bounds):
        for copy in sib_copies(part, lo, hi) + plane_copies(part, lo, hi):
            copy.wait_send()
    copy_out.wait()
    copy_ig.wait()


def step(x, dy, shard, wide):
    outer, inner = factors(wide)
    n, rows = x.shape[0], shard.shape[0]
    toks = n * SEQ
    groups = n // GROUP
    padded = (rows + 15) // 16 * 16
    half = padded // 2
    vecs = (USED_ROWS - 1) // rows - VEC_AT // rows + 1
    vm, dma = pltpu.VMEM, pltpu.SemaphoreType.DMA
    sm = vm((2, n * ROWS + 8, LANES), F32)
    tok = vm((toks, 256), BF16)
    tile = (8, LANES)
    scratch = (
        [vm(x.shape, BF16), vm(x.shape, BF16), vm(x.shape, BF16), vm(x.shape, F32)]
        + [vm((wide * rows, LANES), F32)] * 2
        + [sm] * 4
        + [vm((groups * 3 * HJ, 256), BF16)] * 2
        + [vm((groups * HJ, 256), F32)]
        + [vm((toks, 256), F32), vm((toks, 1), F32), vm((toks, 256), F32)]
        + [tok, tok, tok, vm((toks, 2 * FF), BF16), tok]
        + [tok, tok, vm((n * ROWS, 3 * 256), BF16)]
        + [vm((256, 256), BF16)] * 4
        + [vm((256, 2 * FF), BF16), vm((FF, 256), BF16), vm((2, FF, 128), F32)]
        + [vm((HJ, 256), BF16), vm((32, 256), BF16), vm((16 * GROUP, 256), BF16), vm((n * ROWS, 256), BF16)]
        + [vm((256, 256), F32), vm((256, 512), F32), vm((256, 256), F32)]
        + [vm((wide, padded, LANES), F32), vm((outer, inner, padded, LANES), F32)]
        + [vm((outer, inner, half, LANES), F32), vm((inner, outer, half, LANES), F32)]
        + [vm((inner - 1, outer, half, LANES), F32)]
        + [vm((outer, half, LANES), F32)] * 2
        + [vm((padded, LANES), F32)]
        + [vm((16, LANES), F32), vm((2 * inner, 16, LANES), F32), vm((outer, 16, LANES), F32)]
        + [vm((wide * rows, LANES), F32)]
        + [vm((2 * inner, *tile), F32), vm((outer, *tile), F32)]
        + [vm((vecs, min(24, padded), LANES), F32)]
        + [dma((4,)), dma((outer - 1,)), dma((outer, inner - 1)), dma((wide,)), dma((wide,)), dma((wide,))]
        + [dma((3, inner))] * 4
        + [dma((outer,)), dma((outer,)), dma((2,))]
        + [dma((2 * inner + outer,))] * 4
        + [dma((vecs, outer + inner - 2)), dma((vecs,))]
    )
    anywhere, vmem = pl.BlockSpec(memory_space=pl.ANY), pl.BlockSpec(memory_space=pltpu.VMEM)
    return pl.pallas_call(
        functools.partial(step_kernel, wide),
        out_shape=(
            jax.ShapeDtypeStruct(x.shape, BF16),
            jax.ShapeDtypeStruct(x.shape, F32),
            jax.ShapeDtypeStruct((rows, LANES), F32),
            jax.ShapeDtypeStruct(tile, F32),
        ),
        in_specs=[anywhere, anywhere, vmem],
        out_specs=(anywhere, anywhere, vmem, vmem),
        scratch_shapes=scratch,
        compiler_params=pltpu.CompilerParams(
            collective_id=0, has_side_effects=True, vmem_limit_bytes=60 * 2**20
        ),
        name="step",
    )(x, dy, shard)


def finish_kernel(*refs):
    big_in, small_in = refs[0:2], refs[2:7]
    big_out, norm_out, small_out = refs[7:9], refs[9], refs[10:15]
    stages, ins, norm, outs = refs[15:17], refs[17:22], refs[22], refs[23:28]
    sem_in, sem_out, sem_small = refs[28:31]
    pieces = []
    for k in range(2):
        size = big_in[k].shape[0] // PIECES
        for p in range(PIECES):
            at = pl.ds(size * p, size)
            pieces.append(
                (
                    pltpu.make_async_copy(big_in[k].at[at], stages[k].at[at], sem_in.at[k, p]),
                    pltpu.make_async_copy(stages[k].at[at], big_out[k].at[at], sem_out.at[k, p]),
                )
            )
    loads = [pltpu.make_async_copy(small_in[k], ins[k], sem_small.at[k]) for k in range(5)]
    for copy in loads:
        copy.start()
    for come, _ in pieces:
        come.start()
    for copy in loads:
        copy.wait()
    own, squares, master, first, second = ins
    clipped, new_master, new_copy, new_first, new_second = outs
    grad_norm = jnp.sqrt(squares[...])
    norm[...] = grad_norm[0:1, 0:1]
    factor = jnp.minimum(1.0, 1.0 / (grad_norm[0:1, :] + 1e-06))
    grad = own[...] * factor
    clipped[...] = grad
    one = 0.5 * first[...] + 0.5 * grad
    two = 0.5 * second[...] + 0.5 * grad * grad
    new_first[...] = one
    new_second[...] = two
    fixed = 1.0 - 0.5**STEP
    old = master[...]
    new = old - 0.05 * ((one / fixed) / (jnp.sqrt(two / fixed) + 1e-08) + 0.1 * old)
    new_master[...] = new
    new_copy[...] = new.astype(BF16)
    stores = [
        pltpu.make_async_copy(src, dst, sem_small.at[5 + k])
        for k, (src, dst) in enumerate(zip((norm, *outs), (norm_out, *small_out)))
    ]
    for copy in stores:
        copy.start()
    for come, go in pieces:
        come.wait()
        go.start()
    for copy in stores:
        copy.wait()
    for _, go in pieces:
        go.wait()


def finish(block_out, input_grad, owned, squares, master, first, second):
    anywhere, vm = pl.BlockSpec(memory_space=pl.ANY), pltpu.VMEM
    one, flat = (1, 1), owned.shape
    kinds = [(flat, F32), (flat, F32), (flat, BF16), (flat, F32), (flat, F32)]
    like = jax.ShapeDtypeStruct
    return pl.pallas_call(
        finish_kernel,
        out_shape=(
            like(block_out.shape, BF16),
            like(input_grad.shape, F32),
            like(one, F32),
            *[like(*kind) for kind in kinds],
        ),
        in_specs=[anywhere] * 7,
        out_specs=(anywhere,) * 8,
        scratch_shapes=[
            vm(block_out.shape, BF16),
            vm(input_grad.shape, F32),
            vm(flat, F32),
            vm(squares.shape, F32),
            vm(flat, F32),
            vm(flat, F32),
            vm(flat, F32),
            vm(one, F32),
            *[vm(*kind) for kind in kinds],
            pltpu.SemaphoreType.DMA((2, PIECES)),
            pltpu.SemaphoreType.DMA((2, PIECES)),
            pltpu.SemaphoreType.DMA((11,)),
        ],
        compiler_params=pltpu.CompilerParams(vmem_limit_bytes=60 * 2**20),
        name="finish",
    )(block_out, input_grad, owned, squares, master, first, second)


def on_device(inputs, cotangent, master, first, second):
    flat = lambda a: a.reshape(-1)
    tall = lambda a: a.reshape(-1, LANES)
    block_out, input_grad, owned, squares = step(
        inputs, cotangent, tall(master), lax.axis_size("wide")
    )
    block_out, input_grad, norm, clipped, new_master, new_copy, new_first, new_second = finish(
        block_out, input_grad, owned, squares, tall(master), tall(first), tall(second)
    )
    return (
        block_out,
        input_grad,
        flat(clipped),
        norm.reshape(()),
        flat(new_master),
        flat(new_copy),
        flat(new_first),
        flat(new_second),
    )


def solution(mesh):
    both, part = P(("wide", "narrow"), None), P("wide")
    return jax.shard_map(
        on_device,
        mesh=mesh,
        in_specs=(both, both, part, part, part),
        out_specs=(both, both, part, P(), part, part, part, part),
        check_vma=False,
    )
```

```python
import functools
import math

import jax
import jax.numpy as jnp
from jax import lax
from jax.experimental import pallas as pl
from jax.experimental.pallas import tpu as pltpu
from jax.sharding import PartitionSpec as P

D = 192
HEADS = 8
HEAD_DIM = 24
FF = 256
SEQ = 34
STEP = 5
ROWS = 40
GROUP = 3
GROWS = GROUP * ROWS
PAIRS = HEADS // 2
PAIR_DIM = 2 * HEAD_DIM
HJ = PAIRS * ROWS
LANES = 128
F32 = jnp.float32
BF16 = jnp.bfloat16
MATS = ((0, D), (288, D), (576, D), (864, D), (1920, FF))
W1_AT = 1152
WIDTH1, WIDTH2, WIDTH3, DW_STEPS = 4, 6, 4, 2
LOCK1, LOCK2 = 8, 4
PIECES = 1
VEC_AT = 2304
USED_ROWS = VEC_AT + 16
QK_ROWS = 576
QKV_ROWS = 864
GELU_C = math.sqrt(2.0 / math.pi)


def nn(a, b):
    return lax.dot_general(a, b, (((1,), (0,)), ((), ())), preferred_element_type=F32)


def nt(a, b):
    return lax.dot_general(a, b, (((1,), (1,)), ((), ())), preferred_element_type=F32)


def tn(a, b):
    return lax.dot_general(a, b, (((0,), (0,)), ((), ())), preferred_element_type=F32)


def low_half(v):
    lane = lax.broadcasted_iota(jnp.int32, v.shape, 1)
    return lane < 64


def load_square(flat, base, rows, tmp, out):
    half = rows // 2
    f0 = flat[pl.ds(base, half, stride=3), :]
    f1 = flat[pl.ds(base + 1, half, stride=3), :]
    f2 = flat[pl.ds(base + 2, half, stride=3), :]
    r1 = pltpu.roll(f1, 64, 1)
    r2 = pltpu.roll(f2, 64, 1)
    left = low_half(f0)
    lo, hi = tmp.at[0], tmp.at[1]
    lo[pl.ds(0, half, stride=2), :] = f0
    hi[pl.ds(0, half, stride=2), :] = jnp.where(left, f1, 0.0)
    lo[pl.ds(1, half, stride=2), :] = jnp.where(left, r1, r2)
    hi[pl.ds(1, half, stride=2), :] = jnp.where(left, r2, 0.0)
    out[0:rows, 0:128] = lo[0:rows, :].astype(BF16)
    out[0:rows, 128:256] = hi[0:rows, :].astype(BF16)
    if rows < 256:
        out[rows:256, :] = jnp.zeros((256 - rows, 256), BF16)


def store_square(val, flat, base, rows, tmp):
    half = rows // 2
    lo, hi = tmp.at[0], tmp.at[1]
    lo[0:rows, :] = val[0:rows, 0:128]
    hi[0:rows, :] = val[0:rows, 128:256]
    e0 = lo[pl.ds(0, half, stride=2), :]
    e1 = hi[pl.ds(0, half, stride=2), :]
    o0 = pltpu.roll(lo[pl.ds(1, half, stride=2), :], 64, 1)
    o1 = pltpu.roll(hi[pl.ds(1, half, stride=2), :], 64, 1)
    left = low_half(e0)
    flat[pl.ds(base, half, stride=3), :] = e0
    flat[pl.ds(base + 1, half, stride=3), :] = jnp.where(left, e1, o0)
    flat[pl.ds(base + 2, half, stride=3), :] = jnp.where(left, o0, o1)


def norm_fwd(x):
    mean = jnp.sum(x, -1, keepdims=True) * (1.0 / D)
    right = x[:, 128:256] - mean
    c = jnp.concatenate([x[:, 0:128] - mean, jnp.where(low_half(right), right, 0.0)], 1)
    var = jnp.sum(c * c, -1, keepdims=True) * (1.0 / D)
    r = lax.rsqrt(var + 1e-05)
    return c * r, r


def norm_back(d, xh, r, g):
    e = d * g
    m1 = jnp.sum(e, -1, keepdims=True) * (1.0 / D)
    m2 = jnp.sum(e * xh, -1, keepdims=True) * (1.0 / D)
    return r * (e - m1 - xh * m2)


def rows8(v):
    return jnp.sum(v.reshape(v.shape[0] // 8, 8, v.shape[1]), 0)


def split_tokens(v, count):
    zero = jnp.zeros((v.shape[0], 256 - D), v.dtype)
    return jnp.concatenate(
        [jnp.concatenate([v[:, D * t : D * (t + 1)], zero], 1) for t in range(count)], 0
    )


def join_tokens(v, n):
    return jnp.concatenate([v[n * t : n * (t + 1), 0:D] for t in range(v.shape[0] // n)], 1)


def factors(wide):
    inner = max(k for k in range(1, int(math.isqrt(wide)) + 1) if wide % k == 0)
    return wide // inner, inner


def remote(src, dst, send, recv, where):
    return pltpu.make_async_remote_copy(
        src_ref=src,
        dst_ref=dst,
        send_sem=send,
        recv_sem=recv,
        device_id=where,
        device_id_type=pl.DeviceIdType.MESH,
    )


def greet(devices):
    for dev in devices:
        pl.semaphore_signal(
            pltpu.get_barrier_semaphore(), inc=1, device_id=dev,
            device_id_type=pl.DeviceIdType.MESH,
        )


def step_kernel(
    wide,
    x_hbm, dy_hbm, shard, out_hbm, ig_hbm, own, squares,
    x_ref, dy_ref, out_ref, ig_ref, flat, gflat,
    qs, ks, vs, os_, kbd, vbd, psc, xh1, r1, dx2s, h, h2, z, dul, o_t, dal, dyt, dqkv,
    wq, wk, wv, wo, w1, w2, tmp, hm2, parity, sample, hs, acc, acc2, acc3,
    buf, parts, sib_in, plane_in, out_p, col_in, out_c, res, vec_own, vec_plane, vec_col,
    vec_at, sq_plane, sq_col, vec_in,
    io_sem, g_col, g_fw, g_sib, g_recv, g_recv_sib, s_send, s_recv, p_send, p_recv, c_send, c_recv,
    f_sem, v_send, v_recv, n_send, n_recv, vg_send, vg_recv,
):
    n = x_ref.shape[0]
    toks = n * SEQ
    pairs = SEQ // 2
    groups = n // GROUP
    rows = shard.shape[0]
    half = buf.shape[1] // 2
    outer, inner = factors(wide)
    me, core = lax.axis_index("wide"), lax.axis_index("narrow")
    zo, pi = me // inner, lax.rem(me, inner)
    mine = pl.ds(pl.multiple_of(core * half, 8), half)
    theirs = pl.ds(pl.multiple_of((1 - core) * half, 8), half)
    sibling = (me, 1 - core)
    around = [lax.rem(pi + k, inner) for k in range(1, inner)]
    along = [lax.rem(zo + k, outer) for k in range(1, outer)]
    plane = [(zo * inner + q, core) for q in around]
    column = [(t * inner + pi, core) for t in along]
    late = -(-QK_ROWS // (rows * inner))
    first = -(-QKV_ROWS // (rows * inner))
    bounds = ((first, outer), (late, first), (0, late))

    copies_in = [
        pltpu.make_async_copy(x_hbm, x_ref, io_sem.at[0]),
        pltpu.make_async_copy(dy_hbm, dy_ref, io_sem.at[1]),
    ]
    for copy in copies_in:
        copy.start()

    cross = [(zo * inner + q, 1 - core) for q in around]
    known = plane + cross + column + [sibling]
    greet(known)
    lane = lax.broadcasted_iota(jnp.int32, (80, 256), 1)
    row = lax.broadcasted_iota(jnp.int32, (80, 256), 0)
    for p in range(PAIRS // 2):
        lo = jnp.where(row < ROWS, PAIR_DIM * 2 * p, PAIR_DIM * (2 * p + 1))
        hm2[80 * p : 80 * (p + 1), :] = jnp.where(
            (lane >= lo) & (lane < lo + PAIR_DIM), 1.0, 0.0
        ).astype(BF16)
    lane16 = lax.broadcasted_iota(jnp.int32, (16, 256), 1)
    for b in range(GROUP):
        query = lax.rem(lane16, LANES)
        sample[16 * b : 16 * (b + 1), :] = jnp.where(
            (query >= ROWS * b) & (query < ROWS * (b + 1)), 1.0, 0.0
        ).astype(BF16)
    head = lane16 // HEAD_DIM
    for k in range(2):
        parity[16 * k : 16 * (k + 1), :] = jnp.where(
            (lax.rem(head, 2) == k) & (head < HEADS), 1.0, 0.0
        ).astype(BF16)
    ones_lane = (lax.broadcasted_iota(jnp.int32, (toks, 64), 1) == 0).astype(F32).astype(BF16)
    o_t[:, D:256] = ones_lane
    for ref in (qs, ks, vs, os_):
        ref[...] = jnp.zeros(ref.shape, F32)

    parts[...] = jnp.zeros(parts.shape, F32)
    vec_at[...] = jnp.zeros(vec_at.shape, F32)
    pl.semaphore_wait(pltpu.get_barrier_semaphore(), len(known))
    buf[me, 0:rows, :] = shard[...]
    buf[me, rows:, :] = jnp.zeros((buf.shape[1] - rows, LANES), F32)

    def push(s, send, recvs, where):
        return remote(buf.at[s, mine], buf.at[s, mine], send, recvs.at[s], where)

    def arrived(s, recvs, part):
        remote(buf.at[s, part], buf.at[s, part], g_sib.at[s], recvs.at[s], sibling).wait_recv()

    def forwards(t, s):
        return [push(s, g_fw.at[t, k], g_recv, where) for k, where in enumerate(plane)]

    vec_rows = [
        (s, max(0, VEC_AT - rows * s) // 8 * 8, max(0, VEC_AT - rows * s), min(rows, USED_ROWS - rows * s))
        for s in range(VEC_AT // rows, (USED_ROWS - 1) // rows + 1)
    ]

    def vec_push(j, where, base):
        return [
            remote(vec_in.at[j], vec_in.at[j], vg_send.at[j, base + k], vg_recv.at[j], dev)
            for k, dev in enumerate(where)
        ]

    def vec_arrived(j):
        remote(vec_in.at[j], vec_in.at[j], vg_send.at[j, 0], vg_recv.at[j], sibling).wait_recv()

    for j, (s, a0, _, end) in enumerate(vec_rows):
        @pl.when(me == s)
        def _(j=j, a0=a0, end=end):
            vec_in[j, 0 : end - a0, :] = shard[a0:end, :]
            for copy in vec_push(j, column, 0) + vec_push(j, plane, outer - 1):
                copy.start()

    own_pushes = [push(me, g_col.at[k], g_recv, where) for k, where in enumerate(column)]
    own_pushes += forwards(zo, me)
    for copy in own_pushes:
        copy.start()

    def to_sibling(s):
        return push(s, g_sib.at[s], g_recv_sib, sibling)

    def forward_level(t):
        s = t * inner + pi

        @pl.when(t != zo)
        def _():
            arrived(s, g_recv, mine)
            for copy in forwards(t, s):
                copy.start()
            to_sibling(s).start()

    def pass_level(t):
        for q in around:
            s = t * inner + q
            arrived(s, g_recv, mine)
            to_sibling(s).start()

    def whole_shard(s):
        @pl.when(s != me)
        def _():
            arrived(s, g_recv_sib, theirs)

    def unpack(s):
        flat[rows * s : rows * (s + 1), :] = buf[s, 0:rows, :]

    for j, (s, _, _, _) in enumerate(vec_rows):
        @pl.when((me != s) & (pi == s % inner))
        def _(j=j):
            vec_arrived(j)
            for copy in vec_push(j, plane, outer - 1):
                copy.start()

    for t in range(outer):
        forward_level(t)

    def tokens_of(ref, t, count):
        return split_tokens(
            ref[:, pl.ds(pl.multiple_of(t * D, 128), count * D)].astype(F32), count
        )

    def put_tokens(ref, t, val):
        for half in range(2):
            for k in range(val.shape[0] // n):
                ref.at[half][pl.ds(t + k, n, stride=ROWS), :] = val[
                    n * k : n * (k + 1), 128 * half : 128 * (half + 1)
                ]

    def get_tokens(ref, t, count):
        return jnp.concatenate(
            [
                jnp.concatenate(
                    [ref.at[half][pl.ds(t + k, n, stride=ROWS), :] for half in range(2)], 1
                )
                for k in range(count)
            ],
            0,
        )

    def over_token_chunks(body, width, carry, hook=lambda i: None):
        whole = pairs // width

        def step(i, c):
            hook(i)
            return body(i * (2 * width), 2 * width, c)

        carry = lax.fori_loop(0, whole, step, carry)
        if pairs % width:
            carry = body(whole * 2 * width, 2 * (pairs % width), carry)
        return carry

    def get_rows(ref, start, count):
        return jnp.concatenate([ref[0, pl.ds(start, count), :], ref[1, pl.ds(start, count), :]], 1)

    def put_rows(ref, start, val):
        for half in range(2):
            ref[half, pl.ds(start, val.shape[0]), :] = val[:, 128 * half : 128 * (half + 1)]

    def rows_at(t, count):
        return pl.ds(pl.multiple_of(t * n, 32), count * n)

    copies_in[0].wait()
    for j, (s, a0, begin, end) in enumerate(vec_rows):
        @pl.when(pi != s % inner)
        def _(j=j):
            vec_arrived(j)

        flat[rows * s + begin : rows * s + end, :] = vec_in[j, begin - a0 : end - a0, :]

    ones3 = (lax.broadcasted_iota(jnp.int32, (1, 64), 1) < 3).astype(F32)

    def vec(k):
        a = VEC_AT + 3 * (k // 2)
        zero = ones3 if k in (1, 6) else jnp.zeros((1, 64), F32)
        if k % 2 == 0:
            return jnp.concatenate([flat[a : a + 1, :], flat[a + 1 : a + 2, 0:64], zero], 1)
        return jnp.concatenate([flat[a + 1 : a + 2, 64:128], flat[a + 2 : a + 3, :], zero], 1)

    g1, n1, bq, bv, bo, g2, n2, b2 = [vec(k) for k in range(8)]
    b1 = jnp.concatenate([flat[VEC_AT + 12 + c : VEC_AT + 13 + c, :] for c in range(4)], 1)

    def norm1(t, count, carry):
        at = rows_at(t, count)
        xh, r = norm_fwd(tokens_of(x_ref, t, count))
        xh1[at, :] = xh
        r1[at, :] = r
        hb = (xh * g1 + n1).astype(BF16)
        h[at, :] = hb
        put_tokens(os_, t, hb.astype(F32))
        return carry

    over_token_chunks(norm1, WIDTH1, 0)

    def bias_rows(b):
        row = lax.broadcasted_iota(jnp.int32, (16, b.shape[1]), 0)
        out = jnp.zeros((16, b.shape[1]), F32)
        for k in range(3):
            part = b.astype(BF16).astype(F32)
            out = jnp.where(row == k, part, out)
            b = b - part
        return out.astype(BF16)

    half_groups = LOCK2 * GROWS

    @pl.loop(0, groups // LOCK2)
    def _(i):
        at = pl.ds(pl.multiple_of(i * half_groups, 16), half_groups)
        hs[at, :] = get_rows(os_, pl.multiple_of(i * half_groups, 8), half_groups).astype(BF16)

    def take_levels(lo, hi):
        for s in range(lo * inner, hi * inner):
            whole_shard(s)
            unpack(s)

    for t in range(late):
        pass_level(t)
    take_levels(0, late)
    for (base, count), ref in zip(MATS[0:2], (wq, wk)):
        load_square(flat, base, count, tmp, ref)
    wq[D : D + 16, :] = bias_rows(bq)

    def pass_v(i):
        @pl.when(i == 1)
        def _():
            for t in range(late, first):
                pass_level(t)

    def dense_qk(t, count, carry):
        hb = h[rows_at(t, count), :]
        put_tokens(qs, t, nn(hb, wq[...]).astype(BF16).astype(F32))
        put_tokens(ks, t, nn(hb, wk[...]).astype(BF16).astype(F32))
        return carry

    over_token_chunks(dense_qk, WIDTH1, 0, pass_v)
    take_levels(late, first)
    load_square(flat, MATS[2][0], MATS[2][1], tmp, wv)
    wv[D : D + 16, :] = bias_rows(bv)

    def dense_v(t, count, carry):
        hb = h[rows_at(t, count), :]
        put_tokens(vs, t, nn(hb, wv[...]).astype(BF16).astype(F32))
        return carry

    over_token_chunks(dense_v, WIDTH1, 0)

    lane3 = lax.rem(lax.broadcasted_iota(jnp.int32, (1, 256), 1), LANES)
    odd_head = lax.rem(lax.broadcasted_iota(jnp.int32, (1, 256), 1) // HEAD_DIM, 2) == 1

    def squeeze(v):
        return jnp.where(
            lane3 < ROWS, v[0:HJ], jnp.where(lane3 < 2 * ROWS, v[HJ : 2 * HJ], v[2 * HJ : 3 * HJ])
        ).reshape(PAIRS, ROWS, 256)

    def by_parity(v):
        v3 = v.reshape(8, 16, 256)
        return jnp.concatenate(
            [(v3 * parity[16 * k : 16 * (k + 1), :][None]).reshape(LANES, 256) for k in range(2)], 0
        )

    def per_query(left, right, b):
        rows2 = jnp.concatenate([left[128 * k + ROWS * b : 128 * k + ROWS * (b + 1)] for k in range(2)], 0)
        both = nn(rows2.astype(BF16), right)
        return jnp.where(odd_head, both[ROWS : 2 * ROWS], both[0:ROWS])

    jrow = lax.broadcasted_iota(jnp.int32, (1, ROWS - 32, 256), 1)
    cexp = math.log2(math.e) / math.sqrt(HEAD_DIM)
    scale = 1.0 / math.sqrt(HEAD_DIM)

    def attn(i, carry):
        @pl.when(i == 1)
        def _():
            for t in range(first, outer):
                pass_level(t)

        r0 = pl.multiple_of(i * (LOCK1 * GROWS), 8)
        base0 = pl.multiple_of(i * (LOCK1 * 3 * HJ), 32)
        p0 = pl.multiple_of(i * (LOCK1 * HJ), 32)
        sets = range(LOCK1)
        qg = [by_parity(get_rows(qs, r0 + GROWS * k, LANES).astype(BF16)) for k in sets]
        for k in sets:
            for src, dst in ((ks, kbd), (vs, vbd)):
                for b in range(GROUP):
                    one = get_rows(src, r0 + GROWS * k + ROWS * b, ROWS)
                    two = jnp.concatenate([one, one], 0).astype(BF16)
                    for p in range(PAIRS // 2):
                        dst[pl.ds(base0 + HJ * (3 * k + b) + 80 * p, 80), :] = (
                            two * hm2[80 * p : 80 * (p + 1), :]
                        )
        st = [squeeze(nt(kbd[pl.ds(base0 + 3 * HJ * k, 3 * HJ), :], qg[k])) for k in sets]
        st = [
            jnp.concatenate([v[:, 0:32], jnp.where(jrow < SEQ - 32, v[:, 32:ROWS], -1e30)], 1)
            for v in st
        ]
        m = [jnp.max(v, 1, keepdims=True) for v in st]
        e = [jnp.exp2((st[k] - m[k]) * cexp) for k in sets]
        l = [1.0 / jnp.sum(v, 1, keepdims=True) for v in e]
        p = [(e[k] * l[k]).reshape(HJ, 256) for k in sets]
        for k in sets:
            psc[pl.ds(p0 + HJ * k, HJ), :] = p[k]
        pt = [v.T for v in p]
        for b in range(GROUP):
            for k in sets:
                ob = per_query(pt[k], vbd[pl.ds(base0 + HJ * (3 * k + b), HJ), :], b)
                put_rows(os_, r0 + GROWS * k + ROWS * b, ob.astype(BF16).astype(F32)[0:SEQ])
        return carry

    lax.fori_loop(0, groups // LOCK1, attn, 0)

    take_levels(first, outer)
    for (base, count), ref in zip(MATS[3:5], (wo, w2)):
        load_square(flat, base, count, tmp, ref)
    for c in range(4):
        part = flat[pl.ds(W1_AT + c, D, stride=4), :]
        w1[0:D, 128 * c : 128 * (c + 1)] = (part if c < 2 else 0.5 * part).astype(BF16)
    w1[D : D + 16, :] = bias_rows(jnp.concatenate([b1[:, 0:FF], 0.5 * b1[:, FF:]], 1))
    w1[D + 16 : 256, :] = jnp.zeros((240 - D, 2 * FF), BF16)
    copies_in[1].wait()

    def dense2(t0, count, carry):
        dg2, dn2, db2 = carry
        at = rows_at(t0, count)
        o = get_tokens(os_, t0, count).astype(BF16)
        o_t[at, 0:D] = o[:, 0:D]
        x2 = tokens_of(x_ref, t0, count) + (nn(o, wo[...]) + bo)
        xh, r = norm_fwd(x2)
        hb = (xh * g2 + n2).astype(BF16)
        h2[at, :] = hb
        u = nn(hb, w1[...])
        gate, up = u[:, :FF], u[:, FF:]
        sq = gate * gate
        t = jnp.tanh(gate * (GELU_C + (GELU_C * 0.044715) * sq))
        t1 = 1.0 + t
        act = gate * t1
        zb = (act * up).astype(BF16)
        z[at, :] = zb
        y = x2 + nn(zb, w2[...]) + b2
        out_ref[:, pl.ds(pl.multiple_of(t0 * D, 128), count * D)] = join_tokens(y, n).astype(BF16)
        dyf = tokens_of(dy_ref, t0, count)
        dyb = dyf.astype(BF16)
        dyt[at, :] = dyb
        dz = nt(dyb, w2[...])
        slope = t1 + act * (1.0 - t) * (GELU_C + (3 * GELU_C * 0.044715) * sq)
        du = jnp.concatenate([(dz * up * slope).astype(BF16), (dz * act).astype(BF16)], 1)
        dul[at, :] = du
        dh = nt(du, w1[...])
        dx2 = dyf + norm_back(dh, xh, r, g2)
        dx2s[at, :] = dx2
        da = dx2.astype(BF16)
        dal[at, :] = da
        put_tokens(os_, t0, nt(da, wo[...]).astype(BF16).astype(F32))
        return dg2 + rows8(dh * xh), dn2 + rows8(dh), db2 + rows8(dyf)

    zero = jnp.zeros((8, 256), F32)
    dg2, dn2, db2 = over_token_chunks(dense2, WIDTH2, (zero, zero, zero))

    copy_out = pltpu.make_async_copy(out_ref, out_hbm, io_sem.at[2])
    copy_out.start()

    def total(v):
        return jnp.sum(v, 0, keepdims=True)

    def over_tokens(*products):
        for acc, _, _ in products:
            acc[...] = jnp.zeros(acc.shape, F32)
        size = products[0][1].shape[0] // DW_STEPS

        @pl.loop(0, DW_STEPS)
        def _(i):
            at = pl.ds(pl.multiple_of(i * size, 16), size)
            for acc, a, b in products:
                acc[...] += tn(a[at, :], b[at, :])

    over_tokens((acc, z, dyt), (acc2, h2, dul), (acc3, o_t, dal))
    store_square(acc[...], gflat, 1920, FF, tmp)
    for c in range(4):
        part = acc2[0 : D + 8, 128 * c : 128 * (c + 1)]
        part = part if c < 2 else 0.5 * part
        gflat[pl.ds(W1_AT + c, D, stride=4), :] = part[0:D]
        vec_own[12 + c : 13 + c, :] = part[D : D + 1]
    store_square(acc3[...], gflat, 864, D, tmp)
    dbo = acc3[D : D + 1, :]

    def pack(lo, hi):
        for s in range(lo * inner, hi * inner):
            stop = min(rows * (s + 1), VEC_AT)
            if stop > rows * s:
                parts[s // inner, s % inner, 0 : stop - rows * s, :] = gflat[rows * s : stop, :]

    places = around + [pi]

    def sib_copies(part, lo, hi):
        return [
            remote(
                parts.at[lo:hi, q, theirs], sib_in.at[lo:hi, q],
                s_send.at[part, k], s_recv.at[part, q], sibling,
            )
            for k, q in enumerate(places)
        ]

    def plane_copies(part, lo, hi):
        return [
            remote(
                out_p.at[k, lo:hi], plane_in.at[pi, lo:hi],
                p_send.at[part, k], p_recv.at[part, pi], plane[k],
            )
            for k in range(inner - 1)
        ]

    def col_copy(t):
        return remote(
            out_c.at[t], col_in.at[zo], c_send.at[t], c_recv.at[zo], (t * inner + pi, core)
        )

    def sum_cores(part):
        lo, hi = bounds[part]
        sends = plane_copies(part, lo, hi)
        for k, q in enumerate(places):
            remote(
                sib_in.at[lo:hi, q], sib_in.at[lo:hi, q],
                s_send.at[part, k], s_recv.at[part, q], sibling,
            ).wait_recv()
            both = parts[lo:hi, q, mine, :] + sib_in[lo:hi, q]
            if k < inner - 1:
                out_p[k, lo:hi] = both
                sends[k].start()
            else:
                plane_in[pi, lo:hi] = both

    def sum_plane(part):
        lo, hi = bounds[part]
        for k, q in enumerate(around):
            remote(
                plane_in.at[q, lo:hi], plane_in.at[q, lo:hi],
                p_send.at[part, k], p_recv.at[part, q], sibling,
            ).wait_recv()
        for t in range(lo, hi):
            line = plane_in[0, t]
            for q in range(1, inner):
                line = line + plane_in[q, t]
            out_c[t] = line

            @pl.when(t != zo)
            def _():
                col_copy(t).start()

    def send_cores(part):
        pack(*bounds[part])
        for copy in sib_copies(part, *bounds[part]):
            copy.start()

    send_cores(0)

    def by_sample(v):
        v = v.reshape(HJ, 256).astype(BF16).reshape(HJ // 16, 16, 256)
        return jnp.concatenate(
            [
                (v * sample[16 * b : 16 * (b + 1), :][None]).reshape(HJ, 256)
                for b in range(GROUP)
            ],
            0,
        )

    pair_lane = lax.broadcasted_iota(jnp.int32, (1, LANES), 1)

    def own_lanes(v):
        v = v.reshape(GROUP, PAIRS, ROWS, 256)
        out = []
        for b in range(GROUP):
            lo = jnp.where(pair_lane < PAIR_DIM, v[b, 0, :, 0:128], v[b, 1, :, 0:128])
            lo = jnp.where(pair_lane < 2 * PAIR_DIM, lo, v[b, 2, :, 0:128])
            hi = jnp.where(
                pair_lane < 3 * PAIR_DIM - 128, v[b, 2, :, 128:256], v[b, 3, :, 128:256]
            )
            out.append(jnp.concatenate([lo, hi], 1))
        return jnp.concatenate(out, 0)

    def probs(at):
        return psc[pl.ds(at, HJ), :].reshape(PAIRS, ROWS, 256)

    def attn_back_v(i, carry):
        @pl.when(i == 3)
        def _():
            sum_cores(0)

        r0 = pl.multiple_of(i * (LOCK2 * GROWS), 8)
        p0 = pl.multiple_of(i * (LOCK2 * HJ), 32)
        out = []
        for k in range(LOCK2):
            dg = by_parity(get_rows(os_, r0 + GROWS * k, LANES).astype(BF16))
            out.append(own_lanes(nn(by_sample(probs(p0 + HJ * k)), dg)))
        out = jnp.concatenate(out, 0).astype(BF16)
        dqkv[pl.ds(pl.multiple_of(i * half_groups, 16), half_groups), 512:768] = out
        put_rows(vs, r0, out.astype(F32))
        return carry

    lax.fori_loop(0, groups // LOCK2, attn_back_v, 0)

    over_tokens((acc, hs, dqkv.at[:, 512:768]))
    store_square(acc[...], gflat, 576, D, tmp)
    dbv = acc[D : D + 1, :]
    send_cores(1)

    def attn_back(i, carry):
        @pl.when(i == 1)
        def _():
            sum_cores(1)

        r0 = pl.multiple_of(i * (LOCK2 * GROWS), 8)
        base0 = pl.multiple_of(i * (LOCK2 * 3 * HJ), 32)
        p0 = pl.multiple_of(i * (LOCK2 * HJ), 32)
        sets = range(LOCK2)
        qg = [by_parity(get_rows(qs, r0 + GROWS * k, LANES).astype(BF16)) for k in sets]
        dg = [by_parity(get_rows(os_, r0 + GROWS * k, LANES).astype(BF16)) for k in sets]
        dp = [squeeze(nt(vbd[pl.ds(base0 + 3 * HJ * k, 3 * HJ), :], dg[k])) for k in sets]
        p = [probs(p0 + HJ * k) for k in sets]
        t = [jnp.sum(p[k] * dp[k], 1, keepdims=True) for k in sets]
        ds = [p[k] * (dp[k] - t[k]) for k in sets]
        dst = [v.reshape(HJ, 256).T for v in ds]
        dk = [own_lanes(nn(by_sample(ds[k]), qg[k])) * scale for k in sets]
        dq = [
            per_query(dst[k], kbd[pl.ds(base0 + HJ * (3 * k + b), HJ), :], b) * scale
            for k in sets
            for b in range(GROUP)
        ]
        at = pl.ds(pl.multiple_of(i * half_groups, 16), half_groups)
        for col, ref, val in ((0, qs, dq), (256, ks, dk)):
            val = jnp.concatenate(val, 0).astype(BF16)
            dqkv[at, col : col + 256] = val
            put_rows(ref, r0, val.astype(F32))
        return carry

    lax.fori_loop(0, groups // LOCK2, attn_back, 0)

    over_tokens((acc2, hs, dqkv.at[:, 0:512]))
    for k in range(2):
        store_square(acc2[:, 256 * k : 256 * (k + 1)], gflat, 288 * k, D, tmp)
    send_cores(2)
    sum_plane(0)

    def dense3(t0, count, carry):
        dg1, dn1 = carry
        at = rows_at(t0, count)
        dh = (
            nt(get_tokens(qs, t0, count).astype(BF16), wq[...])
            + nt(get_tokens(ks, t0, count).astype(BF16), wk[...])
            + nt(get_tokens(vs, t0, count).astype(BF16), wv[...])
        )
        xh = xh1[at, :]
        ig = dx2s[at, :] + norm_back(dh, xh, r1[at, :], g1)
        ig_ref[:, pl.ds(pl.multiple_of(t0 * D, 128), count * D)] = join_tokens(ig, n)
        return dg1 + rows8(dh * xh), dn1 + rows8(dh)

    def hook3(i):
        @pl.when(i == 1)
        def _():
            sum_cores(2)
            sum_plane(1)

    dg1, dn1 = over_token_chunks(dense3, WIDTH3, (zero, zero), hook3)

    vecs = [
        total(dg1), total(dn1), acc2[D : D + 1, 0:256], dbv,
        dbo, total(dg2), total(dn2), total(db2),
    ]
    for k in range(4):
        a, b = vecs[2 * k], vecs[2 * k + 1]
        vec_own[3 * k : 3 * k + 1, :] = a[:, 0:128]
        vec_own[3 * k + 1 : 3 * k + 2, :] = jnp.concatenate([a[:, 128:192], b[:, 0:64]], 1)
        vec_own[3 * k + 2 : 3 * k + 3, :] = b[:, 64:192]
    copy_ig = pltpu.make_async_copy(ig_ref, ig_hbm, io_sem.at[3])
    copy_ig.start()

    def spread(slots, at, sends, recvs, base, where):
        out = [
            remote(slots.at[at], slots.at[at], sends.at[base + k], recvs.at[base + at], dev)
            for k, dev in enumerate(where)
        ]
        for copy in out:
            copy.start()
        return out

    def collected(slots, others, sends, recvs, base):
        for k, q in enumerate(others):
            remote(
                slots.at[q], slots.at[q], sends.at[base + k], recvs.at[base + q], sibling
            ).wait_recv()
        return jnp.sum(slots[...], 0)

    slot = 2 * pi + core
    near = [2 * q + core for q in around] + [2 * q + 1 - core for q in around] + [2 * pi + 1 - core]
    disc = plane + cross + [sibling]
    vec_plane[slot] = vec_own[...]
    vec_sends = spread(vec_plane, slot, v_send, v_recv, 0, disc)
    sum_plane(2)
    vec_col[zo] = collected(vec_plane, near, v_send, v_recv, 0)
    vec_sends += spread(vec_col, zo, v_send, v_recv, 2 * inner, column)

    col_in[zo] = out_c[zo]
    for t in along:
        remote(col_in.at[t], col_in.at[t], c_send.at[t], c_recv.at[t], sibling).wait_recv()
    line = col_in[0]
    for t in range(1, outer):
        line = line + col_in[t]
    res[mine, :] = line
    last = remote(res.at[mine], res.at[mine], f_sem.at[0], f_sem.at[1], sibling)
    last.start()
    sq_plane[slot] = rows8(line * line)
    sq_sends = spread(sq_plane, slot, n_send, n_recv, 0, disc)
    vec = collected(vec_col, along, v_send, v_recv, 2 * inner)
    vec_at[VEC_AT:USED_ROWS, :] = vec
    remote(res.at[theirs], res.at[theirs], f_sem.at[0], f_sem.at[1], sibling).wait_recv()
    own[...] = res[0:rows, :] + vec_at[pl.ds(me * rows, rows), :]
    sq_col[zo] = collected(sq_plane, near, n_send, n_recv, 0)
    sq_sends += spread(sq_col, zo, n_send, n_recv, 2 * inner, column)
    both = collected(sq_col, along, n_send, n_recv, 2 * inner) + rows8(vec * vec)
    squares[...] = jnp.broadcast_to(jnp.sum(both, keepdims=True), squares.shape)

    for copy in own_pushes + vec_sends + sq_sends + [last]:
        copy.wait_send()
    for t in range(outer):
        @pl.when(t != zo)
        def _(t=t):
            for copy in forwards(t, t * inner + pi):
                copy.wait_send()
            to_sibling(t * inner + pi).wait_send()
            col_copy(t).wait_send()

        for q in around:
            to_sibling(t * inner + q).wait_send()
    for j, (s, _, _, _) in enumerate(vec_rows):
        @pl.when(me == s)
        def _(j=j):
            for copy in vec_push(j, column, 0):
                copy.wait_send()

        @pl.when(pi == s % inner)
        def _(j=j):
            for copy in vec_push(j, plane, outer - 1):
                copy.wait_send()

    for part, (lo, hi) in enumerate(bounds):
        for copy in sib_copies(part, lo, hi) + plane_copies(part, lo, hi):
            copy.wait_send()
    copy_out.wait()
    copy_ig.wait()


def step(x, dy, shard, wide):
    outer, inner = factors(wide)
    n, rows = x.shape[0], shard.shape[0]
    toks = n * SEQ
    groups = n // GROUP
    padded = (rows + 15) // 16 * 16
    half = padded // 2
    vecs = (USED_ROWS - 1) // rows - VEC_AT // rows + 1
    vm, dma = pltpu.VMEM, pltpu.SemaphoreType.DMA
    sm = vm((2, n * ROWS + 8, LANES), F32)
    tok = vm((toks, 256), BF16)
    tile = (8, LANES)
    scratch = (
        [vm(x.shape, BF16), vm(x.shape, BF16), vm(x.shape, BF16), vm(x.shape, F32)]
        + [vm((wide * rows, LANES), F32)] * 2
        + [sm] * 4
        + [vm((groups * 3 * HJ, 256), BF16)] * 2
        + [vm((groups * HJ, 256), F32)]
        + [vm((toks, 256), F32), vm((toks, 1), F32), vm((toks, 256), F32)]
        + [tok, tok, tok, vm((toks, 2 * FF), BF16), tok]
        + [tok, tok, vm((n * ROWS, 3 * 256), BF16)]
        + [vm((256, 256), BF16)] * 4
        + [vm((256, 2 * FF), BF16), vm((FF, 256), BF16), vm((2, FF, 128), F32)]
        + [vm((HJ, 256), BF16), vm((32, 256), BF16), vm((16 * GROUP, 256), BF16), vm((n * ROWS, 256), BF16)]
        + [vm((256, 256), F32), vm((256, 512), F32), vm((256, 256), F32)]
        + [vm((wide, padded, LANES), F32), vm((outer, inner, padded, LANES), F32)]
        + [vm((outer, inner, half, LANES), F32), vm((inner, outer, half, LANES), F32)]
        + [vm((inner - 1, outer, half, LANES), F32)]
        + [vm((outer, half, LANES), F32)] * 2
        + [vm((padded, LANES), F32)]
        + [vm((16, LANES), F32), vm((2 * inner, 16, LANES), F32), vm((outer, 16, LANES), F32)]
        + [vm((wide * rows, LANES), F32)]
        + [vm((2 * inner, *tile), F32), vm((outer, *tile), F32)]
        + [vm((vecs, min(24, padded), LANES), F32)]
        + [dma((4,)), dma((outer - 1,)), dma((outer, inner - 1)), dma((wide,)), dma((wide,)), dma((wide,))]
        + [dma((3, inner))] * 4
        + [dma((outer,)), dma((outer,)), dma((2,))]
        + [dma((2 * inner + outer,))] * 4
        + [dma((vecs, outer + inner - 2)), dma((vecs,))]
    )
    anywhere, vmem = pl.BlockSpec(memory_space=pl.ANY), pl.BlockSpec(memory_space=pltpu.VMEM)
    return pl.pallas_call(
        functools.partial(step_kernel, wide),
        out_shape=(
            jax.ShapeDtypeStruct(x.shape, BF16),
            jax.ShapeDtypeStruct(x.shape, F32),
            jax.ShapeDtypeStruct((rows, LANES), F32),
            jax.ShapeDtypeStruct(tile, F32),
        ),
        in_specs=[anywhere, anywhere, vmem],
        out_specs=(anywhere, anywhere, vmem, vmem),
        scratch_shapes=scratch,
        compiler_params=pltpu.CompilerParams(
            collective_id=0, has_side_effects=True, vmem_limit_bytes=60 * 2**20
        ),
        name="step",
    )(x, dy, shard)


def finish_kernel(*refs):
    big_in, small_in = refs[0:2], refs[2:7]
    big_out, norm_out, small_out = refs[7:9], refs[9], refs[10:15]
    stages, ins, norm, outs = refs[15:17], refs[17:22], refs[22], refs[23:28]
    sem_in, sem_out, sem_small = refs[28:31]
    pieces = []
    for k in range(2):
        size = big_in[k].shape[0] // PIECES
        for p in range(PIECES):
            at = pl.ds(size * p, size)
            pieces.append(
                (
                    pltpu.make_async_copy(big_in[k].at[at], stages[k].at[at], sem_in.at[k, p]),
                    pltpu.make_async_copy(stages[k].at[at], big_out[k].at[at], sem_out.at[k, p]),
                )
            )
    loads = [pltpu.make_async_copy(small_in[k], ins[k], sem_small.at[k]) for k in range(5)]
    for copy in loads:
        copy.start()
    for come, _ in pieces:
        come.start()
    for copy in loads:
        copy.wait()
    own, squares, master, first, second = ins
    clipped, new_master, new_copy, new_first, new_second = outs
    grad_norm = jnp.sqrt(squares[...])
    norm[...] = grad_norm[0:1, 0:1]
    factor = jnp.minimum(1.0, 1.0 / (grad_norm[0:1, :] + 1e-06))
    grad = own[...] * factor
    clipped[...] = grad
    one = 0.5 * first[...] + 0.5 * grad
    two = 0.5 * second[...] + 0.5 * grad * grad
    new_first[...] = one
    new_second[...] = two
    fixed = 1.0 - 0.5**STEP
    old = master[...]
    new = old - 0.05 * ((one / fixed) / (jnp.sqrt(two / fixed) + 1e-08) + 0.1 * old)
    new_master[...] = new
    new_copy[...] = new.astype(BF16)
    stores = [
        pltpu.make_async_copy(src, dst, sem_small.at[5 + k])
        for k, (src, dst) in enumerate(zip((norm, *outs), (norm_out, *small_out)))
    ]
    for copy in stores:
        copy.start()
    for come, go in pieces:
        come.wait()
        go.start()
    for copy in stores:
        copy.wait()
    for _, go in pieces:
        go.wait()


def finish(block_out, input_grad, owned, squares, master, first, second):
    anywhere, vm = pl.BlockSpec(memory_space=pl.ANY), pltpu.VMEM
    one, flat = (1, 1), owned.shape
    kinds = [(flat, F32), (flat, F32), (flat, BF16), (flat, F32), (flat, F32)]
    like = jax.ShapeDtypeStruct
    return pl.pallas_call(
        finish_kernel,
        out_shape=(
            like(block_out.shape, BF16),
            like(input_grad.shape, F32),
            like(one, F32),
            *[like(*kind) for kind in kinds],
        ),
        in_specs=[anywhere] * 7,
        out_specs=(anywhere,) * 8,
        scratch_shapes=[
            vm(block_out.shape, BF16),
            vm(input_grad.shape, F32),
            vm(flat, F32),
            vm(squares.shape, F32),
            vm(flat, F32),
            vm(flat, F32),
            vm(flat, F32),
            vm(one, F32),
            *[vm(*kind) for kind in kinds],
            pltpu.SemaphoreType.DMA((2, PIECES)),
            pltpu.SemaphoreType.DMA((2, PIECES)),
            pltpu.SemaphoreType.DMA((11,)),
        ],
        compiler_params=pltpu.CompilerParams(vmem_limit_bytes=60 * 2**20),
        name="finish",
    )(block_out, input_grad, owned, squares, master, first, second)


def on_device(inputs, cotangent, master, first, second):
    flat = lambda a: a.reshape(-1)
    tall = lambda a: a.reshape(-1, LANES)
    block_out, input_grad, owned, squares = step(
        inputs, cotangent, tall(master), lax.axis_size("wide")
    )
    block_out, input_grad, norm, clipped, new_master, new_copy, new_first, new_second = finish(
        block_out, input_grad, owned, squares, tall(master), tall(first), tall(second)
    )
    return (
        block_out,
        input_grad,
        flat(clipped),
        norm.reshape(()),
        flat(new_master),
        flat(new_copy),
        flat(new_first),
        flat(new_second),
    )


def solution(mesh):
    both, part = P(("wide", "narrow"), None), P("wide")
    return jax.shard_map(
        on_device,
        mesh=mesh,
        in_specs=(both, both, part, part, part),
        out_specs=(both, both, part, P(), part, part, part, part),
        check_vma=False,
    )
```

```python
import functools
import math

import jax
import jax.numpy as jnp
from jax import lax
from jax.experimental import pallas as pl
from jax.experimental.pallas import tpu as pltpu
from jax.sharding import PartitionSpec as P

D = 192
HEADS = 8
HEAD_DIM = 24
FF = 256
SEQ = 34
STEP = 5
ROWS = 40
GROUP = 3
GROWS = GROUP * ROWS
PAIRS = HEADS // 2
PAIR_DIM = 2 * HEAD_DIM
HJ = PAIRS * ROWS
LANES = 128
F32 = jnp.float32
BF16 = jnp.bfloat16
MATS = ((0, D), (288, D), (576, D), (864, D), (1920, FF))
W1_AT = 1152
WIDTH1, WIDTH2, WIDTH3, DW_STEPS = 4, 6, 4, 2
LOCK1, LOCK2 = 8, 4
PIECES = 1
VEC_AT = 2304
USED_ROWS = VEC_AT + 16
QK_ROWS = 576
QKV_ROWS = 864
GELU_C = math.sqrt(2.0 / math.pi)


def nn(a, b):
    return lax.dot_general(a, b, (((1,), (0,)), ((), ())), preferred_element_type=F32)


def nt(a, b):
    return lax.dot_general(a, b, (((1,), (1,)), ((), ())), preferred_element_type=F32)


def tn(a, b):
    return lax.dot_general(a, b, (((0,), (0,)), ((), ())), preferred_element_type=F32)


def low_half(v):
    lane = lax.broadcasted_iota(jnp.int32, v.shape, 1)
    return lane < 64


def load_square(flat, base, rows, tmp, out):
    half = rows // 2
    f0 = flat[pl.ds(base, half, stride=3), :]
    f1 = flat[pl.ds(base + 1, half, stride=3), :]
    f2 = flat[pl.ds(base + 2, half, stride=3), :]
    r1 = pltpu.roll(f1, 64, 1)
    r2 = pltpu.roll(f2, 64, 1)
    left = low_half(f0)
    lo, hi = tmp.at[0], tmp.at[1]
    lo[pl.ds(0, half, stride=2), :] = f0
    hi[pl.ds(0, half, stride=2), :] = jnp.where(left, f1, 0.0)
    lo[pl.ds(1, half, stride=2), :] = jnp.where(left, r1, r2)
    hi[pl.ds(1, half, stride=2), :] = jnp.where(left, r2, 0.0)
    out[0:rows, 0:128] = lo[0:rows, :].astype(BF16)
    out[0:rows, 128:256] = hi[0:rows, :].astype(BF16)
    if rows < 256:
        out[rows:256, :] = jnp.zeros((256 - rows, 256), BF16)


def store_square(val, flat, base, rows, tmp):
    half = rows // 2
    lo, hi = tmp.at[0], tmp.at[1]
    lo[0:rows, :] = val[0:rows, 0:128]
    hi[0:rows, :] = val[0:rows, 128:256]
    e0 = lo[pl.ds(0, half, stride=2), :]
    e1 = hi[pl.ds(0, half, stride=2), :]
    o0 = pltpu.roll(lo[pl.ds(1, half, stride=2), :], 64, 1)
    o1 = pltpu.roll(hi[pl.ds(1, half, stride=2), :], 64, 1)
    left = low_half(e0)
    flat[pl.ds(base, half, stride=3), :] = e0
    flat[pl.ds(base + 1, half, stride=3), :] = jnp.where(left, e1, o0)
    flat[pl.ds(base + 2, half, stride=3), :] = jnp.where(left, o0, o1)


def norm_fwd(x):
    mean = jnp.sum(x, -1, keepdims=True) * (1.0 / D)
    right = x[:, 128:256] - mean
    c = jnp.concatenate([x[:, 0:128] - mean, jnp.where(low_half(right), right, 0.0)], 1)
    var = jnp.sum(c * c, -1, keepdims=True) * (1.0 / D)
    r = lax.rsqrt(var + 1e-05)
    return c * r, r


def norm_back(d, xh, r, g):
    e = d * g
    m1 = jnp.sum(e, -1, keepdims=True) * (1.0 / D)
    m2 = jnp.sum(e * xh, -1, keepdims=True) * (1.0 / D)
    return r * (e - m1 - xh * m2)


def rows8(v):
    return jnp.sum(v.reshape(v.shape[0] // 8, 8, v.shape[1]), 0)


def split_tokens(v, count):
    zero = jnp.zeros((v.shape[0], 256 - D), v.dtype)
    return jnp.concatenate(
        [jnp.concatenate([v[:, D * t : D * (t + 1)], zero], 1) for t in range(count)], 0
    )


def join_tokens(v, n):
    return jnp.concatenate([v[n * t : n * (t + 1), 0:D] for t in range(v.shape[0] // n)], 1)


def factors(wide):
    inner = max(k for k in range(1, int(math.isqrt(wide)) + 1) if wide % k == 0)
    return wide // inner, inner


def remote(src, dst, send, recv, where):
    return pltpu.make_async_remote_copy(
        src_ref=src,
        dst_ref=dst,
        send_sem=send,
        recv_sem=recv,
        device_id=where,
        device_id_type=pl.DeviceIdType.MESH,
    )


def greet(devices):
    for dev in devices:
        pl.semaphore_signal(
            pltpu.get_barrier_semaphore(), inc=1, device_id=dev,
            device_id_type=pl.DeviceIdType.MESH,
        )


def step_kernel(
    wide,
    x_hbm, dy_hbm, shard, out_hbm, ig_hbm, own, squares,
    x_ref, dy_ref, out_ref, ig_ref, flat, gflat,
    qs, ks, vs, os_, kbd, vbd, psc, xb, xh1, r1, dx2s, h, h2, z, dul, o_t, dal, dyt, dqkv,
    wq, wk, wv, wo, w1, w2, tmp, hm2, parity, sample, hs, acc, acc2, acc3,
    buf, parts, sib_in, plane_in, out_p, col_in, out_c, res, vec_own, vec_plane, vec_col,
    vec_at, sq_plane, sq_col, vec_in,
    io_sem, g_col, g_fw, g_sib, g_recv, g_recv_sib, s_send, s_recv, p_send, p_recv, c_send, c_recv,
    f_sem, v_send, v_recv, n_send, n_recv, vg_send, vg_recv,
):
    n = x_ref.shape[0]
    toks = n * SEQ
    pairs = SEQ // 2
    groups = n // GROUP
    rows = shard.shape[0]
    half = buf.shape[1] // 2
    outer, inner = factors(wide)
    me, core = lax.axis_index("wide"), lax.axis_index("narrow")
    zo, pi = me // inner, lax.rem(me, inner)
    mine = pl.ds(pl.multiple_of(core * half, 8), half)
    theirs = pl.ds(pl.multiple_of((1 - core) * half, 8), half)
    sibling = (me, 1 - core)
    around = [lax.rem(pi + k, inner) for k in range(1, inner)]
    along = [lax.rem(zo + k, outer) for k in range(1, outer)]
    plane = [(zo * inner + q, core) for q in around]
    column = [(t * inner + pi, core) for t in along]
    late = -(-QK_ROWS // (rows * inner))
    first = -(-QKV_ROWS // (rows * inner))
    bounds = ((first, outer), (late, first), (0, late))

    copies_in = [
        pltpu.make_async_copy(x_hbm, x_ref, io_sem.at[0]),
        pltpu.make_async_copy(dy_hbm, dy_ref, io_sem.at[1]),
    ]
    for copy in copies_in:
        copy.start()

    cross = [(zo * inner + q, 1 - core) for q in around]
    known = plane + cross + column + [sibling]
    greet(known)
    lane = lax.broadcasted_iota(jnp.int32, (80, 256), 1)
    row = lax.broadcasted_iota(jnp.int32, (80, 256), 0)
    for p in range(PAIRS // 2):
        lo = jnp.where(row < ROWS, PAIR_DIM * 2 * p, PAIR_DIM * (2 * p + 1))
        hm2[80 * p : 80 * (p + 1), :] = jnp.where(
            (lane >= lo) & (lane < lo + PAIR_DIM), 1.0, 0.0
        ).astype(BF16)
    lane16 = lax.broadcasted_iota(jnp.int32, (16, 256), 1)
    for b in range(GROUP):
        query = lax.rem(lane16, LANES)
        sample[16 * b : 16 * (b + 1), :] = jnp.where(
            (query >= ROWS * b) & (query < ROWS * (b + 1)), 1.0, 0.0
        ).astype(BF16)
    head = lane16 // HEAD_DIM
    for k in range(2):
        parity[16 * k : 16 * (k + 1), :] = jnp.where(
            (lax.rem(head, 2) == k) & (head < HEADS), 1.0, 0.0
        ).astype(BF16)
    ones_lane = (lax.broadcasted_iota(jnp.int32, (toks, 64), 1) == 0).astype(F32).astype(BF16)
    o_t[:, D:256] = ones_lane
    for ref in (qs, ks, vs, os_):
        ref[...] = jnp.zeros(ref.shape, F32)

    parts[...] = jnp.zeros(parts.shape, F32)
    vec_at[...] = jnp.zeros(vec_at.shape, F32)
    pl.semaphore_wait(pltpu.get_barrier_semaphore(), len(known))
    buf[me, 0:rows, :] = shard[...]
    buf[me, rows:, :] = jnp.zeros((buf.shape[1] - rows, LANES), F32)

    def push(s, send, recvs, where):
        return remote(buf.at[s, mine], buf.at[s, mine], send, recvs.at[s], where)

    def arrived(s, recvs, part):
        remote(buf.at[s, part], buf.at[s, part], g_sib.at[s], recvs.at[s], sibling).wait_recv()

    def forwards(t, s):
        return [push(s, g_fw.at[t, k], g_recv, where) for k, where in enumerate(plane)]

    vec_rows = [
        (s, max(0, VEC_AT - rows * s) // 8 * 8, max(0, VEC_AT - rows * s), min(rows, USED_ROWS - rows * s))
        for s in range(VEC_AT // rows, (USED_ROWS - 1) // rows + 1)
    ]

    def vec_push(j, where, base):
        return [
            remote(vec_in.at[j], vec_in.at[j], vg_send.at[j, base + k], vg_recv.at[j], dev)
            for k, dev in enumerate(where)
        ]

    def vec_arrived(j):
        remote(vec_in.at[j], vec_in.at[j], vg_send.at[j, 0], vg_recv.at[j], sibling).wait_recv()

    for j, (s, a0, _, end) in enumerate(vec_rows):
        @pl.when(me == s)
        def _(j=j, a0=a0, end=end):
            vec_in[j, 0 : end - a0, :] = shard[a0:end, :]
            for copy in vec_push(j, column, 0) + vec_push(j, plane, outer - 1):
                copy.start()

    own_pushes = [push(me, g_col.at[k], g_recv, where) for k, where in enumerate(column)]
    own_pushes += forwards(zo, me)
    for copy in own_pushes:
        copy.start()

    def to_sibling(s):
        return push(s, g_sib.at[s], g_recv_sib, sibling)

    def forward_level(t):
        s = t * inner + pi

        @pl.when(t != zo)
        def _():
            arrived(s, g_recv, mine)
            for copy in forwards(t, s):
                copy.start()
            to_sibling(s).start()

    def pass_level(t):
        for q in around:
            s = t * inner + q
            arrived(s, g_recv, mine)
            to_sibling(s).start()

    def whole_shard(s):
        @pl.when(s != me)
        def _():
            arrived(s, g_recv_sib, theirs)

    def unpack(s):
        flat[rows * s : rows * (s + 1), :] = buf[s, 0:rows, :]

    for j, (s, _, _, _) in enumerate(vec_rows):
        @pl.when((me != s) & (pi == s % inner))
        def _(j=j):
            vec_arrived(j)
            for copy in vec_push(j, plane, outer - 1):
                copy.start()

    for t in range(outer):
        forward_level(t)

    def tokens_of(ref, t, count):
        return split_tokens(
            ref[:, pl.ds(pl.multiple_of(t * D, 128), count * D)].astype(F32), count
        )

    def put_tokens(ref, t, val):
        for half in range(2):
            for k in range(val.shape[0] // n):
                ref.at[half][pl.ds(t + k, n, stride=ROWS), :] = val[
                    n * k : n * (k + 1), 128 * half : 128 * (half + 1)
                ]

    def get_tokens(ref, t, count):
        return jnp.concatenate(
            [
                jnp.concatenate(
                    [ref.at[half][pl.ds(t + k, n, stride=ROWS), :] for half in range(2)], 1
                )
                for k in range(count)
            ],
            0,
        )

    def over_token_chunks(body, width, carry, hook=lambda i: None):
        whole = pairs // width

        def step(i, c):
            hook(i)
            return body(i * (2 * width), 2 * width, c)

        carry = lax.fori_loop(0, whole, step, carry)
        if pairs % width:
            carry = body(whole * 2 * width, 2 * (pairs % width), carry)
        return carry

    def get_rows(ref, start, count):
        return jnp.concatenate([ref[0, pl.ds(start, count), :], ref[1, pl.ds(start, count), :]], 1)

    def put_rows(ref, start, val):
        for half in range(2):
            ref[half, pl.ds(start, val.shape[0]), :] = val[:, 128 * half : 128 * (half + 1)]

    def rows_at(t, count):
        return pl.ds(pl.multiple_of(t * n, 32), count * n)

    copies_in[0].wait()
    for j, (s, a0, begin, end) in enumerate(vec_rows):
        @pl.when(pi != s % inner)
        def _(j=j):
            vec_arrived(j)

        flat[rows * s + begin : rows * s + end, :] = vec_in[j, begin - a0 : end - a0, :]

    ones3 = (lax.broadcasted_iota(jnp.int32, (1, 64), 1) < 3).astype(F32)

    def vec(k):
        a = VEC_AT + 3 * (k // 2)
        zero = ones3 if k in (1, 6) else jnp.zeros((1, 64), F32)
        if k % 2 == 0:
            return jnp.concatenate([flat[a : a + 1, :], flat[a + 1 : a + 2, 0:64], zero], 1)
        return jnp.concatenate([flat[a + 1 : a + 2, 64:128], flat[a + 2 : a + 3, :], zero], 1)

    g1, n1, bq, bv, bo, g2, n2, b2 = [vec(k) for k in range(8)]
    b1 = jnp.concatenate([flat[VEC_AT + 12 + c : VEC_AT + 13 + c, :] for c in range(4)], 1)

    def norm1(t, count, carry):
        at = rows_at(t, count)
        x = tokens_of(x_ref, t, count)
        xh, r = norm_fwd(x)
        xh1[at, :] = xh
        r1[at, :] = r
        hb = (xh * g1 + n1).astype(BF16)
        h[at, :] = hb
        put_tokens(os_, t, hb.astype(F32))
        xb[at, :] = x + bo
        return carry

    over_token_chunks(norm1, WIDTH1, 0)

    def take_dy(t, count, db2):
        dy = tokens_of(dy_ref, t, count)
        dyt[rows_at(t, count), :] = dy.astype(BF16)
        return db2 + rows8(dy)

    zero = jnp.zeros((8, 256), F32)
    copies_in[1].wait()
    db2 = over_token_chunks(take_dy, WIDTH1, zero)

    def bias_rows(b):
        row = lax.broadcasted_iota(jnp.int32, (16, b.shape[1]), 0)
        out = jnp.zeros((16, b.shape[1]), F32)
        for k in range(3):
            part = b.astype(BF16).astype(F32)
            out = jnp.where(row == k, part, out)
            b = b - part
        return out.astype(BF16)

    half_groups = LOCK2 * GROWS

    @pl.loop(0, groups // LOCK2)
    def _(i):
        at = pl.ds(pl.multiple_of(i * half_groups, 16), half_groups)
        hs[at, :] = get_rows(os_, pl.multiple_of(i * half_groups, 8), half_groups).astype(BF16)

    def take_levels(lo, hi):
        for s in range(lo * inner, hi * inner):
            whole_shard(s)
            unpack(s)

    for t in range(late):
        pass_level(t)
    take_levels(0, late)
    for (base, count), ref in zip(MATS[0:2], (wq, wk)):
        load_square(flat, base, count, tmp, ref)
    wq[D : D + 16, :] = bias_rows(bq)

    def pass_v(i):
        @pl.when(i == 1)
        def _():
            for t in range(late, first):
                pass_level(t)

    def dense_qk(t, count, carry):
        hb = h[rows_at(t, count), :]
        put_tokens(qs, t, nn(hb, wq[...]).astype(BF16).astype(F32))
        put_tokens(ks, t, nn(hb, wk[...]).astype(BF16).astype(F32))
        return carry

    over_token_chunks(dense_qk, WIDTH1, 0, pass_v)
    take_levels(late, first)
    load_square(flat, MATS[2][0], MATS[2][1], tmp, wv)
    wv[D : D + 16, :] = bias_rows(bv)

    def dense_v(t, count, carry):
        hb = h[rows_at(t, count), :]
        put_tokens(vs, t, nn(hb, wv[...]).astype(BF16).astype(F32))
        return carry

    over_token_chunks(dense_v, WIDTH1, 0)

    lane3 = lax.rem(lax.broadcasted_iota(jnp.int32, (1, 256), 1), LANES)
    odd_head = lax.rem(lax.broadcasted_iota(jnp.int32, (1, 256), 1) // HEAD_DIM, 2) == 1

    def squeeze(v):
        return jnp.where(
            lane3 < ROWS, v[0:HJ], jnp.where(lane3 < 2 * ROWS, v[HJ : 2 * HJ], v[2 * HJ : 3 * HJ])
        ).reshape(PAIRS, ROWS, 256)

    def by_parity(v):
        v3 = v.reshape(8, 16, 256)
        return jnp.concatenate(
            [(v3 * parity[16 * k : 16 * (k + 1), :][None]).reshape(LANES, 256) for k in range(2)], 0
        )

    def per_query(left, right, b):
        rows2 = jnp.concatenate([left[128 * k + ROWS * b : 128 * k + ROWS * (b + 1)] for k in range(2)], 0)
        both = nn(rows2.astype(BF16), right)
        return jnp.where(odd_head, both[ROWS : 2 * ROWS], both[0:ROWS])

    jrow = lax.broadcasted_iota(jnp.int32, (1, ROWS - 32, 256), 1)
    cexp = math.log2(math.e) / math.sqrt(HEAD_DIM)
    scale = 1.0 / math.sqrt(HEAD_DIM)

    def attn(i, carry):
        @pl.when(i == 1)
        def _():
            for t in range(first, outer):
                pass_level(t)

        r0 = pl.multiple_of(i * (LOCK1 * GROWS), 8)
        base0 = pl.multiple_of(i * (LOCK1 * 3 * HJ), 32)
        p0 = pl.multiple_of(i * (LOCK1 * HJ), 32)
        sets = range(LOCK1)
        qg = [by_parity(get_rows(qs, r0 + GROWS * k, LANES).astype(BF16)) for k in sets]
        for k in sets:
            for src, dst in ((ks, kbd), (vs, vbd)):
                for b in range(GROUP):
                    one = get_rows(src, r0 + GROWS * k + ROWS * b, ROWS)
                    two = jnp.concatenate([one, one], 0).astype(BF16)
                    for p in range(PAIRS // 2):
                        dst[pl.ds(base0 + HJ * (3 * k + b) + 80 * p, 80), :] = (
                            two * hm2[80 * p : 80 * (p + 1), :]
                        )
        st = [squeeze(nt(kbd[pl.ds(base0 + 3 * HJ * k, 3 * HJ), :], qg[k])) for k in sets]
        st = [
            jnp.concatenate([v[:, 0:32], jnp.where(jrow < SEQ - 32, v[:, 32:ROWS], -1e30)], 1)
            for v in st
        ]
        m = [jnp.max(v, 1, keepdims=True) for v in st]
        e = [jnp.exp2((st[k] - m[k]) * cexp) for k in sets]
        l = [1.0 / jnp.sum(v, 1, keepdims=True) for v in e]
        p = [(e[k] * l[k]).reshape(HJ, 256) for k in sets]
        for k in sets:
            psc[pl.ds(p0 + HJ * k, HJ), :] = p[k]
        pt = [v.T for v in p]
        for b in range(GROUP):
            for k in sets:
                ob = per_query(pt[k], vbd[pl.ds(base0 + HJ * (3 * k + b), HJ), :], b)
                put_rows(os_, r0 + GROWS * k + ROWS * b, ob.astype(BF16).astype(F32)[0:SEQ])
        return carry

    lax.fori_loop(0, groups // LOCK1, attn, 0)

    take_levels(first, outer)
    for (base, count), ref in zip(MATS[3:5], (wo, w2)):
        load_square(flat, base, count, tmp, ref)
    for c in range(4):
        part = flat[pl.ds(W1_AT + c, D, stride=4), :]
        w1[0:D, 128 * c : 128 * (c + 1)] = (part if c < 2 else 0.5 * part).astype(BF16)
    w1[D : D + 16, :] = bias_rows(jnp.concatenate([b1[:, 0:FF], 0.5 * b1[:, FF:]], 1))
    w1[D + 16 : 256, :] = jnp.zeros((240 - D, 2 * FF), BF16)
    def dense2(t0, count, carry):
        dg2, dn2 = carry
        at = rows_at(t0, count)
        o = get_tokens(os_, t0, count).astype(BF16)
        o_t[at, 0:D] = o[:, 0:D]
        x2 = xb[at, :] + nn(o, wo[...])
        xh, r = norm_fwd(x2)
        hb = (xh * g2 + n2).astype(BF16)
        h2[at, :] = hb
        u = nn(hb, w1[...])
        gate, up = u[:, :FF], u[:, FF:]
        sq = gate * gate
        t = jnp.tanh(gate * (GELU_C + (GELU_C * 0.044715) * sq))
        t1 = 1.0 + t
        act = gate * t1
        zb = (act * up).astype(BF16)
        z[at, :] = zb
        y = x2 + nn(zb, w2[...]) + b2
        out_ref[:, pl.ds(pl.multiple_of(t0 * D, 128), count * D)] = join_tokens(y, n).astype(BF16)
        dyb = dyt[at, :]
        dyf = dyb.astype(F32)
        dz = nt(dyb, w2[...])
        slope = t1 + act * (1.0 - t) * (GELU_C + (3 * GELU_C * 0.044715) * sq)
        du = jnp.concatenate([(dz * up * slope).astype(BF16), (dz * act).astype(BF16)], 1)
        dul[at, :] = du
        dh = nt(du, w1[...])
        dx2 = dyf + norm_back(dh, xh, r, g2)
        dx2s[at, :] = dx2
        da = dx2.astype(BF16)
        dal[at, :] = da
        put_tokens(os_, t0, nt(da, wo[...]).astype(BF16).astype(F32))
        acc[...] += tn(zb, dyb)
        acc2[...] += tn(hb, du)
        acc3[...] += tn(o_t[at, :], da)
        return dg2 + rows8(dh * xh), dn2 + rows8(dh)

    for ref in (acc, acc2, acc3):
        ref[...] = jnp.zeros(ref.shape, F32)
    dg2, dn2 = over_token_chunks(dense2, WIDTH2, (zero, zero))

    copy_out = pltpu.make_async_copy(out_ref, out_hbm, io_sem.at[2])
    copy_out.start()

    def total(v):
        return jnp.sum(v, 0, keepdims=True)

    def over_tokens(*products):
        for acc, _, _ in products:
            acc[...] = jnp.zeros(acc.shape, F32)
        size = products[0][1].shape[0] // DW_STEPS

        @pl.loop(0, DW_STEPS)
        def _(i):
            at = pl.ds(pl.multiple_of(i * size, 16), size)
            for acc, a, b in products:
                acc[...] += tn(a[at, :], b[at, :])

    store_square(acc[...], gflat, 1920, FF, tmp)
    for c in range(4):
        part = acc2[0 : D + 8, 128 * c : 128 * (c + 1)]
        part = part if c < 2 else 0.5 * part
        gflat[pl.ds(W1_AT + c, D, stride=4), :] = part[0:D]
        vec_own[12 + c : 13 + c, :] = part[D : D + 1]
    store_square(acc3[...], gflat, 864, D, tmp)
    dbo = acc3[D : D + 1, :]

    def pack(lo, hi):
        for s in range(lo * inner, hi * inner):
            stop = min(rows * (s + 1), VEC_AT)
            if stop > rows * s:
                parts[s // inner, s % inner, 0 : stop - rows * s, :] = gflat[rows * s : stop, :]

    places = around + [pi]

    def sib_copies(part, lo, hi):
        return [
            remote(
                parts.at[lo:hi, q, theirs], sib_in.at[lo:hi, q],
                s_send.at[part, k], s_recv.at[part, q], sibling,
            )
            for k, q in enumerate(places)
        ]

    def plane_copies(part, lo, hi):
        return [
            remote(
                out_p.at[k, lo:hi], plane_in.at[pi, lo:hi],
                p_send.at[part, k], p_recv.at[part, pi], plane[k],
            )
            for k in range(inner - 1)
        ]

    def col_copy(t):
        return remote(
            out_c.at[t], col_in.at[zo], c_send.at[t], c_recv.at[zo], (t * inner + pi, core)
        )

    def sum_cores(part):
        lo, hi = bounds[part]
        sends = plane_copies(part, lo, hi)
        for k, q in enumerate(places):
            remote(
                sib_in.at[lo:hi, q], sib_in.at[lo:hi, q],
                s_send.at[part, k], s_recv.at[part, q], sibling,
            ).wait_recv()
            both = parts[lo:hi, q, mine, :] + sib_in[lo:hi, q]
            if k < inner - 1:
                out_p[k, lo:hi] = both
                sends[k].start()
            else:
                plane_in[pi, lo:hi] = both

    def sum_plane(part):
        lo, hi = bounds[part]
        for k, q in enumerate(around):
            remote(
                plane_in.at[q, lo:hi], plane_in.at[q, lo:hi],
                p_send.at[part, k], p_recv.at[part, q], sibling,
            ).wait_recv()
        for t in range(lo, hi):
            line = plane_in[0, t]
            for q in range(1, inner):
                line = line + plane_in[q, t]
            out_c[t] = line

            @pl.when(t != zo)
            def _():
                col_copy(t).start()

    def send_cores(part):
        pack(*bounds[part])
        for copy in sib_copies(part, *bounds[part]):
            copy.start()

    send_cores(0)

    def by_sample(v):
        v = v.reshape(HJ, 256).astype(BF16).reshape(HJ // 16, 16, 256)
        return jnp.concatenate(
            [
                (v * sample[16 * b : 16 * (b + 1), :][None]).reshape(HJ, 256)
                for b in range(GROUP)
            ],
            0,
        )

    pair_lane = lax.broadcasted_iota(jnp.int32, (1, LANES), 1)

    def own_lanes(v):
        v = v.reshape(GROUP, PAIRS, ROWS, 256)
        out = []
        for b in range(GROUP):
            lo = jnp.where(pair_lane < PAIR_DIM, v[b, 0, :, 0:128], v[b, 1, :, 0:128])
            lo = jnp.where(pair_lane < 2 * PAIR_DIM, lo, v[b, 2, :, 0:128])
            hi = jnp.where(
                pair_lane < 3 * PAIR_DIM - 128, v[b, 2, :, 128:256], v[b, 3, :, 128:256]
            )
            out.append(jnp.concatenate([lo, hi], 1))
        return jnp.concatenate(out, 0)

    def probs(at):
        return psc[pl.ds(at, HJ), :].reshape(PAIRS, ROWS, 256)

    def attn_back_v(i, carry):
        @pl.when(i == 3)
        def _():
            sum_cores(0)

        r0 = pl.multiple_of(i * (LOCK2 * GROWS), 8)
        p0 = pl.multiple_of(i * (LOCK2 * HJ), 32)
        out = []
        for k in range(LOCK2):
            dg = by_parity(get_rows(os_, r0 + GROWS * k, LANES).astype(BF16))
            out.append(own_lanes(nn(by_sample(probs(p0 + HJ * k)), dg)))
        out = jnp.concatenate(out, 0).astype(BF16)
        dqkv[pl.ds(pl.multiple_of(i * half_groups, 16), half_groups), 512:768] = out
        put_rows(vs, r0, out.astype(F32))
        return carry

    lax.fori_loop(0, groups // LOCK2, attn_back_v, 0)

    over_tokens((acc, hs, dqkv.at[:, 512:768]))
    store_square(acc[...], gflat, 576, D, tmp)
    dbv = acc[D : D + 1, :]
    send_cores(1)

    def attn_back(i, carry):
        @pl.when(i == 1)
        def _():
            sum_cores(1)

        r0 = pl.multiple_of(i * (LOCK2 * GROWS), 8)
        base0 = pl.multiple_of(i * (LOCK2 * 3 * HJ), 32)
        p0 = pl.multiple_of(i * (LOCK2 * HJ), 32)
        sets = range(LOCK2)
        qg = [by_parity(get_rows(qs, r0 + GROWS * k, LANES).astype(BF16)) for k in sets]
        dg = [by_parity(get_rows(os_, r0 + GROWS * k, LANES).astype(BF16)) for k in sets]
        dp = [squeeze(nt(vbd[pl.ds(base0 + 3 * HJ * k, 3 * HJ), :], dg[k])) for k in sets]
        p = [probs(p0 + HJ * k) for k in sets]
        t = [jnp.sum(p[k] * dp[k], 1, keepdims=True) for k in sets]
        ds = [p[k] * (dp[k] - t[k]) for k in sets]
        dst = [v.reshape(HJ, 256).T for v in ds]
        dk = [own_lanes(nn(by_sample(ds[k]), qg[k])) * scale for k in sets]
        dq = [
            per_query(dst[k], kbd[pl.ds(base0 + HJ * (3 * k + b), HJ), :], b) * scale
            for k in sets
            for b in range(GROUP)
        ]
        at = pl.ds(pl.multiple_of(i * half_groups, 16), half_groups)
        for col, ref, val in ((0, qs, dq), (256, ks, dk)):
            val = jnp.concatenate(val, 0).astype(BF16)
            dqkv[at, col : col + 256] = val
            put_rows(ref, r0, val.astype(F32))
        return carry

    lax.fori_loop(0, groups // LOCK2, attn_back, 0)

    over_tokens((acc2, hs, dqkv.at[:, 0:512]))
    for k in range(2):
        store_square(acc2[:, 256 * k : 256 * (k + 1)], gflat, 288 * k, D, tmp)
    send_cores(2)
    sum_plane(0)

    def dense3(t0, count, carry):
        dg1, dn1 = carry
        at = rows_at(t0, count)
        dh = (
            nt(get_tokens(qs, t0, count).astype(BF16), wq[...])
            + nt(get_tokens(ks, t0, count).astype(BF16), wk[...])
            + nt(get_tokens(vs, t0, count).astype(BF16), wv[...])
        )
        xh = xh1[at, :]
        ig = dx2s[at, :] + norm_back(dh, xh, r1[at, :], g1)
        ig_ref[:, pl.ds(pl.multiple_of(t0 * D, 128), count * D)] = join_tokens(ig, n)
        return dg1 + rows8(dh * xh), dn1 + rows8(dh)

    def hook3(i):
        @pl.when(i == 1)
        def _():
            sum_cores(2)
            sum_plane(1)

    dg1, dn1 = over_token_chunks(dense3, WIDTH3, (zero, zero), hook3)

    vecs = [
        total(dg1), total(dn1), acc2[D : D + 1, 0:256], dbv,
        dbo, total(dg2), total(dn2), total(db2),
    ]
    for k in range(4):
        a, b = vecs[2 * k], vecs[2 * k + 1]
        vec_own[3 * k : 3 * k + 1, :] = a[:, 0:128]
        vec_own[3 * k + 1 : 3 * k + 2, :] = jnp.concatenate([a[:, 128:192], b[:, 0:64]], 1)
        vec_own[3 * k + 2 : 3 * k + 3, :] = b[:, 64:192]
    copy_ig = pltpu.make_async_copy(ig_ref, ig_hbm, io_sem.at[3])
    copy_ig.start()

    def spread(slots, at, sends, recvs, base, where):
        out = [
            remote(slots.at[at], slots.at[at], sends.at[base + k], recvs.at[base + at], dev)
            for k, dev in enumerate(where)
        ]
        for copy in out:
            copy.start()
        return out

    def collected(slots, others, sends, recvs, base):
        for k, q in enumerate(others):
            remote(
                slots.at[q], slots.at[q], sends.at[base + k], recvs.at[base + q], sibling
            ).wait_recv()
        return jnp.sum(slots[...], 0)

    slot = 2 * pi + core
    near = [2 * q + core for q in around] + [2 * q + 1 - core for q in around] + [2 * pi + 1 - core]
    disc = plane + cross + [sibling]
    vec_plane[slot] = vec_own[...]
    vec_sends = spread(vec_plane, slot, v_send, v_recv, 0, disc)
    sum_plane(2)
    vec_col[zo] = collected(vec_plane, near, v_send, v_recv, 0)
    vec_sends += spread(vec_col, zo, v_send, v_recv, 2 * inner, column)

    col_in[zo] = out_c[zo]
    for t in along:
        remote(col_in.at[t], col_in.at[t], c_send.at[t], c_recv.at[t], sibling).wait_recv()
    line = col_in[0]
    for t in range(1, outer):
        line = line + col_in[t]
    res[mine, :] = line
    last = remote(res.at[mine], res.at[mine], f_sem.at[0], f_sem.at[1], sibling)
    last.start()
    sq_plane[slot] = rows8(line * line)
    sq_sends = spread(sq_plane, slot, n_send, n_recv, 0, disc)
    vec = collected(vec_col, along, v_send, v_recv, 2 * inner)
    vec_at[VEC_AT:USED_ROWS, :] = vec
    remote(res.at[theirs], res.at[theirs], f_sem.at[0], f_sem.at[1], sibling).wait_recv()
    own[...] = res[0:rows, :] + vec_at[pl.ds(me * rows, rows), :]
    sq_col[zo] = collected(sq_plane, near, n_send, n_recv, 0)
    sq_sends += spread(sq_col, zo, n_send, n_recv, 2 * inner, column)
    both = collected(sq_col, along, n_send, n_recv, 2 * inner) + rows8(vec * vec)
    squares[...] = jnp.broadcast_to(jnp.sum(both, keepdims=True), squares.shape)

    for copy in own_pushes + vec_sends + sq_sends + [last]:
        copy.wait_send()
    for t in range(outer):
        @pl.when(t != zo)
        def _(t=t):
            for copy in forwards(t, t * inner + pi):
                copy.wait_send()
            to_sibling(t * inner + pi).wait_send()
            col_copy(t).wait_send()

        for q in around:
            to_sibling(t * inner + q).wait_send()
    for j, (s, _, _, _) in enumerate(vec_rows):
        @pl.when(me == s)
        def _(j=j):
            for copy in vec_push(j, column, 0):
                copy.wait_send()

        @pl.when(pi == s % inner)
        def _(j=j):
            for copy in vec_push(j, plane, outer - 1):
                copy.wait_send()

    for part, (lo, hi) in enumerate(bounds):
        for copy in sib_copies(part, lo, hi) + plane_copies(part, lo, hi):
            copy.wait_send()
    copy_out.wait()
    copy_ig.wait()


def step(x, dy, shard, wide):
    outer, inner = factors(wide)
    n, rows = x.shape[0], shard.shape[0]
    toks = n * SEQ
    groups = n // GROUP
    padded = (rows + 15) // 16 * 16
    half = padded // 2
    vecs = (USED_ROWS - 1) // rows - VEC_AT // rows + 1
    vm, dma = pltpu.VMEM, pltpu.SemaphoreType.DMA
    sm = vm((2, n * ROWS + 8, LANES), F32)
    tok = vm((toks, 256), BF16)
    tile = (8, LANES)
    scratch = (
        [vm(x.shape, BF16), vm(x.shape, BF16), vm(x.shape, BF16), vm(x.shape, F32)]
        + [vm((wide * rows, LANES), F32)] * 2
        + [sm] * 4
        + [vm((groups * 3 * HJ, 256), BF16)] * 2
        + [vm((groups * HJ, 256), F32)]
        + [vm((toks, 256), F32)] * 2
        + [vm((toks, 1), F32), vm((toks, 256), F32)]
        + [tok, tok, tok, vm((toks, 2 * FF), BF16), tok]
        + [tok, tok, vm((n * ROWS, 3 * 256), BF16)]
        + [vm((256, 256), BF16)] * 4
        + [vm((256, 2 * FF), BF16), vm((FF, 256), BF16), vm((2, FF, 128), F32)]
        + [vm((HJ, 256), BF16), vm((32, 256), BF16), vm((16 * GROUP, 256), BF16), vm((n * ROWS, 256), BF16)]
        + [vm((256, 256), F32), vm((256, 512), F32), vm((256, 256), F32)]
        + [vm((wide, padded, LANES), F32), vm((outer, inner, padded, LANES), F32)]
        + [vm((outer, inner, half, LANES), F32), vm((inner, outer, half, LANES), F32)]
        + [vm((inner - 1, outer, half, LANES), F32)]
        + [vm((outer, half, LANES), F32)] * 2
        + [vm((padded, LANES), F32)]
        + [vm((16, LANES), F32), vm((2 * inner, 16, LANES), F32), vm((outer, 16, LANES), F32)]
        + [vm((wide * rows, LANES), F32)]
        + [vm((2 * inner, *tile), F32), vm((outer, *tile), F32)]
        + [vm((vecs, min(24, padded), LANES), F32)]
        + [dma((4,)), dma((outer - 1,)), dma((outer, inner - 1)), dma((wide,)), dma((wide,)), dma((wide,))]
        + [dma((3, inner))] * 4
        + [dma((outer,)), dma((outer,)), dma((2,))]
        + [dma((2 * inner + outer,))] * 4
        + [dma((vecs, outer + inner - 2)), dma((vecs,))]
    )
    anywhere, vmem = pl.BlockSpec(memory_space=pl.ANY), pl.BlockSpec(memory_space=pltpu.VMEM)
    return pl.pallas_call(
        functools.partial(step_kernel, wide),
        out_shape=(
            jax.ShapeDtypeStruct(x.shape, BF16),
            jax.ShapeDtypeStruct(x.shape, F32),
            jax.ShapeDtypeStruct((rows, LANES), F32),
            jax.ShapeDtypeStruct(tile, F32),
        ),
        in_specs=[anywhere, anywhere, vmem],
        out_specs=(anywhere, anywhere, vmem, vmem),
        scratch_shapes=scratch,
        compiler_params=pltpu.CompilerParams(
            collective_id=0, has_side_effects=True, vmem_limit_bytes=60 * 2**20
        ),
        name="step",
    )(x, dy, shard)


def finish_kernel(*refs):
    big_in, small_in = refs[0:2], refs[2:7]
    big_out, norm_out, small_out = refs[7:9], refs[9], refs[10:15]
    stages, ins, norm, outs = refs[15:17], refs[17:22], refs[22], refs[23:28]
    sem_in, sem_out, sem_small = refs[28:31]
    pieces = []
    for k in range(2):
        size = big_in[k].shape[0] // PIECES
        for p in range(PIECES):
            at = pl.ds(size * p, size)
            pieces.append(
                (
                    pltpu.make_async_copy(big_in[k].at[at], stages[k].at[at], sem_in.at[k, p]),
                    pltpu.make_async_copy(stages[k].at[at], big_out[k].at[at], sem_out.at[k, p]),
                )
            )
    loads = [pltpu.make_async_copy(small_in[k], ins[k], sem_small.at[k]) for k in range(5)]
    for copy in loads:
        copy.start()
    for come, _ in pieces:
        come.start()
    for copy in loads:
        copy.wait()
    own, squares, master, first, second = ins
    clipped, new_master, new_copy, new_first, new_second = outs
    grad_norm = jnp.sqrt(squares[...])
    norm[...] = grad_norm[0:1, 0:1]
    factor = jnp.minimum(1.0, 1.0 / (grad_norm[0:1, :] + 1e-06))
    grad = own[...] * factor
    clipped[...] = grad
    one = 0.5 * first[...] + 0.5 * grad
    two = 0.5 * second[...] + 0.5 * grad * grad
    new_first[...] = one
    new_second[...] = two
    fixed = 1.0 - 0.5**STEP
    old = master[...]
    new = old - 0.05 * ((one / fixed) / (jnp.sqrt(two / fixed) + 1e-08) + 0.1 * old)
    new_master[...] = new
    new_copy[...] = new.astype(BF16)
    stores = [
        pltpu.make_async_copy(src, dst, sem_small.at[5 + k])
        for k, (src, dst) in enumerate(zip((norm, *outs), (norm_out, *small_out)))
    ]
    for copy in stores:
        copy.start()
    for come, go in pieces:
        come.wait()
        go.start()
    for copy in stores:
        copy.wait()
    for _, go in pieces:
        go.wait()


def finish(block_out, input_grad, owned, squares, master, first, second):
    anywhere, vm = pl.BlockSpec(memory_space=pl.ANY), pltpu.VMEM
    one, flat = (1, 1), owned.shape
    kinds = [(flat, F32), (flat, F32), (flat, BF16), (flat, F32), (flat, F32)]
    like = jax.ShapeDtypeStruct
    return pl.pallas_call(
        finish_kernel,
        out_shape=(
            like(block_out.shape, BF16),
            like(input_grad.shape, F32),
            like(one, F32),
            *[like(*kind) for kind in kinds],
        ),
        in_specs=[anywhere] * 7,
        out_specs=(anywhere,) * 8,
        scratch_shapes=[
            vm(block_out.shape, BF16),
            vm(input_grad.shape, F32),
            vm(flat, F32),
            vm(squares.shape, F32),
            vm(flat, F32),
            vm(flat, F32),
            vm(flat, F32),
            vm(one, F32),
            *[vm(*kind) for kind in kinds],
            pltpu.SemaphoreType.DMA((2, PIECES)),
            pltpu.SemaphoreType.DMA((2, PIECES)),
            pltpu.SemaphoreType.DMA((11,)),
        ],
        compiler_params=pltpu.CompilerParams(vmem_limit_bytes=60 * 2**20),
        name="finish",
    )(block_out, input_grad, owned, squares, master, first, second)


def on_device(inputs, cotangent, master, first, second):
    flat = lambda a: a.reshape(-1)
    tall = lambda a: a.reshape(-1, LANES)
    block_out, input_grad, owned, squares = step(
        inputs, cotangent, tall(master), lax.axis_size("wide")
    )
    block_out, input_grad, norm, clipped, new_master, new_copy, new_first, new_second = finish(
        block_out, input_grad, owned, squares, tall(master), tall(first), tall(second)
    )
    return (
        block_out,
        input_grad,
        flat(clipped),
        norm.reshape(()),
        flat(new_master),
        flat(new_copy),
        flat(new_first),
        flat(new_second),
    )


def solution(mesh):
    both, part = P(("wide", "narrow"), None), P("wide")
    return jax.shard_map(
        on_device,
        mesh=mesh,
        in_specs=(both, both, part, part, part),
        out_specs=(both, both, part, P(), part, part, part, part),
        check_vma=False,
    )
```

```python
import functools
import math

import jax
import jax.numpy as jnp
from jax import lax
from jax.experimental import pallas as pl
from jax.experimental.pallas import tpu as pltpu
from jax.sharding import PartitionSpec as P

D = 192
HEADS = 8
HEAD_DIM = 24
FF = 256
SEQ = 34
STEP = 5
ROWS = 40
GROUP = 3
GROWS = GROUP * ROWS
PAIRS = HEADS // 2
PAIR_DIM = 2 * HEAD_DIM
HJ = PAIRS * ROWS
LANES = 128
F32 = jnp.float32
BF16 = jnp.bfloat16
MATS = ((0, D), (288, D), (576, D), (864, D), (1920, FF))
W1_AT = 1152
WIDTH1, WIDTH2, WIDTH3, DW_STEPS = 4, 6, 4, 2
LOCK1, LOCK2 = 8, 4
PIECES = 1
VEC_AT = 2304
USED_ROWS = VEC_AT + 16
QK_ROWS = 576
QKV_ROWS = 864
GELU_C = math.sqrt(2.0 / math.pi)


def nn(a, b):
    return lax.dot_general(a, b, (((1,), (0,)), ((), ())), preferred_element_type=F32)


def nt(a, b):
    return lax.dot_general(a, b, (((1,), (1,)), ((), ())), preferred_element_type=F32)


def tn(a, b):
    return lax.dot_general(a, b, (((0,), (0,)), ((), ())), preferred_element_type=F32)


def low_half(v):
    lane = lax.broadcasted_iota(jnp.int32, v.shape, 1)
    return lane < 64


def load_square(flat, base, rows, tmp, out):
    half = rows // 2
    f0 = flat[pl.ds(base, half, stride=3), :]
    f1 = flat[pl.ds(base + 1, half, stride=3), :]
    f2 = flat[pl.ds(base + 2, half, stride=3), :]
    r1 = pltpu.roll(f1, 64, 1)
    r2 = pltpu.roll(f2, 64, 1)
    left = low_half(f0)
    lo, hi = tmp.at[0], tmp.at[1]
    lo[pl.ds(0, half, stride=2), :] = f0
    hi[pl.ds(0, half, stride=2), :] = jnp.where(left, f1, 0.0)
    lo[pl.ds(1, half, stride=2), :] = jnp.where(left, r1, r2)
    hi[pl.ds(1, half, stride=2), :] = jnp.where(left, r2, 0.0)
    out[0:rows, 0:128] = lo[0:rows, :].astype(BF16)
    out[0:rows, 128:256] = hi[0:rows, :].astype(BF16)
    if rows < 256:
        out[rows:256, :] = jnp.zeros((256 - rows, 256), BF16)


def store_square(val, flat, base, rows, tmp):
    half = rows // 2
    lo, hi = tmp.at[0], tmp.at[1]
    lo[0:rows, :] = val[0:rows, 0:128]
    hi[0:rows, :] = val[0:rows, 128:256]
    e0 = lo[pl.ds(0, half, stride=2), :]
    e1 = hi[pl.ds(0, half, stride=2), :]
    o0 = pltpu.roll(lo[pl.ds(1, half, stride=2), :], 64, 1)
    o1 = pltpu.roll(hi[pl.ds(1, half, stride=2), :], 64, 1)
    left = low_half(e0)
    flat[pl.ds(base, half, stride=3), :] = e0
    flat[pl.ds(base + 1, half, stride=3), :] = jnp.where(left, e1, o0)
    flat[pl.ds(base + 2, half, stride=3), :] = jnp.where(left, o0, o1)


def norm_fwd(x):
    mean = jnp.sum(x, -1, keepdims=True) * (1.0 / D)
    right = x[:, 128:256] - mean
    c = jnp.concatenate([x[:, 0:128] - mean, jnp.where(low_half(right), right, 0.0)], 1)
    var = jnp.sum(c * c, -1, keepdims=True) * (1.0 / D)
    r = lax.rsqrt(var + 1e-05)
    return c * r, r


def norm_back(d, xh, r, g):
    e = d * g
    m1 = jnp.sum(e, -1, keepdims=True) * (1.0 / D)
    m2 = jnp.sum(e * xh, -1, keepdims=True) * (1.0 / D)
    return r * (e - m1 - xh * m2)


def rows8(v):
    return jnp.sum(v.reshape(v.shape[0] // 8, 8, v.shape[1]), 0)


def split_tokens(v, count):
    zero = jnp.zeros((v.shape[0], 256 - D), v.dtype)
    return jnp.concatenate(
        [jnp.concatenate([v[:, D * t : D * (t + 1)], zero], 1) for t in range(count)], 0
    )


def join_tokens(v, n):
    return jnp.concatenate([v[n * t : n * (t + 1), 0:D] for t in range(v.shape[0] // n)], 1)


def factors(wide):
    inner = max(k for k in range(1, int(math.isqrt(wide)) + 1) if wide % k == 0)
    return wide // inner, inner


def remote(src, dst, send, recv, where):
    return pltpu.make_async_remote_copy(
        src_ref=src,
        dst_ref=dst,
        send_sem=send,
        recv_sem=recv,
        device_id=where,
        device_id_type=pl.DeviceIdType.MESH,
    )


def greet(devices):
    for dev in devices:
        pl.semaphore_signal(
            pltpu.get_barrier_semaphore(), inc=1, device_id=dev,
            device_id_type=pl.DeviceIdType.MESH,
        )


def step_kernel(
    wide,
    x_hbm, dy_hbm, shard_hbm, out_hbm, ig_hbm, own_hbm, squares,
    shard, own, x_ref, dy_ref, out_ref, ig_ref, flat, gflat,
    qs, ks, vs, os_, kbd, vbd, psc, xb, xh1, r1, dx2s, h, h2, z, dul, o_t, dal, dyt, dqkv,
    wq, wk, wv, wo, w1, w2, tmp, hm2, parity, sample, hs, acc, acc2, acc3,
    buf, parts, sib_in, plane_in, out_p, col_in, out_c, res, vec_own, vec_plane, vec_col,
    vec_at, sq_plane, sq_col, vec_in,
    io_sem, g_col, g_fw, g_sib, g_recv, g_recv_sib, s_send, s_recv, p_send, p_recv, c_send, c_recv,
    f_sem, v_send, v_recv, n_send, n_recv, vg_send, vg_recv,
):
    n = x_ref.shape[0]
    toks = n * SEQ
    pairs = SEQ // 2
    groups = n // GROUP
    rows = shard.shape[0]
    half = buf.shape[1] // 2
    outer, inner = factors(wide)
    me, core = lax.axis_index("wide"), lax.axis_index("narrow")
    zo, pi = me // inner, lax.rem(me, inner)
    mine = pl.ds(pl.multiple_of(core * half, 8), half)
    theirs = pl.ds(pl.multiple_of((1 - core) * half, 8), half)
    sibling = (me, 1 - core)
    around = [lax.rem(pi + k, inner) for k in range(1, inner)]
    along = [lax.rem(zo + k, outer) for k in range(1, outer)]
    plane = [(zo * inner + q, core) for q in around]
    column = [(t * inner + pi, core) for t in along]
    late = -(-QK_ROWS // (rows * inner))
    first = -(-QKV_ROWS // (rows * inner))
    bounds = ((first, outer), (late, first), (0, late))

    copies_in = [
        pltpu.make_async_copy(x_hbm, x_ref, io_sem.at[0]),
        pltpu.make_async_copy(dy_hbm, dy_ref, io_sem.at[1]),
        pltpu.make_async_copy(shard_hbm, shard, io_sem.at[4]),
    ]

    cross = [(zo * inner + q, 1 - core) for q in around]
    known = plane + cross + column + [sibling]
    greet(known)
    for copy in (copies_in[2], copies_in[0], copies_in[1]):
        copy.start()
    lane = lax.broadcasted_iota(jnp.int32, (80, 256), 1)
    row = lax.broadcasted_iota(jnp.int32, (80, 256), 0)
    for p in range(PAIRS // 2):
        lo = jnp.where(row < ROWS, PAIR_DIM * 2 * p, PAIR_DIM * (2 * p + 1))
        hm2[80 * p : 80 * (p + 1), :] = jnp.where(
            (lane >= lo) & (lane < lo + PAIR_DIM), 1.0, 0.0
        ).astype(BF16)
    lane16 = lax.broadcasted_iota(jnp.int32, (16, 256), 1)
    for b in range(GROUP):
        query = lax.rem(lane16, LANES)
        sample[16 * b : 16 * (b + 1), :] = jnp.where(
            (query >= ROWS * b) & (query < ROWS * (b + 1)), 1.0, 0.0
        ).astype(BF16)
    head = lane16 // HEAD_DIM
    for k in range(2):
        parity[16 * k : 16 * (k + 1), :] = jnp.where(
            (lax.rem(head, 2) == k) & (head < HEADS), 1.0, 0.0
        ).astype(BF16)
    ones_lane = (lax.broadcasted_iota(jnp.int32, (toks, 64), 1) == 0).astype(F32).astype(BF16)
    o_t[:, D:256] = ones_lane
    for ref in (qs, ks, vs, os_):
        ref[...] = jnp.zeros(ref.shape, F32)

    parts[...] = jnp.zeros(parts.shape, F32)
    vec_at[...] = jnp.zeros(vec_at.shape, F32)
    copies_in[2].wait()
    pl.semaphore_wait(pltpu.get_barrier_semaphore(), len(known))
    buf[me, 0:rows, :] = shard[...]
    buf[me, rows:, :] = jnp.zeros((buf.shape[1] - rows, LANES), F32)

    def push(s, send, recvs, where):
        return remote(buf.at[s, mine], buf.at[s, mine], send, recvs.at[s], where)

    def arrived(s, recvs, part):
        remote(buf.at[s, part], buf.at[s, part], g_sib.at[s], recvs.at[s], sibling).wait_recv()

    def forwards(t, s):
        return [push(s, g_fw.at[t, k], g_recv, where) for k, where in enumerate(plane)]

    vec_rows = [
        (s, max(0, VEC_AT - rows * s) // 8 * 8, max(0, VEC_AT - rows * s), min(rows, USED_ROWS - rows * s))
        for s in range(VEC_AT // rows, (USED_ROWS - 1) // rows + 1)
    ]

    def vec_push(j, where, base):
        return [
            remote(vec_in.at[j], vec_in.at[j], vg_send.at[j, base + k], vg_recv.at[j], dev)
            for k, dev in enumerate(where)
        ]

    def vec_arrived(j):
        remote(vec_in.at[j], vec_in.at[j], vg_send.at[j, 0], vg_recv.at[j], sibling).wait_recv()

    for j, (s, a0, _, end) in enumerate(vec_rows):
        @pl.when(me == s)
        def _(j=j, a0=a0, end=end):
            vec_in[j, 0 : end - a0, :] = shard[a0:end, :]
            for copy in vec_push(j, column, 0) + vec_push(j, plane, outer - 1):
                copy.start()

    own_pushes = [push(me, g_col.at[k], g_recv, where) for k, where in enumerate(column)]
    own_pushes += forwards(zo, me)
    for copy in own_pushes:
        copy.start()

    def to_sibling(s):
        return push(s, g_sib.at[s], g_recv_sib, sibling)

    def forward_level(t):
        s = t * inner + pi

        @pl.when(t != zo)
        def _():
            arrived(s, g_recv, mine)
            for copy in forwards(t, s):
                copy.start()
            to_sibling(s).start()

    def pass_level(t):
        for q in around:
            s = t * inner + q
            arrived(s, g_recv, mine)
            to_sibling(s).start()

    def whole_shard(s):
        @pl.when(s != me)
        def _():
            arrived(s, g_recv_sib, theirs)

    def unpack(s):
        flat[rows * s : rows * (s + 1), :] = buf[s, 0:rows, :]

    for j, (s, _, _, _) in enumerate(vec_rows):
        @pl.when((me != s) & (pi == s % inner))
        def _(j=j):
            vec_arrived(j)
            for copy in vec_push(j, plane, outer - 1):
                copy.start()

    for t in range(outer):
        forward_level(t)

    def tokens_of(ref, t, count):
        return split_tokens(
            ref[:, pl.ds(pl.multiple_of(t * D, 128), count * D)].astype(F32), count
        )

    def put_tokens(ref, t, val):
        for half in range(2):
            for k in range(val.shape[0] // n):
                ref.at[half][pl.ds(t + k, n, stride=ROWS), :] = val[
                    n * k : n * (k + 1), 128 * half : 128 * (half + 1)
                ]

    def get_tokens(ref, t, count):
        return jnp.concatenate(
            [
                jnp.concatenate(
                    [ref.at[half][pl.ds(t + k, n, stride=ROWS), :] for half in range(2)], 1
                )
                for k in range(count)
            ],
            0,
        )

    def over_token_chunks(body, width, carry, hook=lambda i: None):
        whole = pairs // width

        def step(i, c):
            hook(i)
            return body(i * (2 * width), 2 * width, c)

        carry = lax.fori_loop(0, whole, step, carry)
        if pairs % width:
            carry = body(whole * 2 * width, 2 * (pairs % width), carry)
        return carry

    def get_rows(ref, start, count):
        return jnp.concatenate([ref[0, pl.ds(start, count), :], ref[1, pl.ds(start, count), :]], 1)

    def put_rows(ref, start, val):
        for half in range(2):
            ref[half, pl.ds(start, val.shape[0]), :] = val[:, 128 * half : 128 * (half + 1)]

    def rows_at(t, count):
        return pl.ds(pl.multiple_of(t * n, 32), count * n)

    copies_in[0].wait()
    for j, (s, a0, begin, end) in enumerate(vec_rows):
        @pl.when(pi != s % inner)
        def _(j=j):
            vec_arrived(j)

        flat[rows * s + begin : rows * s + end, :] = vec_in[j, begin - a0 : end - a0, :]

    ones3 = (lax.broadcasted_iota(jnp.int32, (1, 64), 1) < 3).astype(F32)

    def vec(k):
        a = VEC_AT + 3 * (k // 2)
        zero = ones3 if k in (1, 6) else jnp.zeros((1, 64), F32)
        if k % 2 == 0:
            return jnp.concatenate([flat[a : a + 1, :], flat[a + 1 : a + 2, 0:64], zero], 1)
        return jnp.concatenate([flat[a + 1 : a + 2, 64:128], flat[a + 2 : a + 3, :], zero], 1)

    g1, n1, bq, bv, bo, g2, n2, b2 = [vec(k) for k in range(8)]
    b1 = jnp.concatenate([flat[VEC_AT + 12 + c : VEC_AT + 13 + c, :] for c in range(4)], 1)

    def norm1(t, count, carry):
        at = rows_at(t, count)
        x = tokens_of(x_ref, t, count)
        xh, r = norm_fwd(x)
        xh1[at, :] = xh
        r1[at, :] = r
        hb = (xh * g1 + n1).astype(BF16)
        h[at, :] = hb
        put_tokens(os_, t, hb.astype(F32))
        xb[at, :] = x + bo
        return carry

    over_token_chunks(norm1, WIDTH1, 0)

    def take_dy(t, count, db2):
        dy = tokens_of(dy_ref, t, count)
        dyt[rows_at(t, count), :] = dy.astype(BF16)
        return db2 + rows8(dy)

    zero = jnp.zeros((8, 256), F32)
    copies_in[1].wait()
    db2 = over_token_chunks(take_dy, WIDTH1, zero)

    def bias_rows(b):
        row = lax.broadcasted_iota(jnp.int32, (16, b.shape[1]), 0)
        out = jnp.zeros((16, b.shape[1]), F32)
        for k in range(3):
            part = b.astype(BF16).astype(F32)
            out = jnp.where(row == k, part, out)
            b = b - part
        return out.astype(BF16)

    half_groups = LOCK2 * GROWS

    @pl.loop(0, groups // LOCK2)
    def _(i):
        at = pl.ds(pl.multiple_of(i * half_groups, 16), half_groups)
        hs[at, :] = get_rows(os_, pl.multiple_of(i * half_groups, 8), half_groups).astype(BF16)

    def take_levels(lo, hi):
        for s in range(lo * inner, hi * inner):
            whole_shard(s)
            unpack(s)

    for t in range(late):
        pass_level(t)
    take_levels(0, late)
    for (base, count), ref in zip(MATS[0:2], (wq, wk)):
        load_square(flat, base, count, tmp, ref)
    wq[D : D + 16, :] = bias_rows(bq)

    def pass_v(i):
        @pl.when(i == 1)
        def _():
            for t in range(late, first):
                pass_level(t)

    def dense_qk(t, count, carry):
        hb = h[rows_at(t, count), :]
        put_tokens(qs, t, nn(hb, wq[...]).astype(BF16).astype(F32))
        put_tokens(ks, t, nn(hb, wk[...]).astype(BF16).astype(F32))
        return carry

    over_token_chunks(dense_qk, WIDTH1, 0, pass_v)
    take_levels(late, first)
    load_square(flat, MATS[2][0], MATS[2][1], tmp, wv)
    wv[D : D + 16, :] = bias_rows(bv)

    def dense_v(t, count, carry):
        hb = h[rows_at(t, count), :]
        put_tokens(vs, t, nn(hb, wv[...]).astype(BF16).astype(F32))
        return carry

    over_token_chunks(dense_v, WIDTH1, 0)

    lane3 = lax.rem(lax.broadcasted_iota(jnp.int32, (1, 256), 1), LANES)
    odd_head = lax.rem(lax.broadcasted_iota(jnp.int32, (1, 256), 1) // HEAD_DIM, 2) == 1

    def squeeze(v):
        return jnp.where(
            lane3 < ROWS, v[0:HJ], jnp.where(lane3 < 2 * ROWS, v[HJ : 2 * HJ], v[2 * HJ : 3 * HJ])
        ).reshape(PAIRS, ROWS, 256)

    def by_parity(v):
        v3 = v.reshape(8, 16, 256)
        return jnp.concatenate(
            [(v3 * parity[16 * k : 16 * (k + 1), :][None]).reshape(LANES, 256) for k in range(2)], 0
        )

    def per_query(left, right, b):
        rows2 = jnp.concatenate([left[128 * k + ROWS * b : 128 * k + ROWS * (b + 1)] for k in range(2)], 0)
        both = nn(rows2.astype(BF16), right)
        return jnp.where(odd_head, both[ROWS : 2 * ROWS], both[0:ROWS])

    jrow = lax.broadcasted_iota(jnp.int32, (1, ROWS - 32, 256), 1)
    cexp = math.log2(math.e) / math.sqrt(HEAD_DIM)
    scale = 1.0 / math.sqrt(HEAD_DIM)

    def attn(i, carry):
        @pl.when(i == 1)
        def _():
            for t in range(first, outer):
                pass_level(t)

        r0 = pl.multiple_of(i * (LOCK1 * GROWS), 8)
        base0 = pl.multiple_of(i * (LOCK1 * 3 * HJ), 32)
        p0 = pl.multiple_of(i * (LOCK1 * HJ), 32)
        sets = range(LOCK1)
        qg = [by_parity(get_rows(qs, r0 + GROWS * k, LANES).astype(BF16)) for k in sets]
        for k in sets:
            for src, dst in ((ks, kbd), (vs, vbd)):
                for b in range(GROUP):
                    one = get_rows(src, r0 + GROWS * k + ROWS * b, ROWS)
                    two = jnp.concatenate([one, one], 0).astype(BF16)
                    for p in range(PAIRS // 2):
                        dst[pl.ds(base0 + HJ * (3 * k + b) + 80 * p, 80), :] = (
                            two * hm2[80 * p : 80 * (p + 1), :]
                        )
        st = [squeeze(nt(kbd[pl.ds(base0 + 3 * HJ * k, 3 * HJ), :], qg[k])) for k in sets]
        st = [
            jnp.concatenate([v[:, 0:32], jnp.where(jrow < SEQ - 32, v[:, 32:ROWS], -1e30)], 1)
            for v in st
        ]
        m = [jnp.max(v, 1, keepdims=True) for v in st]
        e = [jnp.exp2((st[k] - m[k]) * cexp) for k in sets]
        l = [1.0 / jnp.sum(v, 1, keepdims=True) for v in e]
        p = [(e[k] * l[k]).reshape(HJ, 256) for k in sets]
        for k in sets:
            psc[pl.ds(p0 + HJ * k, HJ), :] = p[k]
        pt = [v.T for v in p]
        for b in range(GROUP):
            for k in sets:
                ob = per_query(pt[k], vbd[pl.ds(base0 + HJ * (3 * k + b), HJ), :], b)
                put_rows(os_, r0 + GROWS * k + ROWS * b, ob.astype(BF16).astype(F32)[0:SEQ])
        return carry

    lax.fori_loop(0, groups // LOCK1, attn, 0)

    take_levels(first, outer)
    for (base, count), ref in zip(MATS[3:5], (wo, w2)):
        load_square(flat, base, count, tmp, ref)
    for c in range(4):
        part = flat[pl.ds(W1_AT + c, D, stride=4), :]
        w1[0:D, 128 * c : 128 * (c + 1)] = (part if c < 2 else 0.5 * part).astype(BF16)
    w1[D : D + 16, :] = bias_rows(jnp.concatenate([b1[:, 0:FF], 0.5 * b1[:, FF:]], 1))
    w1[D + 16 : 256, :] = jnp.zeros((240 - D, 2 * FF), BF16)
    def dense2(t0, count, carry):
        dg2, dn2 = carry
        at = rows_at(t0, count)
        o = get_tokens(os_, t0, count).astype(BF16)
        o_t[at, 0:D] = o[:, 0:D]
        x2 = xb[at, :] + nn(o, wo[...])
        xh, r = norm_fwd(x2)
        hb = (xh * g2 + n2).astype(BF16)
        h2[at, :] = hb
        u = nn(hb, w1[...])
        gate, up = u[:, :FF], u[:, FF:]
        sq = gate * gate
        t = jnp.tanh(gate * (GELU_C + (GELU_C * 0.044715) * sq))
        t1 = 1.0 + t
        act = gate * t1
        zb = (act * up).astype(BF16)
        z[at, :] = zb
        y = x2 + nn(zb, w2[...]) + b2
        out_ref[:, pl.ds(pl.multiple_of(t0 * D, 128), count * D)] = join_tokens(y, n).astype(BF16)
        dyb = dyt[at, :]
        dyf = dyb.astype(F32)
        dz = nt(dyb, w2[...])
        slope = t1 + act * (1.0 - t) * (GELU_C + (3 * GELU_C * 0.044715) * sq)
        du = jnp.concatenate([(dz * up * slope).astype(BF16), (dz * act).astype(BF16)], 1)
        dul[at, :] = du
        dh = nt(du, w1[...])
        dx2 = dyf + norm_back(dh, xh, r, g2)
        dx2s[at, :] = dx2
        da = dx2.astype(BF16)
        dal[at, :] = da
        put_tokens(os_, t0, nt(da, wo[...]).astype(BF16).astype(F32))
        acc[...] += tn(zb, dyb)
        acc2[...] += tn(hb, du)
        acc3[...] += tn(o_t[at, :], da)
        return dg2 + rows8(dh * xh), dn2 + rows8(dh)

    for ref in (acc, acc2, acc3):
        ref[...] = jnp.zeros(ref.shape, F32)
    dg2, dn2 = over_token_chunks(dense2, WIDTH2, (zero, zero))

    copy_out = pltpu.make_async_copy(out_ref, out_hbm, io_sem.at[2])
    copy_out.start()

    def total(v):
        return jnp.sum(v, 0, keepdims=True)

    def over_tokens(*products):
        for acc, _, _ in products:
            acc[...] = jnp.zeros(acc.shape, F32)
        size = products[0][1].shape[0] // DW_STEPS

        @pl.loop(0, DW_STEPS)
        def _(i):
            at = pl.ds(pl.multiple_of(i * size, 16), size)
            for acc, a, b in products:
                acc[...] += tn(a[at, :], b[at, :])

    store_square(acc[...], gflat, 1920, FF, tmp)
    for c in range(4):
        part = acc2[0 : D + 8, 128 * c : 128 * (c + 1)]
        part = part if c < 2 else 0.5 * part
        gflat[pl.ds(W1_AT + c, D, stride=4), :] = part[0:D]
        vec_own[12 + c : 13 + c, :] = part[D : D + 1]
    store_square(acc3[...], gflat, 864, D, tmp)
    dbo = acc3[D : D + 1, :]

    def pack(lo, hi):
        for s in range(lo * inner, hi * inner):
            stop = min(rows * (s + 1), VEC_AT)
            if stop > rows * s:
                parts[s // inner, s % inner, 0 : stop - rows * s, :] = gflat[rows * s : stop, :]

    places = around + [pi]

    def sib_copies(part, lo, hi):
        return [
            remote(
                parts.at[lo:hi, q, theirs], sib_in.at[lo:hi, q],
                s_send.at[part, k], s_recv.at[part, q], sibling,
            )
            for k, q in enumerate(places)
        ]

    def plane_copies(part, lo, hi):
        return [
            remote(
                out_p.at[k, lo:hi], plane_in.at[pi, lo:hi],
                p_send.at[part, k], p_recv.at[part, pi], plane[k],
            )
            for k in range(inner - 1)
        ]

    def col_copy(t):
        return remote(
            out_c.at[t], col_in.at[zo], c_send.at[t], c_recv.at[zo], (t * inner + pi, core)
        )

    def sum_cores(part):
        lo, hi = bounds[part]
        sends = plane_copies(part, lo, hi)
        for k, q in enumerate(places):
            remote(
                sib_in.at[lo:hi, q], sib_in.at[lo:hi, q],
                s_send.at[part, k], s_recv.at[part, q], sibling,
            ).wait_recv()
            both = parts[lo:hi, q, mine, :] + sib_in[lo:hi, q]
            if k < inner - 1:
                out_p[k, lo:hi] = both
                sends[k].start()
            else:
                plane_in[pi, lo:hi] = both

    def sum_plane(part):
        lo, hi = bounds[part]
        for k, q in enumerate(around):
            remote(
                plane_in.at[q, lo:hi], plane_in.at[q, lo:hi],
                p_send.at[part, k], p_recv.at[part, q], sibling,
            ).wait_recv()
        for t in range(lo, hi):
            line = plane_in[0, t]
            for q in range(1, inner):
                line = line + plane_in[q, t]
            out_c[t] = line

            @pl.when(t != zo)
            def _():
                col_copy(t).start()

    def send_cores(part):
        pack(*bounds[part])
        for copy in sib_copies(part, *bounds[part]):
            copy.start()

    send_cores(0)

    def by_sample(v):
        v = v.reshape(HJ, 256).astype(BF16).reshape(HJ // 16, 16, 256)
        return jnp.concatenate(
            [
                (v * sample[16 * b : 16 * (b + 1), :][None]).reshape(HJ, 256)
                for b in range(GROUP)
            ],
            0,
        )

    pair_lane = lax.broadcasted_iota(jnp.int32, (1, LANES), 1)

    def own_lanes(v):
        v = v.reshape(GROUP, PAIRS, ROWS, 256)
        out = []
        for b in range(GROUP):
            lo = jnp.where(pair_lane < PAIR_DIM, v[b, 0, :, 0:128], v[b, 1, :, 0:128])
            lo = jnp.where(pair_lane < 2 * PAIR_DIM, lo, v[b, 2, :, 0:128])
            hi = jnp.where(
                pair_lane < 3 * PAIR_DIM - 128, v[b, 2, :, 128:256], v[b, 3, :, 128:256]
            )
            out.append(jnp.concatenate([lo, hi], 1))
        return jnp.concatenate(out, 0)

    def probs(at):
        return psc[pl.ds(at, HJ), :].reshape(PAIRS, ROWS, 256)

    def attn_back_v(i, carry):
        @pl.when(i == 3)
        def _():
            sum_cores(0)

        r0 = pl.multiple_of(i * (LOCK2 * GROWS), 8)
        p0 = pl.multiple_of(i * (LOCK2 * HJ), 32)
        out = []
        for k in range(LOCK2):
            dg = by_parity(get_rows(os_, r0 + GROWS * k, LANES).astype(BF16))
            out.append(own_lanes(nn(by_sample(probs(p0 + HJ * k)), dg)))
        out = jnp.concatenate(out, 0).astype(BF16)
        dqkv[pl.ds(pl.multiple_of(i * half_groups, 16), half_groups), 512:768] = out
        put_rows(vs, r0, out.astype(F32))
        return carry

    lax.fori_loop(0, groups // LOCK2, attn_back_v, 0)

    over_tokens((acc, hs, dqkv.at[:, 512:768]))
    store_square(acc[...], gflat, 576, D, tmp)
    dbv = acc[D : D + 1, :]
    send_cores(1)

    def attn_back(i, carry):
        @pl.when(i == 1)
        def _():
            sum_cores(1)

        r0 = pl.multiple_of(i * (LOCK2 * GROWS), 8)
        base0 = pl.multiple_of(i * (LOCK2 * 3 * HJ), 32)
        p0 = pl.multiple_of(i * (LOCK2 * HJ), 32)
        sets = range(LOCK2)
        qg = [by_parity(get_rows(qs, r0 + GROWS * k, LANES).astype(BF16)) for k in sets]
        dg = [by_parity(get_rows(os_, r0 + GROWS * k, LANES).astype(BF16)) for k in sets]
        dp = [squeeze(nt(vbd[pl.ds(base0 + 3 * HJ * k, 3 * HJ), :], dg[k])) for k in sets]
        p = [probs(p0 + HJ * k) for k in sets]
        t = [jnp.sum(p[k] * dp[k], 1, keepdims=True) for k in sets]
        ds = [p[k] * (dp[k] - t[k]) for k in sets]
        dst = [v.reshape(HJ, 256).T for v in ds]
        dk = [own_lanes(nn(by_sample(ds[k]), qg[k])) * scale for k in sets]
        dq = [
            per_query(dst[k], kbd[pl.ds(base0 + HJ * (3 * k + b), HJ), :], b) * scale
            for k in sets
            for b in range(GROUP)
        ]
        at = pl.ds(pl.multiple_of(i * half_groups, 16), half_groups)
        for col, ref, val in ((0, qs, dq), (256, ks, dk)):
            val = jnp.concatenate(val, 0).astype(BF16)
            dqkv[at, col : col + 256] = val
            put_rows(ref, r0, val.astype(F32))
        return carry

    lax.fori_loop(0, groups // LOCK2, attn_back, 0)

    over_tokens((acc2, hs, dqkv.at[:, 0:512]))
    for k in range(2):
        store_square(acc2[:, 256 * k : 256 * (k + 1)], gflat, 288 * k, D, tmp)
    send_cores(2)
    sum_plane(0)

    def dense3(t0, count, carry):
        dg1, dn1 = carry
        at = rows_at(t0, count)
        dh = (
            nt(get_tokens(qs, t0, count).astype(BF16), wq[...])
            + nt(get_tokens(ks, t0, count).astype(BF16), wk[...])
            + nt(get_tokens(vs, t0, count).astype(BF16), wv[...])
        )
        xh = xh1[at, :]
        ig = dx2s[at, :] + norm_back(dh, xh, r1[at, :], g1)
        ig_ref[:, pl.ds(pl.multiple_of(t0 * D, 128), count * D)] = join_tokens(ig, n)
        return dg1 + rows8(dh * xh), dn1 + rows8(dh)

    def hook3(i):
        @pl.when(i == 1)
        def _():
            sum_cores(2)
            sum_plane(1)

    dg1, dn1 = over_token_chunks(dense3, WIDTH3, (zero, zero), hook3)

    vecs = [
        total(dg1), total(dn1), acc2[D : D + 1, 0:256], dbv,
        dbo, total(dg2), total(dn2), total(db2),
    ]
    for k in range(4):
        a, b = vecs[2 * k], vecs[2 * k + 1]
        vec_own[3 * k : 3 * k + 1, :] = a[:, 0:128]
        vec_own[3 * k + 1 : 3 * k + 2, :] = jnp.concatenate([a[:, 128:192], b[:, 0:64]], 1)
        vec_own[3 * k + 2 : 3 * k + 3, :] = b[:, 64:192]
    copy_ig = pltpu.make_async_copy(ig_ref, ig_hbm, io_sem.at[3])
    copy_ig.start()

    def spread(slots, at, sends, recvs, base, where):
        out = [
            remote(slots.at[at], slots.at[at], sends.at[base + k], recvs.at[base + at], dev)
            for k, dev in enumerate(where)
        ]
        for copy in out:
            copy.start()
        return out

    def collected(slots, others, sends, recvs, base):
        for k, q in enumerate(others):
            remote(
                slots.at[q], slots.at[q], sends.at[base + k], recvs.at[base + q], sibling
            ).wait_recv()
        return jnp.sum(slots[...], 0)

    slot = 2 * pi + core
    near = [2 * q + core for q in around] + [2 * q + 1 - core for q in around] + [2 * pi + 1 - core]
    disc = plane + cross + [sibling]
    vec_plane[slot] = vec_own[...]
    vec_sends = spread(vec_plane, slot, v_send, v_recv, 0, disc)
    sum_plane(2)
    vec_col[zo] = collected(vec_plane, near, v_send, v_recv, 0)
    vec_sends += spread(vec_col, zo, v_send, v_recv, 2 * inner, column)

    col_in[zo] = out_c[zo]
    for t in along:
        remote(col_in.at[t], col_in.at[t], c_send.at[t], c_recv.at[t], sibling).wait_recv()
    line = col_in[0]
    for t in range(1, outer):
        line = line + col_in[t]
    res[mine, :] = line
    last = remote(res.at[mine], res.at[mine], f_sem.at[0], f_sem.at[1], sibling)
    last.start()
    sq_plane[slot] = rows8(line * line)
    sq_sends = spread(sq_plane, slot, n_send, n_recv, 0, disc)
    vec = collected(vec_col, along, v_send, v_recv, 2 * inner)
    vec_at[VEC_AT:USED_ROWS, :] = vec
    remote(res.at[theirs], res.at[theirs], f_sem.at[0], f_sem.at[1], sibling).wait_recv()
    own[...] = res[0:rows, :] + vec_at[pl.ds(me * rows, rows), :]
    copy_own = pltpu.make_async_copy(own, own_hbm, io_sem.at[5])
    copy_own.start()
    sq_col[zo] = collected(sq_plane, near, n_send, n_recv, 0)
    sq_sends += spread(sq_col, zo, n_send, n_recv, 2 * inner, column)
    both = collected(sq_col, along, n_send, n_recv, 2 * inner) + rows8(vec * vec)
    squares[...] = jnp.broadcast_to(jnp.sum(both, keepdims=True), squares.shape)

    for copy in own_pushes + vec_sends + sq_sends + [last]:
        copy.wait_send()
    for t in range(outer):
        @pl.when(t != zo)
        def _(t=t):
            for copy in forwards(t, t * inner + pi):
                copy.wait_send()
            to_sibling(t * inner + pi).wait_send()
            col_copy(t).wait_send()

        for q in around:
            to_sibling(t * inner + q).wait_send()
    for j, (s, _, _, _) in enumerate(vec_rows):
        @pl.when(me == s)
        def _(j=j):
            for copy in vec_push(j, column, 0):
                copy.wait_send()

        @pl.when(pi == s % inner)
        def _(j=j):
            for copy in vec_push(j, plane, outer - 1):
                copy.wait_send()

    for part, (lo, hi) in enumerate(bounds):
        for copy in sib_copies(part, lo, hi) + plane_copies(part, lo, hi):
            copy.wait_send()
    copy_out.wait()
    copy_ig.wait()
    copy_own.wait()


def step(x, dy, shard, wide):
    outer, inner = factors(wide)
    n, rows = x.shape[0], shard.shape[0]
    toks = n * SEQ
    groups = n // GROUP
    padded = (rows + 15) // 16 * 16
    half = padded // 2
    vecs = (USED_ROWS - 1) // rows - VEC_AT // rows + 1
    vm, dma = pltpu.VMEM, pltpu.SemaphoreType.DMA
    sm = vm((2, n * ROWS + 8, LANES), F32)
    tok = vm((toks, 256), BF16)
    tile = (8, LANES)
    scratch = (
        [vm((rows, LANES), F32)] * 2
        + [vm(x.shape, BF16), vm(x.shape, BF16), vm(x.shape, BF16), vm(x.shape, F32)]
        + [vm((wide * rows, LANES), F32)] * 2
        + [sm] * 4
        + [vm((groups * 3 * HJ, 256), BF16)] * 2
        + [vm((groups * HJ, 256), F32)]
        + [vm((toks, 256), F32)] * 2
        + [vm((toks, 1), F32), vm((toks, 256), F32)]
        + [tok, tok, tok, vm((toks, 2 * FF), BF16), tok]
        + [tok, tok, vm((n * ROWS, 3 * 256), BF16)]
        + [vm((256, 256), BF16)] * 4
        + [vm((256, 2 * FF), BF16), vm((FF, 256), BF16), vm((2, FF, 128), F32)]
        + [vm((HJ, 256), BF16), vm((32, 256), BF16), vm((16 * GROUP, 256), BF16), vm((n * ROWS, 256), BF16)]
        + [vm((256, 256), F32), vm((256, 512), F32), vm((256, 256), F32)]
        + [vm((wide, padded, LANES), F32), vm((outer, inner, padded, LANES), F32)]
        + [vm((outer, inner, half, LANES), F32), vm((inner, outer, half, LANES), F32)]
        + [vm((inner - 1, outer, half, LANES), F32)]
        + [vm((outer, half, LANES), F32)] * 2
        + [vm((padded, LANES), F32)]
        + [vm((16, LANES), F32), vm((2 * inner, 16, LANES), F32), vm((outer, 16, LANES), F32)]
        + [vm((wide * rows, LANES), F32)]
        + [vm((2 * inner, *tile), F32), vm((outer, *tile), F32)]
        + [vm((vecs, min(24, padded), LANES), F32)]
        + [dma((6,)), dma((outer - 1,)), dma((outer, inner - 1)), dma((wide,)), dma((wide,)), dma((wide,))]
        + [dma((3, inner))] * 4
        + [dma((outer,)), dma((outer,)), dma((2,))]
        + [dma((2 * inner + outer,))] * 4
        + [dma((vecs, outer + inner - 2)), dma((vecs,))]
    )
    anywhere, vmem = pl.BlockSpec(memory_space=pl.ANY), pl.BlockSpec(memory_space=pltpu.VMEM)
    return pl.pallas_call(
        functools.partial(step_kernel, wide),
        out_shape=(
            jax.ShapeDtypeStruct(x.shape, BF16),
            jax.ShapeDtypeStruct(x.shape, F32),
            jax.ShapeDtypeStruct((rows, LANES), F32),
            jax.ShapeDtypeStruct(tile, F32),
        ),
        in_specs=[anywhere] * 3,
        out_specs=(anywhere, anywhere, anywhere, vmem),
        scratch_shapes=scratch,
        compiler_params=pltpu.CompilerParams(
            collective_id=0, has_side_effects=True, vmem_limit_bytes=60 * 2**20
        ),
        name="step",
    )(x, dy, shard)


def finish_kernel(*refs):
    big_in, small_in = refs[0:2], refs[2:7]
    big_out, norm_out, small_out = refs[7:9], refs[9], refs[10:15]
    stages, ins, norm, outs = refs[15:17], refs[17:22], refs[22], refs[23:28]
    sem_in, sem_out, sem_small = refs[28:31]
    pieces = []
    for k in range(2):
        size = big_in[k].shape[0] // PIECES
        for p in range(PIECES):
            at = pl.ds(size * p, size)
            pieces.append(
                (
                    pltpu.make_async_copy(big_in[k].at[at], stages[k].at[at], sem_in.at[k, p]),
                    pltpu.make_async_copy(stages[k].at[at], big_out[k].at[at], sem_out.at[k, p]),
                )
            )
    loads = [pltpu.make_async_copy(small_in[k], ins[k], sem_small.at[k]) for k in range(5)]
    for copy in loads:
        copy.start()
    for come, _ in pieces:
        come.start()
    for copy in loads:
        copy.wait()
    own, squares, master, first, second = ins
    clipped, new_master, new_copy, new_first, new_second = outs
    grad_norm = jnp.sqrt(squares[...])
    norm[...] = grad_norm[0:1, 0:1]
    factor = jnp.minimum(1.0, 1.0 / (grad_norm[0:1, :] + 1e-06))
    grad = own[...] * factor
    clipped[...] = grad
    one = 0.5 * first[...] + 0.5 * grad
    two = 0.5 * second[...] + 0.5 * grad * grad
    new_first[...] = one
    new_second[...] = two
    fixed = 1.0 - 0.5**STEP
    old = master[...]
    new = old - 0.05 * ((one / fixed) / (jnp.sqrt(two / fixed) + 1e-08) + 0.1 * old)
    new_master[...] = new
    new_copy[...] = new.astype(BF16)
    stores = [
        pltpu.make_async_copy(src, dst, sem_small.at[5 + k])
        for k, (src, dst) in enumerate(zip((norm, *outs), (norm_out, *small_out)))
    ]
    for copy in stores:
        copy.start()
    for come, go in pieces:
        come.wait()
        go.start()
    for copy in stores:
        copy.wait()
    for _, go in pieces:
        go.wait()


def finish(block_out, input_grad, owned, squares, master, first, second):
    anywhere, vm = pl.BlockSpec(memory_space=pl.ANY), pltpu.VMEM
    one, flat = (1, 1), owned.shape
    kinds = [(flat, F32), (flat, F32), (flat, BF16), (flat, F32), (flat, F32)]
    like = jax.ShapeDtypeStruct
    return pl.pallas_call(
        finish_kernel,
        out_shape=(
            like(block_out.shape, BF16),
            like(input_grad.shape, F32),
            like(one, F32),
            *[like(*kind) for kind in kinds],
        ),
        in_specs=[anywhere] * 7,
        out_specs=(anywhere,) * 8,
        scratch_shapes=[
            vm(block_out.shape, BF16),
            vm(input_grad.shape, F32),
            vm(flat, F32),
            vm(squares.shape, F32),
            vm(flat, F32),
            vm(flat, F32),
            vm(flat, F32),
            vm(one, F32),
            *[vm(*kind) for kind in kinds],
            pltpu.SemaphoreType.DMA((2, PIECES)),
            pltpu.SemaphoreType.DMA((2, PIECES)),
            pltpu.SemaphoreType.DMA((11,)),
        ],
        compiler_params=pltpu.CompilerParams(vmem_limit_bytes=60 * 2**20),
        name="finish",
    )(block_out, input_grad, owned, squares, master, first, second)


def on_device(inputs, cotangent, master, first, second):
    flat = lambda a: a.reshape(-1)
    tall = lambda a: a.reshape(-1, LANES)
    block_out, input_grad, owned, squares = step(
        inputs, cotangent, tall(master), lax.axis_size("wide")
    )
    block_out, input_grad, norm, clipped, new_master, new_copy, new_first, new_second = finish(
        block_out, input_grad, owned, squares, tall(master), tall(first), tall(second)
    )
    return (
        block_out,
        input_grad,
        flat(clipped),
        norm.reshape(()),
        flat(new_master),
        flat(new_copy),
        flat(new_first),
        flat(new_second),
    )


def solution(mesh):
    both, part = P(("wide", "narrow"), None), P("wide")
    return jax.shard_map(
        on_device,
        mesh=mesh,
        in_specs=(both, both, part, part, part),
        out_specs=(both, both, part, P(), part, part, part, part),
        check_vma=False,
    )
```

```python
import functools
import math

import jax
import jax.numpy as jnp
from jax import lax
from jax.experimental import pallas as pl
from jax.experimental.pallas import tpu as pltpu
from jax.sharding import PartitionSpec as P

D = 192
HEADS = 8
HEAD_DIM = 24
FF = 256
SEQ = 34
STEP = 5
ROWS = 40
GROUP = 3
GROWS = GROUP * ROWS
PAIRS = HEADS // 2
PAIR_DIM = 2 * HEAD_DIM
HJ = PAIRS * ROWS
LANES = 128
F32 = jnp.float32
BF16 = jnp.bfloat16
MATS = ((0, D), (288, D), (576, D), (864, D), (1920, FF))
W1_AT = 1152
WIDTH1, WIDTH2, WIDTH3, DW_STEPS = 8, 6, 3, 2
LOCK1, LOCK2 = 8, 4
PIECES = 1
VEC_AT = 2304
USED_ROWS = VEC_AT + 16
QK_ROWS = 576
QKV_ROWS = 864
GELU_C = math.sqrt(2.0 / math.pi)


def nn(a, b):
    return lax.dot_general(a, b, (((1,), (0,)), ((), ())), preferred_element_type=F32)


def nt(a, b):
    return lax.dot_general(a, b, (((1,), (1,)), ((), ())), preferred_element_type=F32)


def tn(a, b):
    return lax.dot_general(a, b, (((0,), (0,)), ((), ())), preferred_element_type=F32)


def low_half(v):
    lane = lax.broadcasted_iota(jnp.int32, v.shape, 1)
    return lane < 64


def load_square(flat, base, rows, tmp, out):
    half = rows // 2
    f0 = flat[pl.ds(base, half, stride=3), :]
    f1 = flat[pl.ds(base + 1, half, stride=3), :]
    f2 = flat[pl.ds(base + 2, half, stride=3), :]
    r1 = pltpu.roll(f1, 64, 1)
    r2 = pltpu.roll(f2, 64, 1)
    left = low_half(f0)
    lo, hi = tmp.at[0], tmp.at[1]
    lo[pl.ds(0, half, stride=2), :] = f0
    hi[pl.ds(0, half, stride=2), :] = jnp.where(left, f1, 0.0)
    lo[pl.ds(1, half, stride=2), :] = jnp.where(left, r1, r2)
    hi[pl.ds(1, half, stride=2), :] = jnp.where(left, r2, 0.0)
    out[0:rows, 0:128] = lo[0:rows, :].astype(BF16)
    out[0:rows, 128:256] = hi[0:rows, :].astype(BF16)
    if rows < 256:
        out[rows:256, :] = jnp.zeros((256 - rows, 256), BF16)


def store_square(val, flat, base, rows, tmp):
    half = rows // 2
    lo, hi = tmp.at[0], tmp.at[1]
    lo[0:rows, :] = val[0:rows, 0:128]
    hi[0:rows, :] = val[0:rows, 128:256]
    e0 = lo[pl.ds(0, half, stride=2), :]
    e1 = hi[pl.ds(0, half, stride=2), :]
    o0 = pltpu.roll(lo[pl.ds(1, half, stride=2), :], 64, 1)
    o1 = pltpu.roll(hi[pl.ds(1, half, stride=2), :], 64, 1)
    left = low_half(e0)
    flat[pl.ds(base, half, stride=3), :] = e0
    flat[pl.ds(base + 1, half, stride=3), :] = jnp.where(left, e1, o0)
    flat[pl.ds(base + 2, half, stride=3), :] = jnp.where(left, o0, o1)


def norm_fwd(x):
    mean = jnp.sum(x, -1, keepdims=True) * (1.0 / D)
    right = x[:, 128:256] - mean
    c = jnp.concatenate([x[:, 0:128] - mean, jnp.where(low_half(right), right, 0.0)], 1)
    var = jnp.sum(c * c, -1, keepdims=True) * (1.0 / D)
    r = lax.rsqrt(var + 1e-05)
    return c * r, r


def norm_back(d, xh, r, g):
    e = d * g
    m1 = jnp.sum(e, -1, keepdims=True) * (1.0 / D)
    m2 = jnp.sum(e * xh, -1, keepdims=True) * (1.0 / D)
    return r * (e - m1 - xh * m2)


def rows8(v):
    return jnp.sum(v.reshape(v.shape[0] // 8, 8, v.shape[1]), 0)


def split_tokens(v, count):
    zero = jnp.zeros((v.shape[0], 256 - D), v.dtype)
    return jnp.concatenate(
        [jnp.concatenate([v[:, D * t : D * (t + 1)], zero], 1) for t in range(count)], 0
    )


def join_tokens(v, n):
    return jnp.concatenate([v[n * t : n * (t + 1), 0:D] for t in range(v.shape[0] // n)], 1)


def factors(wide):
    inner = max(k for k in range(1, int(math.isqrt(wide)) + 1) if wide % k == 0)
    return wide // inner, inner


def remote(src, dst, send, recv, where):
    return pltpu.make_async_remote_copy(
        src_ref=src,
        dst_ref=dst,
        send_sem=send,
        recv_sem=recv,
        device_id=where,
        device_id_type=pl.DeviceIdType.MESH,
    )


def greet(devices):
    for dev in devices:
        pl.semaphore_signal(
            pltpu.get_barrier_semaphore(), inc=1, device_id=dev,
            device_id_type=pl.DeviceIdType.MESH,
        )


def step_kernel(
    wide,
    x_hbm, dy_hbm, shard_hbm, out_hbm, ig_hbm, own_hbm, squares,
    shard, own, x_ref, dy_ref, out_ref, ig_ref, flat, gflat,
    qs, ks, vs, os_, kbd, vbd, psc, xb, xh1, r1, dx2s, h, h2, z, dul, o_t, dal, dyt, dqkv,
    wq, wk, wv, wo, w1, w2, tmp, hm2, parity, sample, hs, acc, acc2, acc3,
    buf, parts, sib_in, plane_in, out_p, col_in, out_c, res, vec_own, vec_plane, vec_col,
    vec_at, sq_plane, sq_col, vec_in,
    io_sem, g_col, g_fw, g_sib, g_recv, g_recv_sib, s_send, s_recv, p_send, p_recv, c_send, c_recv,
    f_sem, v_send, v_recv, n_send, n_recv, vg_send, vg_recv,
):
    n = x_ref.shape[0]
    toks = n * SEQ
    pairs = SEQ // 2
    groups = n // GROUP
    rows = shard.shape[0]
    half = buf.shape[1] // 2
    outer, inner = factors(wide)
    me, core = lax.axis_index("wide"), lax.axis_index("narrow")
    zo, pi = me // inner, lax.rem(me, inner)
    mine = pl.ds(pl.multiple_of(core * half, 8), half)
    theirs = pl.ds(pl.multiple_of((1 - core) * half, 8), half)
    sibling = (me, 1 - core)
    around = [lax.rem(pi + k, inner) for k in range(1, inner)]
    along = [lax.rem(zo + k, outer) for k in range(1, outer)]
    plane = [(zo * inner + q, core) for q in around]
    column = [(t * inner + pi, core) for t in along]
    late = -(-QK_ROWS // (rows * inner))
    first = -(-QKV_ROWS // (rows * inner))
    bounds = ((first, outer), (late, first), (0, late))

    copies_in = [
        pltpu.make_async_copy(x_hbm, x_ref, io_sem.at[0]),
        pltpu.make_async_copy(dy_hbm, dy_ref, io_sem.at[1]),
        pltpu.make_async_copy(shard_hbm, shard, io_sem.at[4]),
    ]

    cross = [(zo * inner + q, 1 - core) for q in around]
    known = plane + cross + column + [sibling]
    greet(known)
    for copy in (copies_in[2], copies_in[0], copies_in[1]):
        copy.start()
    lane = lax.broadcasted_iota(jnp.int32, (80, 256), 1)
    row = lax.broadcasted_iota(jnp.int32, (80, 256), 0)
    for p in range(PAIRS // 2):
        lo = jnp.where(row < ROWS, PAIR_DIM * 2 * p, PAIR_DIM * (2 * p + 1))
        hm2[80 * p : 80 * (p + 1), :] = jnp.where(
            (lane >= lo) & (lane < lo + PAIR_DIM), 1.0, 0.0
        ).astype(BF16)
    lane16 = lax.broadcasted_iota(jnp.int32, (16, 256), 1)
    for b in range(GROUP):
        query = lax.rem(lane16, LANES)
        sample[16 * b : 16 * (b + 1), :] = jnp.where(
            (query >= ROWS * b) & (query < ROWS * (b + 1)), 1.0, 0.0
        ).astype(BF16)
    head = lane16 // HEAD_DIM
    for k in range(2):
        parity[16 * k : 16 * (k + 1), :] = jnp.where(
            (lax.rem(head, 2) == k) & (head < HEADS), 1.0, 0.0
        ).astype(BF16)
    ones_lane = (lax.broadcasted_iota(jnp.int32, (toks, 64), 1) == 0).astype(F32).astype(BF16)
    o_t[:, D:256] = ones_lane
    for ref in (qs, ks, vs, os_):
        ref[...] = jnp.zeros(ref.shape, F32)

    parts[...] = jnp.zeros(parts.shape, F32)
    vec_at[...] = jnp.zeros(vec_at.shape, F32)
    copies_in[2].wait()
    pl.semaphore_wait(pltpu.get_barrier_semaphore(), len(known))
    buf[me, 0:rows, :] = shard[...]
    buf[me, rows:, :] = jnp.zeros((buf.shape[1] - rows, LANES), F32)

    def push(s, send, recvs, where):
        return remote(buf.at[s, mine], buf.at[s, mine], send, recvs.at[s], where)

    def arrived(s, recvs, part):
        remote(buf.at[s, part], buf.at[s, part], g_sib.at[s], recvs.at[s], sibling).wait_recv()

    def forwards(t, s):
        return [push(s, g_fw.at[t, k], g_recv, where) for k, where in enumerate(plane)]

    vec_rows = [
        (s, max(0, VEC_AT - rows * s) // 8 * 8, max(0, VEC_AT - rows * s), min(rows, USED_ROWS - rows * s))
        for s in range(VEC_AT // rows, (USED_ROWS - 1) // rows + 1)
    ]

    def vec_push(j, where, base):
        return [
            remote(vec_in.at[j], vec_in.at[j], vg_send.at[j, base + k], vg_recv.at[j], dev)
            for k, dev in enumerate(where)
        ]

    def vec_arrived(j):
        remote(vec_in.at[j], vec_in.at[j], vg_send.at[j, 0], vg_recv.at[j], sibling).wait_recv()

    for j, (s, a0, _, end) in enumerate(vec_rows):
        @pl.when(me == s)
        def _(j=j, a0=a0, end=end):
            vec_in[j, 0 : end - a0, :] = shard[a0:end, :]
            for copy in vec_push(j, column, 0) + vec_push(j, plane, outer - 1):
                copy.start()

    own_pushes = [push(me, g_col.at[k], g_recv, where) for k, where in enumerate(column)]
    own_pushes += forwards(zo, me)
    for copy in own_pushes:
        copy.start()

    def to_sibling(s):
        return push(s, g_sib.at[s], g_recv_sib, sibling)

    def forward_level(t):
        s = t * inner + pi

        @pl.when(t != zo)
        def _():
            arrived(s, g_recv, mine)
            for copy in forwards(t, s):
                copy.start()
            to_sibling(s).start()

    def pass_level(t):
        for q in around:
            s = t * inner + q
            arrived(s, g_recv, mine)
            to_sibling(s).start()

    def whole_shard(s):
        @pl.when(s != me)
        def _():
            arrived(s, g_recv_sib, theirs)

    def unpack(s):
        flat[rows * s : rows * (s + 1), :] = buf[s, 0:rows, :]

    for j, (s, _, _, _) in enumerate(vec_rows):
        @pl.when((me != s) & (pi == s % inner))
        def _(j=j):
            vec_arrived(j)
            for copy in vec_push(j, plane, outer - 1):
                copy.start()

    for t in range(outer):
        forward_level(t)

    def tokens_of(ref, t, count):
        return split_tokens(
            ref[:, pl.ds(pl.multiple_of(t * D, 128), count * D)].astype(F32), count
        )

    def put_tokens(ref, t, val):
        for half in range(2):
            for k in range(val.shape[0] // n):
                ref.at[half][pl.ds(t + k, n, stride=ROWS), :] = val[
                    n * k : n * (k + 1), 128 * half : 128 * (half + 1)
                ]

    def get_tokens(ref, t, count):
        return jnp.concatenate(
            [
                jnp.concatenate(
                    [ref.at[half][pl.ds(t + k, n, stride=ROWS), :] for half in range(2)], 1
                )
                for k in range(count)
            ],
            0,
        )

    def over_token_chunks(body, width, carry, hook=lambda i: None):
        whole = pairs // width

        def step(i, c):
            hook(i)
            return body(i * (2 * width), 2 * width, c)

        carry = lax.fori_loop(0, whole, step, carry)
        if pairs % width:
            carry = body(whole * 2 * width, 2 * (pairs % width), carry)
        return carry

    def get_rows(ref, start, count):
        return jnp.concatenate([ref[0, pl.ds(start, count), :], ref[1, pl.ds(start, count), :]], 1)

    def put_rows(ref, start, val):
        for half in range(2):
            ref[half, pl.ds(start, val.shape[0]), :] = val[:, 128 * half : 128 * (half + 1)]

    def rows_at(t, count):
        return pl.ds(pl.multiple_of(t * n, 32), count * n)

    copies_in[0].wait()
    for j, (s, a0, begin, end) in enumerate(vec_rows):
        @pl.when(pi != s % inner)
        def _(j=j):
            vec_arrived(j)

        flat[rows * s + begin : rows * s + end, :] = vec_in[j, begin - a0 : end - a0, :]

    ones3 = (lax.broadcasted_iota(jnp.int32, (1, 64), 1) < 3).astype(F32)

    def vec(k):
        a = VEC_AT + 3 * (k // 2)
        zero = ones3 if k in (1, 6) else jnp.zeros((1, 64), F32)
        if k % 2 == 0:
            return jnp.concatenate([flat[a : a + 1, :], flat[a + 1 : a + 2, 0:64], zero], 1)
        return jnp.concatenate([flat[a + 1 : a + 2, 64:128], flat[a + 2 : a + 3, :], zero], 1)

    g1, n1, bq, bv, bo, g2, n2, b2 = [vec(k) for k in range(8)]
    b1 = jnp.concatenate([flat[VEC_AT + 12 + c : VEC_AT + 13 + c, :] for c in range(4)], 1)

    def norm1(t, count, carry):
        at = rows_at(t, count)
        x = tokens_of(x_ref, t, count)
        xh, r = norm_fwd(x)
        xh1[at, :] = xh
        r1[at, :] = r
        hb = (xh * g1 + n1).astype(BF16)
        h[at, :] = hb
        put_tokens(os_, t, hb.astype(F32))
        xb[at, :] = x + bo
        return carry

    over_token_chunks(norm1, WIDTH1, 0)

    def take_dy(t, count, db2):
        dy = tokens_of(dy_ref, t, count)
        dyt[rows_at(t, count), :] = dy.astype(BF16)
        return db2 + rows8(dy)

    zero = jnp.zeros((8, 256), F32)
    copies_in[1].wait()
    db2 = over_token_chunks(take_dy, WIDTH1, zero)

    def bias_rows(b):
        row = lax.broadcasted_iota(jnp.int32, (16, b.shape[1]), 0)
        out = jnp.zeros((16, b.shape[1]), F32)
        for k in range(3):
            part = b.astype(BF16).astype(F32)
            out = jnp.where(row == k, part, out)
            b = b - part
        return out.astype(BF16)

    half_groups = LOCK2 * GROWS

    @pl.loop(0, groups // LOCK2)
    def _(i):
        at = pl.ds(pl.multiple_of(i * half_groups, 16), half_groups)
        hs[at, :] = get_rows(os_, pl.multiple_of(i * half_groups, 8), half_groups).astype(BF16)

    def take_levels(lo, hi):
        for s in range(lo * inner, hi * inner):
            whole_shard(s)
            unpack(s)

    for t in range(late):
        pass_level(t)
    take_levels(0, late)
    for (base, count), ref in zip(MATS[0:2], (wq, wk)):
        load_square(flat, base, count, tmp, ref)
    wq[D : D + 16, :] = bias_rows(bq)

    def pass_v(i):
        @pl.when(i == 1)
        def _():
            for t in range(late, first):
                pass_level(t)

    def dense_qk(t, count, carry):
        hb = h[rows_at(t, count), :]
        put_tokens(qs, t, nn(hb, wq[...]).astype(BF16).astype(F32))
        put_tokens(ks, t, nn(hb, wk[...]).astype(BF16).astype(F32))
        return carry

    over_token_chunks(dense_qk, WIDTH1, 0, pass_v)
    take_levels(late, first)
    load_square(flat, MATS[2][0], MATS[2][1], tmp, wv)
    wv[D : D + 16, :] = bias_rows(bv)

    def dense_v(t, count, carry):
        hb = h[rows_at(t, count), :]
        put_tokens(vs, t, nn(hb, wv[...]).astype(BF16).astype(F32))
        return carry

    over_token_chunks(dense_v, WIDTH1, 0)

    lane3 = lax.rem(lax.broadcasted_iota(jnp.int32, (1, 256), 1), LANES)
    odd_head = lax.rem(lax.broadcasted_iota(jnp.int32, (1, 256), 1) // HEAD_DIM, 2) == 1

    def squeeze(v):
        return jnp.where(
            lane3 < ROWS, v[0:HJ], jnp.where(lane3 < 2 * ROWS, v[HJ : 2 * HJ], v[2 * HJ : 3 * HJ])
        ).reshape(PAIRS, ROWS, 256)

    def by_parity(v):
        v3 = v.reshape(8, 16, 256)
        return jnp.concatenate(
            [(v3 * parity[16 * k : 16 * (k + 1), :][None]).reshape(LANES, 256) for k in range(2)], 0
        )

    def per_query(left, right, b):
        rows2 = jnp.concatenate([left[128 * k + ROWS * b : 128 * k + ROWS * (b + 1)] for k in range(2)], 0)
        both = nn(rows2.astype(BF16), right)
        return jnp.where(odd_head, both[ROWS : 2 * ROWS], both[0:ROWS])

    jrow = lax.broadcasted_iota(jnp.int32, (1, ROWS - 32, 256), 1)
    cexp = math.log2(math.e) / math.sqrt(HEAD_DIM)
    scale = 1.0 / math.sqrt(HEAD_DIM)

    def attn(i, carry):
        @pl.when(i == 1)
        def _():
            for t in range(first, outer):
                pass_level(t)

        r0 = pl.multiple_of(i * (LOCK1 * GROWS), 8)
        base0 = pl.multiple_of(i * (LOCK1 * 3 * HJ), 32)
        p0 = pl.multiple_of(i * (LOCK1 * HJ), 32)
        sets = range(LOCK1)
        qg = [by_parity(get_rows(qs, r0 + GROWS * k, LANES).astype(BF16)) for k in sets]
        for k in sets:
            for src, dst in ((ks, kbd), (vs, vbd)):
                for b in range(GROUP):
                    one = get_rows(src, r0 + GROWS * k + ROWS * b, ROWS)
                    two = jnp.concatenate([one, one], 0).astype(BF16)
                    for p in range(PAIRS // 2):
                        dst[pl.ds(base0 + HJ * (3 * k + b) + 80 * p, 80), :] = (
                            two * hm2[80 * p : 80 * (p + 1), :]
                        )
        st = [squeeze(nt(kbd[pl.ds(base0 + 3 * HJ * k, 3 * HJ), :], qg[k])) for k in sets]
        st = [
            jnp.concatenate([v[:, 0:32], jnp.where(jrow < SEQ - 32, v[:, 32:ROWS], -1e30)], 1)
            for v in st
        ]
        m = [jnp.max(v, 1, keepdims=True) for v in st]
        e = [jnp.exp2((st[k] - m[k]) * cexp) for k in sets]
        l = [1.0 / jnp.sum(v, 1, keepdims=True) for v in e]
        p = [(e[k] * l[k]).reshape(HJ, 256) for k in sets]
        for k in sets:
            psc[pl.ds(p0 + HJ * k, HJ), :] = p[k]
        pt = [v.T for v in p]
        for b in range(GROUP):
            for k in sets:
                ob = per_query(pt[k], vbd[pl.ds(base0 + HJ * (3 * k + b), HJ), :], b)
                put_rows(os_, r0 + GROWS * k + ROWS * b, ob.astype(BF16).astype(F32)[0:SEQ])
        return carry

    lax.fori_loop(0, groups // LOCK1, attn, 0)

    take_levels(first, outer)
    for (base, count), ref in zip(MATS[3:5], (wo, w2)):
        load_square(flat, base, count, tmp, ref)
    for c in range(4):
        part = flat[pl.ds(W1_AT + c, D, stride=4), :]
        w1[0:D, 128 * c : 128 * (c + 1)] = (part if c < 2 else 0.5 * part).astype(BF16)
    w1[D : D + 16, :] = bias_rows(jnp.concatenate([b1[:, 0:FF], 0.5 * b1[:, FF:]], 1))
    w1[D + 16 : 256, :] = jnp.zeros((240 - D, 2 * FF), BF16)
    def dense2(t0, count, carry):
        dg2, dn2 = carry
        at = rows_at(t0, count)
        o = get_tokens(os_, t0, count).astype(BF16)
        o_t[at, 0:D] = o[:, 0:D]
        x2 = xb[at, :] + nn(o, wo[...])
        xh, r = norm_fwd(x2)
        hb = (xh * g2 + n2).astype(BF16)
        h2[at, :] = hb
        u = nn(hb, w1[...])
        gate, up = u[:, :FF], u[:, FF:]
        sq = gate * gate
        t = jnp.tanh(gate * (GELU_C + (GELU_C * 0.044715) * sq))
        t1 = 1.0 + t
        act = gate * t1
        zb = (act * up).astype(BF16)
        z[at, :] = zb
        y = x2 + nn(zb, w2[...]) + b2
        out_ref[:, pl.ds(pl.multiple_of(t0 * D, 128), count * D)] = join_tokens(y, n).astype(BF16)
        dyb = dyt[at, :]
        dyf = dyb.astype(F32)
        dz = nt(dyb, w2[...])
        slope = t1 + act * (1.0 - t) * (GELU_C + (3 * GELU_C * 0.044715) * sq)
        du = jnp.concatenate([(dz * up * slope).astype(BF16), (dz * act).astype(BF16)], 1)
        dul[at, :] = du
        dh = nt(du, w1[...])
        dx2 = dyf + norm_back(dh, xh, r, g2)
        dx2s[at, :] = dx2
        da = dx2.astype(BF16)
        dal[at, :] = da
        put_tokens(os_, t0, nt(da, wo[...]).astype(BF16).astype(F32))
        acc[...] += tn(zb, dyb)
        acc2[...] += tn(hb, du)
        acc3[...] += tn(o_t[at, :], da)
        return dg2 + rows8(dh * xh), dn2 + rows8(dh)

    for ref in (acc, acc2, acc3):
        ref[...] = jnp.zeros(ref.shape, F32)
    dg2, dn2 = over_token_chunks(dense2, WIDTH2, (zero, zero))

    copy_out = pltpu.make_async_copy(out_ref, out_hbm, io_sem.at[2])
    copy_out.start()

    def total(v):
        return jnp.sum(v, 0, keepdims=True)

    def over_tokens(*products):
        for acc, _, _ in products:
            acc[...] = jnp.zeros(acc.shape, F32)
        size = products[0][1].shape[0] // DW_STEPS

        @pl.loop(0, DW_STEPS)
        def _(i):
            at = pl.ds(pl.multiple_of(i * size, 16), size)
            for acc, a, b in products:
                acc[...] += tn(a[at, :], b[at, :])

    store_square(acc[...], gflat, 1920, FF, tmp)
    for c in range(4):
        part = acc2[0 : D + 8, 128 * c : 128 * (c + 1)]
        part = part if c < 2 else 0.5 * part
        gflat[pl.ds(W1_AT + c, D, stride=4), :] = part[0:D]
        vec_own[12 + c : 13 + c, :] = part[D : D + 1]
    store_square(acc3[...], gflat, 864, D, tmp)
    dbo = acc3[D : D + 1, :]

    def pack(lo, hi):
        for s in range(lo * inner, hi * inner):
            stop = min(rows * (s + 1), VEC_AT)
            if stop > rows * s:
                parts[s // inner, s % inner, 0 : stop - rows * s, :] = gflat[rows * s : stop, :]

    places = around + [pi]

    def sib_copies(part, lo, hi):
        return [
            remote(
                parts.at[lo:hi, q, theirs], sib_in.at[lo:hi, q],
                s_send.at[part, k], s_recv.at[part, q], sibling,
            )
            for k, q in enumerate(places)
        ]

    def plane_copies(part, lo, hi):
        return [
            remote(
                out_p.at[k, lo:hi], plane_in.at[pi, lo:hi],
                p_send.at[part, k], p_recv.at[part, pi], plane[k],
            )
            for k in range(inner - 1)
        ]

    def col_copy(t):
        return remote(
            out_c.at[t], col_in.at[zo], c_send.at[t], c_recv.at[zo], (t * inner + pi, core)
        )

    def sum_cores(part):
        lo, hi = bounds[part]
        sends = plane_copies(part, lo, hi)
        for k, q in enumerate(places):
            remote(
                sib_in.at[lo:hi, q], sib_in.at[lo:hi, q],
                s_send.at[part, k], s_recv.at[part, q], sibling,
            ).wait_recv()
            both = parts[lo:hi, q, mine, :] + sib_in[lo:hi, q]
            if k < inner - 1:
                out_p[k, lo:hi] = both
                sends[k].start()
            else:
                plane_in[pi, lo:hi] = both

    def sum_plane(part):
        lo, hi = bounds[part]
        for k, q in enumerate(around):
            remote(
                plane_in.at[q, lo:hi], plane_in.at[q, lo:hi],
                p_send.at[part, k], p_recv.at[part, q], sibling,
            ).wait_recv()
        for t in range(lo, hi):
            line = plane_in[0, t]
            for q in range(1, inner):
                line = line + plane_in[q, t]
            out_c[t] = line

            @pl.when(t != zo)
            def _():
                col_copy(t).start()

    def send_cores(part):
        pack(*bounds[part])
        for copy in sib_copies(part, *bounds[part]):
            copy.start()

    send_cores(0)

    def by_sample(v):
        v = v.reshape(HJ, 256).astype(BF16).reshape(HJ // 16, 16, 256)
        return jnp.concatenate(
            [
                (v * sample[16 * b : 16 * (b + 1), :][None]).reshape(HJ, 256)
                for b in range(GROUP)
            ],
            0,
        )

    pair_lane = lax.broadcasted_iota(jnp.int32, (1, LANES), 1)

    def own_lanes(v):
        v = v.reshape(GROUP, PAIRS, ROWS, 256)
        out = []
        for b in range(GROUP):
            lo = jnp.where(pair_lane < PAIR_DIM, v[b, 0, :, 0:128], v[b, 1, :, 0:128])
            lo = jnp.where(pair_lane < 2 * PAIR_DIM, lo, v[b, 2, :, 0:128])
            hi = jnp.where(
                pair_lane < 3 * PAIR_DIM - 128, v[b, 2, :, 128:256], v[b, 3, :, 128:256]
            )
            out.append(jnp.concatenate([lo, hi], 1))
        return jnp.concatenate(out, 0)

    def probs(at):
        return psc[pl.ds(at, HJ), :].reshape(PAIRS, ROWS, 256)

    def attn_back_v(i, carry):
        @pl.when(i == 3)
        def _():
            sum_cores(0)

        r0 = pl.multiple_of(i * (LOCK2 * GROWS), 8)
        p0 = pl.multiple_of(i * (LOCK2 * HJ), 32)
        out = []
        for k in range(LOCK2):
            dg = by_parity(get_rows(os_, r0 + GROWS * k, LANES).astype(BF16))
            out.append(own_lanes(nn(by_sample(probs(p0 + HJ * k)), dg)))
        out = jnp.concatenate(out, 0).astype(BF16)
        dqkv[pl.ds(pl.multiple_of(i * half_groups, 16), half_groups), 512:768] = out
        put_rows(vs, r0, out.astype(F32))
        return carry

    lax.fori_loop(0, groups // LOCK2, attn_back_v, 0)

    over_tokens((acc, hs, dqkv.at[:, 512:768]))
    store_square(acc[...], gflat, 576, D, tmp)
    dbv = acc[D : D + 1, :]
    send_cores(1)

    def attn_back(i, carry):
        @pl.when(i == 1)
        def _():
            sum_cores(1)

        r0 = pl.multiple_of(i * (LOCK2 * GROWS), 8)
        base0 = pl.multiple_of(i * (LOCK2 * 3 * HJ), 32)
        p0 = pl.multiple_of(i * (LOCK2 * HJ), 32)
        sets = range(LOCK2)
        qg = [by_parity(get_rows(qs, r0 + GROWS * k, LANES).astype(BF16)) for k in sets]
        dg = [by_parity(get_rows(os_, r0 + GROWS * k, LANES).astype(BF16)) for k in sets]
        dp = [squeeze(nt(vbd[pl.ds(base0 + 3 * HJ * k, 3 * HJ), :], dg[k])) for k in sets]
        p = [probs(p0 + HJ * k) for k in sets]
        t = [jnp.sum(p[k] * dp[k], 1, keepdims=True) for k in sets]
        ds = [p[k] * (dp[k] - t[k]) for k in sets]
        dst = [v.reshape(HJ, 256).T for v in ds]
        dk = [own_lanes(nn(by_sample(ds[k]), qg[k])) * scale for k in sets]
        dq = [
            per_query(dst[k], kbd[pl.ds(base0 + HJ * (3 * k + b), HJ), :], b) * scale
            for k in sets
            for b in range(GROUP)
        ]
        at = pl.ds(pl.multiple_of(i * half_groups, 16), half_groups)
        for col, ref, val in ((0, qs, dq), (256, ks, dk)):
            val = jnp.concatenate(val, 0).astype(BF16)
            dqkv[at, col : col + 256] = val
            put_rows(ref, r0, val.astype(F32))
        return carry

    lax.fori_loop(0, groups // LOCK2, attn_back, 0)

    over_tokens((acc2, hs, dqkv.at[:, 0:512]))
    for k in range(2):
        store_square(acc2[:, 256 * k : 256 * (k + 1)], gflat, 288 * k, D, tmp)
    send_cores(2)
    sum_plane(0)

    def dense3(t0, count, carry):
        dg1, dn1 = carry
        at = rows_at(t0, count)
        dh = (
            nt(get_tokens(qs, t0, count).astype(BF16), wq[...])
            + nt(get_tokens(ks, t0, count).astype(BF16), wk[...])
            + nt(get_tokens(vs, t0, count).astype(BF16), wv[...])
        )
        xh = xh1[at, :]
        ig = dx2s[at, :] + norm_back(dh, xh, r1[at, :], g1)
        ig_ref[:, pl.ds(pl.multiple_of(t0 * D, 128), count * D)] = join_tokens(ig, n)
        return dg1 + rows8(dh * xh), dn1 + rows8(dh)

    def hook3(i):
        @pl.when(i == 1)
        def _():
            sum_cores(2)
            sum_plane(1)

    dg1, dn1 = over_token_chunks(dense3, WIDTH3, (zero, zero), hook3)

    vecs = [
        total(dg1), total(dn1), acc2[D : D + 1, 0:256], dbv,
        dbo, total(dg2), total(dn2), total(db2),
    ]
    for k in range(4):
        a, b = vecs[2 * k], vecs[2 * k + 1]
        vec_own[3 * k : 3 * k + 1, :] = a[:, 0:128]
        vec_own[3 * k + 1 : 3 * k + 2, :] = jnp.concatenate([a[:, 128:192], b[:, 0:64]], 1)
        vec_own[3 * k + 2 : 3 * k + 3, :] = b[:, 64:192]
    copy_ig = pltpu.make_async_copy(ig_ref, ig_hbm, io_sem.at[3])
    copy_ig.start()

    def spread(slots, at, sends, recvs, base, where):
        out = [
            remote(slots.at[at], slots.at[at], sends.at[base + k], recvs.at[base + at], dev)
            for k, dev in enumerate(where)
        ]
        for copy in out:
            copy.start()
        return out

    def collected(slots, others, sends, recvs, base):
        for k, q in enumerate(others):
            remote(
                slots.at[q], slots.at[q], sends.at[base + k], recvs.at[base + q], sibling
            ).wait_recv()
        return jnp.sum(slots[...], 0)

    slot = 2 * pi + core
    near = [2 * q + core for q in around] + [2 * q + 1 - core for q in around] + [2 * pi + 1 - core]
    disc = plane + cross + [sibling]
    vec_plane[slot] = vec_own[...]
    vec_sends = spread(vec_plane, slot, v_send, v_recv, 0, disc)
    sum_plane(2)
    vec_col[zo] = collected(vec_plane, near, v_send, v_recv, 0)
    vec_sends += spread(vec_col, zo, v_send, v_recv, 2 * inner, column)

    col_in[zo] = out_c[zo]
    for t in along:
        remote(col_in.at[t], col_in.at[t], c_send.at[t], c_recv.at[t], sibling).wait_recv()
    line = col_in[0]
    for t in range(1, outer):
        line = line + col_in[t]
    res[mine, :] = line
    last = remote(res.at[mine], res.at[mine], f_sem.at[0], f_sem.at[1], sibling)
    last.start()
    sq_plane[slot] = rows8(line * line)
    sq_sends = spread(sq_plane, slot, n_send, n_recv, 0, disc)
    vec = collected(vec_col, along, v_send, v_recv, 2 * inner)
    vec_at[VEC_AT:USED_ROWS, :] = vec
    remote(res.at[theirs], res.at[theirs], f_sem.at[0], f_sem.at[1], sibling).wait_recv()
    own[...] = res[0:rows, :] + vec_at[pl.ds(me * rows, rows), :]
    copy_own = pltpu.make_async_copy(own, own_hbm, io_sem.at[5])
    copy_own.start()
    sq_col[zo] = collected(sq_plane, near, n_send, n_recv, 0)
    sq_sends += spread(sq_col, zo, n_send, n_recv, 2 * inner, column)
    both = collected(sq_col, along, n_send, n_recv, 2 * inner) + rows8(vec * vec)
    squares[...] = jnp.broadcast_to(jnp.sum(both, keepdims=True), squares.shape)

    for copy in own_pushes + vec_sends + sq_sends + [last]:
        copy.wait_send()
    for t in range(outer):
        @pl.when(t != zo)
        def _(t=t):
            for copy in forwards(t, t * inner + pi):
                copy.wait_send()
            to_sibling(t * inner + pi).wait_send()
            col_copy(t).wait_send()

        for q in around:
            to_sibling(t * inner + q).wait_send()
    for j, (s, _, _, _) in enumerate(vec_rows):
        @pl.when(me == s)
        def _(j=j):
            for copy in vec_push(j, column, 0):
                copy.wait_send()

        @pl.when(pi == s % inner)
        def _(j=j):
            for copy in vec_push(j, plane, outer - 1):
                copy.wait_send()

    for part, (lo, hi) in enumerate(bounds):
        for copy in sib_copies(part, lo, hi) + plane_copies(part, lo, hi):
            copy.wait_send()
    copy_out.wait()
    copy_ig.wait()
    copy_own.wait()


def step(x, dy, shard, wide):
    outer, inner = factors(wide)
    n, rows = x.shape[0], shard.shape[0]
    toks = n * SEQ
    groups = n // GROUP
    padded = (rows + 15) // 16 * 16
    half = padded // 2
    vecs = (USED_ROWS - 1) // rows - VEC_AT // rows + 1
    vm, dma = pltpu.VMEM, pltpu.SemaphoreType.DMA
    sm = vm((2, n * ROWS + 8, LANES), F32)
    tok = vm((toks, 256), BF16)
    tile = (8, LANES)
    scratch = (
        [vm((rows, LANES), F32)] * 2
        + [vm(x.shape, BF16), vm(x.shape, BF16), vm(x.shape, BF16), vm(x.shape, F32)]
        + [vm((wide * rows, LANES), F32)] * 2
        + [sm] * 4
        + [vm((groups * 3 * HJ, 256), BF16)] * 2
        + [vm((groups * HJ, 256), F32)]
        + [vm((toks, 256), F32)] * 2
        + [vm((toks, 1), F32), vm((toks, 256), F32)]
        + [tok, tok, tok, vm((toks, 2 * FF), BF16), tok]
        + [tok, tok, vm((n * ROWS, 3 * 256), BF16)]
        + [vm((256, 256), BF16)] * 4
        + [vm((256, 2 * FF), BF16), vm((FF, 256), BF16), vm((2, FF, 128), F32)]
        + [vm((HJ, 256), BF16), vm((32, 256), BF16), vm((16 * GROUP, 256), BF16), vm((n * ROWS, 256), BF16)]
        + [vm((256, 256), F32), vm((256, 512), F32), vm((256, 256), F32)]
        + [vm((wide, padded, LANES), F32), vm((outer, inner, padded, LANES), F32)]
        + [vm((outer, inner, half, LANES), F32), vm((inner, outer, half, LANES), F32)]
        + [vm((inner - 1, outer, half, LANES), F32)]
        + [vm((outer, half, LANES), F32)] * 2
        + [vm((padded, LANES), F32)]
        + [vm((16, LANES), F32), vm((2 * inner, 16, LANES), F32), vm((outer, 16, LANES), F32)]
        + [vm((wide * rows, LANES), F32)]
        + [vm((2 * inner, *tile), F32), vm((outer, *tile), F32)]
        + [vm((vecs, min(24, padded), LANES), F32)]
        + [dma((6,)), dma((outer - 1,)), dma((outer, inner - 1)), dma((wide,)), dma((wide,)), dma((wide,))]
        + [dma((3, inner))] * 4
        + [dma((outer,)), dma((outer,)), dma((2,))]
        + [dma((2 * inner + outer,))] * 4
        + [dma((vecs, outer + inner - 2)), dma((vecs,))]
    )
    anywhere, vmem = pl.BlockSpec(memory_space=pl.ANY), pl.BlockSpec(memory_space=pltpu.VMEM)
    return pl.pallas_call(
        functools.partial(step_kernel, wide),
        out_shape=(
            jax.ShapeDtypeStruct(x.shape, BF16),
            jax.ShapeDtypeStruct(x.shape, F32),
            jax.ShapeDtypeStruct((rows, LANES), F32),
            jax.ShapeDtypeStruct(tile, F32),
        ),
        in_specs=[anywhere] * 3,
        out_specs=(anywhere, anywhere, anywhere, vmem),
        scratch_shapes=scratch,
        compiler_params=pltpu.CompilerParams(
            collective_id=0, has_side_effects=True, vmem_limit_bytes=60 * 2**20
        ),
        name="step",
    )(x, dy, shard)


def finish_kernel(*refs):
    big_in, small_in = refs[0:2], refs[2:7]
    big_out, norm_out, small_out = refs[7:9], refs[9], refs[10:15]
    stages, ins, norm, outs = refs[15:17], refs[17:22], refs[22], refs[23:28]
    sem_in, sem_out, sem_small = refs[28:31]
    pieces = []
    for k in range(2):
        size = big_in[k].shape[0] // PIECES
        for p in range(PIECES):
            at = pl.ds(size * p, size)
            pieces.append(
                (
                    pltpu.make_async_copy(big_in[k].at[at], stages[k].at[at], sem_in.at[k, p]),
                    pltpu.make_async_copy(stages[k].at[at], big_out[k].at[at], sem_out.at[k, p]),
                )
            )
    loads = [pltpu.make_async_copy(small_in[k], ins[k], sem_small.at[k]) for k in range(5)]
    for copy in loads:
        copy.start()
    for come, _ in pieces:
        come.start()
    for copy in loads:
        copy.wait()
    own, squares, master, first, second = ins
    clipped, new_master, new_copy, new_first, new_second = outs
    grad_norm = jnp.sqrt(squares[...])
    norm[...] = grad_norm[0:1, 0:1]
    factor = jnp.minimum(1.0, 1.0 / (grad_norm[0:1, :] + 1e-06))
    grad = own[...] * factor
    clipped[...] = grad
    one = 0.5 * first[...] + 0.5 * grad
    two = 0.5 * second[...] + 0.5 * grad * grad
    new_first[...] = one
    new_second[...] = two
    fixed = 1.0 - 0.5**STEP
    old = master[...]
    new = old - 0.05 * ((one / fixed) / (jnp.sqrt(two / fixed) + 1e-08) + 0.1 * old)
    new_master[...] = new
    new_copy[...] = new.astype(BF16)
    stores = [
        pltpu.make_async_copy(src, dst, sem_small.at[5 + k])
        for k, (src, dst) in enumerate(zip((norm, *outs), (norm_out, *small_out)))
    ]
    for copy in stores:
        copy.start()
    for come, go in pieces:
        come.wait()
        go.start()
    for copy in stores:
        copy.wait()
    for _, go in pieces:
        go.wait()


def finish(block_out, input_grad, owned, squares, master, first, second):
    anywhere, vm = pl.BlockSpec(memory_space=pl.ANY), pltpu.VMEM
    one, flat = (1, 1), owned.shape
    kinds = [(flat, F32), (flat, F32), (flat, BF16), (flat, F32), (flat, F32)]
    like = jax.ShapeDtypeStruct
    return pl.pallas_call(
        finish_kernel,
        out_shape=(
            like(block_out.shape, BF16),
            like(input_grad.shape, F32),
            like(one, F32),
            *[like(*kind) for kind in kinds],
        ),
        in_specs=[anywhere] * 7,
        out_specs=(anywhere,) * 8,
        scratch_shapes=[
            vm(block_out.shape, BF16),
            vm(input_grad.shape, F32),
            vm(flat, F32),
            vm(squares.shape, F32),
            vm(flat, F32),
            vm(flat, F32),
            vm(flat, F32),
            vm(one, F32),
            *[vm(*kind) for kind in kinds],
            pltpu.SemaphoreType.DMA((2, PIECES)),
            pltpu.SemaphoreType.DMA((2, PIECES)),
            pltpu.SemaphoreType.DMA((11,)),
        ],
        compiler_params=pltpu.CompilerParams(vmem_limit_bytes=60 * 2**20),
        name="finish",
    )(block_out, input_grad, owned, squares, master, first, second)


def on_device(inputs, cotangent, master, first, second):
    flat = lambda a: a.reshape(-1)
    tall = lambda a: a.reshape(-1, LANES)
    block_out, input_grad, owned, squares = step(
        inputs, cotangent, tall(master), lax.axis_size("wide")
    )
    block_out, input_grad, norm, clipped, new_master, new_copy, new_first, new_second = finish(
        block_out, input_grad, owned, squares, tall(master), tall(first), tall(second)
    )
    return (
        block_out,
        input_grad,
        flat(clipped),
        norm.reshape(()),
        flat(new_master),
        flat(new_copy),
        flat(new_first),
        flat(new_second),
    )


def solution(mesh):
    both, part = P(("wide", "narrow"), None), P("wide")
    return jax.shard_map(
        on_device,
        mesh=mesh,
        in_specs=(both, both, part, part, part),
        out_specs=(both, both, part, P(), part, part, part, part),
        check_vma=False,
    )
```

```python
import functools
import math

import jax
import jax.numpy as jnp
from jax import lax
from jax.experimental import pallas as pl
from jax.experimental.pallas import tpu as pltpu
from jax.sharding import PartitionSpec as P

D = 192
HEADS = 8
HEAD_DIM = 24
FF = 256
SEQ = 34
STEP = 5
ROWS = 40
GROUP = 3
GROWS = GROUP * ROWS
PAIRS = HEADS // 2
PAIR_DIM = 2 * HEAD_DIM
HJ = PAIRS * ROWS
LANES = 128
F32 = jnp.float32
BF16 = jnp.bfloat16
MATS = ((0, D), (288, D), (576, D), (864, D), (1920, FF))
W1_AT = 1152
WIDTH1, WIDTH2, WIDTH3, DW_STEPS = 8, 6, 3, 2
LOCK1, LOCK2, LOCK3 = 8, 8, 4
PIECES = 1
VEC_AT = 2304
USED_ROWS = VEC_AT + 16
QK_ROWS = 576
QKV_ROWS = 864
GELU_C = math.sqrt(2.0 / math.pi)


def nn(a, b):
    return lax.dot_general(a, b, (((1,), (0,)), ((), ())), preferred_element_type=F32)


def nt(a, b):
    return lax.dot_general(a, b, (((1,), (1,)), ((), ())), preferred_element_type=F32)


def tn(a, b):
    return lax.dot_general(a, b, (((0,), (0,)), ((), ())), preferred_element_type=F32)


def low_half(v):
    lane = lax.broadcasted_iota(jnp.int32, v.shape, 1)
    return lane < 64


def load_square(flat, base, rows, tmp, out):
    half = rows // 2
    f0 = flat[pl.ds(base, half, stride=3), :]
    f1 = flat[pl.ds(base + 1, half, stride=3), :]
    f2 = flat[pl.ds(base + 2, half, stride=3), :]
    r1 = pltpu.roll(f1, 64, 1)
    r2 = pltpu.roll(f2, 64, 1)
    left = low_half(f0)
    lo, hi = tmp.at[0], tmp.at[1]
    lo[pl.ds(0, half, stride=2), :] = f0
    hi[pl.ds(0, half, stride=2), :] = jnp.where(left, f1, 0.0)
    lo[pl.ds(1, half, stride=2), :] = jnp.where(left, r1, r2)
    hi[pl.ds(1, half, stride=2), :] = jnp.where(left, r2, 0.0)
    out[0:rows, 0:128] = lo[0:rows, :].astype(BF16)
    out[0:rows, 128:256] = hi[0:rows, :].astype(BF16)
    if rows < 256:
        out[rows:256, :] = jnp.zeros((256 - rows, 256), BF16)


def store_square(val, flat, base, rows, tmp):
    half = rows // 2
    lo, hi = tmp.at[0], tmp.at[1]
    lo[0:rows, :] = val[0:rows, 0:128]
    hi[0:rows, :] = val[0:rows, 128:256]
    e0 = lo[pl.ds(0, half, stride=2), :]
    e1 = hi[pl.ds(0, half, stride=2), :]
    o0 = pltpu.roll(lo[pl.ds(1, half, stride=2), :], 64, 1)
    o1 = pltpu.roll(hi[pl.ds(1, half, stride=2), :], 64, 1)
    left = low_half(e0)
    flat[pl.ds(base, half, stride=3), :] = e0
    flat[pl.ds(base + 1, half, stride=3), :] = jnp.where(left, e1, o0)
    flat[pl.ds(base + 2, half, stride=3), :] = jnp.where(left, o0, o1)


def norm_fwd(x):
    mean = jnp.sum(x, -1, keepdims=True) * (1.0 / D)
    right = x[:, 128:256] - mean
    c = jnp.concatenate([x[:, 0:128] - mean, jnp.where(low_half(right), right, 0.0)], 1)
    var = jnp.sum(c * c, -1, keepdims=True) * (1.0 / D)
    r = lax.rsqrt(var + 1e-05)
    return c * r, r


def norm_back(d, xh, r, g):
    e = d * g
    m1 = jnp.sum(e, -1, keepdims=True) * (1.0 / D)
    m2 = jnp.sum(e * xh, -1, keepdims=True) * (1.0 / D)
    return r * (e - m1 - xh * m2)


def rows8(v):
    return jnp.sum(v.reshape(v.shape[0] // 8, 8, v.shape[1]), 0)


def split_tokens(v, count):
    zero = jnp.zeros((v.shape[0], 256 - D), v.dtype)
    return jnp.concatenate(
        [jnp.concatenate([v[:, D * t : D * (t + 1)], zero], 1) for t in range(count)], 0
    )


def join_tokens(v, n):
    return jnp.concatenate([v[n * t : n * (t + 1), 0:D] for t in range(v.shape[0] // n)], 1)


def factors(wide):
    inner = max(k for k in range(1, int(math.isqrt(wide)) + 1) if wide % k == 0)
    return wide // inner, inner


def remote(src, dst, send, recv, where):
    return pltpu.make_async_remote_copy(
        src_ref=src,
        dst_ref=dst,
        send_sem=send,
        recv_sem=recv,
        device_id=where,
        device_id_type=pl.DeviceIdType.MESH,
    )


def greet(devices):
    for dev in devices:
        pl.semaphore_signal(
            pltpu.get_barrier_semaphore(), inc=1, device_id=dev,
            device_id_type=pl.DeviceIdType.MESH,
        )


def step_kernel(
    wide,
    x_hbm, dy_hbm, shard_hbm, out_hbm, ig_hbm, own_hbm, squares,
    shard, own, x_ref, dy_ref, out_ref, ig_ref, flat, gflat,
    qs, ks, vs, os_, kbd, vbd, psc, xb, xh1, r1, dx2s, h, h2, z, dul, o_t, dal, dyt, dqkv,
    wq, wk, wv, wo, w1, w2, tmp, hm2, parity, sample, hs, acc, acc2, acc3,
    buf, parts, sib_in, plane_in, out_p, col_in, out_c, res, vec_own, vec_plane, vec_col,
    vec_at, sq_plane, sq_col, vec_in,
    io_sem, g_col, g_fw, g_sib, g_recv, g_recv_sib, s_send, s_recv, p_send, p_recv, c_send, c_recv,
    f_sem, v_send, v_recv, n_send, n_recv, vg_send, vg_recv,
):
    n = x_ref.shape[0]
    toks = n * SEQ
    pairs = SEQ // 2
    groups = n // GROUP
    rows = shard.shape[0]
    half = buf.shape[1] // 2
    outer, inner = factors(wide)
    me, core = lax.axis_index("wide"), lax.axis_index("narrow")
    zo, pi = me // inner, lax.rem(me, inner)
    mine = pl.ds(pl.multiple_of(core * half, 8), half)
    theirs = pl.ds(pl.multiple_of((1 - core) * half, 8), half)
    sibling = (me, 1 - core)
    around = [lax.rem(pi + k, inner) for k in range(1, inner)]
    along = [lax.rem(zo + k, outer) for k in range(1, outer)]
    plane = [(zo * inner + q, core) for q in around]
    column = [(t * inner + pi, core) for t in along]
    late = -(-QK_ROWS // (rows * inner))
    first = -(-QKV_ROWS // (rows * inner))
    bounds = ((first, outer), (late, first), (0, late))

    copies_in = [
        pltpu.make_async_copy(x_hbm, x_ref, io_sem.at[0]),
        pltpu.make_async_copy(dy_hbm, dy_ref, io_sem.at[1]),
        pltpu.make_async_copy(shard_hbm, shard, io_sem.at[4]),
    ]

    cross = [(zo * inner + q, 1 - core) for q in around]
    known = plane + cross + column + [sibling]
    greet(known)
    for copy in (copies_in[2], copies_in[0], copies_in[1]):
        copy.start()
    lane = lax.broadcasted_iota(jnp.int32, (80, 256), 1)
    row = lax.broadcasted_iota(jnp.int32, (80, 256), 0)
    for p in range(PAIRS // 2):
        lo = jnp.where(row < ROWS, PAIR_DIM * 2 * p, PAIR_DIM * (2 * p + 1))
        hm2[80 * p : 80 * (p + 1), :] = jnp.where(
            (lane >= lo) & (lane < lo + PAIR_DIM), 1.0, 0.0
        ).astype(BF16)
    lane16 = lax.broadcasted_iota(jnp.int32, (16, 256), 1)
    for b in range(GROUP):
        query = lax.rem(lane16, LANES)
        sample[16 * b : 16 * (b + 1), :] = jnp.where(
            (query >= ROWS * b) & (query < ROWS * (b + 1)), 1.0, 0.0
        ).astype(BF16)
    head = lane16 // HEAD_DIM
    for k in range(2):
        parity[16 * k : 16 * (k + 1), :] = jnp.where(
            (lax.rem(head, 2) == k) & (head < HEADS), 1.0, 0.0
        ).astype(BF16)
    ones_lane = (lax.broadcasted_iota(jnp.int32, (toks, 64), 1) == 0).astype(F32).astype(BF16)
    o_t[:, D:256] = ones_lane
    for ref in (qs, ks, vs, os_):
        ref[...] = jnp.zeros(ref.shape, F32)

    parts[...] = jnp.zeros(parts.shape, F32)
    vec_at[...] = jnp.zeros(vec_at.shape, F32)
    copies_in[2].wait()
    pl.semaphore_wait(pltpu.get_barrier_semaphore(), len(known))
    buf[me, 0:rows, :] = shard[...]
    buf[me, rows:, :] = jnp.zeros((buf.shape[1] - rows, LANES), F32)

    def push(s, send, recvs, where):
        return remote(buf.at[s, mine], buf.at[s, mine], send, recvs.at[s], where)

    def arrived(s, recvs, part):
        remote(buf.at[s, part], buf.at[s, part], g_sib.at[s], recvs.at[s], sibling).wait_recv()

    def forwards(t, s):
        return [push(s, g_fw.at[t, k], g_recv, where) for k, where in enumerate(plane)]

    vec_rows = [
        (s, max(0, VEC_AT - rows * s) // 8 * 8, max(0, VEC_AT - rows * s), min(rows, USED_ROWS - rows * s))
        for s in range(VEC_AT // rows, (USED_ROWS - 1) // rows + 1)
    ]

    def vec_push(j, where, base):
        return [
            remote(vec_in.at[j], vec_in.at[j], vg_send.at[j, base + k], vg_recv.at[j], dev)
            for k, dev in enumerate(where)
        ]

    def vec_arrived(j):
        remote(vec_in.at[j], vec_in.at[j], vg_send.at[j, 0], vg_recv.at[j], sibling).wait_recv()

    for j, (s, a0, _, end) in enumerate(vec_rows):
        @pl.when(me == s)
        def _(j=j, a0=a0, end=end):
            vec_in[j, 0 : end - a0, :] = shard[a0:end, :]
            for copy in vec_push(j, column, 0) + vec_push(j, plane, outer - 1):
                copy.start()

    own_pushes = [push(me, g_col.at[k], g_recv, where) for k, where in enumerate(column)]
    own_pushes += forwards(zo, me)
    for copy in own_pushes:
        copy.start()

    def to_sibling(s):
        return push(s, g_sib.at[s], g_recv_sib, sibling)

    def forward_level(t):
        s = t * inner + pi

        @pl.when(t != zo)
        def _():
            arrived(s, g_recv, mine)
            for copy in forwards(t, s):
                copy.start()
            to_sibling(s).start()

    def pass_level(t):
        for q in around:
            s = t * inner + q
            arrived(s, g_recv, mine)
            to_sibling(s).start()

    def whole_shard(s):
        @pl.when(s != me)
        def _():
            arrived(s, g_recv_sib, theirs)

    def unpack(s):
        flat[rows * s : rows * (s + 1), :] = buf[s, 0:rows, :]

    for j, (s, _, _, _) in enumerate(vec_rows):
        @pl.when((me != s) & (pi == s % inner))
        def _(j=j):
            vec_arrived(j)
            for copy in vec_push(j, plane, outer - 1):
                copy.start()

    for t in range(outer):
        forward_level(t)

    def tokens_of(ref, t, count):
        return split_tokens(
            ref[:, pl.ds(pl.multiple_of(t * D, 128), count * D)].astype(F32), count
        )

    def put_tokens(ref, t, val):
        for half in range(2):
            for k in range(val.shape[0] // n):
                ref.at[half][pl.ds(t + k, n, stride=ROWS), :] = val[
                    n * k : n * (k + 1), 128 * half : 128 * (half + 1)
                ]

    def get_tokens(ref, t, count):
        return jnp.concatenate(
            [
                jnp.concatenate(
                    [ref.at[half][pl.ds(t + k, n, stride=ROWS), :] for half in range(2)], 1
                )
                for k in range(count)
            ],
            0,
        )

    def over_token_chunks(body, width, carry, hook=lambda i: None):
        whole = pairs // width

        def step(i, c):
            hook(i)
            return body(i * (2 * width), 2 * width, c)

        carry = lax.fori_loop(0, whole, step, carry)
        if pairs % width:
            carry = body(whole * 2 * width, 2 * (pairs % width), carry)
        return carry

    def get_rows(ref, start, count):
        return jnp.concatenate([ref[0, pl.ds(start, count), :], ref[1, pl.ds(start, count), :]], 1)

    def put_rows(ref, start, val):
        for half in range(2):
            ref[half, pl.ds(start, val.shape[0]), :] = val[:, 128 * half : 128 * (half + 1)]

    def rows_at(t, count):
        return pl.ds(pl.multiple_of(t * n, 32), count * n)

    copies_in[0].wait()
    for j, (s, a0, begin, end) in enumerate(vec_rows):
        @pl.when(pi != s % inner)
        def _(j=j):
            vec_arrived(j)

        flat[rows * s + begin : rows * s + end, :] = vec_in[j, begin - a0 : end - a0, :]

    ones3 = (lax.broadcasted_iota(jnp.int32, (1, 64), 1) < 3).astype(F32)

    def vec(k):
        a = VEC_AT + 3 * (k // 2)
        zero = ones3 if k in (1, 6) else jnp.zeros((1, 64), F32)
        if k % 2 == 0:
            return jnp.concatenate([flat[a : a + 1, :], flat[a + 1 : a + 2, 0:64], zero], 1)
        return jnp.concatenate([flat[a + 1 : a + 2, 64:128], flat[a + 2 : a + 3, :], zero], 1)

    g1, n1, bq, bv, bo, g2, n2, b2 = [vec(k) for k in range(8)]
    b1 = jnp.concatenate([flat[VEC_AT + 12 + c : VEC_AT + 13 + c, :] for c in range(4)], 1)

    def norm1(t, count, carry):
        at = rows_at(t, count)
        x = tokens_of(x_ref, t, count)
        xh, r = norm_fwd(x)
        xh1[at, :] = xh
        r1[at, :] = r
        hb = (xh * g1 + n1).astype(BF16)
        h[at, :] = hb
        put_tokens(os_, t, hb.astype(F32))
        xb[at, :] = x + bo
        return carry

    over_token_chunks(norm1, WIDTH1, 0)

    def take_dy(t, count, db2):
        dy = tokens_of(dy_ref, t, count)
        dyt[rows_at(t, count), :] = dy.astype(BF16)
        return db2 + rows8(dy)

    zero = jnp.zeros((8, 256), F32)
    copies_in[1].wait()
    db2 = over_token_chunks(take_dy, WIDTH1, zero)

    def bias_rows(b):
        row = lax.broadcasted_iota(jnp.int32, (16, b.shape[1]), 0)
        out = jnp.zeros((16, b.shape[1]), F32)
        for k in range(3):
            part = b.astype(BF16).astype(F32)
            out = jnp.where(row == k, part, out)
            b = b - part
        return out.astype(BF16)

    half_groups = LOCK3 * GROWS

    @pl.loop(0, groups // LOCK3)
    def _(i):
        at = pl.ds(pl.multiple_of(i * half_groups, 16), half_groups)
        hs[at, :] = get_rows(os_, pl.multiple_of(i * half_groups, 8), half_groups).astype(BF16)

    def take_levels(lo, hi):
        for s in range(lo * inner, hi * inner):
            whole_shard(s)
            unpack(s)

    for t in range(late):
        pass_level(t)
    take_levels(0, late)
    for (base, count), ref in zip(MATS[0:2], (wq, wk)):
        load_square(flat, base, count, tmp, ref)
    wq[D : D + 16, :] = bias_rows(bq)

    def pass_v(i):
        @pl.when(i == 1)
        def _():
            for t in range(late, first):
                pass_level(t)

    def dense_qk(t, count, carry):
        hb = h[rows_at(t, count), :]
        put_tokens(qs, t, nn(hb, wq[...]).astype(BF16).astype(F32))
        put_tokens(ks, t, nn(hb, wk[...]).astype(BF16).astype(F32))
        return carry

    over_token_chunks(dense_qk, WIDTH1, 0, pass_v)
    take_levels(late, first)
    load_square(flat, MATS[2][0], MATS[2][1], tmp, wv)
    wv[D : D + 16, :] = bias_rows(bv)

    def dense_v(t, count, carry):
        hb = h[rows_at(t, count), :]
        put_tokens(vs, t, nn(hb, wv[...]).astype(BF16).astype(F32))
        return carry

    over_token_chunks(dense_v, WIDTH1, 0)

    lane3 = lax.rem(lax.broadcasted_iota(jnp.int32, (1, 256), 1), LANES)
    odd_head = lax.rem(lax.broadcasted_iota(jnp.int32, (1, 256), 1) // HEAD_DIM, 2) == 1

    def squeeze(v):
        return jnp.where(
            lane3 < ROWS, v[0:HJ], jnp.where(lane3 < 2 * ROWS, v[HJ : 2 * HJ], v[2 * HJ : 3 * HJ])
        ).reshape(PAIRS, ROWS, 256)

    def by_parity(v):
        v3 = v.reshape(8, 16, 256)
        return jnp.concatenate(
            [(v3 * parity[16 * k : 16 * (k + 1), :][None]).reshape(LANES, 256) for k in range(2)], 0
        )

    def per_query(left, right, b):
        rows2 = jnp.concatenate([left[128 * k + ROWS * b : 128 * k + ROWS * (b + 1)] for k in range(2)], 0)
        both = nn(rows2.astype(BF16), right)
        return jnp.where(odd_head, both[ROWS : 2 * ROWS], both[0:ROWS])

    jrow = lax.broadcasted_iota(jnp.int32, (1, ROWS - 32, 256), 1)
    cexp = math.log2(math.e) / math.sqrt(HEAD_DIM)
    scale = 1.0 / math.sqrt(HEAD_DIM)

    def attn(i, carry):
        @pl.when(i == 1)
        def _():
            for t in range(first, outer):
                pass_level(t)

        r0 = pl.multiple_of(i * (LOCK1 * GROWS), 8)
        base0 = pl.multiple_of(i * (LOCK1 * 3 * HJ), 32)
        p0 = pl.multiple_of(i * (LOCK1 * HJ), 32)
        sets = range(LOCK1)
        qg = [by_parity(get_rows(qs, r0 + GROWS * k, LANES).astype(BF16)) for k in sets]
        for k in sets:
            for src, dst in ((ks, kbd), (vs, vbd)):
                for b in range(GROUP):
                    one = get_rows(src, r0 + GROWS * k + ROWS * b, ROWS)
                    two = jnp.concatenate([one, one], 0).astype(BF16)
                    for p in range(PAIRS // 2):
                        dst[pl.ds(base0 + HJ * (3 * k + b) + 80 * p, 80), :] = (
                            two * hm2[80 * p : 80 * (p + 1), :]
                        )
        st = [squeeze(nt(kbd[pl.ds(base0 + 3 * HJ * k, 3 * HJ), :], qg[k])) for k in sets]
        st = [
            jnp.concatenate([v[:, 0:32], jnp.where(jrow < SEQ - 32, v[:, 32:ROWS], -1e30)], 1)
            for v in st
        ]
        m = [jnp.max(v, 1, keepdims=True) for v in st]
        e = [jnp.exp2((st[k] - m[k]) * cexp) for k in sets]
        l = [1.0 / jnp.sum(v, 1, keepdims=True) for v in e]
        p = [(e[k] * l[k]).reshape(HJ, 256) for k in sets]
        for k in sets:
            psc[pl.ds(p0 + HJ * k, HJ), :] = p[k]
        pt = [v.T for v in p]
        for b in range(GROUP):
            for k in sets:
                ob = per_query(pt[k], vbd[pl.ds(base0 + HJ * (3 * k + b), HJ), :], b)
                put_rows(os_, r0 + GROWS * k + ROWS * b, ob.astype(BF16).astype(F32)[0:SEQ])
        return carry

    lax.fori_loop(0, groups // LOCK1, attn, 0)

    take_levels(first, outer)
    for (base, count), ref in zip(MATS[3:5], (wo, w2)):
        load_square(flat, base, count, tmp, ref)
    for c in range(4):
        part = flat[pl.ds(W1_AT + c, D, stride=4), :]
        w1[0:D, 128 * c : 128 * (c + 1)] = (part if c < 2 else 0.5 * part).astype(BF16)
    w1[D : D + 16, :] = bias_rows(jnp.concatenate([b1[:, 0:FF], 0.5 * b1[:, FF:]], 1))
    w1[D + 16 : 256, :] = jnp.zeros((240 - D, 2 * FF), BF16)
    def dense2(t0, count, carry):
        dg2, dn2 = carry
        at = rows_at(t0, count)
        o = get_tokens(os_, t0, count).astype(BF16)
        o_t[at, 0:D] = o[:, 0:D]
        x2 = xb[at, :] + nn(o, wo[...])
        xh, r = norm_fwd(x2)
        hb = (xh * g2 + n2).astype(BF16)
        h2[at, :] = hb
        u = nn(hb, w1[...])
        gate, up = u[:, :FF], u[:, FF:]
        sq = gate * gate
        t = jnp.tanh(gate * (GELU_C + (GELU_C * 0.044715) * sq))
        t1 = 1.0 + t
        act = gate * t1
        zb = (act * up).astype(BF16)
        z[at, :] = zb
        y = x2 + nn(zb, w2[...]) + b2
        out_ref[:, pl.ds(pl.multiple_of(t0 * D, 128), count * D)] = join_tokens(y, n).astype(BF16)
        dyb = dyt[at, :]
        dyf = dyb.astype(F32)
        dz = nt(dyb, w2[...])
        slope = t1 + act * (1.0 - t) * (GELU_C + (3 * GELU_C * 0.044715) * sq)
        du = jnp.concatenate([(dz * up * slope).astype(BF16), (dz * act).astype(BF16)], 1)
        dul[at, :] = du
        dh = nt(du, w1[...])
        dx2 = dyf + norm_back(dh, xh, r, g2)
        dx2s[at, :] = dx2
        da = dx2.astype(BF16)
        dal[at, :] = da
        put_tokens(os_, t0, nt(da, wo[...]).astype(BF16).astype(F32))
        acc[...] += tn(zb, dyb)
        acc2[...] += tn(hb, du)
        acc3[...] += tn(o_t[at, :], da)
        return dg2 + rows8(dh * xh), dn2 + rows8(dh)

    for ref in (acc, acc2, acc3):
        ref[...] = jnp.zeros(ref.shape, F32)
    dg2, dn2 = over_token_chunks(dense2, WIDTH2, (zero, zero))

    copy_out = pltpu.make_async_copy(out_ref, out_hbm, io_sem.at[2])
    copy_out.start()

    def total(v):
        return jnp.sum(v, 0, keepdims=True)

    def over_tokens(*products):
        for acc, _, _ in products:
            acc[...] = jnp.zeros(acc.shape, F32)
        size = products[0][1].shape[0] // DW_STEPS

        @pl.loop(0, DW_STEPS)
        def _(i):
            at = pl.ds(pl.multiple_of(i * size, 16), size)
            for acc, a, b in products:
                acc[...] += tn(a[at, :], b[at, :])

    store_square(acc[...], gflat, 1920, FF, tmp)
    for c in range(4):
        part = acc2[0 : D + 8, 128 * c : 128 * (c + 1)]
        part = part if c < 2 else 0.5 * part
        gflat[pl.ds(W1_AT + c, D, stride=4), :] = part[0:D]
        vec_own[12 + c : 13 + c, :] = part[D : D + 1]
    store_square(acc3[...], gflat, 864, D, tmp)
    dbo = acc3[D : D + 1, :]

    def pack(lo, hi):
        for s in range(lo * inner, hi * inner):
            stop = min(rows * (s + 1), VEC_AT)
            if stop > rows * s:
                parts[s // inner, s % inner, 0 : stop - rows * s, :] = gflat[rows * s : stop, :]

    places = around + [pi]

    def sib_copies(part, lo, hi):
        return [
            remote(
                parts.at[lo:hi, q, theirs], sib_in.at[lo:hi, q],
                s_send.at[part, k], s_recv.at[part, q], sibling,
            )
            for k, q in enumerate(places)
        ]

    def plane_copies(part, lo, hi):
        return [
            remote(
                out_p.at[k, lo:hi], plane_in.at[pi, lo:hi],
                p_send.at[part, k], p_recv.at[part, pi], plane[k],
            )
            for k in range(inner - 1)
        ]

    def col_copy(t):
        return remote(
            out_c.at[t], col_in.at[zo], c_send.at[t], c_recv.at[zo], (t * inner + pi, core)
        )

    def sum_cores(part):
        lo, hi = bounds[part]
        sends = plane_copies(part, lo, hi)
        for k, q in enumerate(places):
            remote(
                sib_in.at[lo:hi, q], sib_in.at[lo:hi, q],
                s_send.at[part, k], s_recv.at[part, q], sibling,
            ).wait_recv()
            both = parts[lo:hi, q, mine, :] + sib_in[lo:hi, q]
            if k < inner - 1:
                out_p[k, lo:hi] = both
                sends[k].start()
            else:
                plane_in[pi, lo:hi] = both

    def sum_plane(part):
        lo, hi = bounds[part]
        for k, q in enumerate(around):
            remote(
                plane_in.at[q, lo:hi], plane_in.at[q, lo:hi],
                p_send.at[part, k], p_recv.at[part, q], sibling,
            ).wait_recv()
        for t in range(lo, hi):
            line = plane_in[0, t]
            for q in range(1, inner):
                line = line + plane_in[q, t]
            out_c[t] = line

            @pl.when(t != zo)
            def _():
                col_copy(t).start()

    def send_cores(part):
        pack(*bounds[part])
        for copy in sib_copies(part, *bounds[part]):
            copy.start()

    send_cores(0)

    def by_sample(v):
        v = v.reshape(HJ, 256).astype(BF16).reshape(HJ // 16, 16, 256)
        return jnp.concatenate(
            [
                (v * sample[16 * b : 16 * (b + 1), :][None]).reshape(HJ, 256)
                for b in range(GROUP)
            ],
            0,
        )

    pair_lane = lax.broadcasted_iota(jnp.int32, (1, LANES), 1)

    def own_lanes(v):
        v = v.reshape(GROUP, PAIRS, ROWS, 256)
        out = []
        for b in range(GROUP):
            lo = jnp.where(pair_lane < PAIR_DIM, v[b, 0, :, 0:128], v[b, 1, :, 0:128])
            lo = jnp.where(pair_lane < 2 * PAIR_DIM, lo, v[b, 2, :, 0:128])
            hi = jnp.where(
                pair_lane < 3 * PAIR_DIM - 128, v[b, 2, :, 128:256], v[b, 3, :, 128:256]
            )
            out.append(jnp.concatenate([lo, hi], 1))
        return jnp.concatenate(out, 0)

    def probs(at):
        return psc[pl.ds(at, HJ), :].reshape(PAIRS, ROWS, 256)

    def attn_back_v(i, carry):
        @pl.when(i == 3)
        def _():
            sum_cores(0)

        r0 = pl.multiple_of(i * (LOCK3 * GROWS), 8)
        p0 = pl.multiple_of(i * (LOCK3 * HJ), 32)
        out = []
        for k in range(LOCK3):
            dg = by_parity(get_rows(os_, r0 + GROWS * k, LANES).astype(BF16))
            out.append(own_lanes(nn(by_sample(probs(p0 + HJ * k)), dg)))
        out = jnp.concatenate(out, 0).astype(BF16)
        dqkv[pl.ds(pl.multiple_of(i * half_groups, 16), half_groups), 512:768] = out
        put_rows(vs, r0, out.astype(F32))
        return carry

    lax.fori_loop(0, groups // LOCK3, attn_back_v, 0)

    over_tokens((acc, hs, dqkv.at[:, 512:768]))
    store_square(acc[...], gflat, 576, D, tmp)
    dbv = acc[D : D + 1, :]
    send_cores(1)

    def attn_back(i, carry):
        @pl.when(i == 1)
        def _():
            sum_cores(1)

        r0 = pl.multiple_of(i * (LOCK2 * GROWS), 8)
        base0 = pl.multiple_of(i * (LOCK2 * 3 * HJ), 32)
        p0 = pl.multiple_of(i * (LOCK2 * HJ), 32)
        sets = range(LOCK2)
        qg = [by_parity(get_rows(qs, r0 + GROWS * k, LANES).astype(BF16)) for k in sets]
        dg = [by_parity(get_rows(os_, r0 + GROWS * k, LANES).astype(BF16)) for k in sets]
        dp = [squeeze(nt(vbd[pl.ds(base0 + 3 * HJ * k, 3 * HJ), :], dg[k])) for k in sets]
        p = [probs(p0 + HJ * k) for k in sets]
        t = [jnp.sum(p[k] * dp[k], 1, keepdims=True) for k in sets]
        ds = [p[k] * (dp[k] - t[k]) for k in sets]
        dst = [v.reshape(HJ, 256).T for v in ds]
        dk = [own_lanes(nn(by_sample(ds[k]), qg[k])) * scale for k in sets]
        dq = [
            per_query(dst[k], kbd[pl.ds(base0 + HJ * (3 * k + b), HJ), :], b) * scale
            for k in sets
            for b in range(GROUP)
        ]
        at = pl.ds(pl.multiple_of(i * (LOCK2 * GROWS), 16), LOCK2 * GROWS)
        for col, ref, val in ((0, qs, dq), (256, ks, dk)):
            val = jnp.concatenate(val, 0).astype(BF16)
            dqkv[at, col : col + 256] = val
            put_rows(ref, r0, val.astype(F32))
        return carry

    lax.fori_loop(0, groups // LOCK2, attn_back, 0)

    over_tokens((acc2, hs, dqkv.at[:, 0:512]))
    for k in range(2):
        store_square(acc2[:, 256 * k : 256 * (k + 1)], gflat, 288 * k, D, tmp)
    send_cores(2)
    sum_plane(0)

    def dense3(t0, count, carry):
        dg1, dn1 = carry
        at = rows_at(t0, count)
        dh = (
            nt(get_tokens(qs, t0, count).astype(BF16), wq[...])
            + nt(get_tokens(ks, t0, count).astype(BF16), wk[...])
            + nt(get_tokens(vs, t0, count).astype(BF16), wv[...])
        )
        xh = xh1[at, :]
        ig = dx2s[at, :] + norm_back(dh, xh, r1[at, :], g1)
        ig_ref[:, pl.ds(pl.multiple_of(t0 * D, 128), count * D)] = join_tokens(ig, n)
        return dg1 + rows8(dh * xh), dn1 + rows8(dh)

    def hook3(i):
        @pl.when(i == 1)
        def _():
            sum_cores(2)

        @pl.when(i == 2)
        def _():
            sum_plane(1)

    dg1, dn1 = over_token_chunks(dense3, WIDTH3, (zero, zero), hook3)

    vecs = [
        total(dg1), total(dn1), acc2[D : D + 1, 0:256], dbv,
        dbo, total(dg2), total(dn2), total(db2),
    ]
    for k in range(4):
        a, b = vecs[2 * k], vecs[2 * k + 1]
        vec_own[3 * k : 3 * k + 1, :] = a[:, 0:128]
        vec_own[3 * k + 1 : 3 * k + 2, :] = jnp.concatenate([a[:, 128:192], b[:, 0:64]], 1)
        vec_own[3 * k + 2 : 3 * k + 3, :] = b[:, 64:192]
    copy_ig = pltpu.make_async_copy(ig_ref, ig_hbm, io_sem.at[3])
    copy_ig.start()

    def spread(slots, at, sends, recvs, base, where):
        out = [
            remote(slots.at[at], slots.at[at], sends.at[base + k], recvs.at[base + at], dev)
            for k, dev in enumerate(where)
        ]
        for copy in out:
            copy.start()
        return out

    def collected(slots, others, sends, recvs, base):
        for k, q in enumerate(others):
            remote(
                slots.at[q], slots.at[q], sends.at[base + k], recvs.at[base + q], sibling
            ).wait_recv()
        return jnp.sum(slots[...], 0)

    slot = 2 * pi + core
    near = [2 * q + core for q in around] + [2 * q + 1 - core for q in around] + [2 * pi + 1 - core]
    disc = plane + cross + [sibling]
    vec_plane[slot] = vec_own[...]
    vec_sends = spread(vec_plane, slot, v_send, v_recv, 0, disc)
    sum_plane(2)
    vec_col[zo] = collected(vec_plane, near, v_send, v_recv, 0)
    vec_sends += spread(vec_col, zo, v_send, v_recv, 2 * inner, column)

    col_in[zo] = out_c[zo]
    for t in along:
        remote(col_in.at[t], col_in.at[t], c_send.at[t], c_recv.at[t], sibling).wait_recv()
    line = col_in[0]
    for t in range(1, outer):
        line = line + col_in[t]
    res[mine, :] = line
    last = remote(res.at[mine], res.at[mine], f_sem.at[0], f_sem.at[1], sibling)
    last.start()
    sq_plane[slot] = rows8(line * line)
    sq_sends = spread(sq_plane, slot, n_send, n_recv, 0, disc)
    vec = collected(vec_col, along, v_send, v_recv, 2 * inner)
    vec_at[VEC_AT:USED_ROWS, :] = vec
    remote(res.at[theirs], res.at[theirs], f_sem.at[0], f_sem.at[1], sibling).wait_recv()
    own[...] = res[0:rows, :] + vec_at[pl.ds(me * rows, rows), :]
    copy_own = pltpu.make_async_copy(own, own_hbm, io_sem.at[5])
    copy_own.start()
    sq_col[zo] = collected(sq_plane, near, n_send, n_recv, 0)
    sq_sends += spread(sq_col, zo, n_send, n_recv, 2 * inner, column)
    both = collected(sq_col, along, n_send, n_recv, 2 * inner) + rows8(vec * vec)
    squares[...] = jnp.broadcast_to(jnp.sum(both, keepdims=True), squares.shape)

    for copy in own_pushes + vec_sends + sq_sends + [last]:
        copy.wait_send()
    for t in range(outer):
        @pl.when(t != zo)
        def _(t=t):
            for copy in forwards(t, t * inner + pi):
                copy.wait_send()
            to_sibling(t * inner + pi).wait_send()
            col_copy(t).wait_send()

        for q in around:
            to_sibling(t * inner + q).wait_send()
    for j, (s, _, _, _) in enumerate(vec_rows):
        @pl.when(me == s)
        def _(j=j):
            for copy in vec_push(j, column, 0):
                copy.wait_send()

        @pl.when(pi == s % inner)
        def _(j=j):
            for copy in vec_push(j, plane, outer - 1):
                copy.wait_send()

    for part, (lo, hi) in enumerate(bounds):
        for copy in sib_copies(part, lo, hi) + plane_copies(part, lo, hi):
            copy.wait_send()
    copy_out.wait()
    copy_ig.wait()
    copy_own.wait()


def step(x, dy, shard, wide):
    outer, inner = factors(wide)
    n, rows = x.shape[0], shard.shape[0]
    toks = n * SEQ
    groups = n // GROUP
    padded = (rows + 15) // 16 * 16
    half = padded // 2
    vecs = (USED_ROWS - 1) // rows - VEC_AT // rows + 1
    vm, dma = pltpu.VMEM, pltpu.SemaphoreType.DMA
    sm = vm((2, (n + 1) * ROWS, LANES), F32)
    tok = vm((toks, 256), BF16)
    tile = (8, LANES)
    scratch = (
        [vm((rows, LANES), F32)] * 2
        + [vm(x.shape, BF16), vm(x.shape, BF16), vm(x.shape, BF16), vm(x.shape, F32)]
        + [vm((wide * rows, LANES), F32)] * 2
        + [sm] * 4
        + [vm((groups * 3 * HJ, 256), BF16)] * 2
        + [vm((groups * HJ, 256), F32)]
        + [vm((toks, 256), F32)] * 2
        + [vm((toks, 1), F32), vm((toks, 256), F32)]
        + [tok, tok, tok, vm((toks, 2 * FF), BF16), tok]
        + [tok, tok, vm((n * ROWS, 3 * 256), BF16)]
        + [vm((256, 256), BF16)] * 4
        + [vm((256, 2 * FF), BF16), vm((FF, 256), BF16), vm((2, FF + 8, 128), F32)]
        + [vm((HJ, 256), BF16), vm((32, 256), BF16), vm((16 * GROUP, 256), BF16), vm((n * ROWS, 256), BF16)]
        + [vm((256, 256), F32), vm((256, 512), F32), vm((256, 256), F32)]
        + [vm((wide, padded, LANES), F32), vm((outer, inner, padded, LANES), F32)]
        + [vm((outer, inner, half, LANES), F32), vm((inner, outer, half, LANES), F32)]
        + [vm((inner - 1, outer, half, LANES), F32)]
        + [vm((outer, half, LANES), F32)] * 2
        + [vm((padded, LANES), F32)]
        + [vm((16, LANES), F32), vm((2 * inner, 16, LANES), F32), vm((outer, 16, LANES), F32)]
        + [vm((wide * rows, LANES), F32)]
        + [vm((2 * inner, *tile), F32), vm((outer, *tile), F32)]
        + [vm((vecs, min(24, padded), LANES), F32)]
        + [dma((6,)), dma((outer - 1,)), dma((outer, inner - 1)), dma((wide,)), dma((wide,)), dma((wide,))]
        + [dma((3, inner))] * 4
        + [dma((outer,)), dma((outer,)), dma((2,))]
        + [dma((2 * inner + outer,))] * 4
        + [dma((vecs, outer + inner - 2)), dma((vecs,))]
    )
    anywhere, vmem = pl.BlockSpec(memory_space=pl.ANY), pl.BlockSpec(memory_space=pltpu.VMEM)
    return pl.pallas_call(
        functools.partial(step_kernel, wide),
        out_shape=(
            jax.ShapeDtypeStruct(x.shape, BF16),
            jax.ShapeDtypeStruct(x.shape, F32),
            jax.ShapeDtypeStruct((rows, LANES), F32),
            jax.ShapeDtypeStruct(tile, F32),
        ),
        in_specs=[anywhere] * 3,
        out_specs=(anywhere, anywhere, anywhere, vmem),
        scratch_shapes=scratch,
        compiler_params=pltpu.CompilerParams(
            collective_id=0, has_side_effects=True, vmem_limit_bytes=60 * 2**20
        ),
        name="step",
    )(x, dy, shard)


def finish_kernel(*refs):
    big_in, small_in = refs[0:2], refs[2:7]
    big_out, norm_out, small_out = refs[7:9], refs[9], refs[10:15]
    stages, ins, norm, outs = refs[15:17], refs[17:22], refs[22], refs[23:28]
    sem_in, sem_out, sem_small = refs[28:31]
    pieces = []
    for k in range(2):
        size = big_in[k].shape[0] // PIECES
        for p in range(PIECES):
            at = pl.ds(size * p, size)
            pieces.append(
                (
                    pltpu.make_async_copy(big_in[k].at[at], stages[k].at[at], sem_in.at[k, p]),
                    pltpu.make_async_copy(stages[k].at[at], big_out[k].at[at], sem_out.at[k, p]),
                )
            )
    loads = [pltpu.make_async_copy(small_in[k], ins[k], sem_small.at[k]) for k in range(5)]
    for copy in loads:
        copy.start()
    for come, _ in pieces:
        come.start()
    for copy in loads:
        copy.wait()
    own, squares, master, first, second = ins
    clipped, new_master, new_copy, new_first, new_second = outs
    grad_norm = jnp.sqrt(squares[...])
    norm[...] = grad_norm[0:1, 0:1]
    factor = jnp.minimum(1.0, 1.0 / (grad_norm[0:1, :] + 1e-06))
    grad = own[...] * factor
    clipped[...] = grad
    one = 0.5 * first[...] + 0.5 * grad
    two = 0.5 * second[...] + 0.5 * grad * grad
    new_first[...] = one
    new_second[...] = two
    fixed = 1.0 - 0.5**STEP
    old = master[...]
    new = old - 0.05 * ((one / fixed) / (jnp.sqrt(two / fixed) + 1e-08) + 0.1 * old)
    new_master[...] = new
    new_copy[...] = new.astype(BF16)
    stores = [
        pltpu.make_async_copy(src, dst, sem_small.at[5 + k])
        for k, (src, dst) in enumerate(zip((norm, *outs), (norm_out, *small_out)))
    ]
    for copy in stores:
        copy.start()
    for come, go in pieces:
        come.wait()
        go.start()
    for copy in stores:
        copy.wait()
    for _, go in pieces:
        go.wait()


def finish(block_out, input_grad, owned, squares, master, first, second):
    anywhere, vm = pl.BlockSpec(memory_space=pl.ANY), pltpu.VMEM
    one, flat = (1, 1), owned.shape
    kinds = [(flat, F32), (flat, F32), (flat, BF16), (flat, F32), (flat, F32)]
    like = jax.ShapeDtypeStruct
    return pl.pallas_call(
        finish_kernel,
        out_shape=(
            like(block_out.shape, BF16),
            like(input_grad.shape, F32),
            like(one, F32),
            *[like(*kind) for kind in kinds],
        ),
        in_specs=[anywhere] * 7,
        out_specs=(anywhere,) * 8,
        scratch_shapes=[
            vm(block_out.shape, BF16),
            vm(input_grad.shape, F32),
            vm(flat, F32),
            vm(squares.shape, F32),
            vm(flat, F32),
            vm(flat, F32),
            vm(flat, F32),
            vm(one, F32),
            *[vm(*kind) for kind in kinds],
            pltpu.SemaphoreType.DMA((2, PIECES)),
            pltpu.SemaphoreType.DMA((2, PIECES)),
            pltpu.SemaphoreType.DMA((11,)),
        ],
        compiler_params=pltpu.CompilerParams(vmem_limit_bytes=60 * 2**20),
        name="finish",
    )(block_out, input_grad, owned, squares, master, first, second)


def on_device(inputs, cotangent, master, first, second):
    flat = lambda a: a.reshape(-1)
    tall = lambda a: a.reshape(-1, LANES)
    block_out, input_grad, owned, squares = step(
        inputs, cotangent, tall(master), lax.axis_size("wide")
    )
    block_out, input_grad, norm, clipped, new_master, new_copy, new_first, new_second = finish(
        block_out, input_grad, owned, squares, tall(master), tall(first), tall(second)
    )
    return (
        block_out,
        input_grad,
        flat(clipped),
        norm.reshape(()),
        flat(new_master),
        flat(new_copy),
        flat(new_first),
        flat(new_second),
    )


def solution(mesh):
    both, part = P(("wide", "narrow"), None), P("wide")
    return jax.shard_map(
        on_device,
        mesh=mesh,
        in_specs=(both, both, part, part, part),
        out_specs=(both, both, part, P(), part, part, part, part),
        check_vma=False,
    )
```
